32 devices in a mesh: dp: 16 (over z, y, x), tensor: 2 (over core).
Axes of the slice: x: 2, y: 2, z: 4, core: 2. Of those that a mesh axis runs over, the one named last changes fastest.
Arguments:
- tokens: bfloat16 [32768, 512], P(('dp', 'tensor')), may hold values from -6 to 6
- block_ids: int32 [32768], P('dp'), may hold values from 0 to 255, never falling along the last dimension, each value on 1 to 256 neighbouring positions
- ln1_gain: bfloat16 [512], P('dp'), may hold values from 0.5 to 1.5
- ln1_bias: bfloat16 [512], P('dp'), may hold values from -1.5 to 1.5
- w_query: bfloat16 [512, 512], P('dp', 'tensor'), may hold values from -0.25 to 0.25
- w_key: bfloat16 [512, 512], P('dp', 'tensor'), may hold values from -0.25 to 0.25
- w_value: bfloat16 [512, 512], P('dp', 'tensor'), may hold values from -0.25 to 0.25
- w_pos: bfloat16 [512, 512], P('dp', 'tensor'), may hold values from -0.25 to 0.25
- bias_u: bfloat16 [512], P('dp'), may hold values from -2.5 to 2.5
- bias_w: bfloat16 [512], P('dp'), may hold values from -2.5 to 2.5
- w_out: bfloat16 [512, 512], P('tensor', 'dp'), may hold values from -1.5 to 1.5
- ln2_gain: bfloat16 [512], P('dp'), may hold values from 0.5 to 1.5
- ln2_bias: bfloat16 [512], P('dp'), may hold values from -1.5 to 1.5
- w_up: bfloat16 [512, 2048], P('dp', 'tensor'), may hold values from -0.25 to 0.25
- bias_up: bfloat16 [2048], P('dp'), may hold values from -1.5 to 1.5
- w_down: bfloat16 [2048, 512], P('tensor', 'dp'), may hold values from -0.125 to 0.125
- bias_down: bfloat16 [512], P('dp'), may hold values from -1.5 to 1.5
- cotangent: bfloat16 [32768, 512], P(('dp', 'tensor')), may hold values from -6 to 6
Outputs:
- output: bfloat16 [32768, 512], P(('dp', 'tensor'))
- grad_tokens: float32 [32768, 512], P(('dp', 'tensor'))
- grad_ln1_gain: float32 [512], P('dp')
- grad_ln1_bias: float32 [512], P('dp')
- grad_w_query: float32 [512, 512], P('dp', 'tensor')
- grad_w_key: float32 [512, 512], P('dp', 'tensor')
- grad_w_value: float32 [512, 512], P('dp', 'tensor')
- grad_w_pos: float32 [512, 512], P('dp', 'tensor')
- grad_bias_u: float32 [512], P('dp')
- grad_bias_w: float32 [512], P('dp')
- grad_w_out: float32 [512, 512], P('tensor', 'dp')
- grad_ln2_gain: float32 [512], P('dp')
- grad_ln2_bias: float32 [512], P('dp')
- grad_w_up: float32 [512, 2048], P('dp', 'tensor')
- grad_bias_up: float32 [2048], P('dp')
- grad_w_down: float32 [2048, 512], P('tensor', 'dp')
- grad_bias_down: float32 [512], P('dp')
The draws below stay inside these ranges and needn't reach their ends.
Inputs may be any that keep to these rules, and one draw needn't show every extreme that they name: `block_ids`: block ids never fall along the tokens; each block has 1 to 256 tokens, and some block has exactly 256.
All inputs are finite; a program needn't handle non-finite values.
Results may differ from the reference program's by a relative error of at most 0.019.
Values may be sent and summed in bfloat16 or wider, within the bound.
A program may use at most 256 MiB of HBM per device.

```python
import math
import jax
import jax.numpy as jnp
import numpy as np
from jax import lax

D = 512
HEADS = 8
HEAD = 64
FF = 2048
L = 2048
QB = 512
BLK = 256
SEQS = 16
TOKENS = 32768


def spiked(array, stream_key, source, target, parts, factor):
    def block_of(dim):
        return (jnp.arange(array.shape[dim]) // (array.shape[dim] // parts)).reshape((-1,) + (1,) * (array.ndim - 1 - dim))

    near = jax.random.permutation(stream_key, parts)[block_of(target)]
    second = (block_of(target) + parts // 2) % parts
    return jnp.where((block_of(source) == near) | (block_of(source) == second), factor * array, array)


def block_levels(key, dims, split, smallest, high):
    def one(dim, shards_of):
        draws = jax.random.uniform(jax.random.fold_in(jax.random.fold_in(key, 6), dim), (shards_of,), jnp.float32, smallest / len(split), high / len(split))
        return jnp.repeat(jnp.exp(draws), dims[dim] // shards_of).reshape((-1,) + (1,) * (len(dims) - dim - 1))

    gain = one(*split[0])
    for cut in split[1:]:
        gain = gain * one(*cut)
    return gain


def split_up(count, total, reach, slope):
    weights = [(1 << 20) // math.isqrt(grade ** slope) + 1 for grade in range(2, count + 1)]
    rest, counts = total - reach - (count - 1), [1] * (count - 1)
    while rest > 0:
        free = [i for i in range(count - 1) if counts[i] < reach]
        mass, left = sum([weights[i] for i in free]), rest
        for i in free:
            more = min(reach - counts[i], max(1, left * weights[i] // mass), rest)
            counts[i] = counts[i] + more
            rest = rest - more
    return np.array([reach] + counts)


def uneven_parts(rng, number_of, total, most, skew):
    if number_of == 2:
        one = jax.random.randint(rng, (), max(1, total - most), min(most, total - 1) + 1)
        return jnp.stack([one, total - one])
    tallies = jnp.asarray(split_up(number_of, total, most, skew), jnp.int32)
    pairs = (number_of - 1) // 2
    donor, receiver = tallies[1:1 + 2 * pairs:2], tallies[2:2 + 2 * pairs:2]
    margin = jnp.minimum(donor - 1, most - receiver)
    moved = jax.random.randint(jax.random.fold_in(rng, 1), (pairs,), 0, 1 << 20) % (margin + 1)
    tallies = tallies.at[1:1 + 2 * pairs:2].set(donor - moved).at[2:2 + 2 * pairs:2].set(receiver + moved)
    return tallies[jax.random.permutation(jax.random.fold_in(rng, 2), number_of)]


def normal_values(own_key, shape, scale, limit, cuts=(), kind=jnp.bfloat16):
    result = jax.random.normal(own_key, shape, jnp.float32) * scale
    if len(cuts) > 0:
        result = block_levels(own_key, shape, cuts, -0.22, 0.18) * result
    return jnp.clip(result, min=-limit, max=limit).astype(kind)


def noise_with(stream_key, dims, scale, most, cuts, heavy, kind=jnp.bfloat16):
    entries = scale * jax.random.normal(stream_key, dims, jnp.float32)
    if cuts:
        entries = entries * block_levels(stream_key, dims, cuts, -0.22, 0.18)
    return jnp.clip(spiked(entries, jax.random.fold_in(stream_key, 3), *heavy), -most, most).astype(kind)


def setup_inputs(seed: int = 0) -> dict:
    key_list = jax.random.split(jax.random.key(seed), 19)
    tokens = normal_values(key_list[0], (TOKENS, D), 1.0, 6.0, ((0, 32),))
    block_ids = jnp.searchsorted(jnp.cumsum(uneven_parts(key_list[1], TOKENS * 2 // BLK, TOKENS, BLK, 0)), jnp.arange(TOKENS), side="right").astype(jnp.int32)
    ln1_gain = jnp.clip(1.0 + 0.1 * jax.random.normal(key_list[2], (D,), jnp.float32), 0.5, 1.5).astype(jnp.bfloat16)
    ln1_bias = normal_values(key_list[3], (D,), 0.3, 1.5, ((0, 16),))
    w_query = normal_values(key_list[4], (D, D), D ** -0.5, 0.25, ((0, 16), (1, 2)))
    w_key = normal_values(key_list[5], (D, D), D ** -0.5, 0.25, ((0, 16), (1, 2)))
    w_value = normal_values(key_list[6], (D, D), D ** -0.5, 0.25, ((0, 16), (1, 2)))
    w_pos = normal_values(key_list[7], (D, D), D ** -0.5, 0.25, ((0, 16), (1, 2)))
    bias_u = normal_values(key_list[8], (D,), 0.5, 2.5, ((0, 16),))
    bias_w = normal_values(key_list[9], (D,), 0.5, 2.5, ((0, 16),))
    w_out = normal_values(key_list[10], (D, D), (D // 32) ** -0.5, 1.5, ((0, 2), (1, 16)))
    ln2_gain = jnp.clip(1.0 + 0.1 * jax.random.normal(key_list[11], (D,), jnp.float32), 0.5, 1.5).astype(jnp.bfloat16)
    ln2_bias = normal_values(key_list[12], (D,), 0.3, 1.5, ((0, 16),))
    w_up = normal_values(key_list[13], (D, FF), D ** -0.5, 0.25, ((0, 16), (1, 2)))
    bias_up = normal_values(key_list[14], (FF,), 0.3, 1.5, ((0, 16),))
    w_down = normal_values(key_list[15], (FF, D), FF ** -0.5, 0.125, ((0, 2), (1, 16)))
    bias_down = normal_values(key_list[16], (D,), 0.3, 1.5, ((0, 16),))
    cotangent = noise_with(key_list[17], (TOKENS, D), 1.0, 6.0, ((0, 32),), (0, 1, 32, 2.75))
    return {"tokens": tokens, "block_ids": block_ids, "ln1_gain": ln1_gain, "ln1_bias": ln1_bias, "w_query": w_query, "w_key": w_key, "w_value": w_value, "w_pos": w_pos, "bias_u": bias_u, "bias_w": bias_w, "w_out": w_out, "ln2_gain": ln2_gain, "ln2_bias": ln2_bias, "w_up": w_up, "bias_up": bias_up, "w_down": w_down, "bias_down": bias_down, "cotangent": cotangent}


@jax.custom_vjp
def low(v):
    return lax.optimization_barrier(v.astype(jnp.bfloat16)).astype(jnp.float32)

@jax.custom_vjp
def low_back(v):
    return v

def low_keep(v):
    return (low(v), None)

def low_pass(kept, grad):
    return (grad,)

def back_keep(v):
    return (v, None)

def back_low(kept, grad):
    return (low(grad),)
low.defvjp(low_keep, low_pass)
low_back.defvjp(back_keep, back_low)
exact_mode = lax.Precision.HIGHEST

def matmul(left, right):
    return jnp.dot(left, right, precision=exact_mode, preferred_element_type=jnp.float32)

def layer_norm(values, gain_vec, shift_vec):
    center = values - lax.optimization_barrier(jnp.mean(values, axis=-1, keepdims=True))
    spread = lax.optimization_barrier(jnp.mean(center * center, axis=-1, keepdims=True))
    return center * lax.rsqrt(spread + 1e-05) * gain_vec + shift_vec

def sinusoid_table(length, table_width):
    distance = (length - 1 - jnp.arange(2 * length - 1, dtype=jnp.int32)).astype(jnp.float32)
    freqs = jnp.exp(jnp.arange(0, table_width, 2, dtype=jnp.int32).astype(jnp.float32) * (-math.log(10000.0) / table_width))
    angles = distance[:, None] * freqs[None, :]
    return jnp.concatenate([jnp.sin(angles), jnp.cos(angles)], axis=1)

def skew_rows(table, block_rows, length):
    head_count = table.shape[0]
    table_width = table.shape[2]
    flat_rows = table.reshape(head_count, block_rows * table_width)
    shifted = flat_rows[:, block_rows - 1:block_rows - 1 + block_rows * (table_width - 1)]
    return shifted.reshape(head_count, block_rows, table_width - 1)[:, :, :length]

def layer_forward(inputs, block_row, parameters, sin_table):
    gain_one, shift_one, query_mat, key_mat, value_mat, pos_mat, bias_one, bias_two, out_mat, gain_two, shift_two, up_mat, up_shift, down_mat, down_shift = parameters
    normed = low(layer_norm(inputs, gain_one, shift_one))
    queries = low_back(matmul(normed, query_mat))
    key_rows = low(low_back(matmul(normed, key_mat)))
    value_rows = low(low_back(matmul(normed, value_mat)))
    query_u = low(queries + bias_one)
    query_w = low(queries + bias_two)
    rel_keys = low(low_back(matmul(sin_table, pos_mat)))
    key_heads = key_rows.reshape(L, HEADS, HEAD)
    value_heads = value_rows.reshape(L, HEADS, HEAD)
    score_scale = 1.0 / math.sqrt(HEAD)

    def attend(first_row):
        qu_block = lax.dynamic_slice_in_dim(query_u, first_row, QB, 0).reshape(QB, HEADS, HEAD)
        qw_block = lax.dynamic_slice_in_dim(query_w, first_row, QB, 0).reshape(QB, HEADS, HEAD)
        rel_block = lax.dynamic_slice_in_dim(rel_keys, L - QB - first_row, QB + L - 1, 0).reshape(QB + L - 1, HEADS, HEAD)
        content = jnp.einsum('ahd,jhd->haj', qu_block, key_heads, precision=exact_mode)
        position = skew_rows(jnp.einsum('ahd,thd->hat', qw_block, rel_block, precision=exact_mode), QB, L)
        scores = low_back(content + position) * score_scale
        ids_query = lax.dynamic_slice_in_dim(block_row, first_row, QB, 0)
        allowed = block_row[None, :] <= ids_query[:, None]
        scores = jnp.where(allowed[None], scores, -1e+30)
        peak_score = lax.optimization_barrier(jnp.max(scores, axis=-1, keepdims=True))
        attn_probs = jnp.exp(scores - peak_score)
        attn_probs = attn_probs / lax.optimization_barrier(jnp.sum(attn_probs, axis=-1, keepdims=True))
        mixed_heads = jnp.einsum('haj,jhd->ahd', low(attn_probs), value_heads, precision=exact_mode)
        return mixed_heads.reshape(QB, D)
    starts = jnp.arange(L // QB, dtype=jnp.int32) * QB
    mixed_rows = lax.map(jax.checkpoint(attend), starts).reshape(L, D)
    mixed_rows = low(low_back(mixed_rows))
    residual = inputs + low_back(matmul(mixed_rows, out_mat))
    normed_two = low(layer_norm(residual, gain_two, shift_two))
    hidden = low_back(matmul(normed_two, up_mat) + up_shift)
    active = low(jax.nn.gelu(hidden))
    return residual + low_back(matmul(active, down_mat)) + down_shift

def reference(tokens, block_ids, ln1_gain, ln1_bias, w_query, w_key, w_value, w_pos, bias_u, bias_w, w_out, ln2_gain, ln2_bias, w_up, bias_up, w_down, bias_down, cotangent):
    parameters = (ln1_gain.astype(jnp.float32), ln1_bias.astype(jnp.float32), w_query.astype(jnp.float32), w_key.astype(jnp.float32), w_value.astype(jnp.float32), w_pos.astype(jnp.float32), bias_u.astype(jnp.float32), bias_w.astype(jnp.float32), w_out.astype(jnp.float32), ln2_gain.astype(jnp.float32), ln2_bias.astype(jnp.float32), w_up.astype(jnp.float32), bias_up.astype(jnp.float32), w_down.astype(jnp.float32), bias_down.astype(jnp.float32))
    sin_table = low(sinusoid_table(L, D))
    token_seqs = tokens.astype(jnp.float32).reshape(SEQS, L, D)
    cotan_seqs = cotangent.astype(jnp.float32).reshape(SEQS, L, D)
    id_seqs = block_ids.reshape(SEQS, L)

    def one_sequence(totals, sequence_items):
        inputs, block_row, cotan_rows = sequence_items

        def forward_only(input_rows, param_list):
            return layer_forward(input_rows, block_row, param_list, sin_table)
        outputs, pullback = jax.vjp(forward_only, inputs, parameters)
        grad_input, grad_params = pullback(cotan_rows)

        def add_pair(first_term, second_term):
            return first_term + second_term
        return (jax.tree.map(add_pair, totals, grad_params), (outputs, grad_input))
    zero_grads = jax.tree.map(jnp.zeros_like, parameters)
    totals, (outputs, grad_input) = lax.scan(one_sequence, zero_grads, (token_seqs, id_seqs, cotan_seqs))
    return (outputs.reshape(TOKENS, D).astype(jnp.bfloat16), grad_input.reshape(TOKENS, D), totals[0], totals[1], totals[2], totals[3], totals[4], totals[5], totals[6], totals[7], totals[8], totals[9], totals[10], totals[11], totals[12], totals[13], totals[14])
```

```python
import math

import jax
import jax.numpy as jnp
import ml_dtypes
import numpy as np
from jax import lax
from jax.experimental import pallas as pl
from jax.experimental.pallas import tpu as pltpu
from jax.sharding import PartitionSpec as P

D = 512
HEAD = 64
L = 2048


def layer_norm(values, gain_vec, shift_vec):
    center = values - jnp.mean(values, axis=-1, keepdims=True)
    spread = jnp.mean(center * center, axis=-1, keepdims=True)
    return center * lax.rsqrt(spread + 1e-05) * gain_vec + shift_vec


def take_rows(array, first_row, row_count):
    return lax.dynamic_slice_in_dim(array, first_row, row_count, 0)


def take_cols(array, first_col, col_count):
    return lax.dynamic_slice_in_dim(array, first_col, col_count, array.ndim - 1)


def contract_rows(left, right):
    return lax.dot_general(
        left, right, (((0,), (0,)), ((), ())), preferred_element_type=jnp.float32
    )


def times_transpose(left, right):
    return lax.dot_general(
        left, right, (((1,), (1,)), ((), ())), preferred_element_type=jnp.float32
    )


def project_cols(weight, row_data):
    return lax.dot_general(
        weight, row_data, (((0,), (1,)), ((), ())), preferred_element_type=jnp.float32
    )


TILE = 256
TILES = L // TILE
AUG = HEAD + 16
LOG2E = 1.4426950408889634


def tiles_seen(tile):
    return min(tile + 2, TILES)


PACK = [TILE * sum(tiles_seen(t) for t in range(tile)) for tile in range(TILES + 1)]


def angle_table():
    freqs = np.exp(np.arange(0, D, 2, dtype=np.float64) * (-math.log(10000.0) / D))
    angles = np.arange(L, dtype=np.float64)[:, None] * freqs[None, :]
    return np.concatenate([np.cos(angles), np.sin(angles)], axis=1).astype(ml_dtypes.bfloat16)


def dot_nn(left, right):
    return jnp.dot(left, right, preferred_element_type=jnp.float32)


def attend_kernel(qu_ref, qw_ref, key_ref, value_ref, pos_ref, ids_ref, row_ref, col_ref, e_ref, o_ref):
    half = D // 2
    for tile in range(TILES):
        rows = slice(tile * TILE, (tile + 1) * TILE)
        width = tiles_seen(tile) * TILE
        both = contract_rows(qw_ref[:, rows], pos_ref[...])
        part_a, part_b = both[:, :half], both[:, half:]
        cos_i = row_ref[rows, :half].astype(jnp.float32)
        sin_i = row_ref[rows, half:].astype(jnp.float32)
        turned = jnp.concatenate(
            [part_a * sin_i + part_b * cos_i, part_b * sin_i - part_a * cos_i], axis=1
        ).astype(jnp.bfloat16)
        scores = dot_nn(turned, col_ref[:, :width]) + contract_rows(
            qu_ref[:, rows], key_ref[:, :width]
        )
        ids_row = ids_ref[:, tile * TILE : width]
        ids_col = jnp.broadcast_to(ids_row[:, :TILE], (8, TILE)).T[:, :1]
        edge = jnp.where(ids_row <= ids_col, scores[:, tile * TILE :], -1e30)
        if tile:
            scores = jnp.concatenate([scores[:, : tile * TILE], edge], axis=1)
        else:
            scores = edge
        peak = jnp.max(scores, axis=1, keepdims=True)
        weights = jnp.exp2(scores - peak).astype(jnp.bfloat16)
        e_ref[:, PACK[tile] : PACK[tile + 1]] = weights
        o_ref[:, rows] = times_transpose(value_ref[:, :width], weights)


def attend_back_kernel(
    e_ref, qu_ref, qw_ref, key_ref, value_ref, pos_ref, aug_ref, scaled_ref, col_ref,
    dqu_ref, dqw_ref, dk_ref, dv_ref, dpos_ref,
):
    half = D // 2
    dk_ref[...] = jnp.zeros_like(dk_ref)
    dv_ref[...] = jnp.zeros_like(dv_ref)
    for tile in range(TILES):
        rows = slice(tile * TILE, (tile + 1) * TILE)
        width = tiles_seen(tile) * TILE
        weights = e_ref[:, PACK[tile] : PACK[tile + 1]]
        grad_probs = contract_rows(aug_ref[:, rows], value_ref[:, :width])
        grad_scores = (weights.astype(jnp.float32) * grad_probs).astype(jnp.bfloat16)
        dv_ref[:, :width] += dot_nn(scaled_ref[:, rows], weights)
        dk_ref[:, :width] += dot_nn(qu_ref[:, rows], grad_scores)
        dqu_ref[:, rows] = times_transpose(key_ref[:, :width], grad_scores)
        turned = times_transpose(col_ref[:, :width], grad_scores)
        part_c, part_s = turned[:half], turned[half:]
        cos_i = col_ref[:half, rows].astype(jnp.float32)
        sin_i = col_ref[half:, rows].astype(jnp.float32)
        both = jnp.concatenate(
            [part_c * sin_i - part_s * cos_i, part_c * cos_i + part_s * sin_i], axis=0
        ).astype(jnp.bfloat16)
        dqw_ref[:, rows] = dot_nn(pos_ref[...], both)
        here = times_transpose(qw_ref[:, rows], both)
        if tile:
            dpos_ref[...] += here
        else:
            dpos_ref[...] = here


def per_head(rows, cols):
    return pl.BlockSpec((None, rows, cols), lambda h: (h, 0, 0))


def shared(rows, cols):
    return pl.BlockSpec((rows, cols), lambda h: (0, 0))


def attend_all(qu, qw, keys, values, pos, ids, row_table, col_table):
    heads = qu.shape[0]
    f32, bf16 = jnp.float32, jnp.bfloat16
    return pl.pallas_call(
        attend_kernel,
        grid=(heads,),
        in_specs=[per_head(HEAD, L)] * 3
        + [per_head(AUG, L), per_head(HEAD, D), shared(1, L), shared(L, D), shared(D, L)],
        out_specs=[per_head(TILE, PACK[-1]), per_head(AUG, L)],
        out_shape=[
            jax.ShapeDtypeStruct((heads, TILE, PACK[-1]), bf16),
            jax.ShapeDtypeStruct((heads, AUG, L), f32),
        ],
        compiler_params=pltpu.CompilerParams(vmem_limit_bytes=56 * 1024 * 1024),
    )(qu, qw, keys, values, pos, ids, row_table, col_table)


def attend_back_all(weights, qu, qw, keys, values, pos, aug, scaled, col_table):
    heads = qu.shape[0]
    f32 = jnp.float32
    return pl.pallas_call(
        attend_back_kernel,
        grid=(heads,),
        in_specs=[per_head(TILE, PACK[-1])]
        + [per_head(HEAD, L)] * 3
        + [per_head(AUG, L), per_head(HEAD, D), per_head(AUG, L), per_head(HEAD, L), shared(D, L)],
        out_specs=[per_head(HEAD, L)] * 4 + [per_head(HEAD, D)],
        out_shape=[jax.ShapeDtypeStruct((heads, HEAD, L), f32)] * 4
        + [jax.ShapeDtypeStruct((heads, HEAD, D), f32)],
        compiler_params=pltpu.CompilerParams(vmem_limit_bytes=56 * 1024 * 1024),
    )(weights, qu, qw, keys, values, pos, aug, scaled, col_table)


def placed(part_vec, length, offset):
    return lax.dynamic_update_slice_in_dim(jnp.zeros((length,), jnp.float32), part_vec, offset, 0)


def local(
    tokens,
    block_ids,
    ln1_gain,
    ln1_bias,
    w_query,
    w_key,
    w_value,
    w_pos,
    bias_u,
    bias_w,
    w_out,
    ln2_gain,
    ln2_bias,
    w_up,
    bias_up,
    w_down,
    bias_down,
    cotangent,
):
    member = lax.axis_index("tensor")
    gathered = (
        lax.all_gather(ln1_gain, "dp", axis=0, tiled=True),
        lax.all_gather(ln1_bias, "dp", axis=0, tiled=True),
        lax.all_gather(w_query, "dp", axis=0, tiled=True),
        lax.all_gather(w_key, "dp", axis=0, tiled=True),
        lax.all_gather(w_value, "dp", axis=0, tiled=True),
        lax.all_gather(w_pos, "dp", axis=0, tiled=True),
        lax.all_gather(bias_u, "dp", axis=0, tiled=True),
        lax.all_gather(bias_w, "dp", axis=0, tiled=True),
        lax.all_gather(w_out, "dp", axis=1, tiled=True),
        lax.all_gather(ln2_gain, "dp", axis=0, tiled=True),
        lax.all_gather(ln2_bias, "dp", axis=0, tiled=True),
        lax.all_gather(w_up, "dp", axis=0, tiled=True),
        lax.all_gather(bias_up, "dp", axis=0, tiled=True),
        lax.all_gather(w_down, "dp", axis=1, tiled=True),
        lax.all_gather(bias_down, "dp", axis=0, tiled=True),
    )
    (
        gain_one,
        shift_one,
        query_mat,
        key_mat,
        value_mat,
        pos_mat,
        bias_one,
        bias_two,
        out_mat,
        gain_two,
        shift_two,
        up_mat,
        up_shift,
        down_mat,
        down_shift,
    ) = gathered
    gain_one = gain_one.astype(jnp.float32)
    shift_one = shift_one.astype(jnp.float32)
    gain_two = gain_two.astype(jnp.float32)
    shift_two = shift_two.astype(jnp.float32)
    local_width = query_mat.shape[1]
    head_count = local_width // HEAD
    hidden_local = up_mat.shape[1]
    full_hidden = up_shift.shape[0]
    own_u = lax.dynamic_slice_in_dim(
        bias_one.astype(jnp.float32), member * local_width, local_width
    )
    own_w = lax.dynamic_slice_in_dim(
        bias_two.astype(jnp.float32), member * local_width, local_width
    )
    score_scale = 1.0 / math.sqrt(HEAD)
    own_rows = tokens.shape[0]
    inputs = tokens.astype(jnp.float32)
    normed = layer_norm(inputs, gain_one, shift_one)
    rows_all = lax.all_gather(normed.astype(jnp.bfloat16), "tensor", axis=0, tiled=True)
    total_rows = rows_all.shape[0]
    queries_t = project_cols(query_mat, rows_all)
    def heads_of(array):
        return array.astype(jnp.bfloat16).reshape(head_count, HEAD, array.shape[-1])

    ids = block_ids.reshape(1, total_rows)
    sum_u = queries_t + own_u[:, None]
    sum_w = queries_t + own_w[:, None]
    fold = score_scale * LOG2E
    query_u = heads_of(sum_u)
    query_w = heads_of(sum_w)
    key_rows = heads_of(project_cols(key_mat, rows_all))
    ones = jnp.ones((head_count, 2, total_rows), jnp.bfloat16)
    blank = jnp.zeros((head_count, AUG - HEAD - 2, total_rows), jnp.bfloat16)
    value_rows = jnp.concatenate(
        [heads_of(project_cols(value_mat, rows_all)), ones, blank], axis=1
    )
    pos_rows = pos_mat.T.reshape(head_count, HEAD, D)
    table = angle_table()
    row_table = jnp.asarray(table)
    col_table = jnp.asarray(np.ascontiguousarray(table.T))
    weights, mixed_sums = attend_all(
        heads_of(sum_u * fold), heads_of(sum_w * fold), key_rows, value_rows, pos_rows, ids,
        row_table, col_table,
    )
    inv_total = 1.0 / mixed_sums[:, HEAD : HEAD + 1]
    mixed_full = mixed_sums[:, :HEAD] * inv_total
    mixed_cols = mixed_full.reshape(local_width, total_rows).astype(jnp.bfloat16)
    residual = inputs + lax.psum_scatter(
        contract_rows(
            take_cols(mixed_cols, jnp.int32(0), own_rows * lax.axis_size("tensor")), out_mat
        ).astype(jnp.bfloat16),
        "tensor",
        scatter_dimension=0,
        tiled=True,
    ).astype(jnp.float32)
    normed_two = layer_norm(residual, gain_two, shift_two)
    grad_output = cotangent.astype(jnp.float32)
    grad_down_bias = placed(jnp.sum(grad_output, axis=0), D, 0)
    own_up = lax.dynamic_slice_in_dim(
        up_shift.astype(jnp.float32), member * hidden_local, hidden_local
    )
    rows_two = lax.all_gather(normed_two.astype(jnp.bfloat16), "tensor", axis=0, tiled=True)
    hidden = jnp.dot(rows_two, up_mat, preferred_element_type=jnp.float32) + own_up
    active = jax.nn.gelu(hidden).astype(jnp.bfloat16)
    output = (
        residual
        + lax.psum_scatter(
            jnp.dot(
                take_rows(active, jnp.int32(0), own_rows * lax.axis_size("tensor")),
                down_mat,
                preferred_element_type=jnp.float32,
            ).astype(jnp.bfloat16),
            "tensor",
            scatter_dimension=0,
            tiled=True,
        ).astype(jnp.float32)
        + down_shift.astype(jnp.float32)
    )
    grad_full = lax.all_gather(cotangent, "tensor", axis=0, tiled=True)
    grad_active = times_transpose(grad_full, down_mat)
    grad_down = contract_rows(active, grad_full)
    gelu_back = jax.vjp(jax.nn.gelu, hidden)[1]
    grad_hidden = gelu_back(grad_active)[0].astype(jnp.bfloat16)
    grad_up_bias = placed(
        jnp.sum(grad_hidden, axis=0, dtype=jnp.float32), full_hidden, member * hidden_local
    )
    grad_up = contract_rows(rows_two, grad_hidden)
    grad_normed_two = lax.psum_scatter(
        times_transpose(
            take_rows(grad_hidden, jnp.int32(0), own_rows * lax.axis_size("tensor")), up_mat
        ).astype(jnp.bfloat16),
        "tensor",
        scatter_dimension=0,
        tiled=True,
    ).astype(jnp.float32)
    norm_back_two = jax.vjp(layer_norm, residual, gain_two, shift_two)[1]
    grad_resid_part, grad_gain_two, grad_shift_two = norm_back_two(grad_normed_two)
    grad_residual = grad_output + grad_resid_part
    ffn_terms = (grad_gain_two, grad_shift_two, grad_up, grad_up_bias, grad_down, grad_down_bias)
    grad_att = lax.all_gather(grad_residual.astype(jnp.bfloat16), "tensor", axis=0, tiled=True)
    grad_out_mat = jnp.dot(mixed_cols, grad_att, preferred_element_type=jnp.float32)
    grad_mixed = (
        times_transpose(out_mat, grad_att)
        .astype(jnp.bfloat16)
        .reshape(head_count, HEAD, total_rows)
    )
    grad_mixed = grad_mixed.astype(jnp.float32)
    grad_scaled = (grad_mixed * inv_total).astype(jnp.bfloat16)
    grad_low = (grad_mixed * (inv_total * score_scale)).astype(jnp.bfloat16)
    inner = -jnp.sum(grad_low.astype(jnp.float32) * mixed_full, axis=1, keepdims=True)
    inner_high = inner.astype(jnp.bfloat16)
    inner_rest = (inner - inner_high.astype(jnp.float32)).astype(jnp.bfloat16)
    grad_aug = jnp.concatenate([grad_low, inner_high, inner_rest, blank], axis=1)
    dqu, dqw, dk, dv, dpos = attend_back_all(
        weights, query_u, query_w, key_rows, value_rows, pos_rows, grad_aug, grad_scaled, col_table
    )
    grad_keys_all = dk.reshape(local_width, total_rows).astype(jnp.bfloat16)
    grad_values_all = dv.reshape(local_width, total_rows).astype(jnp.bfloat16)
    grad_pos = dpos.reshape(local_width, D).T
    grad_query_u = dqu.reshape(local_width, total_rows)
    grad_query_w = dqw.reshape(local_width, total_rows)
    grad_bias_one = placed(jnp.sum(grad_query_u, axis=1), D, member * local_width)
    grad_bias_two = placed(jnp.sum(grad_query_w, axis=1), D, member * local_width)
    grad_query = (grad_query_u + grad_query_w).astype(jnp.bfloat16)
    grad_query_mat = times_transpose(rows_all.T, grad_query)
    grad_key_mat = times_transpose(rows_all.T, grad_keys_all)
    grad_value_mat = times_transpose(rows_all.T, grad_values_all)
    first_row = jnp.int32(0)
    part_sum = times_transpose(
        take_cols(grad_query, first_row, own_rows * lax.axis_size("tensor")).T, query_mat
    )
    part_sum = part_sum + times_transpose(
        take_cols(grad_keys_all, first_row, own_rows * lax.axis_size("tensor")).T, key_mat
    )
    grad_normed = lax.psum_scatter(
        (
            part_sum
            + times_transpose(
                take_cols(grad_values_all, first_row, own_rows * lax.axis_size("tensor")).T,
                value_mat,
            )
        ).astype(jnp.bfloat16),
        "tensor",
        scatter_dimension=0,
        tiled=True,
    ).astype(jnp.float32)
    norm_back_one = jax.vjp(layer_norm, inputs, gain_one, shift_one)[1]
    grad_in_part, grad_gain_one, grad_shift_one = norm_back_one(grad_normed)
    grad_tokens = grad_residual + grad_in_part
    shards = (
        lax.psum_scatter(grad_gain_one, "dp", scatter_dimension=0, tiled=True),
        lax.psum_scatter(grad_shift_one, "dp", scatter_dimension=0, tiled=True),
        lax.psum_scatter(grad_query_mat, "dp", scatter_dimension=0, tiled=True),
        lax.psum_scatter(grad_key_mat, "dp", scatter_dimension=0, tiled=True),
        lax.psum_scatter(grad_value_mat, "dp", scatter_dimension=0, tiled=True),
        lax.psum_scatter(grad_pos, "dp", scatter_dimension=0, tiled=True),
        lax.psum_scatter(grad_bias_one, "dp", scatter_dimension=0, tiled=True),
        lax.psum_scatter(grad_bias_two, "dp", scatter_dimension=0, tiled=True),
        lax.psum_scatter(grad_out_mat, "dp", scatter_dimension=1, tiled=True),
        lax.psum_scatter(ffn_terms[0], "dp", scatter_dimension=0, tiled=True),
        lax.psum_scatter(ffn_terms[1], "dp", scatter_dimension=0, tiled=True),
        lax.psum_scatter(ffn_terms[2], "dp", scatter_dimension=0, tiled=True),
        lax.psum_scatter(ffn_terms[3], "dp", scatter_dimension=0, tiled=True),
        lax.psum_scatter(ffn_terms[4], "dp", scatter_dimension=1, tiled=True),
        lax.psum_scatter(ffn_terms[5], "dp", scatter_dimension=0, tiled=True),
    )
    summed = lax.psum(
        (shards[0], shards[1], shards[6], shards[7], shards[9], shards[10], shards[12], shards[14]),
        "tensor",
    )
    return (
        output.astype(jnp.bfloat16),
        grad_tokens,
        summed[0],
        summed[1],
        shards[2],
        shards[3],
        shards[4],
        shards[5],
        summed[2],
        summed[3],
        shards[8],
        summed[4],
        summed[5],
        shards[11],
        summed[6],
        shards[13],
        summed[7],
    )


def solution(mesh):
    in_specs = (
        P(("dp", "tensor"), None),
        P("dp"),
        P("dp"),
        P("dp"),
        P("dp", "tensor"),
        P("dp", "tensor"),
        P("dp", "tensor"),
        P("dp", "tensor"),
        P("dp"),
        P("dp"),
        P("tensor", "dp"),
        P("dp"),
        P("dp"),
        P("dp", "tensor"),
        P("dp"),
        P("tensor", "dp"),
        P("dp"),
        P(("dp", "tensor"), None),
    )
    out_specs = (
        P(("dp", "tensor"), None),
        P(("dp", "tensor"), None),
        P("dp"),
        P("dp"),
        P("dp", "tensor"),
        P("dp", "tensor"),
        P("dp", "tensor"),
        P("dp", "tensor"),
        P("dp"),
        P("dp"),
        P("tensor", "dp"),
        P("dp"),
        P("dp"),
        P("dp", "tensor"),
        P("dp"),
        P("tensor", "dp"),
        P("dp"),
    )
    return jax.shard_map(local, mesh=mesh, in_specs=in_specs, out_specs=out_specs, check_vma=False)
```

```python
import math

import jax
import jax.numpy as jnp
import ml_dtypes
import numpy as np
from jax import lax
from jax.experimental import pallas as pl
from jax.experimental.pallas import tpu as pltpu
from jax.sharding import PartitionSpec as P

D = 512
HEAD = 64
L = 2048


MESH = pl.DeviceIdType.MESH
VECS = 128


def peer_at(offset):
    count = lax.axis_size("dp")
    return lax.rem(lax.axis_index("dp") + offset, count)


def greet_all(count):
    barrier = pltpu.get_barrier_semaphore()

    def greet(offset, carry):
        pl.semaphore_signal(
            barrier, inc=1, device_id={"dp": peer_at(offset)}, device_id_type=MESH
        )
        return carry

    lax.fori_loop(1, count, greet, 0)
    pl.semaphore_wait(barrier, count - 1)


def gather_kernel(count, part_refs, whole_refs, send_sems, recv_sems, own_sems):
    me = lax.axis_index("dp")

    def copy_to(index, offset):
        part, whole = part_refs[index], whole_refs[index]
        rows = part.shape[0]
        start = pl.multiple_of(me * rows, rows)
        return pltpu.make_async_remote_copy(
            src_ref=part,
            dst_ref=whole.at[pl.ds(start, rows)],
            send_sem=send_sems.at[index, offset - 1],
            recv_sem=recv_sems.at[index, offset - 1],
            device_id={"dp": peer_at(offset)},
            device_id_type=MESH,
        )

    greet_all(count)
    for index in range(len(part_refs)):

        def begin(offset, carry):
            copy_to(index, offset).start()
            return carry

        lax.fori_loop(1, count, begin, 0)
    for index, (part, whole) in enumerate(zip(part_refs, whole_refs)):
        rows = part.shape[0]
        start = pl.multiple_of(me * rows, rows)
        own = pltpu.make_async_copy(part, whole.at[pl.ds(start, rows)], own_sems.at[index])
        own.start()
        own.wait()

        def finish(offset, carry):
            copy_to(index, offset).wait()
            return carry

        lax.fori_loop(1, count, finish, 0)


def gather_all(parts):
    count = lax.axis_size("dp")
    number = len(parts)

    def body(*refs):
        gather_kernel(count, refs[:number], refs[number : 2 * number], *refs[2 * number :])

    return pl.pallas_call(
        body,
        in_specs=[pl.BlockSpec(memory_space=pltpu.VMEM)] * number,
        out_specs=[pl.BlockSpec(memory_space=pltpu.VMEM)] * number,
        out_shape=[
            jax.ShapeDtypeStruct((count * part.shape[0], part.shape[1]), part.dtype)
            for part in parts
        ],
        scratch_shapes=[
            pltpu.SemaphoreType.DMA((number, count - 1)),
            pltpu.SemaphoreType.DMA((number, count - 1)),
            pltpu.SemaphoreType.DMA((number,)),
        ],
        compiler_params=pltpu.CompilerParams(collective_id=0, has_side_effects=True),
    )(*parts)


def scatter_kernel(count, whole_refs, out_refs, slot_refs, send_sems, recv_sems):
    me = lax.axis_index("dp")

    def copy_to(index, offset):
        rows = out_refs[index].shape[0]
        peer = peer_at(offset)
        return pltpu.make_async_remote_copy(
            src_ref=whole_refs[index].at[pl.ds(pl.multiple_of(peer * rows, rows), rows)],
            dst_ref=slot_refs[index].at[offset - 1],
            send_sem=send_sems.at[index, offset - 1],
            recv_sem=recv_sems.at[index, offset - 1],
            device_id={"dp": peer},
            device_id_type=MESH,
        )

    greet_all(count)
    for index in range(len(out_refs)):

        def begin(offset, carry):
            copy_to(index, offset).start()
            return carry

        lax.fori_loop(1, count, begin, 0)
    for index, out in enumerate(out_refs):
        rows = out.shape[0]
        start = pl.multiple_of(me * rows, rows)
        out[...] = whole_refs[index][pl.ds(start, rows), :].astype(jnp.float32)

        def finish(offset, carry):
            copy_to(index, offset).wait()
            out[...] += slot_refs[index][offset - 1].astype(jnp.float32)
            return carry

        lax.fori_loop(1, count, finish, 0)


def scatter_all(wholes):
    count = lax.axis_size("dp")
    number = len(wholes)

    def body(*refs):
        scatter_kernel(
            count, refs[:number], refs[number : 2 * number], refs[2 * number : 3 * number],
            *refs[3 * number :]
        )

    return pl.pallas_call(
        body,
        in_specs=[pl.BlockSpec(memory_space=pltpu.VMEM)] * number,
        out_specs=[pl.BlockSpec(memory_space=pltpu.VMEM)] * number,
        out_shape=[
            jax.ShapeDtypeStruct((whole.shape[0] // count, whole.shape[1]), jnp.float32)
            for whole in wholes
        ],
        scratch_shapes=[
            pltpu.VMEM((count - 1, whole.shape[0] // count, whole.shape[1]), whole.dtype)
            for whole in wholes
        ]
        + [
            pltpu.SemaphoreType.DMA((number, count - 1)),
            pltpu.SemaphoreType.DMA((number, count - 1)),
        ],
        compiler_params=pltpu.CompilerParams(
            collective_id=1, has_side_effects=True, vmem_limit_bytes=40 * 1024 * 1024
        ),
    )(*wholes)


def layer_norm(values, gain_vec, shift_vec):
    center = values - jnp.mean(values, axis=-1, keepdims=True)
    spread = jnp.mean(center * center, axis=-1, keepdims=True)
    return center * lax.rsqrt(spread + 1e-05) * gain_vec + shift_vec


def take_rows(array, first_row, row_count):
    return lax.dynamic_slice_in_dim(array, first_row, row_count, 0)


def take_cols(array, first_col, col_count):
    return lax.dynamic_slice_in_dim(array, first_col, col_count, array.ndim - 1)


def contract_rows(left, right):
    return lax.dot_general(
        left, right, (((0,), (0,)), ((), ())), preferred_element_type=jnp.float32
    )


def times_transpose(left, right):
    return lax.dot_general(
        left, right, (((1,), (1,)), ((), ())), preferred_element_type=jnp.float32
    )


def project_cols(weight, row_data):
    return lax.dot_general(
        weight, row_data, (((0,), (1,)), ((), ())), preferred_element_type=jnp.float32
    )


TILE = 256
TILES = L // TILE
AUG = HEAD + 16
LOG2E = 1.4426950408889634


def tiles_seen(tile):
    return min(tile + 2, TILES)


PACK = [TILE * sum(tiles_seen(t) for t in range(tile)) for tile in range(TILES + 1)]


def angle_table():
    freqs = np.exp(np.arange(0, D, 2, dtype=np.float64) * (-math.log(10000.0) / D))
    angles = np.arange(L, dtype=np.float64)[:, None] * freqs[None, :]
    return np.concatenate([np.cos(angles), np.sin(angles)], axis=1).astype(ml_dtypes.bfloat16)


def dot_nn(left, right):
    return jnp.dot(left, right, preferred_element_type=jnp.float32)


def attend_kernel(qu_ref, qw_ref, key_ref, value_ref, pos_ref, ids_ref, row_ref, col_ref, e_ref, o_ref):
    half = D // 2
    for tile in range(TILES):
        rows = slice(tile * TILE, (tile + 1) * TILE)
        width = tiles_seen(tile) * TILE
        both = contract_rows(qw_ref[:, rows], pos_ref[...])
        part_a, part_b = both[:, :half], both[:, half:]
        cos_i = row_ref[rows, :half].astype(jnp.float32)
        sin_i = row_ref[rows, half:].astype(jnp.float32)
        turned = jnp.concatenate(
            [part_a * sin_i + part_b * cos_i, part_b * sin_i - part_a * cos_i], axis=1
        ).astype(jnp.bfloat16)
        scores = dot_nn(turned, col_ref[:, :width]) + contract_rows(
            qu_ref[:, rows], key_ref[:, :width]
        )
        ids_row = ids_ref[:, tile * TILE : width]
        ids_col = jnp.broadcast_to(ids_row[:, :TILE], (8, TILE)).T[:, :1]
        edge = jnp.where(ids_row <= ids_col, scores[:, tile * TILE :], -1e30)
        if tile:
            scores = jnp.concatenate([scores[:, : tile * TILE], edge], axis=1)
        else:
            scores = edge
        peak = jnp.max(scores, axis=1, keepdims=True)
        weights = jnp.exp2(scores - peak).astype(jnp.bfloat16)
        e_ref[:, PACK[tile] : PACK[tile + 1]] = weights
        o_ref[:, rows] = times_transpose(value_ref[:, :width], weights)


def attend_back_kernel(
    e_ref, qu_ref, qw_ref, key_ref, value_ref, pos_ref, aug_ref, scaled_ref, col_ref,
    dqu_ref, dqw_ref, dk_ref, dv_ref, dpos_ref,
):
    half = D // 2
    dk_ref[...] = jnp.zeros_like(dk_ref)
    dv_ref[...] = jnp.zeros_like(dv_ref)
    for tile in range(TILES):
        rows = slice(tile * TILE, (tile + 1) * TILE)
        width = tiles_seen(tile) * TILE
        weights = e_ref[:, PACK[tile] : PACK[tile + 1]]
        grad_probs = contract_rows(aug_ref[:, rows], value_ref[:, :width])
        grad_scores = (weights.astype(jnp.float32) * grad_probs).astype(jnp.bfloat16)
        dv_ref[:, :width] += dot_nn(scaled_ref[:, rows], weights)
        dk_ref[:, :width] += dot_nn(qu_ref[:, rows], grad_scores)
        dqu_ref[:, rows] = times_transpose(key_ref[:, :width], grad_scores)
        turned = times_transpose(col_ref[:, :width], grad_scores)
        part_c, part_s = turned[:half], turned[half:]
        cos_i = col_ref[:half, rows].astype(jnp.float32)
        sin_i = col_ref[half:, rows].astype(jnp.float32)
        both = jnp.concatenate(
            [part_c * sin_i - part_s * cos_i, part_c * cos_i + part_s * sin_i], axis=0
        ).astype(jnp.bfloat16)
        dqw_ref[:, rows] = dot_nn(pos_ref[...], both)
        here = times_transpose(qw_ref[:, rows], both)
        if tile:
            dpos_ref[...] += here
        else:
            dpos_ref[...] = here


def per_head(rows, cols):
    return pl.BlockSpec((None, rows, cols), lambda h: (h, 0, 0))


def shared(rows, cols):
    return pl.BlockSpec((rows, cols), lambda h: (0, 0))


def attend_all(qu, qw, keys, values, pos, ids, row_table, col_table):
    heads = qu.shape[0]
    f32, bf16 = jnp.float32, jnp.bfloat16
    return pl.pallas_call(
        attend_kernel,
        grid=(heads,),
        in_specs=[per_head(HEAD, L)] * 3
        + [per_head(AUG, L), per_head(HEAD, D), shared(1, L), shared(L, D), shared(D, L)],
        out_specs=[per_head(TILE, PACK[-1]), per_head(AUG, L)],
        out_shape=[
            jax.ShapeDtypeStruct((heads, TILE, PACK[-1]), bf16),
            jax.ShapeDtypeStruct((heads, AUG, L), f32),
        ],
        compiler_params=pltpu.CompilerParams(vmem_limit_bytes=56 * 1024 * 1024),
    )(qu, qw, keys, values, pos, ids, row_table, col_table)


def attend_back_all(weights, qu, qw, keys, values, pos, aug, scaled, col_table):
    heads = qu.shape[0]
    f32 = jnp.float32
    return pl.pallas_call(
        attend_back_kernel,
        grid=(heads,),
        in_specs=[per_head(TILE, PACK[-1])]
        + [per_head(HEAD, L)] * 3
        + [per_head(AUG, L), per_head(HEAD, D), per_head(AUG, L), per_head(HEAD, L), shared(D, L)],
        out_specs=[per_head(HEAD, L)] * 4 + [per_head(HEAD, D)],
        out_shape=[jax.ShapeDtypeStruct((heads, HEAD, L), f32)] * 4
        + [jax.ShapeDtypeStruct((heads, HEAD, D), f32)],
        compiler_params=pltpu.CompilerParams(vmem_limit_bytes=56 * 1024 * 1024),
    )(weights, qu, qw, keys, values, pos, aug, scaled, col_table)


def placed(part_vec, length, offset):
    return lax.dynamic_update_slice_in_dim(jnp.zeros((length,), jnp.float32), part_vec, offset, 0)


def local(
    tokens,
    block_ids,
    ln1_gain,
    ln1_bias,
    w_query,
    w_key,
    w_value,
    w_pos,
    bias_u,
    bias_w,
    w_out,
    ln2_gain,
    ln2_bias,
    w_up,
    bias_up,
    w_down,
    bias_down,
    cotangent,
):
    member = lax.axis_index("tensor")
    shard_rows = w_query.shape[0]
    direct = shard_rows % 16 == 0
    squares = (w_query, w_key, w_value, w_pos, w_out.T)
    wide = (w_up, w_down.T)
    vectors = (ln1_gain, ln1_bias, bias_u, bias_w, ln2_gain, ln2_bias, bias_down)
    if direct:
        columns = jnp.stack(vectors, axis=1)
        columns = jnp.pad(columns, ((0, 0), (0, VECS - len(vectors))))
        up_row = jnp.pad(bias_up.reshape(1, -1), ((0, 15), (0, 0)))
        near, far, up_rows = gather_all(
            [jnp.concatenate(squares + (columns,), axis=1), jnp.concatenate(wide, axis=1), up_row]
        )
        near_mats = jnp.split(near[:, : -VECS], len(squares), axis=1)
        far_mats = jnp.split(far, len(wide), axis=1)
        vec_rows = near[:, -VECS:].T
        full_vecs = [vec_rows[v] for v in range(len(vectors))]
        up_shift = up_rows.reshape(-1, 16, up_rows.shape[1])[:, 0].reshape(-1)
    else:
        near_mats = [lax.all_gather(m, "dp", axis=0, tiled=True) for m in squares]
        far_mats = [lax.all_gather(m, "dp", axis=0, tiled=True) for m in wide]
        full_vecs = [lax.all_gather(v, "dp", axis=0, tiled=True) for v in vectors]
        up_shift = lax.all_gather(bias_up, "dp", axis=0, tiled=True)
    query_mat, key_mat, value_mat, pos_mat, out_back = near_mats
    out_mat = out_back.T
    up_mat, down_back = far_mats
    down_mat = down_back.T
    gain_one, shift_one, bias_one, bias_two, gain_two, shift_two, down_shift = full_vecs
    gain_one = gain_one.astype(jnp.float32)
    shift_one = shift_one.astype(jnp.float32)
    gain_two = gain_two.astype(jnp.float32)
    shift_two = shift_two.astype(jnp.float32)
    local_width = query_mat.shape[1]
    head_count = local_width // HEAD
    hidden_local = up_mat.shape[1]
    full_hidden = up_shift.shape[0]
    own_u = lax.dynamic_slice_in_dim(
        bias_one.astype(jnp.float32), member * local_width, local_width
    )
    own_w = lax.dynamic_slice_in_dim(
        bias_two.astype(jnp.float32), member * local_width, local_width
    )
    score_scale = 1.0 / math.sqrt(HEAD)
    own_rows = tokens.shape[0]
    inputs = tokens.astype(jnp.float32)
    normed = layer_norm(inputs, gain_one, shift_one)
    rows_all = lax.all_gather(normed.astype(jnp.bfloat16), "tensor", axis=0, tiled=True)
    total_rows = rows_all.shape[0]
    queries_t = project_cols(query_mat, rows_all)
    def heads_of(array):
        return array.astype(jnp.bfloat16).reshape(head_count, HEAD, array.shape[-1])

    ids = block_ids.reshape(1, total_rows)
    sum_u = queries_t + own_u[:, None]
    sum_w = queries_t + own_w[:, None]
    fold = score_scale * LOG2E
    query_u = heads_of(sum_u)
    query_w = heads_of(sum_w)
    key_rows = heads_of(project_cols(key_mat, rows_all))
    ones = jnp.ones((head_count, 2, total_rows), jnp.bfloat16)
    blank = jnp.zeros((head_count, AUG - HEAD - 2, total_rows), jnp.bfloat16)
    value_rows = jnp.concatenate(
        [heads_of(project_cols(value_mat, rows_all)), ones, blank], axis=1
    )
    pos_rows = pos_mat.T.reshape(head_count, HEAD, D)
    table = angle_table()
    row_table = jnp.asarray(table)
    col_table = jnp.asarray(np.ascontiguousarray(table.T))
    weights, mixed_sums = attend_all(
        heads_of(sum_u * fold), heads_of(sum_w * fold), key_rows, value_rows, pos_rows, ids,
        row_table, col_table,
    )
    inv_total = 1.0 / mixed_sums[:, HEAD : HEAD + 1]
    mixed_full = mixed_sums[:, :HEAD] * inv_total
    mixed_cols = mixed_full.reshape(local_width, total_rows).astype(jnp.bfloat16)
    residual = inputs + lax.psum_scatter(
        contract_rows(
            take_cols(mixed_cols, jnp.int32(0), own_rows * lax.axis_size("tensor")), out_mat
        ).astype(jnp.bfloat16),
        "tensor",
        scatter_dimension=0,
        tiled=True,
    ).astype(jnp.float32)
    normed_two = layer_norm(residual, gain_two, shift_two)
    grad_output = cotangent.astype(jnp.float32)
    grad_down_bias = placed(jnp.sum(grad_output, axis=0), D, 0)
    own_up = lax.dynamic_slice_in_dim(
        up_shift.astype(jnp.float32), member * hidden_local, hidden_local
    )
    rows_two = lax.all_gather(normed_two.astype(jnp.bfloat16), "tensor", axis=0, tiled=True)
    hidden = jnp.dot(rows_two, up_mat, preferred_element_type=jnp.float32) + own_up
    active = jax.nn.gelu(hidden).astype(jnp.bfloat16)
    output = (
        residual
        + lax.psum_scatter(
            jnp.dot(
                take_rows(active, jnp.int32(0), own_rows * lax.axis_size("tensor")),
                down_mat,
                preferred_element_type=jnp.float32,
            ).astype(jnp.bfloat16),
            "tensor",
            scatter_dimension=0,
            tiled=True,
        ).astype(jnp.float32)
        + down_shift.astype(jnp.float32)
    )
    grad_full = lax.all_gather(cotangent, "tensor", axis=0, tiled=True)
    grad_active = times_transpose(grad_full, down_mat)
    grad_down = contract_rows(active, grad_full)
    gelu_back = jax.vjp(jax.nn.gelu, hidden)[1]
    grad_hidden = gelu_back(grad_active)[0].astype(jnp.bfloat16)
    grad_up_bias = placed(
        jnp.sum(grad_hidden, axis=0, dtype=jnp.float32), full_hidden, member * hidden_local
    )
    grad_up = contract_rows(rows_two, grad_hidden)
    grad_normed_two = lax.psum_scatter(
        times_transpose(
            take_rows(grad_hidden, jnp.int32(0), own_rows * lax.axis_size("tensor")), up_mat
        ).astype(jnp.bfloat16),
        "tensor",
        scatter_dimension=0,
        tiled=True,
    ).astype(jnp.float32)
    norm_back_two = jax.vjp(layer_norm, residual, gain_two, shift_two)[1]
    grad_resid_part, grad_gain_two, grad_shift_two = norm_back_two(grad_normed_two)
    grad_residual = grad_output + grad_resid_part
    ffn_terms = (grad_gain_two, grad_shift_two, grad_up, grad_up_bias, grad_down, grad_down_bias)
    grad_att = lax.all_gather(grad_residual.astype(jnp.bfloat16), "tensor", axis=0, tiled=True)
    grad_out_mat = jnp.dot(mixed_cols, grad_att, preferred_element_type=jnp.float32)
    grad_mixed = (
        times_transpose(out_mat, grad_att)
        .astype(jnp.bfloat16)
        .reshape(head_count, HEAD, total_rows)
    )
    grad_mixed = grad_mixed.astype(jnp.float32)
    grad_scaled = (grad_mixed * inv_total).astype(jnp.bfloat16)
    grad_low = (grad_mixed * (inv_total * score_scale)).astype(jnp.bfloat16)
    inner = -jnp.sum(grad_low.astype(jnp.float32) * mixed_full, axis=1, keepdims=True)
    inner_high = inner.astype(jnp.bfloat16)
    inner_rest = (inner - inner_high.astype(jnp.float32)).astype(jnp.bfloat16)
    grad_aug = jnp.concatenate([grad_low, inner_high, inner_rest, blank], axis=1)
    dqu, dqw, dk, dv, dpos = attend_back_all(
        weights, query_u, query_w, key_rows, value_rows, pos_rows, grad_aug, grad_scaled, col_table
    )
    grad_keys_all = dk.reshape(local_width, total_rows).astype(jnp.bfloat16)
    grad_values_all = dv.reshape(local_width, total_rows).astype(jnp.bfloat16)
    grad_pos = dpos.reshape(local_width, D).T
    grad_query_u = dqu.reshape(local_width, total_rows)
    grad_query_w = dqw.reshape(local_width, total_rows)
    grad_bias_one = placed(jnp.sum(grad_query_u, axis=1), D, member * local_width)
    grad_bias_two = placed(jnp.sum(grad_query_w, axis=1), D, member * local_width)
    grad_query = (grad_query_u + grad_query_w).astype(jnp.bfloat16)
    grad_query_mat = times_transpose(rows_all.T, grad_query)
    grad_key_mat = times_transpose(rows_all.T, grad_keys_all)
    grad_value_mat = times_transpose(rows_all.T, grad_values_all)
    first_row = jnp.int32(0)
    part_sum = times_transpose(
        take_cols(grad_query, first_row, own_rows * lax.axis_size("tensor")).T, query_mat
    )
    part_sum = part_sum + times_transpose(
        take_cols(grad_keys_all, first_row, own_rows * lax.axis_size("tensor")).T, key_mat
    )
    grad_normed = lax.psum_scatter(
        (
            part_sum
            + times_transpose(
                take_cols(grad_values_all, first_row, own_rows * lax.axis_size("tensor")).T,
                value_mat,
            )
        ).astype(jnp.bfloat16),
        "tensor",
        scatter_dimension=0,
        tiled=True,
    ).astype(jnp.float32)
    norm_back_one = jax.vjp(layer_norm, inputs, gain_one, shift_one)[1]
    grad_in_part, grad_gain_one, grad_shift_one = norm_back_one(grad_normed)
    grad_tokens = grad_residual + grad_in_part
    grad_squares = (grad_query_mat, grad_key_mat, grad_value_mat, grad_pos, grad_out_mat.T)
    grad_wides = (grad_up, grad_down.T)
    grad_vecs = jnp.stack(
        (
            grad_gain_one, grad_shift_one, grad_bias_one, grad_bias_two,
            ffn_terms[0], ffn_terms[1], ffn_terms[5],
        )
    )
    grad_vecs, grad_up_row = lax.psum((grad_vecs, ffn_terms[3]), "tensor")
    if direct:
        bf16 = jnp.bfloat16
        columns = jnp.pad(grad_vecs.T, ((0, 0), (0, VECS - grad_vecs.shape[0]))).astype(bf16)
        pieces = D // shard_rows
        up_rows = jnp.pad(grad_up_row.reshape(pieces, 1, -1), ((0, 0), (0, 15), (0, 0)))
        near, far, up_rows = scatter_all(
            [
                jnp.concatenate([m.astype(bf16) for m in grad_squares] + [columns], axis=1),
                jnp.concatenate([m.astype(bf16) for m in grad_wides], axis=1),
                up_rows.reshape(pieces * 16, -1).astype(bf16),
            ]
        )
        squares = jnp.split(near[:, :-VECS], len(grad_squares), axis=1)
        wides = jnp.split(far, 2, axis=1)
        vec_rows = near[:, -VECS:].T
        vecs = [vec_rows[v] for v in range(grad_vecs.shape[0])]
        up_part = up_rows[0]
    else:

        def share(array):
            return lax.psum_scatter(array, "dp", scatter_dimension=0, tiled=True)

        squares = [share(m) for m in grad_squares]
        wides = [share(m) for m in grad_wides]
        vecs = [share(v) for v in grad_vecs]
        up_part = share(grad_up_row)
    return (
        output.astype(jnp.bfloat16),
        grad_tokens,
        vecs[0],
        vecs[1],
        squares[0],
        squares[1],
        squares[2],
        squares[3],
        vecs[2],
        vecs[3],
        squares[4].T,
        vecs[4],
        vecs[5],
        wides[0],
        up_part,
        wides[1].T,
        vecs[6],
    )


def solution(mesh):
    in_specs = (
        P(("dp", "tensor"), None),
        P("dp"),
        P("dp"),
        P("dp"),
        P("dp", "tensor"),
        P("dp", "tensor"),
        P("dp", "tensor"),
        P("dp", "tensor"),
        P("dp"),
        P("dp"),
        P("tensor", "dp"),
        P("dp"),
        P("dp"),
        P("dp", "tensor"),
        P("dp"),
        P("tensor", "dp"),
        P("dp"),
        P(("dp", "tensor"), None),
    )
    out_specs = (
        P(("dp", "tensor"), None),
        P(("dp", "tensor"), None),
        P("dp"),
        P("dp"),
        P("dp", "tensor"),
        P("dp", "tensor"),
        P("dp", "tensor"),
        P("dp", "tensor"),
        P("dp"),
        P("dp"),
        P("tensor", "dp"),
        P("dp"),
        P("dp"),
        P("dp", "tensor"),
        P("dp"),
        P("tensor", "dp"),
        P("dp"),
    )
    return jax.shard_map(local, mesh=mesh, in_specs=in_specs, out_specs=out_specs, check_vma=False)
```

```python
import functools
import math

import jax
import jax.numpy as jnp
import ml_dtypes
import numpy as np
from jax import lax
from jax.experimental import pallas as pl
from jax.experimental.pallas import tpu as pltpu
from jax.sharding import PartitionSpec as P

D = 512
HEAD = 64
L = 2048


MESH = pl.DeviceIdType.MESH
VECS = 128


def peer_at(offset):
    count = lax.axis_size("dp")
    return lax.rem(lax.axis_index("dp") + offset, count)


def greet_all(count, with_pair=False):
    barrier = pltpu.get_barrier_semaphore()

    def greet(offset, carry):
        pl.semaphore_signal(
            barrier, inc=1, device_id={"dp": peer_at(offset)}, device_id_type=MESH
        )
        return carry

    lax.fori_loop(1, count, greet, 0)
    if with_pair:
        pl.semaphore_signal(
            barrier, inc=1, device_id={"tensor": 1 - lax.axis_index("tensor")}, device_id_type=MESH
        )
    pl.semaphore_wait(barrier, count if with_pair else count - 1)


def layer_norm(values, gain_vec, shift_vec):
    center = values - jnp.mean(values, axis=-1, keepdims=True)
    spread = jnp.mean(center * center, axis=-1, keepdims=True)
    return center * lax.rsqrt(spread + 1e-05) * gain_vec + shift_vec


def take_rows(array, first_row, row_count):
    return lax.dynamic_slice_in_dim(array, first_row, row_count, 0)


def take_cols(array, first_col, col_count):
    return lax.dynamic_slice_in_dim(array, first_col, col_count, array.ndim - 1)


def contract_rows(left, right):
    return lax.dot_general(
        left, right, (((0,), (0,)), ((), ())), preferred_element_type=jnp.float32
    )


def times_transpose(left, right):
    return lax.dot_general(
        left, right, (((1,), (1,)), ((), ())), preferred_element_type=jnp.float32
    )


def project_cols(weight, row_data):
    return lax.dot_general(
        weight, row_data, (((0,), (1,)), ((), ())), preferred_element_type=jnp.float32
    )


TILE = 256
TILES = L // TILE
AUG = HEAD + 16
LOG2E = 1.4426950408889634


def tiles_seen(tile):
    return min(tile + 2, TILES)


PACK = [TILE * sum(tiles_seen(t) for t in range(tile)) for tile in range(TILES + 1)]


def angle_table():
    freqs = np.exp(np.arange(0, D, 2, dtype=np.float64) * (-math.log(10000.0) / D))
    angles = np.arange(L, dtype=np.float64)[:, None] * freqs[None, :]
    return np.concatenate([np.cos(angles), np.sin(angles)], axis=1).astype(ml_dtypes.bfloat16)


def dot_nn(left, right):
    return jnp.dot(left, right, preferred_element_type=jnp.float32)


def attend_kernel(qu_ref, qw_ref, key_ref, value_ref, pos_ref, ids_ref, row_ref, col_ref, e_ref, o_ref):
    half = D // 2
    for tile in range(TILES):
        rows = slice(tile * TILE, (tile + 1) * TILE)
        width = tiles_seen(tile) * TILE
        both = contract_rows(qw_ref[:, rows], pos_ref[...])
        part_a, part_b = both[:, :half], both[:, half:]
        cos_i = row_ref[rows, :half].astype(jnp.float32)
        sin_i = row_ref[rows, half:].astype(jnp.float32)
        turned = jnp.concatenate(
            [part_a * sin_i + part_b * cos_i, part_b * sin_i - part_a * cos_i], axis=1
        ).astype(jnp.bfloat16)
        scores = dot_nn(turned, col_ref[:, :width]) + contract_rows(
            qu_ref[:, rows], key_ref[:, :width]
        )
        ids_row = ids_ref[:, tile * TILE : width]
        ids_col = jnp.broadcast_to(ids_row[:, :TILE], (8, TILE)).T[:, :1]
        edge = jnp.where(ids_row <= ids_col, scores[:, tile * TILE :], -1e30)
        if tile:
            scores = jnp.concatenate([scores[:, : tile * TILE], edge], axis=1)
        else:
            scores = edge
        peak = jnp.max(scores, axis=1, keepdims=True)
        weights = jnp.exp2(scores - peak).astype(jnp.bfloat16)
        e_ref[:, PACK[tile] : PACK[tile + 1]] = weights
        o_ref[:, rows] = times_transpose(value_ref[:, :width], weights)


def attend_back_kernel(
    e_ref, qu_ref, qw_ref, key_ref, value_ref, pos_ref, aug_ref, scaled_ref, col_ref,
    dqu_ref, dqw_ref, dk_ref, dv_ref, dpos_ref,
):
    half = D // 2
    dk_ref[...] = jnp.zeros_like(dk_ref)
    dv_ref[...] = jnp.zeros_like(dv_ref)
    for tile in range(TILES):
        rows = slice(tile * TILE, (tile + 1) * TILE)
        width = tiles_seen(tile) * TILE
        weights = e_ref[:, PACK[tile] : PACK[tile + 1]]
        grad_probs = contract_rows(aug_ref[:, rows], value_ref[:, :width])
        grad_scores = (weights.astype(jnp.float32) * grad_probs).astype(jnp.bfloat16)
        dv_ref[:, :width] += dot_nn(scaled_ref[:, rows], weights)
        dk_ref[:, :width] += dot_nn(qu_ref[:, rows], grad_scores)
        dqu_ref[:, rows] = times_transpose(key_ref[:, :width], grad_scores)
        turned = times_transpose(col_ref[:, :width], grad_scores)
        part_c, part_s = turned[:half], turned[half:]
        cos_i = col_ref[:half, rows].astype(jnp.float32)
        sin_i = col_ref[half:, rows].astype(jnp.float32)
        both = jnp.concatenate(
            [part_c * sin_i - part_s * cos_i, part_c * cos_i + part_s * sin_i], axis=0
        ).astype(jnp.bfloat16)
        dqw_ref[:, rows] = dot_nn(pos_ref[...], both)
        here = times_transpose(qw_ref[:, rows], both)
        if tile:
            dpos_ref[...] += here
        else:
            dpos_ref[...] = here


def per_head(rows, cols):
    return pl.BlockSpec((None, rows, cols), lambda h: (h, 0, 0))


def shared(rows, cols):
    return pl.BlockSpec((rows, cols), lambda h: (0, 0))


def attend_all(qu, qw, keys, values, pos, ids, row_table, col_table):
    heads = qu.shape[0]
    f32, bf16 = jnp.float32, jnp.bfloat16
    return pl.pallas_call(
        attend_kernel,
        grid=(heads,),
        in_specs=[per_head(HEAD, L)] * 3
        + [per_head(AUG, L), per_head(HEAD, D), shared(1, L), shared(L, D), shared(D, L)],
        out_specs=[per_head(TILE, PACK[-1]), per_head(AUG, L)],
        out_shape=[
            jax.ShapeDtypeStruct((heads, TILE, PACK[-1]), bf16),
            jax.ShapeDtypeStruct((heads, AUG, L), f32),
        ],
        compiler_params=pltpu.CompilerParams(vmem_limit_bytes=56 * 1024 * 1024),
    )(qu, qw, keys, values, pos, ids, row_table, col_table)


def attend_back_all(weights, qu, qw, keys, values, pos, aug, scaled, col_table):
    heads = qu.shape[0]
    f32 = jnp.float32
    return pl.pallas_call(
        attend_back_kernel,
        grid=(heads,),
        in_specs=[per_head(TILE, PACK[-1])]
        + [per_head(HEAD, L)] * 3
        + [per_head(AUG, L), per_head(HEAD, D), per_head(AUG, L), per_head(HEAD, L), shared(D, L)],
        out_specs=[per_head(HEAD, L)] * 4 + [per_head(HEAD, D)],
        out_shape=[jax.ShapeDtypeStruct((heads, HEAD, L), f32)] * 4
        + [jax.ShapeDtypeStruct((heads, HEAD, D), f32)],
        compiler_params=pltpu.CompilerParams(vmem_limit_bytes=56 * 1024 * 1024),
    )(weights, qu, qw, keys, values, pos, aug, scaled, col_table)


def placed(part_vec, length, offset):
    return lax.dynamic_update_slice_in_dim(jnp.zeros((length,), jnp.float32), part_vec, offset, 0)


NEAR = 4 * 256


def first_kernel(
    count, tok_ref, cot_ref, near_ref, far_ref, up_ref, ids_ref, row_ref, col_ref,
    e_ref, qu_ref, qw_ref, key_ref, va_ref, o_ref, mix_ref, norm_ref, pos_ref,
    near_all, far_all, up_all, cot_all,
    tok_all, quf_ref, qwf_ref, turn_ref, e_buf,
    send_sems, recv_sems, own_sems, pair_send, pair_recv, e_sems,
):
    half = D // 2
    me, member = lax.axis_index("dp"), lax.axis_index("tensor")
    pair = {"tensor": 1 - member}
    own_rows = tok_ref.shape[0]
    own = pl.ds(pl.multiple_of(member * own_rows, own_rows), own_rows)
    parts = (near_ref, far_ref, up_ref)
    wholes = (near_all, far_all, up_all)

    def copy_to(index, offset):
        rows = parts[index].shape[0]
        return pltpu.make_async_remote_copy(
            src_ref=parts[index],
            dst_ref=wholes[index].at[pl.ds(pl.multiple_of(me * rows, rows), rows)],
            send_sem=send_sems.at[index, offset - 1],
            recv_sem=recv_sems.at[index, offset - 1],
            device_id={"dp": peer_at(offset)},
            device_id_type=MESH,
        )

    def own_copy(index):
        rows = parts[index].shape[0]
        target = wholes[index].at[pl.ds(pl.multiple_of(me * rows, rows), rows)]
        return pltpu.make_async_copy(parts[index], target, own_sems.at[index])

    def begin_gather(index):
        def begin(offset, carry):
            copy_to(index, offset).start()
            return carry

        lax.fori_loop(1, count, begin, 0)
        own_copy(index).start()

    def finish_gather(index):
        def finish(offset, carry):
            copy_to(index, offset).wait()
            return carry

        lax.fori_loop(1, count, finish, 0)
        own_copy(index).wait()

    def to_pair(source, target, slot):
        return pltpu.make_async_remote_copy(
            src_ref=source,
            dst_ref=target.at[own],
            send_sem=pair_send.at[slot],
            recv_sem=pair_recv.at[slot],
            device_id=pair,
            device_id_type=MESH,
        )

    greet_all(count, True)
    begin_gather(0)
    exchanges = (to_pair(tok_ref, tok_all, 0), to_pair(cot_ref, cot_all, 1))
    keeps = (
        pltpu.make_async_copy(tok_ref, tok_all.at[own], own_sems.at[3]),
        pltpu.make_async_copy(cot_ref, cot_all.at[own], own_sems.at[4]),
    )
    for copy in exchanges + keeps:
        copy.start()
    finish_gather(0)
    begin_gather(1)
    begin_gather(2)
    for copy in exchanges + keeps:
        copy.wait()

    vec_block = near_all[:, NEAR:].astype(jnp.float32)
    vec_rows = vec_block.T
    gain, shift = vec_rows[0:1], vec_rows[1:2]
    turn_ref[...] = near_all[:, :768].T
    pos_ref[...] = near_all[:, 768:NEAR].T
    width = qu_ref.shape[0]
    heads = width // HEAD
    own_cols = pl.ds(pl.multiple_of(member * width, width), width)
    vec_cols = near_all[own_cols, NEAR:].astype(jnp.float32)
    bias_u, bias_w = vec_cols[:, 2:3], vec_cols[:, 3:4]
    fold = LOG2E / math.sqrt(HEAD)
    place = lax.broadcasted_iota(jnp.int32, (AUG - HEAD, TILE), 0)
    marks = jnp.where(place < 2, 1.0, 0.0).astype(jnp.bfloat16)
    for tile in range(TILES):
        rows = slice(tile * TILE, (tile + 1) * TILE)
        normed = layer_norm(tok_all[rows, :].astype(jnp.float32), gain, shift)
        normed = normed.astype(jnp.bfloat16)
        norm_ref[rows, :] = normed
        projected = times_transpose(turn_ref[...], normed)
        sum_u = projected[:width] + bias_u
        sum_w = projected[:width] + bias_w
        qu_ref[:, rows] = sum_u.astype(jnp.bfloat16)
        qw_ref[:, rows] = sum_w.astype(jnp.bfloat16)
        quf_ref[:, rows] = (sum_u * fold).astype(jnp.bfloat16)
        qwf_ref[:, rows] = (sum_w * fold).astype(jnp.bfloat16)
        key_ref[:, rows] = projected[width : 2 * width].astype(jnp.bfloat16)
        for head in range(heads):
            values = projected[2 * width + head * HEAD : 2 * width + (head + 1) * HEAD]
            va_ref[head * AUG : head * AUG + HEAD, rows] = values.astype(jnp.bfloat16)
            va_ref[head * AUG + HEAD : (head + 1) * AUG, rows] = marks

    def e_copy(head, slot):
        return pltpu.make_async_copy(e_buf.at[slot], e_ref.at[head], e_sems.at[slot])

    def one_head(head, carry):
        slot = lax.rem(head, 2)
        lines = pl.ds(pl.multiple_of(head * HEAD, HEAD), HEAD)
        more = pl.ds(pl.multiple_of(head * AUG, AUG), AUG)
        upper = pl.ds(pl.multiple_of(head * AUG, 16), HEAD)
        lower = pl.ds(pl.multiple_of(head * AUG + HEAD, 16), AUG - HEAD)

        @pl.when(head >= 2)
        def _():
            e_copy(head - 2, slot).wait()

        for tile in range(TILES):
            rows = slice(tile * TILE, (tile + 1) * TILE)
            width = tiles_seen(tile) * TILE
            both = contract_rows(qwf_ref[lines, rows], pos_ref[lines, :])
            part_a, part_b = both[:, :half], both[:, half:]
            cos_i = row_ref[rows, :half].astype(jnp.float32)
            sin_i = row_ref[rows, half:].astype(jnp.float32)
            turned = jnp.concatenate(
                [part_a * sin_i + part_b * cos_i, part_b * sin_i - part_a * cos_i], axis=1
            ).astype(jnp.bfloat16)
            scores = dot_nn(turned, col_ref[:, :width]) + contract_rows(
                quf_ref[lines, rows], key_ref[lines, :width]
            )
            ids_row = ids_ref[:, tile * TILE : width]
            ids_col = jnp.broadcast_to(ids_row[:, :TILE], (8, TILE)).T[:, :1]
            edge = jnp.where(ids_row <= ids_col, scores[:, tile * TILE :], -1e30)
            if tile:
                scores = jnp.concatenate([scores[:, : tile * TILE], edge], axis=1)
            else:
                scores = edge
            peak = jnp.max(scores, axis=1, keepdims=True)
            weights = jnp.exp2(scores - peak).astype(jnp.bfloat16)
            e_buf[slot, :, PACK[tile] : PACK[tile + 1]] = weights
            sums = times_transpose(va_ref[more, :width], weights)
            inverse = 1.0 / sums[HEAD : HEAD + 1]
            mixed = sums[:HEAD] * inverse
            o_ref[upper, rows] = mixed
            o_ref[lower, rows] = jnp.broadcast_to(inverse, (AUG - HEAD, TILE))
            mix_ref[lines, rows] = mixed.astype(jnp.bfloat16)
        e_copy(head, slot).start()
        return carry

    lax.fori_loop(0, heads, one_head, 0)
    for head in range(max(heads - 2, 0), heads):
        e_copy(head, head % 2).wait()
    finish_gather(1)
    finish_gather(2)


VMEM_SPEC = pl.BlockSpec(memory_space=pltpu.VMEM)
ANY_SPEC = pl.BlockSpec(memory_space=pl.ANY)


def first_call(tokens, cotangent, near, far, up_row, ids, row_table, col_table):
    count = lax.axis_size("dp")
    rows = ids.shape[1]
    width = NEAR // 4
    heads = width // HEAD
    f32, bf16 = jnp.float32, jnp.bfloat16

    def shape(*dims, kind=bf16):
        return jax.ShapeDtypeStruct(dims, kind)

    return pl.pallas_call(
        functools.partial(first_kernel, count),
        in_specs=[VMEM_SPEC, ANY_SPEC] + [VMEM_SPEC] * 6,
        out_specs=[ANY_SPEC] + [VMEM_SPEC] * 11 + [ANY_SPEC],
        out_shape=[
            shape(heads, TILE, PACK[-1]),
            shape(width, rows),
            shape(width, rows),
            shape(width, rows),
            shape(heads * AUG, rows),
            shape(heads * AUG, rows, kind=f32),
            shape(width, rows),
            shape(rows, D),
            shape(width, D),
            shape(count * near.shape[0], near.shape[1]),
            shape(count * far.shape[0], far.shape[1]),
            shape(count * up_row.shape[0], up_row.shape[1]),
            shape(rows, D),
        ],
        scratch_shapes=[
            pltpu.VMEM((rows, D), bf16),
            pltpu.VMEM((width, rows), bf16),
            pltpu.VMEM((width, rows), bf16),
            pltpu.VMEM((3 * width, D), bf16),
            pltpu.VMEM((2, TILE, PACK[-1]), bf16),
            pltpu.SemaphoreType.DMA((3, count - 1)),
            pltpu.SemaphoreType.DMA((3, count - 1)),
            pltpu.SemaphoreType.DMA((5,)),
            pltpu.SemaphoreType.DMA((2,)),
            pltpu.SemaphoreType.DMA((2,)),
            pltpu.SemaphoreType.DMA((2,)),
        ],
        compiler_params=pltpu.CompilerParams(
            collective_id=0, has_side_effects=True, vmem_limit_bytes=60 * 1024 * 1024
        ),
    )(tokens, cotangent, near, far, up_row, ids, row_table, col_table)


CHUNK = 256
GELU_SCALE = math.sqrt(2.0 / math.pi)


def fold_rows(values):
    return jnp.sum(values.reshape(values.shape[0] // 8, 8, values.shape[1]), axis=0)


def norm_parts(values):
    center = values - jnp.mean(values, axis=-1, keepdims=True)
    spread = jnp.mean(center * center, axis=-1, keepdims=True)
    rate = lax.rsqrt(spread + 1e-05)
    return center * rate, rate


def norm_grad(grad, gain, normed, rate):
    scaled = grad * gain
    mean = jnp.mean(scaled, axis=-1, keepdims=True)
    along = jnp.mean(scaled * normed, axis=-1, keepdims=True)
    return rate * (scaled - mean - normed * along)


def to_other(source, target, send_sem, recv_sem):
    return pltpu.make_async_remote_copy(
        src_ref=source,
        dst_ref=target,
        send_sem=send_sem,
        recv_sem=recv_sem,
        device_id={"tensor": 1 - lax.axis_index("tensor")},
        device_id_type=MESH,
    )


def dot_tt(left, right):
    return lax.dot_general(
        left, right, (((0,), (1,)), ((), ())), preferred_element_type=jnp.float32
    )


def middle_kernel(
    mix_ref, tok_ref, cot_ref, far_ref, vec_ref, up_ref,
    out_ref, gres_ref, gatt_ref, gfar_ref, vec_out, bup_out,
    send_a, recv_a, res_ref, n2_ref, n2t_ref, cott_ref, act_ref, gh_ref,
    osend, orecv, oacc, gacc, bup_acc, vec_acc, send_sems, recv_sems,
):
    member = lax.axis_index("tensor")
    own_rows = tok_ref.shape[0]
    chunks = own_rows // CHUNK
    own0 = pl.multiple_of(member * own_rows, own_rows)
    oth0 = pl.multiple_of((1 - member) * own_rows, own_rows)
    hidden = act_ref.shape[1]
    up_cols, down_cols = slice(0, hidden), slice(hidden, 2 * hidden)
    out_cols = slice(2 * hidden, far_ref.shape[1])

    def at(base, chunk):
        return pl.ds(pl.multiple_of(base + chunk * CHUNK, CHUNK), CHUNK)

    barrier = pltpu.get_barrier_semaphore()
    pl.semaphore_signal(barrier, inc=1, device_id={"tensor": 1 - member}, device_id_type=MESH)
    pl.semaphore_wait(barrier, 1)

    def pass_on(stage, chunk):
        here = at(0, chunk)
        pairs = (
            (send_a.at[here], recv_a.at[here]),
            (n2_ref.at[at(own0, chunk)], n2_ref.at[at(own0, chunk)]),
            (osend.at[0, here], orecv.at[0, here]),
            (osend.at[1, here], orecv.at[1, here]),
            (gatt_ref.at[at(own0, chunk)], gatt_ref.at[at(own0, chunk)]),
        )
        source, target = pairs[stage]
        return to_other(
            source, target, send_sems.at[stage, chunk], recv_sems.at[stage, chunk]
        )

    vec_rows = vec_ref[:, NEAR:].astype(jnp.float32).T
    gain, shift, down_shift = vec_rows[4:5], vec_rows[5:6], vec_rows[6:7]
    ups = hidden // 128
    up_block = up_ref[pl.ds(pl.multiple_of(member * ups * 16, 16), ups * 16), :].astype(jnp.float32)
    up_shift = jnp.concatenate([up_block[16 * k : 16 * k + 1] for k in range(ups)], axis=1)

    def branch(rows):
        return dot_tt(mix_ref[:, rows], far_ref[:, out_cols])

    for chunk in range(chunks):
        send_a[at(0, chunk), :] = branch(at(oth0, chunk)).astype(jnp.bfloat16)
        pass_on(0, chunk).start()
    for chunk in range(chunks):
        here = at(0, chunk)
        part = branch(at(own0, chunk))
        pass_on(0, chunk).wait()
        residual = tok_ref[here, :].astype(jnp.float32) + part + recv_a[here, :].astype(jnp.float32)
        res_ref[here, :] = residual
        n2_ref[at(own0, chunk), :] = (norm_parts(residual)[0] * gain + shift).astype(jnp.bfloat16)
        pass_on(1, chunk).start()

    bup_acc[...] = jnp.zeros_like(bup_acc)
    vec_acc[...] = jnp.zeros_like(vec_acc)

    def ffn(rows):
        normed = n2_ref[rows, :]
        grads = cot_ref[rows, :]
        value = dot_nn(normed, far_ref[:, up_cols]) + up_shift
        square = value * value
        bend = jnp.tanh(GELU_SCALE * value * (1.0 + 0.044715 * square))
        half = 0.5 * (1.0 + bend)
        active = (value * half).astype(jnp.bfloat16)
        slope = half + 0.5 * value * (1.0 - bend * bend) * (
            GELU_SCALE * (1.0 + 3.0 * 0.044715 * square)
        )
        grad_hidden = (dot_nn(grads, far_ref[:, down_cols]) * slope).astype(jnp.bfloat16)
        act_ref[rows, :] = active
        gh_ref[rows, :] = grad_hidden
        n2t_ref[:, rows] = normed.T
        cott_ref[:, rows] = grads.T
        bup_acc[...] += fold_rows(grad_hidden.astype(jnp.float32))
        return (
            times_transpose(active, far_ref[:, down_cols]),
            times_transpose(grad_hidden, far_ref[:, up_cols]),
        )

    def ffn_own(chunk, carry):
        oacc[at(0, chunk), :], gacc[at(0, chunk), :] = ffn(at(own0, chunk))
        return carry

    def ffn_other(chunk, carry):
        pass_on(1, chunk).wait()
        here = at(0, chunk)
        for stage, part in zip((2, 3), ffn(at(oth0, chunk))):
            osend[stage - 2, here, :] = part.astype(jnp.bfloat16)
            pass_on(stage, chunk).start()
        return carry

    lax.fori_loop(0, 1, ffn_own, 0)
    lax.fori_loop(0, chunks, ffn_other, 0)
    lax.fori_loop(1, chunks, ffn_own, 0)

    def close(chunk, carry):
        here = at(0, chunk)
        pass_on(2, chunk).wait()
        pass_on(3, chunk).wait()
        residual = res_ref[here, :]
        out = residual + oacc[here, :] + orecv[0, here, :].astype(jnp.float32) + down_shift
        out_ref[here, :] = out.astype(jnp.bfloat16)
        grad = gacc[here, :] + orecv[1, here, :].astype(jnp.float32)
        normed, rate = norm_parts(residual)
        top = cot_ref[at(own0, chunk), :].astype(jnp.float32)
        grad_res = top + norm_grad(grad, gain, normed, rate)
        gres_ref[here, :] = grad_res
        gatt_ref[at(own0, chunk), :] = grad_res.astype(jnp.bfloat16)
        pass_on(4, chunk).start()
        vec_acc[0:8, :] += fold_rows(grad * normed)
        vec_acc[8:16, :] += fold_rows(grad)
        vec_acc[16:24, :] += fold_rows(top)
        return carry

    lax.fori_loop(0, chunks, close, 0)
    for part in range(hidden // CHUNK):
        cols = slice(part * CHUNK, (part + 1) * CHUNK)
        gfar_ref[:, cols] = dot_nn(n2t_ref[...], gh_ref[:, cols]).astype(jnp.bfloat16)
        gfar_ref[:, hidden + part * CHUNK : hidden + (part + 1) * CHUNK] = dot_nn(
            cott_ref[...], act_ref[:, cols]
        ).astype(jnp.bfloat16)
    vec_out[...] = jnp.concatenate(
        [jnp.sum(vec_acc[8 * v : 8 * v + 8, :], axis=0, keepdims=True) for v in range(3)]
        + [jnp.zeros((5, vec_acc.shape[1]), jnp.float32)],
        axis=0,
    )
    for k in range(ups):
        bup_out[8 * k : 8 * k + 8, :] = bup_acc[:, 128 * k : 128 * k + 128]
    for chunk in range(chunks):
        pass_on(4, chunk).wait()
    gfar_ref[:, out_cols] = dot_tt(gatt_ref[...], mix_ref[...]).astype(jnp.bfloat16)


def middle_call(mix, tokens, cot_all, far_all, near_all, up_all):
    rows, own_rows = cot_all.shape[0], tokens.shape[0]
    chunks = own_rows // CHUNK
    hidden = (far_all.shape[1] - mix.shape[0]) // 2
    f32, bf16 = jnp.float32, jnp.bfloat16
    return pl.pallas_call(
        middle_kernel,
        in_specs=[VMEM_SPEC] * 6,
        out_specs=[VMEM_SPEC] * 6,
        out_shape=[
            jax.ShapeDtypeStruct((own_rows, D), bf16),
            jax.ShapeDtypeStruct((own_rows, D), f32),
            jax.ShapeDtypeStruct((rows, D), bf16),
            jax.ShapeDtypeStruct(far_all.shape, bf16),
            jax.ShapeDtypeStruct((8, D), f32),
            jax.ShapeDtypeStruct((hidden // 16, 128), f32),
        ],
        scratch_shapes=[
            pltpu.VMEM((own_rows, D), bf16),
            pltpu.VMEM((own_rows, D), bf16),
            pltpu.VMEM((own_rows, D), f32),
            pltpu.VMEM((rows, D), bf16),
            pltpu.VMEM((D, rows), bf16),
            pltpu.VMEM((D, rows), bf16),
            pltpu.VMEM((rows, hidden), bf16),
            pltpu.VMEM((rows, hidden), bf16),
            pltpu.VMEM((2, own_rows, D), bf16),
            pltpu.VMEM((2, own_rows, D), bf16),
            pltpu.VMEM((own_rows, D), f32),
            pltpu.VMEM((own_rows, D), f32),
            pltpu.VMEM((8, hidden), f32),
            pltpu.VMEM((24, D), f32),
            pltpu.SemaphoreType.DMA((5, chunks)),
            pltpu.SemaphoreType.DMA((5, chunks)),
        ],
        compiler_params=pltpu.CompilerParams(
            collective_id=1, has_side_effects=True, vmem_limit_bytes=60 * 1024 * 1024
        ),
    )(mix, tokens, cot_all, far_all, near_all, up_all)


def last_kernel(
    count, e_ref, qu_ref, qw_ref, key_ref, va_ref, o_ref, pos_ref, col_ref, gatt_ref, wout_ref,
    near_ref, norm_ref, tok_ref, gres_ref, gfar_ref, vec_ref, bup_ref,
    gtok_ref, gq_ref, gk_ref, gv_ref, gp_ref, gup_ref, gdown_ref, gout_ref, gvec_ref, gbup_ref,
    e_buf, far_slots, near_pack, near_slots, vec_mine, vec_other, vec_cols, vec_slots,
    bup_all, bup_slots, aug_ref, scd_ref, dqkv_ref, dk_acc, dv_acc, dpos_ref, pos_acc, bias_acc,
    normt_ref, part_send, part_recv, far_sum, near_sum, vec_sum, bup_sum, vec_acc,
    send_sems, recv_sems, pair_send, pair_recv, e_sems,
):
    half = D // 2
    me, member = lax.axis_index("dp"), lax.axis_index("tensor")
    own_rows = tok_ref.shape[0]
    chunks = own_rows // CHUNK
    own0 = pl.multiple_of(member * own_rows, own_rows)
    oth0 = pl.multiple_of((1 - member) * own_rows, own_rows)
    width = qu_ref.shape[0]
    heads = width // HEAD
    score_scale = 1.0 / math.sqrt(HEAD)
    sources = (gfar_ref, near_pack, vec_cols, bup_all)
    slots = (far_slots, near_slots, vec_slots, bup_slots)
    totals = (far_sum, near_sum, vec_sum, bup_sum)

    def at(base, chunk):
        return pl.ds(pl.multiple_of(base + chunk * CHUNK, CHUNK), CHUNK)

    def piece(index, device):
        rows = totals[index].shape[0]
        return sources[index].at[pl.ds(pl.multiple_of(device * rows, rows), rows)]

    def share_to(index, offset):
        peer = peer_at(offset)
        return pltpu.make_async_remote_copy(
            src_ref=piece(index, peer),
            dst_ref=slots[index].at[offset - 1],
            send_sem=send_sems.at[index, offset - 1],
            recv_sem=recv_sems.at[index, offset - 1],
            device_id={"dp": peer},
            device_id_type=MESH,
        )

    def begin_share(index):
        def begin(offset, carry):
            share_to(index, offset).start()
            return carry

        lax.fori_loop(1, count, begin, 0)

    def finish_share(index):
        total = totals[index]
        total[...] = piece(index, me)[...].astype(jnp.float32)

        def finish(offset, carry):
            share_to(index, offset).wait()
            total[...] += slots[index][offset - 1].astype(jnp.float32)
            return carry

        lax.fori_loop(1, count, finish, 0)

    def e_copy(head, slot):
        return pltpu.make_async_copy(e_ref.at[head], e_buf.at[slot], e_sems.at[slot])

    e_copy(0, 0).start()
    greet_all(count, True)
    begin_share(0)
    own_bup = pl.ds(pl.multiple_of(member * bup_ref.shape[0], 8), bup_ref.shape[0])
    bup_all[own_bup, :] = bup_ref[...]
    bup_copy = to_other(bup_ref, bup_all.at[own_bup], pair_send.at[chunks], pair_recv.at[chunks])
    bup_copy.start()

    out_mat = wout_ref[:, wout_ref.shape[1] - width :].T
    place = lax.broadcasted_iota(jnp.int32, (AUG - HEAD, CHUNK), 0)
    for tile in range(TILES):
        rows = slice(tile * TILE, (tile + 1) * TILE)
        grads = times_transpose(out_mat, gatt_ref[rows, :])
        grads = grads.astype(jnp.bfloat16).astype(jnp.float32)
        for head in range(heads):
            lines = slice(head * HEAD, (head + 1) * HEAD)
            first = head * AUG
            inverse = o_ref[first + HEAD : first + HEAD + 1, rows]
            mixed = o_ref[first : first + HEAD, rows]
            scaled = grads[lines] * inverse
            low = (scaled * score_scale).astype(jnp.bfloat16)
            inner = -jnp.sum(low.astype(jnp.float32) * mixed, axis=0, keepdims=True)
            high = inner.astype(jnp.bfloat16).astype(jnp.float32)
            tail = jnp.where(place == 0, high, jnp.where(place == 1, inner - high, 0.0))
            scd_ref[lines, rows] = scaled.astype(jnp.bfloat16)
            aug_ref[first : first + HEAD, rows] = low
            aug_ref[first + HEAD : first + AUG, rows] = tail.astype(jnp.bfloat16)
    bias_acc[...] = jnp.zeros_like(bias_acc)

    def one_head(head, carry):
        slot = lax.rem(head, 2)
        first = pl.multiple_of(head * HEAD, HEAD)
        lines = pl.ds(first, HEAD)
        more = pl.ds(pl.multiple_of(head * AUG, 16), AUG)

        @pl.when(head + 1 < heads)
        def _():
            e_copy(head + 1, 1 - slot).start()

        e_copy(head, slot).wait()
        dk_acc[...] = jnp.zeros_like(dk_acc)
        dv_acc[...] = jnp.zeros_like(dv_acc)
        for tile in range(TILES):
            rows = slice(tile * TILE, (tile + 1) * TILE)
            seen = tiles_seen(tile) * TILE
            weights = e_buf[slot, :, PACK[tile] : PACK[tile + 1]]
            grad_probs = contract_rows(aug_ref[more, rows], va_ref[more, :seen])
            grad_scores = (weights.astype(jnp.float32) * grad_probs).astype(jnp.bfloat16)
            dv_acc[:, :seen] += dot_nn(scd_ref[lines, rows], weights)
            dk_acc[:, :seen] += dot_nn(qu_ref[lines, rows], grad_scores)
            grad_u = times_transpose(key_ref[lines, :seen], grad_scores)
            turned = times_transpose(col_ref[:, :seen], grad_scores)
            part_c, part_s = turned[:half], turned[half:]
            cos_i = col_ref[:half, rows].astype(jnp.float32)
            sin_i = col_ref[half:, rows].astype(jnp.float32)
            both = jnp.concatenate(
                [part_c * sin_i - part_s * cos_i, part_c * cos_i + part_s * sin_i], axis=0
            ).astype(jnp.bfloat16)
            grad_w = dot_nn(pos_ref[lines, :], both)
            dqkv_ref[lines, rows] = (grad_u + grad_w).astype(jnp.bfloat16)
            bias_acc[lines, :] += grad_u[:, :128] + grad_u[:, 128:]
            bias_acc[pl.ds(pl.multiple_of(width + first, HEAD), HEAD), :] += (
                grad_w[:, :128] + grad_w[:, 128:]
            )
            here = times_transpose(qw_ref[lines, rows], both)
            if tile:
                pos_acc[...] += here
            else:
                pos_acc[...] = here
        key_lines = pl.ds(pl.multiple_of(width + first, HEAD), HEAD)
        value_lines = pl.ds(pl.multiple_of(2 * width + first, HEAD), HEAD)
        dqkv_ref[key_lines, :] = dk_acc[...].astype(jnp.bfloat16)
        dqkv_ref[value_lines, :] = dv_acc[...].astype(jnp.bfloat16)
        dpos_ref[lines, :] = pos_acc[...].astype(jnp.bfloat16)
        return carry

    lax.fori_loop(0, heads, one_head, 0)

    for tile in range(TILES):
        rows = slice(tile * TILE, (tile + 1) * TILE)
        normt_ref[:, rows] = norm_ref[rows, :].T
    for part in range(3):
        lines = slice(part * width, (part + 1) * width)
        near_pack[:, lines] = times_transpose(normt_ref[...], dqkv_ref[lines, :]).astype(
            jnp.bfloat16
        )
    near_pack[:, 3 * width :] = dpos_ref[...].T
    begin_share(1)
    bup_copy.wait()
    begin_share(3)

    def pass_on(chunk):
        here = at(0, chunk)
        return to_other(
            part_send.at[here], part_recv.at[here], pair_send.at[chunk], pair_recv.at[chunk]
        )

    def backward(rows):
        return dot_tt(dqkv_ref[:, rows], near_ref[:, : 3 * width])

    for chunk in range(chunks):
        part_send[at(0, chunk), :] = backward(at(oth0, chunk)).astype(jnp.bfloat16)
        pass_on(chunk).start()
    vec_rows = near_ref[:, NEAR:].astype(jnp.float32).T
    gain = vec_rows[0:1]
    vec_acc[...] = jnp.zeros_like(vec_acc)
    for chunk in range(chunks):
        here = at(0, chunk)
        part = backward(at(own0, chunk))
        pass_on(chunk).wait()
        grad = part + part_recv[here, :].astype(jnp.float32)
        normed, rate = norm_parts(tok_ref[here, :].astype(jnp.float32))
        gtok_ref[here, :] = gres_ref[here, :] + norm_grad(grad, gain, normed, rate)
        vec_acc[0:8, :] += fold_rows(grad * normed)
        vec_acc[8:16, :] += fold_rows(grad)
    sums = jnp.sum(bias_acc[...].T, axis=0, keepdims=True)
    own_cols = pl.ds(pl.multiple_of(member * width, width), width)
    vec_mine[...] = jnp.zeros_like(vec_mine)
    vec_mine[0:1, :] = jnp.sum(vec_acc[0:8, :], axis=0, keepdims=True)
    vec_mine[1:2, :] = jnp.sum(vec_acc[8:16, :], axis=0, keepdims=True)
    vec_mine[2:3, own_cols] = sums[:, :width]
    vec_mine[3:4, own_cols] = sums[:, width:]
    vec_mine[4:7, :] = vec_ref[0:3, :]
    vec_copy = to_other(
        vec_mine, vec_other, pair_send.at[chunks + 1], pair_recv.at[chunks + 1]
    )
    vec_copy.start()
    finish_share(0)
    gup_ref[...] = far_sum[:, : gup_ref.shape[1]]
    gdown_ref[...] = far_sum[:, gup_ref.shape[1] : 2 * gup_ref.shape[1]]
    gout_ref[...] = far_sum[:, 2 * gup_ref.shape[1] :]
    vec_copy.wait()
    both = vec_mine[...] + vec_other[...]
    vec_cols[...] = jnp.concatenate([both, jnp.zeros((VECS - 8, D), jnp.float32)], axis=0).T
    begin_share(2)
    finish_share(3)
    gbup_ref[...] = jnp.sum(bup_sum[...], axis=0, keepdims=True)
    finish_share(1)
    for part, ref in enumerate((gq_ref, gk_ref, gv_ref, gp_ref)):
        ref[...] = near_sum[:, part * width : (part + 1) * width]
    finish_share(2)
    gvec_ref[...] = vec_sum[...].T[:8]


def last_call(e, qu, qw, key, va, o, pos, col, gatt, far, near, norm, tok, gres, gfar, vec, bup):
    count = lax.axis_size("dp")
    rows, own_rows = norm.shape[0], tok.shape[0]
    chunks = own_rows // CHUNK
    width = qu.shape[0]
    hidden = (far.shape[1] - width) // 2
    shard = D // count
    f32, bf16 = jnp.float32, jnp.bfloat16

    def shape(*dims):
        return jax.ShapeDtypeStruct(dims, f32)

    def room(*dims, kind=f32):
        return pltpu.VMEM(dims, kind)

    return pl.pallas_call(
        functools.partial(last_kernel, count),
        in_specs=[ANY_SPEC] + [VMEM_SPEC] * 16,
        out_specs=[VMEM_SPEC] * 10,
        out_shape=[shape(own_rows, D)]
        + [shape(shard, width)] * 4
        + [shape(shard, hidden)] * 2
        + [shape(shard, width), shape(8, shard), shape(1, 128)],
        scratch_shapes=[
            room(2, TILE, PACK[-1], kind=bf16),
            room(count - 1, shard, far.shape[1], kind=bf16),
            room(D, 4 * width, kind=bf16),
            room(count - 1, shard, 4 * width, kind=bf16),
            room(8, D),
            room(8, D),
            room(D, VECS),
            room(count - 1, shard, VECS),
            room(8 * count, 128),
            room(count - 1, 8, 128),
            room(va.shape[0], rows, kind=bf16),
            room(width, rows, kind=bf16),
            room(3 * width, rows, kind=bf16),
            room(HEAD, rows),
            room(HEAD, rows),
            room(width, D, kind=bf16),
            room(HEAD, D),
            room(2 * width, 128),
            room(D, rows, kind=bf16),
            room(own_rows, D, kind=bf16),
            room(own_rows, D, kind=bf16),
            room(shard, far.shape[1]),
            room(shard, 4 * width),
            room(shard, VECS),
            room(8, 128),
            room(16, D),
            pltpu.SemaphoreType.DMA((4, count - 1)),
            pltpu.SemaphoreType.DMA((4, count - 1)),
            pltpu.SemaphoreType.DMA((chunks + 2,)),
            pltpu.SemaphoreType.DMA((chunks + 2,)),
            pltpu.SemaphoreType.DMA((2,)),
        ],
        compiler_params=pltpu.CompilerParams(
            collective_id=2, has_side_effects=True, vmem_limit_bytes=62 * 1024 * 1024
        ),
    )(e, qu, qw, key, va, o, pos, col, gatt, far, near, norm, tok, gres, gfar, vec, bup)


def local_plain(
    tokens,
    block_ids,
    ln1_gain,
    ln1_bias,
    w_query,
    w_key,
    w_value,
    w_pos,
    bias_u,
    bias_w,
    w_out,
    ln2_gain,
    ln2_bias,
    w_up,
    bias_up,
    w_down,
    bias_down,
    cotangent,
):
    member = lax.axis_index("tensor")
    squares = (w_query, w_key, w_value, w_pos, w_out.T)
    wide = (w_up, w_down.T)
    vectors = (ln1_gain, ln1_bias, bias_u, bias_w, ln2_gain, ln2_bias, bias_down)
    near_mats = [lax.all_gather(m, "dp", axis=0, tiled=True) for m in squares]
    far_mats = [lax.all_gather(m, "dp", axis=0, tiled=True) for m in wide]
    full_vecs = [lax.all_gather(v, "dp", axis=0, tiled=True) for v in vectors]
    up_shift = lax.all_gather(bias_up, "dp", axis=0, tiled=True)
    query_mat, key_mat, value_mat, pos_mat, out_back = near_mats
    out_mat = out_back.T
    up_mat, down_back = far_mats
    down_mat = down_back.T
    gain_one, shift_one, bias_one, bias_two, gain_two, shift_two, down_shift = full_vecs
    gain_one = gain_one.astype(jnp.float32)
    shift_one = shift_one.astype(jnp.float32)
    gain_two = gain_two.astype(jnp.float32)
    shift_two = shift_two.astype(jnp.float32)
    local_width = query_mat.shape[1]
    head_count = local_width // HEAD
    hidden_local = up_mat.shape[1]
    full_hidden = up_shift.shape[0]
    own_u = lax.dynamic_slice_in_dim(
        bias_one.astype(jnp.float32), member * local_width, local_width
    )
    own_w = lax.dynamic_slice_in_dim(
        bias_two.astype(jnp.float32), member * local_width, local_width
    )
    score_scale = 1.0 / math.sqrt(HEAD)
    own_rows = tokens.shape[0]
    inputs = tokens.astype(jnp.float32)
    normed = layer_norm(inputs, gain_one, shift_one)
    rows_all = lax.all_gather(normed.astype(jnp.bfloat16), "tensor", axis=0, tiled=True)
    total_rows = rows_all.shape[0]
    queries_t = project_cols(query_mat, rows_all)
    def heads_of(array):
        return array.astype(jnp.bfloat16).reshape(head_count, HEAD, array.shape[-1])

    ids = block_ids.reshape(1, total_rows)
    sum_u = queries_t + own_u[:, None]
    sum_w = queries_t + own_w[:, None]
    fold = score_scale * LOG2E
    query_u = heads_of(sum_u)
    query_w = heads_of(sum_w)
    key_rows = heads_of(project_cols(key_mat, rows_all))
    ones = jnp.ones((head_count, 2, total_rows), jnp.bfloat16)
    blank = jnp.zeros((head_count, AUG - HEAD - 2, total_rows), jnp.bfloat16)
    value_rows = jnp.concatenate(
        [heads_of(project_cols(value_mat, rows_all)), ones, blank], axis=1
    )
    pos_rows = pos_mat.T.reshape(head_count, HEAD, D)
    table = angle_table()
    row_table = jnp.asarray(table)
    col_table = jnp.asarray(np.ascontiguousarray(table.T))
    weights, mixed_sums = attend_all(
        heads_of(sum_u * fold), heads_of(sum_w * fold), key_rows, value_rows, pos_rows, ids,
        row_table, col_table,
    )
    inv_total = 1.0 / mixed_sums[:, HEAD : HEAD + 1]
    mixed_full = mixed_sums[:, :HEAD] * inv_total
    mixed_cols = mixed_full.reshape(local_width, total_rows).astype(jnp.bfloat16)
    residual = inputs + lax.psum_scatter(
        contract_rows(
            take_cols(mixed_cols, jnp.int32(0), own_rows * lax.axis_size("tensor")), out_mat
        ).astype(jnp.bfloat16),
        "tensor",
        scatter_dimension=0,
        tiled=True,
    ).astype(jnp.float32)
    normed_two = layer_norm(residual, gain_two, shift_two)
    grad_output = cotangent.astype(jnp.float32)
    grad_down_bias = placed(jnp.sum(grad_output, axis=0), D, 0)
    own_up = lax.dynamic_slice_in_dim(
        up_shift.astype(jnp.float32), member * hidden_local, hidden_local
    )
    rows_two = lax.all_gather(normed_two.astype(jnp.bfloat16), "tensor", axis=0, tiled=True)
    hidden = jnp.dot(rows_two, up_mat, preferred_element_type=jnp.float32) + own_up
    active = jax.nn.gelu(hidden).astype(jnp.bfloat16)
    output = (
        residual
        + lax.psum_scatter(
            jnp.dot(
                take_rows(active, jnp.int32(0), own_rows * lax.axis_size("tensor")),
                down_mat,
                preferred_element_type=jnp.float32,
            ).astype(jnp.bfloat16),
            "tensor",
            scatter_dimension=0,
            tiled=True,
        ).astype(jnp.float32)
        + down_shift.astype(jnp.float32)
    )
    grad_full = lax.all_gather(cotangent, "tensor", axis=0, tiled=True)
    grad_active = times_transpose(grad_full, down_mat)
    grad_down = contract_rows(active, grad_full)
    gelu_back = jax.vjp(jax.nn.gelu, hidden)[1]
    grad_hidden = gelu_back(grad_active)[0].astype(jnp.bfloat16)
    grad_up_bias = placed(
        jnp.sum(grad_hidden, axis=0, dtype=jnp.float32), full_hidden, member * hidden_local
    )
    grad_up = contract_rows(rows_two, grad_hidden)
    grad_normed_two = lax.psum_scatter(
        times_transpose(
            take_rows(grad_hidden, jnp.int32(0), own_rows * lax.axis_size("tensor")), up_mat
        ).astype(jnp.bfloat16),
        "tensor",
        scatter_dimension=0,
        tiled=True,
    ).astype(jnp.float32)
    norm_back_two = jax.vjp(layer_norm, residual, gain_two, shift_two)[1]
    grad_resid_part, grad_gain_two, grad_shift_two = norm_back_two(grad_normed_two)
    grad_residual = grad_output + grad_resid_part
    ffn_terms = (grad_gain_two, grad_shift_two, grad_up, grad_up_bias, grad_down, grad_down_bias)
    grad_att = lax.all_gather(grad_residual.astype(jnp.bfloat16), "tensor", axis=0, tiled=True)
    grad_out_mat = jnp.dot(mixed_cols, grad_att, preferred_element_type=jnp.float32)
    grad_mixed = (
        times_transpose(out_mat, grad_att)
        .astype(jnp.bfloat16)
        .reshape(head_count, HEAD, total_rows)
    )
    grad_mixed = grad_mixed.astype(jnp.float32)
    grad_scaled = (grad_mixed * inv_total).astype(jnp.bfloat16)
    grad_low = (grad_mixed * (inv_total * score_scale)).astype(jnp.bfloat16)
    inner = -jnp.sum(grad_low.astype(jnp.float32) * mixed_full, axis=1, keepdims=True)
    inner_high = inner.astype(jnp.bfloat16)
    inner_rest = (inner - inner_high.astype(jnp.float32)).astype(jnp.bfloat16)
    grad_aug = jnp.concatenate([grad_low, inner_high, inner_rest, blank], axis=1)
    dqu, dqw, dk, dv, dpos = attend_back_all(
        weights, query_u, query_w, key_rows, value_rows, pos_rows, grad_aug, grad_scaled, col_table
    )
    grad_keys_all = dk.reshape(local_width, total_rows).astype(jnp.bfloat16)
    grad_values_all = dv.reshape(local_width, total_rows).astype(jnp.bfloat16)
    grad_pos = dpos.reshape(local_width, D).T
    grad_query_u = dqu.reshape(local_width, total_rows)
    grad_query_w = dqw.reshape(local_width, total_rows)
    grad_bias_one = placed(jnp.sum(grad_query_u, axis=1), D, member * local_width)
    grad_bias_two = placed(jnp.sum(grad_query_w, axis=1), D, member * local_width)
    grad_query = (grad_query_u + grad_query_w).astype(jnp.bfloat16)
    grad_query_mat = times_transpose(rows_all.T, grad_query)
    grad_key_mat = times_transpose(rows_all.T, grad_keys_all)
    grad_value_mat = times_transpose(rows_all.T, grad_values_all)
    first_row = jnp.int32(0)
    part_sum = times_transpose(
        take_cols(grad_query, first_row, own_rows * lax.axis_size("tensor")).T, query_mat
    )
    part_sum = part_sum + times_transpose(
        take_cols(grad_keys_all, first_row, own_rows * lax.axis_size("tensor")).T, key_mat
    )
    grad_normed = lax.psum_scatter(
        (
            part_sum
            + times_transpose(
                take_cols(grad_values_all, first_row, own_rows * lax.axis_size("tensor")).T,
                value_mat,
            )
        ).astype(jnp.bfloat16),
        "tensor",
        scatter_dimension=0,
        tiled=True,
    ).astype(jnp.float32)
    norm_back_one = jax.vjp(layer_norm, inputs, gain_one, shift_one)[1]
    grad_in_part, grad_gain_one, grad_shift_one = norm_back_one(grad_normed)
    grad_tokens = grad_residual + grad_in_part
    grad_squares = (grad_query_mat, grad_key_mat, grad_value_mat, grad_pos, grad_out_mat.T)
    grad_wides = (grad_up, grad_down.T)
    grad_vecs = jnp.stack(
        (
            grad_gain_one, grad_shift_one, grad_bias_one, grad_bias_two,
            ffn_terms[0], ffn_terms[1], ffn_terms[5],
        )
    )
    grad_vecs, grad_up_row = lax.psum((grad_vecs, ffn_terms[3]), "tensor")
    def share(array):
        return lax.psum_scatter(array, "dp", scatter_dimension=0, tiled=True)

    squares = [share(m) for m in grad_squares]
    wides = [share(m) for m in grad_wides]
    vecs = [share(v) for v in grad_vecs]
    up_part = share(grad_up_row)
    return (
        output.astype(jnp.bfloat16),
        grad_tokens,
        vecs[0],
        vecs[1],
        squares[0],
        squares[1],
        squares[2],
        squares[3],
        vecs[2],
        vecs[3],
        squares[4].T,
        vecs[4],
        vecs[5],
        wides[0],
        up_part,
        wides[1].T,
        vecs[6],
    )


def local_direct(
    tokens,
    block_ids,
    ln1_gain,
    ln1_bias,
    w_query,
    w_key,
    w_value,
    w_pos,
    bias_u,
    bias_w,
    w_out,
    ln2_gain,
    ln2_bias,
    w_up,
    bias_up,
    w_down,
    bias_down,
    cotangent,
):
    total_rows = block_ids.shape[0]
    vectors = (ln1_gain, ln1_bias, bias_u, bias_w, ln2_gain, ln2_bias, bias_down)
    columns = jnp.pad(jnp.stack(vectors, axis=1), ((0, 0), (0, VECS - len(vectors))))
    up_row = jnp.pad(bias_up.reshape(1, -1), ((0, 15), (0, 0)))
    table = angle_table()
    row_table = jnp.asarray(table)
    col_table = jnp.asarray(np.ascontiguousarray(table.T))
    (
        weights, query_u, query_w, key_rows, value_aug, mixed_sums, mixed_cols, rows_all, pos_back,
        near, far, up_rows, grad_full,
    ) = first_call(
        tokens,
        cotangent,
        jnp.concatenate((w_query, w_key, w_value, w_pos, columns), axis=1),
        jnp.concatenate((w_up, w_down.T, w_out.T), axis=1),
        up_row,
        block_ids.reshape(1, total_rows),
        row_table,
        col_table,
    )
    out, grad_res, grad_att, grad_far, grad_vec, grad_up_part = middle_call(
        mixed_cols, tokens, grad_full, far, near, up_rows
    )
    (
        grad_tokens, grad_query_mat, grad_key_mat, grad_value_mat, grad_pos, grad_up, grad_down,
        grad_out, grad_vecs, grad_up_row,
    ) = last_call(
        weights, query_u, query_w, key_rows, value_aug, mixed_sums, pos_back, col_table, grad_att,
        far, near, rows_all, tokens, grad_res, grad_far, grad_vec, grad_up_part,
    )
    return (
        out,
        grad_tokens,
        grad_vecs[0],
        grad_vecs[1],
        grad_query_mat,
        grad_key_mat,
        grad_value_mat,
        grad_pos,
        grad_vecs[2],
        grad_vecs[3],
        grad_out.T,
        grad_vecs[4],
        grad_vecs[5],
        grad_up,
        grad_up_row.reshape(-1),
        grad_down.T,
        grad_vecs[6],
    )


def solution(mesh):
    in_specs = (
        P(("dp", "tensor"), None),
        P("dp"),
        P("dp"),
        P("dp"),
        P("dp", "tensor"),
        P("dp", "tensor"),
        P("dp", "tensor"),
        P("dp", "tensor"),
        P("dp"),
        P("dp"),
        P("tensor", "dp"),
        P("dp"),
        P("dp"),
        P("dp", "tensor"),
        P("dp"),
        P("tensor", "dp"),
        P("dp"),
        P(("dp", "tensor"), None),
    )
    out_specs = (
        P(("dp", "tensor"), None),
        P(("dp", "tensor"), None),
        P("dp"),
        P("dp"),
        P("dp", "tensor"),
        P("dp", "tensor"),
        P("dp", "tensor"),
        P("dp", "tensor"),
        P("dp"),
        P("dp"),
        P("tensor", "dp"),
        P("dp"),
        P("dp"),
        P("dp", "tensor"),
        P("dp"),
        P("tensor", "dp"),
        P("dp"),
    )
    pieces = D // mesh.shape["dp"]
    whole_tiles = pieces % 16 == 0 and mesh.shape["tensor"] == 2
    local = local_direct if whole_tiles else local_plain
    return jax.shard_map(local, mesh=mesh, in_specs=in_specs, out_specs=out_specs, check_vma=False)
```

```python
import functools
import math

import jax
import jax.numpy as jnp
import ml_dtypes
import numpy as np
from jax import lax
from jax.experimental import pallas as pl
from jax.experimental.pallas import tpu as pltpu
from jax.sharding import PartitionSpec as P

D = 512
HEAD = 64
L = 2048


MESH = pl.DeviceIdType.MESH
VECS = 128


def peer_at(offset):
    count = lax.axis_size("dp")
    return lax.rem(lax.axis_index("dp") + offset, count)


PLANE = 4


def place_of(me, count):
    return lax.div(me, PLANE), lax.rem(me, PLANE), count // PLANE


def along(me, count, offset):
    level, spot, levels = place_of(me, count)
    return lax.rem(level + offset, levels) * PLANE + spot


def across(me, count, offset):
    level, spot, _ = place_of(me, count)
    return level * PLANE + lax.rem(spot + offset, PLANE)


def remote(source, target, send_sem, recv_sem, device):
    return pltpu.make_async_remote_copy(
        src_ref=source,
        dst_ref=target,
        send_sem=send_sem,
        recv_sem=recv_sem,
        device_id={"dp": device},
        device_id_type=MESH,
    )


def greet_all(count, with_pair=False):
    barrier = pltpu.get_barrier_semaphore()

    def greet(offset, carry):
        pl.semaphore_signal(
            barrier, inc=1, device_id={"dp": peer_at(offset)}, device_id_type=MESH
        )
        return carry

    lax.fori_loop(1, count, greet, 0)
    if with_pair:
        pl.semaphore_signal(
            barrier, inc=1, device_id={"tensor": 1 - lax.axis_index("tensor")}, device_id_type=MESH
        )
    pl.semaphore_wait(barrier, count if with_pair else count - 1)


def layer_norm(values, gain_vec, shift_vec):
    center = values - jnp.mean(values, axis=-1, keepdims=True)
    spread = jnp.mean(center * center, axis=-1, keepdims=True)
    return center * lax.rsqrt(spread + 1e-05) * gain_vec + shift_vec


def take_rows(array, first_row, row_count):
    return lax.dynamic_slice_in_dim(array, first_row, row_count, 0)


def take_cols(array, first_col, col_count):
    return lax.dynamic_slice_in_dim(array, first_col, col_count, array.ndim - 1)


def contract_rows(left, right):
    return lax.dot_general(
        left, right, (((0,), (0,)), ((), ())), preferred_element_type=jnp.float32
    )


def times_transpose(left, right):
    return lax.dot_general(
        left, right, (((1,), (1,)), ((), ())), preferred_element_type=jnp.float32
    )


def project_cols(weight, row_data):
    return lax.dot_general(
        weight, row_data, (((0,), (1,)), ((), ())), preferred_element_type=jnp.float32
    )


TILE = 256
TILES = L // TILE
AUG = HEAD + 16
LOG2E = 1.4426950408889634


def tiles_seen(tile):
    return min(tile + 2, TILES)


PACK = [TILE * sum(tiles_seen(t) for t in range(tile)) for tile in range(TILES + 1)]


def angle_table():
    freqs = np.exp(np.arange(0, D, 2, dtype=np.float64) * (-math.log(10000.0) / D))
    angles = np.arange(L, dtype=np.float64)[:, None] * freqs[None, :]
    return np.concatenate([np.cos(angles), np.sin(angles)], axis=1).astype(ml_dtypes.bfloat16)


def dot_nn(left, right):
    return jnp.dot(left, right, preferred_element_type=jnp.float32)


def attend_kernel(qu_ref, qw_ref, key_ref, value_ref, pos_ref, ids_ref, row_ref, col_ref, e_ref, o_ref):
    half = D // 2
    for tile in range(TILES):
        rows = slice(tile * TILE, (tile + 1) * TILE)
        width = tiles_seen(tile) * TILE
        both = contract_rows(qw_ref[:, rows], pos_ref[...])
        part_a, part_b = both[:, :half], both[:, half:]
        cos_i = row_ref[rows, :half].astype(jnp.float32)
        sin_i = row_ref[rows, half:].astype(jnp.float32)
        turned = jnp.concatenate(
            [part_a * sin_i + part_b * cos_i, part_b * sin_i - part_a * cos_i], axis=1
        ).astype(jnp.bfloat16)
        scores = dot_nn(turned, col_ref[:, :width]) + contract_rows(
            qu_ref[:, rows], key_ref[:, :width]
        )
        ids_row = ids_ref[:, tile * TILE : width]
        ids_col = jnp.broadcast_to(ids_row[:, :TILE], (8, TILE)).T[:, :1]
        edge = jnp.where(ids_row <= ids_col, scores[:, tile * TILE :], -1e30)
        if tile:
            scores = jnp.concatenate([scores[:, : tile * TILE], edge], axis=1)
        else:
            scores = edge
        peak = jnp.max(scores, axis=1, keepdims=True)
        weights = jnp.exp2(scores - peak).astype(jnp.bfloat16)
        e_ref[:, PACK[tile] : PACK[tile + 1]] = weights
        o_ref[:, rows] = times_transpose(value_ref[:, :width], weights)


def attend_back_kernel(
    e_ref, qu_ref, qw_ref, key_ref, value_ref, pos_ref, aug_ref, scaled_ref, col_ref,
    dqu_ref, dqw_ref, dk_ref, dv_ref, dpos_ref,
):
    half = D // 2
    dk_ref[...] = jnp.zeros_like(dk_ref)
    dv_ref[...] = jnp.zeros_like(dv_ref)
    for tile in range(TILES):
        rows = slice(tile * TILE, (tile + 1) * TILE)
        width = tiles_seen(tile) * TILE
        weights = e_ref[:, PACK[tile] : PACK[tile + 1]]
        grad_probs = contract_rows(aug_ref[:, rows], value_ref[:, :width])
        grad_scores = (weights.astype(jnp.float32) * grad_probs).astype(jnp.bfloat16)
        dv_ref[:, :width] += dot_nn(scaled_ref[:, rows], weights)
        dk_ref[:, :width] += dot_nn(qu_ref[:, rows], grad_scores)
        dqu_ref[:, rows] = times_transpose(key_ref[:, :width], grad_scores)
        turned = times_transpose(col_ref[:, :width], grad_scores)
        part_c, part_s = turned[:half], turned[half:]
        cos_i = col_ref[:half, rows].astype(jnp.float32)
        sin_i = col_ref[half:, rows].astype(jnp.float32)
        both = jnp.concatenate(
            [part_c * sin_i - part_s * cos_i, part_c * cos_i + part_s * sin_i], axis=0
        ).astype(jnp.bfloat16)
        dqw_ref[:, rows] = dot_nn(pos_ref[...], both)
        here = times_transpose(qw_ref[:, rows], both)
        if tile:
            dpos_ref[...] += here
        else:
            dpos_ref[...] = here


def per_head(rows, cols):
    return pl.BlockSpec((None, rows, cols), lambda h: (h, 0, 0))


def shared(rows, cols):
    return pl.BlockSpec((rows, cols), lambda h: (0, 0))


def attend_all(qu, qw, keys, values, pos, ids, row_table, col_table):
    heads = qu.shape[0]
    f32, bf16 = jnp.float32, jnp.bfloat16
    return pl.pallas_call(
        attend_kernel,
        grid=(heads,),
        in_specs=[per_head(HEAD, L)] * 3
        + [per_head(AUG, L), per_head(HEAD, D), shared(1, L), shared(L, D), shared(D, L)],
        out_specs=[per_head(TILE, PACK[-1]), per_head(AUG, L)],
        out_shape=[
            jax.ShapeDtypeStruct((heads, TILE, PACK[-1]), bf16),
            jax.ShapeDtypeStruct((heads, AUG, L), f32),
        ],
        compiler_params=pltpu.CompilerParams(vmem_limit_bytes=56 * 1024 * 1024),
    )(qu, qw, keys, values, pos, ids, row_table, col_table)


def attend_back_all(weights, qu, qw, keys, values, pos, aug, scaled, col_table):
    heads = qu.shape[0]
    f32 = jnp.float32
    return pl.pallas_call(
        attend_back_kernel,
        grid=(heads,),
        in_specs=[per_head(TILE, PACK[-1])]
        + [per_head(HEAD, L)] * 3
        + [per_head(AUG, L), per_head(HEAD, D), per_head(AUG, L), per_head(HEAD, L), shared(D, L)],
        out_specs=[per_head(HEAD, L)] * 4 + [per_head(HEAD, D)],
        out_shape=[jax.ShapeDtypeStruct((heads, HEAD, L), f32)] * 4
        + [jax.ShapeDtypeStruct((heads, HEAD, D), f32)],
        compiler_params=pltpu.CompilerParams(vmem_limit_bytes=56 * 1024 * 1024),
    )(weights, qu, qw, keys, values, pos, aug, scaled, col_table)


def placed(part_vec, length, offset):
    return lax.dynamic_update_slice_in_dim(jnp.zeros((length,), jnp.float32), part_vec, offset, 0)


NEAR = 4 * 256


def first_kernel(
    count, tok_ref, cot_ref, wq_ref, wk_ref, wv_ref, wp_ref, wu_ref, wd_ref, wo_ref, *refs
):
    vec_refs, bup_ref, ids_ref, row_ref, col_ref = refs[:7], refs[7], refs[8], refs[9], refs[10]
    (
        e_ref, qu_ref, qw_ref, key_ref, va_ref, o_ref, mix_ref, norm_ref, pos_ref,
        near_all, far_all, up_all, cot_all,
        near_ref, far_ref, up_ref, vec_ref, tok_all, quf_ref, qwf_ref, turn_ref, e_buf,
        along_send, along_recv, across_send, across_recv, own_sems, pair_send, pair_recv, e_sems,
    ) = refs[11:]
    half = D // 2
    me, member = lax.axis_index("dp"), lax.axis_index("tensor")
    levels = count // PLANE
    pair = {"tensor": 1 - member}
    own_rows = tok_ref.shape[0]
    own = pl.ds(pl.multiple_of(member * own_rows, own_rows), own_rows)
    parts = (near_ref, far_ref, up_ref)
    wholes = (near_all, far_all, up_all)

    def rows_of(index, device):
        rows = parts[index].shape[0]
        return wholes[index].at[pl.ds(pl.multiple_of(device * rows, rows), rows)]

    def go_along(index, offset):
        return remote(
            parts[index], rows_of(index, me),
            along_send.at[index, offset - 1], along_recv.at[index, offset - 1],
            along(me, count, offset),
        )

    def go_across(index, offset, step):
        owner = along(me, count, levels - step)
        return remote(
            parts[index] if step == 0 else rows_of(index, owner), rows_of(index, owner),
            across_send.at[index, offset - 1, step], across_recv.at[index, offset - 1, step],
            across(me, count, offset),
        )

    def own_copy(index):
        return pltpu.make_async_copy(parts[index], rows_of(index, me), own_sems.at[index])

    def begin_gather(index):
        for offset in range(1, levels):
            go_along(index, offset).start()
        for offset in range(1, PLANE):
            go_across(index, offset, 0).start()
        own_copy(index).start()

    def forward(index):
        for step in range(1, levels):
            go_along(index, step).wait()
            for offset in range(1, PLANE):
                go_across(index, offset, step).start()

    def finish_gather(index):
        for step in range(levels):
            for offset in range(1, PLANE):
                go_across(index, offset, step).wait()
        own_copy(index).wait()

    width = wq_ref.shape[1]
    hidden = wu_ref.shape[1]
    shard = wq_ref.shape[0]
    vec_ref[...] = jnp.zeros_like(vec_ref)
    for place, ref in enumerate(vec_refs):
        vec_ref[place : place + 1, :shard] = ref[...].astype(jnp.float32)
    near_ref[:, NEAR:] = vec_ref[...].T[:shard].astype(jnp.bfloat16)
    for place, ref in enumerate((wq_ref, wk_ref, wv_ref, wp_ref)):
        near_ref[:, place * width : (place + 1) * width] = ref[...]
    far_ref[:, :hidden] = wu_ref[...]
    far_ref[:, hidden : 2 * hidden] = wd_ref[...]
    far_ref[:, 2 * hidden :] = wo_ref[...]
    up_ref[...] = jnp.broadcast_to(bup_ref[...].astype(jnp.float32), up_ref.shape).astype(
        jnp.bfloat16
    )

    def to_pair(source, target, slot):
        return pltpu.make_async_remote_copy(
            src_ref=source,
            dst_ref=target.at[own],
            send_sem=pair_send.at[slot],
            recv_sem=pair_recv.at[slot],
            device_id=pair,
            device_id_type=MESH,
        )

    greet_all(count, True)
    begin_gather(0)
    begin_gather(2)
    exchanges = (to_pair(tok_ref, tok_all, 0), to_pair(cot_ref, cot_all, 1))
    keeps = (
        pltpu.make_async_copy(tok_ref, tok_all.at[own], own_sems.at[3]),
        pltpu.make_async_copy(cot_ref, cot_all.at[own], own_sems.at[4]),
    )
    for copy in exchanges + keeps:
        copy.start()
    forward(0)
    begin_gather(1)
    forward(2)
    finish_gather(0)
    exchanges[0].wait()
    keeps[0].wait()

    vec_block = near_all[:, NEAR:].astype(jnp.float32)
    vec_rows = vec_block.T
    gain, shift = vec_rows[0:1], vec_rows[1:2]
    turn_ref[...] = near_all[:, :768].T
    pos_ref[...] = near_all[:, 768:NEAR].T
    heads = width // HEAD
    own_cols = pl.ds(pl.multiple_of(member * width, width), width)
    vec_cols = near_all[own_cols, NEAR:].astype(jnp.float32)
    bias_u, bias_w = vec_cols[:, 2:3], vec_cols[:, 3:4]
    fold = LOG2E / math.sqrt(HEAD)
    place = lax.broadcasted_iota(jnp.int32, (AUG - HEAD, TILE), 0)
    marks = jnp.where(place < 2, 1.0, 0.0).astype(jnp.bfloat16)
    for tile in range(TILES):
        rows = slice(tile * TILE, (tile + 1) * TILE)
        normed = layer_norm(tok_all[rows, :].astype(jnp.float32), gain, shift)
        normed = normed.astype(jnp.bfloat16)
        norm_ref[rows, :] = normed
        projected = times_transpose(turn_ref[...], normed)
        sum_u = projected[:width] + bias_u
        sum_w = projected[:width] + bias_w
        qu_ref[:, rows] = sum_u.astype(jnp.bfloat16)
        qw_ref[:, rows] = sum_w.astype(jnp.bfloat16)
        quf_ref[:, rows] = (sum_u * fold).astype(jnp.bfloat16)
        qwf_ref[:, rows] = (sum_w * fold).astype(jnp.bfloat16)
        key_ref[:, rows] = projected[width : 2 * width].astype(jnp.bfloat16)
        for head in range(heads):
            values = projected[2 * width + head * HEAD : 2 * width + (head + 1) * HEAD]
            va_ref[head * AUG : head * AUG + HEAD, rows] = values.astype(jnp.bfloat16)
            va_ref[head * AUG + HEAD : (head + 1) * AUG, rows] = marks

    def e_copy(head, slot):
        return pltpu.make_async_copy(e_buf.at[slot], e_ref.at[head], e_sems.at[slot])

    def one_head(head, carry):
        slot = lax.rem(head, 2)
        lines = pl.ds(pl.multiple_of(head * HEAD, HEAD), HEAD)
        more = pl.ds(pl.multiple_of(head * AUG, AUG), AUG)
        upper = pl.ds(pl.multiple_of(head * AUG, 16), HEAD)
        lower = pl.ds(pl.multiple_of(head * AUG + HEAD, 16), AUG - HEAD)

        @pl.when(head >= 2)
        def _():
            e_copy(head - 2, slot).wait()

        for tile in range(TILES):
            rows = slice(tile * TILE, (tile + 1) * TILE)
            seen = tiles_seen(tile) * TILE
            both = contract_rows(qwf_ref[lines, rows], pos_ref[lines, :])
            part_a, part_b = both[:, :half], both[:, half:]
            cos_i = row_ref[rows, :half].astype(jnp.float32)
            sin_i = row_ref[rows, half:].astype(jnp.float32)
            turned = jnp.concatenate(
                [part_a * sin_i + part_b * cos_i, part_b * sin_i - part_a * cos_i], axis=1
            ).astype(jnp.bfloat16)
            scores = dot_nn(turned, col_ref[:, :seen]) + contract_rows(
                quf_ref[lines, rows], key_ref[lines, :seen]
            )
            ids_row = ids_ref[:, tile * TILE : seen]
            ids_col = jnp.broadcast_to(ids_row[:, :TILE], (8, TILE)).T[:, :1]
            edge = jnp.where(ids_row <= ids_col, scores[:, tile * TILE :], -1e30)
            if tile:
                scores = jnp.concatenate([scores[:, : tile * TILE], edge], axis=1)
            else:
                scores = edge
            peak = jnp.max(scores, axis=1, keepdims=True)
            weights = jnp.exp2(scores - peak).astype(jnp.bfloat16)
            e_buf[slot, :, PACK[tile] : PACK[tile + 1]] = weights
            sums = times_transpose(va_ref[more, :seen], weights)
            inverse = 1.0 / sums[HEAD : HEAD + 1]
            mixed = sums[:HEAD] * inverse
            o_ref[upper, rows] = mixed
            o_ref[lower, rows] = jnp.broadcast_to(inverse, (AUG - HEAD, TILE))
            mix_ref[lines, rows] = mixed.astype(jnp.bfloat16)
        e_copy(head, slot).start()

        @pl.when(head == 0)
        def _():
            forward(1)

        return carry

    lax.fori_loop(0, heads, one_head, 0)
    for head in range(max(heads - 2, 0), heads):
        e_copy(head, head % 2).wait()
    exchanges[1].wait()
    keeps[1].wait()
    finish_gather(1)
    finish_gather(2)


VMEM_SPEC = pl.BlockSpec(memory_space=pltpu.VMEM)
ANY_SPEC = pl.BlockSpec(memory_space=pl.ANY)


def first_call(tokens, cotangent, squares, wides, vectors, bup, ids, row_table, col_table):
    count = lax.axis_size("dp")
    levels = count // PLANE
    rows = ids.shape[1]
    shard, width = squares[0].shape
    hidden = wides[0].shape[1]
    heads = width // HEAD
    far_width = 2 * hidden + width
    f32, bf16 = jnp.float32, jnp.bfloat16

    def shape(*dims, kind=bf16):
        return jax.ShapeDtypeStruct(dims, kind)

    return pl.pallas_call(
        functools.partial(first_kernel, count),
        in_specs=[VMEM_SPEC] * 20,
        out_specs=[ANY_SPEC] + [VMEM_SPEC] * 12,
        out_shape=[
            shape(heads, TILE, PACK[-1]),
            shape(width, rows),
            shape(width, rows),
            shape(width, rows),
            shape(heads * AUG, rows),
            shape(heads * AUG, rows, kind=f32),
            shape(width, rows),
            shape(rows, D),
            shape(width, D),
            shape(D, NEAR + VECS),
            shape(D, far_width),
            shape(16 * count, bup.shape[1]),
            shape(rows, D),
        ],
        scratch_shapes=[
            pltpu.VMEM((shard, NEAR + VECS), bf16),
            pltpu.VMEM((shard, far_width), bf16),
            pltpu.VMEM((16, bup.shape[1]), bf16),
            pltpu.VMEM((VECS, VECS), f32),
            pltpu.VMEM((rows, D), bf16),
            pltpu.VMEM((width, rows), bf16),
            pltpu.VMEM((width, rows), bf16),
            pltpu.VMEM((3 * width, D), bf16),
            pltpu.VMEM((2, TILE, PACK[-1]), bf16),
            pltpu.SemaphoreType.DMA((3, levels - 1)),
            pltpu.SemaphoreType.DMA((3, levels - 1)),
            pltpu.SemaphoreType.DMA((3, PLANE - 1, levels)),
            pltpu.SemaphoreType.DMA((3, PLANE - 1, levels)),
            pltpu.SemaphoreType.DMA((5,)),
            pltpu.SemaphoreType.DMA((2,)),
            pltpu.SemaphoreType.DMA((2,)),
            pltpu.SemaphoreType.DMA((2,)),
        ],
        compiler_params=pltpu.CompilerParams(
            collective_id=0, has_side_effects=True, vmem_limit_bytes=60 * 1024 * 1024
        ),
    )(tokens, cotangent, *squares, *wides, *vectors, bup, ids, row_table, col_table)


CHUNK = 256
GELU_SCALE = math.sqrt(2.0 / math.pi)


def fold_rows(values):
    return jnp.sum(values.reshape(values.shape[0] // 8, 8, values.shape[1]), axis=0)


def norm_parts(values):
    center = values - jnp.mean(values, axis=-1, keepdims=True)
    spread = jnp.mean(center * center, axis=-1, keepdims=True)
    rate = lax.rsqrt(spread + 1e-05)
    return center * rate, rate


def norm_grad(grad, gain, normed, rate):
    scaled = grad * gain
    mean = jnp.mean(scaled, axis=-1, keepdims=True)
    along = jnp.mean(scaled * normed, axis=-1, keepdims=True)
    return rate * (scaled - mean - normed * along)


def to_other(source, target, send_sem, recv_sem):
    return pltpu.make_async_remote_copy(
        src_ref=source,
        dst_ref=target,
        send_sem=send_sem,
        recv_sem=recv_sem,
        device_id={"tensor": 1 - lax.axis_index("tensor")},
        device_id_type=MESH,
    )


def dot_tt(left, right):
    return lax.dot_general(
        left, right, (((0,), (1,)), ((), ())), preferred_element_type=jnp.float32
    )


def middle_kernel(
    mix_ref, tok_ref, cot_ref, far_ref, vec_ref, up_ref,
    out_ref, gres_ref, gatt_ref, gfar_ref, vec_out, bup_out,
    send_a, recv_a, res_ref, n2_ref, n2t_ref, cott_ref, act_ref, gh_ref,
    osend, orecv, oacc, gacc, bup_acc, vec_acc, send_sems, recv_sems,
):
    member = lax.axis_index("tensor")
    own_rows = tok_ref.shape[0]
    chunks = own_rows // CHUNK
    own0 = pl.multiple_of(member * own_rows, own_rows)
    oth0 = pl.multiple_of((1 - member) * own_rows, own_rows)
    hidden = act_ref.shape[1]
    up_cols, down_cols = slice(0, hidden), slice(hidden, 2 * hidden)
    out_cols = slice(2 * hidden, far_ref.shape[1])

    def at(base, chunk):
        return pl.ds(pl.multiple_of(base + chunk * CHUNK, CHUNK), CHUNK)

    barrier = pltpu.get_barrier_semaphore()
    pl.semaphore_signal(barrier, inc=1, device_id={"tensor": 1 - member}, device_id_type=MESH)
    pl.semaphore_wait(barrier, 1)

    def pass_on(stage, chunk):
        here = at(0, chunk)
        pairs = (
            (send_a.at[here], recv_a.at[here]),
            (n2_ref.at[at(own0, chunk)], n2_ref.at[at(own0, chunk)]),
            (osend.at[0, here], orecv.at[0, here]),
            (osend.at[1, here], orecv.at[1, here]),
            (gatt_ref.at[at(own0, chunk)], gatt_ref.at[at(own0, chunk)]),
        )
        source, target = pairs[stage]
        return to_other(
            source, target, send_sems.at[stage, chunk], recv_sems.at[stage, chunk]
        )

    vec_rows = vec_ref[:, NEAR:].astype(jnp.float32).T
    gain, shift, down_shift = vec_rows[4:5], vec_rows[5:6], vec_rows[6:7]
    ups = hidden // 128
    up_block = up_ref[pl.ds(pl.multiple_of(member * ups * 16, 16), ups * 16), :].astype(jnp.float32)
    up_shift = jnp.concatenate([up_block[16 * k : 16 * k + 1] for k in range(ups)], axis=1)

    def branch(rows):
        return dot_tt(mix_ref[:, rows], far_ref[:, out_cols])

    for chunk in range(chunks):
        send_a[at(0, chunk), :] = branch(at(oth0, chunk)).astype(jnp.bfloat16)
        pass_on(0, chunk).start()
    for chunk in range(chunks):
        here = at(0, chunk)
        part = branch(at(own0, chunk))
        pass_on(0, chunk).wait()
        residual = tok_ref[here, :].astype(jnp.float32) + part + recv_a[here, :].astype(jnp.float32)
        res_ref[here, :] = residual
        n2_ref[at(own0, chunk), :] = (norm_parts(residual)[0] * gain + shift).astype(jnp.bfloat16)
        pass_on(1, chunk).start()

    bup_acc[...] = jnp.zeros_like(bup_acc)
    vec_acc[...] = jnp.zeros_like(vec_acc)

    def ffn(rows):
        normed = n2_ref[rows, :]
        grads = cot_ref[rows, :]
        value = dot_nn(normed, far_ref[:, up_cols]) + up_shift
        square = value * value
        bend = jnp.tanh(GELU_SCALE * value * (1.0 + 0.044715 * square))
        half = 0.5 * (1.0 + bend)
        active = (value * half).astype(jnp.bfloat16)
        slope = half + 0.5 * value * (1.0 - bend * bend) * (
            GELU_SCALE * (1.0 + 3.0 * 0.044715 * square)
        )
        grad_hidden = (dot_nn(grads, far_ref[:, down_cols]) * slope).astype(jnp.bfloat16)
        act_ref[rows, :] = active
        gh_ref[rows, :] = grad_hidden
        n2t_ref[:, rows] = normed.T
        cott_ref[:, rows] = grads.T
        bup_acc[...] += fold_rows(grad_hidden.astype(jnp.float32))
        return (
            times_transpose(active, far_ref[:, down_cols]),
            times_transpose(grad_hidden, far_ref[:, up_cols]),
        )

    def ffn_own(chunk, carry):
        oacc[at(0, chunk), :], gacc[at(0, chunk), :] = ffn(at(own0, chunk))
        return carry

    def ffn_other(chunk, carry):
        pass_on(1, chunk).wait()
        here = at(0, chunk)
        for stage, part in zip((2, 3), ffn(at(oth0, chunk))):
            osend[stage - 2, here, :] = part.astype(jnp.bfloat16)
            pass_on(stage, chunk).start()
        return carry

    lax.fori_loop(0, 1, ffn_own, 0)
    lax.fori_loop(0, chunks, ffn_other, 0)
    lax.fori_loop(1, chunks, ffn_own, 0)

    def close(chunk, carry):
        here = at(0, chunk)
        pass_on(2, chunk).wait()
        pass_on(3, chunk).wait()
        residual = res_ref[here, :]
        out = residual + oacc[here, :] + orecv[0, here, :].astype(jnp.float32) + down_shift
        out_ref[here, :] = out.astype(jnp.bfloat16)
        grad = gacc[here, :] + orecv[1, here, :].astype(jnp.float32)
        normed, rate = norm_parts(residual)
        top = cot_ref[at(own0, chunk), :].astype(jnp.float32)
        grad_res = top + norm_grad(grad, gain, normed, rate)
        gres_ref[here, :] = grad_res
        gatt_ref[at(own0, chunk), :] = grad_res.astype(jnp.bfloat16)
        pass_on(4, chunk).start()
        vec_acc[0:8, :] += fold_rows(grad * normed)
        vec_acc[8:16, :] += fold_rows(grad)
        vec_acc[16:24, :] += fold_rows(top)
        return carry

    lax.fori_loop(0, chunks, close, 0)
    for part in range(hidden // CHUNK):
        cols = slice(part * CHUNK, (part + 1) * CHUNK)
        gfar_ref[:, cols] = dot_nn(n2t_ref[...], gh_ref[:, cols]).astype(jnp.bfloat16)
        gfar_ref[:, hidden + part * CHUNK : hidden + (part + 1) * CHUNK] = dot_nn(
            cott_ref[...], act_ref[:, cols]
        ).astype(jnp.bfloat16)
    vec_out[...] = jnp.concatenate(
        [jnp.sum(vec_acc[8 * v : 8 * v + 8, :], axis=0, keepdims=True) for v in range(3)]
        + [jnp.zeros((5, vec_acc.shape[1]), jnp.float32)],
        axis=0,
    )
    for k in range(ups):
        bup_out[8 * k : 8 * k + 8, :] = bup_acc[:, 128 * k : 128 * k + 128]
    for chunk in range(chunks):
        pass_on(4, chunk).wait()
    gfar_ref[:, out_cols] = dot_tt(gatt_ref[...], mix_ref[...]).astype(jnp.bfloat16)


def middle_call(mix, tokens, cot_all, far_all, near_all, up_all):
    rows, own_rows = cot_all.shape[0], tokens.shape[0]
    chunks = own_rows // CHUNK
    hidden = (far_all.shape[1] - mix.shape[0]) // 2
    f32, bf16 = jnp.float32, jnp.bfloat16
    return pl.pallas_call(
        middle_kernel,
        in_specs=[VMEM_SPEC] * 6,
        out_specs=[VMEM_SPEC] * 6,
        out_shape=[
            jax.ShapeDtypeStruct((own_rows, D), bf16),
            jax.ShapeDtypeStruct((own_rows, D), f32),
            jax.ShapeDtypeStruct((rows, D), bf16),
            jax.ShapeDtypeStruct(far_all.shape, bf16),
            jax.ShapeDtypeStruct((8, D), f32),
            jax.ShapeDtypeStruct((hidden // 16, 128), f32),
        ],
        scratch_shapes=[
            pltpu.VMEM((own_rows, D), bf16),
            pltpu.VMEM((own_rows, D), bf16),
            pltpu.VMEM((own_rows, D), f32),
            pltpu.VMEM((rows, D), bf16),
            pltpu.VMEM((D, rows), bf16),
            pltpu.VMEM((D, rows), bf16),
            pltpu.VMEM((rows, hidden), bf16),
            pltpu.VMEM((rows, hidden), bf16),
            pltpu.VMEM((2, own_rows, D), bf16),
            pltpu.VMEM((2, own_rows, D), bf16),
            pltpu.VMEM((own_rows, D), f32),
            pltpu.VMEM((own_rows, D), f32),
            pltpu.VMEM((8, hidden), f32),
            pltpu.VMEM((24, D), f32),
            pltpu.SemaphoreType.DMA((5, chunks)),
            pltpu.SemaphoreType.DMA((5, chunks)),
        ],
        compiler_params=pltpu.CompilerParams(
            collective_id=1, has_side_effects=True, vmem_limit_bytes=60 * 1024 * 1024
        ),
    )(mix, tokens, cot_all, far_all, near_all, up_all)


def last_kernel(
    count, e_ref, qu_ref, qw_ref, key_ref, va_ref, o_ref, pos_ref, col_ref, gatt_ref, wout_ref,
    near_ref, norm_ref, tok_ref, gres_ref, gfar_ref, vec_ref, bup_ref,
    gtok_ref, gq_ref, gk_ref, gv_ref, gp_ref, gup_ref, gdown_ref, gout_ref, gvec_ref, gbup_ref,
    e_buf, far_slots, far_along, far_back, near_pack, near_slots, near_along, near_back, vec_mine, vec_other, vec_cols, vec_slots,
    bup_all, bup_slots, aug_ref, scd_ref, dqkv_ref, dk_acc, dv_acc, dpos_ref, pos_acc, bias_acc,
    normt_ref, part_send, part_recv, far_sum, near_sum, vec_sum, bup_sum, vec_acc,
    send_sems, recv_sems, across_send, across_recv, along_send, along_recv,
    pair_send, pair_recv, e_sems,
):
    half = D // 2
    me, member = lax.axis_index("dp"), lax.axis_index("tensor")
    own_rows = tok_ref.shape[0]
    chunks = own_rows // CHUNK
    own0 = pl.multiple_of(member * own_rows, own_rows)
    oth0 = pl.multiple_of((1 - member) * own_rows, own_rows)
    width = qu_ref.shape[0]
    heads = width // HEAD
    score_scale = 1.0 / math.sqrt(HEAD)
    sources = (gfar_ref, near_pack, vec_cols, bup_all)
    slots = (far_slots, near_slots, vec_slots, bup_slots)
    totals = (far_sum, near_sum, vec_sum, bup_sum)

    def at(base, chunk):
        return pl.ds(pl.multiple_of(base + chunk * CHUNK, CHUNK), CHUNK)

    def piece(index, device):
        rows = totals[index].shape[0]
        return sources[index].at[pl.ds(pl.multiple_of(device * rows, rows), rows)]

    def share_to(index, offset):
        peer = peer_at(offset)
        return pltpu.make_async_remote_copy(
            src_ref=piece(index, peer),
            dst_ref=slots[index].at[offset - 1],
            send_sem=send_sems.at[index - 2, offset - 1],
            recv_sem=recv_sems.at[index - 2, offset - 1],
            device_id={"dp": peer},
            device_id_type=MESH,
        )

    def begin_share(index):
        def begin(offset, carry):
            share_to(index, offset).start()
            return carry

        lax.fori_loop(1, count, begin, 0)

    def finish_share(index):
        total = totals[index]
        total[...] = piece(index, me)[...].astype(jnp.float32)

        def finish(offset, carry):
            share_to(index, offset).wait()
            total[...] += slots[index][offset - 1].astype(jnp.float32)
            return carry

        lax.fori_loop(1, count, finish, 0)

    levels = count // PLANE
    along_out, along_in = (far_along, near_along), (far_back, near_back)

    def go_across(index, offset, step):
        peer = across(me, count, offset)
        return remote(
            piece(index, along(peer, count, step)), slots[index].at[offset - 1, step],
            across_send.at[index, offset - 1, step], across_recv.at[index, offset - 1, step], peer,
        )

    def go_along(index, step):
        return remote(
            along_out[index].at[step - 1], along_in[index].at[step - 1],
            along_send.at[index, step - 1], along_recv.at[index, step - 1],
            along(me, count, step),
        )

    order = list(range(1, levels)) + [0]

    def begin_sum(index):
        for step in order:
            for offset in range(1, PLANE):
                go_across(index, offset, step).start()

    def pass_sum(index):
        for step in order:
            total = piece(index, along(me, count, step))[...].astype(jnp.float32)
            for offset in range(1, PLANE):
                go_across(index, offset, step).wait()
                total = total + slots[index][offset - 1, step].astype(jnp.float32)
            if step:
                along_out[index][step - 1] = total.astype(jnp.bfloat16)
                go_along(index, step).start()
            else:
                totals[index][...] = total

    def finish_sum(index):
        for step in range(1, levels):
            go_along(index, step).wait()
            totals[index][...] += along_in[index][step - 1].astype(jnp.float32)

    def e_copy(head, slot):
        return pltpu.make_async_copy(e_ref.at[head], e_buf.at[slot], e_sems.at[slot])

    e_copy(0, 0).start()
    greet_all(count, True)
    begin_sum(0)
    own_bup = pl.ds(pl.multiple_of(member * bup_ref.shape[0], 8), bup_ref.shape[0])
    bup_all[own_bup, :] = bup_ref[...]
    bup_copy = to_other(bup_ref, bup_all.at[own_bup], pair_send.at[chunks], pair_recv.at[chunks])
    bup_copy.start()

    out_mat = wout_ref[:, wout_ref.shape[1] - width :].T
    place = lax.broadcasted_iota(jnp.int32, (AUG - HEAD, CHUNK), 0)
    for tile in range(TILES):
        rows = slice(tile * TILE, (tile + 1) * TILE)
        grads = times_transpose(out_mat, gatt_ref[rows, :])
        grads = grads.astype(jnp.bfloat16).astype(jnp.float32)
        for head in range(heads):
            lines = slice(head * HEAD, (head + 1) * HEAD)
            first = head * AUG
            inverse = o_ref[first + HEAD : first + HEAD + 1, rows]
            mixed = o_ref[first : first + HEAD, rows]
            scaled = grads[lines] * inverse
            low = (scaled * score_scale).astype(jnp.bfloat16)
            inner = -jnp.sum(low.astype(jnp.float32) * mixed, axis=0, keepdims=True)
            high = inner.astype(jnp.bfloat16).astype(jnp.float32)
            tail = jnp.where(place == 0, high, jnp.where(place == 1, inner - high, 0.0))
            scd_ref[lines, rows] = scaled.astype(jnp.bfloat16)
            aug_ref[first : first + HEAD, rows] = low
            aug_ref[first + HEAD : first + AUG, rows] = tail.astype(jnp.bfloat16)
    bias_acc[...] = jnp.zeros_like(bias_acc)

    def one_head(head, carry):
        slot = lax.rem(head, 2)
        first = pl.multiple_of(head * HEAD, HEAD)
        lines = pl.ds(first, HEAD)
        more = pl.ds(pl.multiple_of(head * AUG, 16), AUG)

        @pl.when(head + 1 < heads)
        def _():
            e_copy(head + 1, 1 - slot).start()

        e_copy(head, slot).wait()
        dk_acc[...] = jnp.zeros_like(dk_acc)
        dv_acc[...] = jnp.zeros_like(dv_acc)
        for tile in range(TILES):
            rows = slice(tile * TILE, (tile + 1) * TILE)
            seen = tiles_seen(tile) * TILE
            weights = e_buf[slot, :, PACK[tile] : PACK[tile + 1]]
            grad_probs = contract_rows(aug_ref[more, rows], va_ref[more, :seen])
            grad_scores = (weights.astype(jnp.float32) * grad_probs).astype(jnp.bfloat16)
            dv_acc[:, :seen] += dot_nn(scd_ref[lines, rows], weights)
            dk_acc[:, :seen] += dot_nn(qu_ref[lines, rows], grad_scores)
            grad_u = times_transpose(key_ref[lines, :seen], grad_scores)
            turned = times_transpose(col_ref[:, :seen], grad_scores)
            part_c, part_s = turned[:half], turned[half:]
            cos_i = col_ref[:half, rows].astype(jnp.float32)
            sin_i = col_ref[half:, rows].astype(jnp.float32)
            both = jnp.concatenate(
                [part_c * sin_i - part_s * cos_i, part_c * cos_i + part_s * sin_i], axis=0
            ).astype(jnp.bfloat16)
            grad_w = dot_nn(pos_ref[lines, :], both)
            dqkv_ref[lines, rows] = (grad_u + grad_w).astype(jnp.bfloat16)
            bias_acc[lines, :] += grad_u[:, :128] + grad_u[:, 128:]
            bias_acc[pl.ds(pl.multiple_of(width + first, HEAD), HEAD), :] += (
                grad_w[:, :128] + grad_w[:, 128:]
            )
            here = times_transpose(qw_ref[lines, rows], both)
            if tile:
                pos_acc[...] += here
            else:
                pos_acc[...] = here
        key_lines = pl.ds(pl.multiple_of(width + first, HEAD), HEAD)
        value_lines = pl.ds(pl.multiple_of(2 * width + first, HEAD), HEAD)
        dqkv_ref[key_lines, :] = dk_acc[...].astype(jnp.bfloat16)
        dqkv_ref[value_lines, :] = dv_acc[...].astype(jnp.bfloat16)
        dpos_ref[lines, :] = pos_acc[...].astype(jnp.bfloat16)

        @pl.when(head == heads - 2)
        def _():
            pass_sum(0)

        return carry

    lax.fori_loop(0, heads, one_head, 0)

    for tile in range(TILES):
        rows = slice(tile * TILE, (tile + 1) * TILE)
        normt_ref[:, rows] = norm_ref[rows, :].T
    for part in range(3):
        lines = slice(part * width, (part + 1) * width)
        near_pack[:, lines] = times_transpose(normt_ref[...], dqkv_ref[lines, :]).astype(
            jnp.bfloat16
        )
    near_pack[:, 3 * width :] = dpos_ref[...].T
    begin_sum(1)
    bup_copy.wait()
    begin_share(3)

    def pass_on(chunk):
        here = at(0, chunk)
        return to_other(
            part_send.at[here], part_recv.at[here], pair_send.at[chunk], pair_recv.at[chunk]
        )

    def backward(rows):
        return dot_tt(dqkv_ref[:, rows], near_ref[:, : 3 * width])

    for chunk in range(chunks):
        part_send[at(0, chunk), :] = backward(at(oth0, chunk)).astype(jnp.bfloat16)
        pass_on(chunk).start()
    vec_rows = near_ref[:, NEAR:].astype(jnp.float32).T
    gain = vec_rows[0:1]
    vec_acc[...] = jnp.zeros_like(vec_acc)
    for chunk in range(chunks):
        here = at(0, chunk)
        part = backward(at(own0, chunk))
        pass_on(chunk).wait()
        grad = part + part_recv[here, :].astype(jnp.float32)
        normed, rate = norm_parts(tok_ref[here, :].astype(jnp.float32))
        gtok_ref[here, :] = gres_ref[here, :] + norm_grad(grad, gain, normed, rate)
        vec_acc[0:8, :] += fold_rows(grad * normed)
        vec_acc[8:16, :] += fold_rows(grad)
    sums = jnp.sum(bias_acc[...].T, axis=0, keepdims=True)
    own_cols = pl.ds(pl.multiple_of(member * width, width), width)
    vec_mine[...] = jnp.zeros_like(vec_mine)
    vec_mine[0:1, :] = jnp.sum(vec_acc[0:8, :], axis=0, keepdims=True)
    vec_mine[1:2, :] = jnp.sum(vec_acc[8:16, :], axis=0, keepdims=True)
    vec_mine[2:3, own_cols] = sums[:, :width]
    vec_mine[3:4, own_cols] = sums[:, width:]
    vec_mine[4:7, :] = vec_ref[0:3, :]
    vec_copy = to_other(
        vec_mine, vec_other, pair_send.at[chunks + 1], pair_recv.at[chunks + 1]
    )
    vec_copy.start()
    pass_sum(1)
    finish_sum(0)
    gup_ref[...] = far_sum[:, : gup_ref.shape[1]]
    gdown_ref[...] = far_sum[:, gup_ref.shape[1] : 2 * gup_ref.shape[1]]
    gout_ref[...] = far_sum[:, 2 * gup_ref.shape[1] :]
    vec_copy.wait()
    both = vec_mine[...] + vec_other[...]
    vec_cols[...] = jnp.concatenate([both, jnp.zeros((VECS - 8, D), jnp.float32)], axis=0).T
    begin_share(2)
    finish_share(3)
    gbup_ref[...] = jnp.sum(bup_sum[...], axis=0, keepdims=True)
    finish_sum(1)
    for part, ref in enumerate((gq_ref, gk_ref, gv_ref, gp_ref)):
        ref[...] = near_sum[:, part * width : (part + 1) * width]
    finish_share(2)
    gvec_ref[...] = vec_sum[...].T[:8]


def last_call(e, qu, qw, key, va, o, pos, col, gatt, far, near, norm, tok, gres, gfar, vec, bup):
    count = lax.axis_size("dp")
    levels = count // PLANE
    rows, own_rows = norm.shape[0], tok.shape[0]
    chunks = own_rows // CHUNK
    width = qu.shape[0]
    hidden = (far.shape[1] - width) // 2
    shard = D // count
    f32, bf16 = jnp.float32, jnp.bfloat16

    def shape(*dims):
        return jax.ShapeDtypeStruct(dims, f32)

    def room(*dims, kind=f32):
        return pltpu.VMEM(dims, kind)

    return pl.pallas_call(
        functools.partial(last_kernel, count),
        in_specs=[ANY_SPEC] + [VMEM_SPEC] * 16,
        out_specs=[VMEM_SPEC] * 10,
        out_shape=[shape(own_rows, D)]
        + [shape(shard, width)] * 4
        + [shape(shard, hidden)] * 2
        + [shape(shard, width), shape(8, shard), shape(1, 128)],
        scratch_shapes=[
            room(2, TILE, PACK[-1], kind=bf16),
            room(PLANE - 1, levels, shard, far.shape[1], kind=bf16),
            room(levels - 1, shard, far.shape[1], kind=bf16),
            room(levels - 1, shard, far.shape[1], kind=bf16),
            room(D, 4 * width, kind=bf16),
            room(PLANE - 1, levels, shard, 4 * width, kind=bf16),
            room(levels - 1, shard, 4 * width, kind=bf16),
            room(levels - 1, shard, 4 * width, kind=bf16),
            room(8, D),
            room(8, D),
            room(D, VECS),
            room(count - 1, shard, VECS),
            room(8 * count, 128),
            room(count - 1, 8, 128),
            room(va.shape[0], rows, kind=bf16),
            room(width, rows, kind=bf16),
            room(3 * width, rows, kind=bf16),
            room(HEAD, rows),
            room(HEAD, rows),
            room(width, D, kind=bf16),
            room(HEAD, D),
            room(2 * width, 128),
            room(D, rows, kind=bf16),
            room(own_rows, D, kind=bf16),
            room(own_rows, D, kind=bf16),
            room(shard, far.shape[1]),
            room(shard, 4 * width),
            room(shard, VECS),
            room(8, 128),
            room(16, D),
            pltpu.SemaphoreType.DMA((2, count - 1)),
            pltpu.SemaphoreType.DMA((2, count - 1)),
            pltpu.SemaphoreType.DMA((2, PLANE - 1, levels)),
            pltpu.SemaphoreType.DMA((2, PLANE - 1, levels)),
            pltpu.SemaphoreType.DMA((2, levels - 1)),
            pltpu.SemaphoreType.DMA((2, levels - 1)),
            pltpu.SemaphoreType.DMA((chunks + 2,)),
            pltpu.SemaphoreType.DMA((chunks + 2,)),
            pltpu.SemaphoreType.DMA((2,)),
        ],
        compiler_params=pltpu.CompilerParams(
            collective_id=2, has_side_effects=True, vmem_limit_bytes=62 * 1024 * 1024
        ),
    )(e, qu, qw, key, va, o, pos, col, gatt, far, near, norm, tok, gres, gfar, vec, bup)


def local_plain(
    tokens,
    block_ids,
    ln1_gain,
    ln1_bias,
    w_query,
    w_key,
    w_value,
    w_pos,
    bias_u,
    bias_w,
    w_out,
    ln2_gain,
    ln2_bias,
    w_up,
    bias_up,
    w_down,
    bias_down,
    cotangent,
):
    member = lax.axis_index("tensor")
    squares = (w_query, w_key, w_value, w_pos, w_out.T)
    wide = (w_up, w_down.T)
    vectors = (ln1_gain, ln1_bias, bias_u, bias_w, ln2_gain, ln2_bias, bias_down)
    near_mats = [lax.all_gather(m, "dp", axis=0, tiled=True) for m in squares]
    far_mats = [lax.all_gather(m, "dp", axis=0, tiled=True) for m in wide]
    full_vecs = [lax.all_gather(v, "dp", axis=0, tiled=True) for v in vectors]
    up_shift = lax.all_gather(bias_up, "dp", axis=0, tiled=True)
    query_mat, key_mat, value_mat, pos_mat, out_back = near_mats
    out_mat = out_back.T
    up_mat, down_back = far_mats
    down_mat = down_back.T
    gain_one, shift_one, bias_one, bias_two, gain_two, shift_two, down_shift = full_vecs
    gain_one = gain_one.astype(jnp.float32)
    shift_one = shift_one.astype(jnp.float32)
    gain_two = gain_two.astype(jnp.float32)
    shift_two = shift_two.astype(jnp.float32)
    local_width = query_mat.shape[1]
    head_count = local_width // HEAD
    hidden_local = up_mat.shape[1]
    full_hidden = up_shift.shape[0]
    own_u = lax.dynamic_slice_in_dim(
        bias_one.astype(jnp.float32), member * local_width, local_width
    )
    own_w = lax.dynamic_slice_in_dim(
        bias_two.astype(jnp.float32), member * local_width, local_width
    )
    score_scale = 1.0 / math.sqrt(HEAD)
    own_rows = tokens.shape[0]
    inputs = tokens.astype(jnp.float32)
    normed = layer_norm(inputs, gain_one, shift_one)
    rows_all = lax.all_gather(normed.astype(jnp.bfloat16), "tensor", axis=0, tiled=True)
    total_rows = rows_all.shape[0]
    queries_t = project_cols(query_mat, rows_all)
    def heads_of(array):
        return array.astype(jnp.bfloat16).reshape(head_count, HEAD, array.shape[-1])

    ids = block_ids.reshape(1, total_rows)
    sum_u = queries_t + own_u[:, None]
    sum_w = queries_t + own_w[:, None]
    fold = score_scale * LOG2E
    query_u = heads_of(sum_u)
    query_w = heads_of(sum_w)
    key_rows = heads_of(project_cols(key_mat, rows_all))
    ones = jnp.ones((head_count, 2, total_rows), jnp.bfloat16)
    blank = jnp.zeros((head_count, AUG - HEAD - 2, total_rows), jnp.bfloat16)
    value_rows = jnp.concatenate(
        [heads_of(project_cols(value_mat, rows_all)), ones, blank], axis=1
    )
    pos_rows = pos_mat.T.reshape(head_count, HEAD, D)
    table = angle_table()
    row_table = jnp.asarray(table)
    col_table = jnp.asarray(np.ascontiguousarray(table.T))
    weights, mixed_sums = attend_all(
        heads_of(sum_u * fold), heads_of(sum_w * fold), key_rows, value_rows, pos_rows, ids,
        row_table, col_table,
    )
    inv_total = 1.0 / mixed_sums[:, HEAD : HEAD + 1]
    mixed_full = mixed_sums[:, :HEAD] * inv_total
    mixed_cols = mixed_full.reshape(local_width, total_rows).astype(jnp.bfloat16)
    residual = inputs + lax.psum_scatter(
        contract_rows(
            take_cols(mixed_cols, jnp.int32(0), own_rows * lax.axis_size("tensor")), out_mat
        ).astype(jnp.bfloat16),
        "tensor",
        scatter_dimension=0,
        tiled=True,
    ).astype(jnp.float32)
    normed_two = layer_norm(residual, gain_two, shift_two)
    grad_output = cotangent.astype(jnp.float32)
    grad_down_bias = placed(jnp.sum(grad_output, axis=0), D, 0)
    own_up = lax.dynamic_slice_in_dim(
        up_shift.astype(jnp.float32), member * hidden_local, hidden_local
    )
    rows_two = lax.all_gather(normed_two.astype(jnp.bfloat16), "tensor", axis=0, tiled=True)
    hidden = jnp.dot(rows_two, up_mat, preferred_element_type=jnp.float32) + own_up
    active = jax.nn.gelu(hidden).astype(jnp.bfloat16)
    output = (
        residual
        + lax.psum_scatter(
            jnp.dot(
                take_rows(active, jnp.int32(0), own_rows * lax.axis_size("tensor")),
                down_mat,
                preferred_element_type=jnp.float32,
            ).astype(jnp.bfloat16),
            "tensor",
            scatter_dimension=0,
            tiled=True,
        ).astype(jnp.float32)
        + down_shift.astype(jnp.float32)
    )
    grad_full = lax.all_gather(cotangent, "tensor", axis=0, tiled=True)
    grad_active = times_transpose(grad_full, down_mat)
    grad_down = contract_rows(active, grad_full)
    gelu_back = jax.vjp(jax.nn.gelu, hidden)[1]
    grad_hidden = gelu_back(grad_active)[0].astype(jnp.bfloat16)
    grad_up_bias = placed(
        jnp.sum(grad_hidden, axis=0, dtype=jnp.float32), full_hidden, member * hidden_local
    )
    grad_up = contract_rows(rows_two, grad_hidden)
    grad_normed_two = lax.psum_scatter(
        times_transpose(
            take_rows(grad_hidden, jnp.int32(0), own_rows * lax.axis_size("tensor")), up_mat
        ).astype(jnp.bfloat16),
        "tensor",
        scatter_dimension=0,
        tiled=True,
    ).astype(jnp.float32)
    norm_back_two = jax.vjp(layer_norm, residual, gain_two, shift_two)[1]
    grad_resid_part, grad_gain_two, grad_shift_two = norm_back_two(grad_normed_two)
    grad_residual = grad_output + grad_resid_part
    ffn_terms = (grad_gain_two, grad_shift_two, grad_up, grad_up_bias, grad_down, grad_down_bias)
    grad_att = lax.all_gather(grad_residual.astype(jnp.bfloat16), "tensor", axis=0, tiled=True)
    grad_out_mat = jnp.dot(mixed_cols, grad_att, preferred_element_type=jnp.float32)
    grad_mixed = (
        times_transpose(out_mat, grad_att)
        .astype(jnp.bfloat16)
        .reshape(head_count, HEAD, total_rows)
    )
    grad_mixed = grad_mixed.astype(jnp.float32)
    grad_scaled = (grad_mixed * inv_total).astype(jnp.bfloat16)
    grad_low = (grad_mixed * (inv_total * score_scale)).astype(jnp.bfloat16)
    inner = -jnp.sum(grad_low.astype(jnp.float32) * mixed_full, axis=1, keepdims=True)
    inner_high = inner.astype(jnp.bfloat16)
    inner_rest = (inner - inner_high.astype(jnp.float32)).astype(jnp.bfloat16)
    grad_aug = jnp.concatenate([grad_low, inner_high, inner_rest, blank], axis=1)
    dqu, dqw, dk, dv, dpos = attend_back_all(
        weights, query_u, query_w, key_rows, value_rows, pos_rows, grad_aug, grad_scaled, col_table
    )
    grad_keys_all = dk.reshape(local_width, total_rows).astype(jnp.bfloat16)
    grad_values_all = dv.reshape(local_width, total_rows).astype(jnp.bfloat16)
    grad_pos = dpos.reshape(local_width, D).T
    grad_query_u = dqu.reshape(local_width, total_rows)
    grad_query_w = dqw.reshape(local_width, total_rows)
    grad_bias_one = placed(jnp.sum(grad_query_u, axis=1), D, member * local_width)
    grad_bias_two = placed(jnp.sum(grad_query_w, axis=1), D, member * local_width)
    grad_query = (grad_query_u + grad_query_w).astype(jnp.bfloat16)
    grad_query_mat = times_transpose(rows_all.T, grad_query)
    grad_key_mat = times_transpose(rows_all.T, grad_keys_all)
    grad_value_mat = times_transpose(rows_all.T, grad_values_all)
    first_row = jnp.int32(0)
    part_sum = times_transpose(
        take_cols(grad_query, first_row, own_rows * lax.axis_size("tensor")).T, query_mat
    )
    part_sum = part_sum + times_transpose(
        take_cols(grad_keys_all, first_row, own_rows * lax.axis_size("tensor")).T, key_mat
    )
    grad_normed = lax.psum_scatter(
        (
            part_sum
            + times_transpose(
                take_cols(grad_values_all, first_row, own_rows * lax.axis_size("tensor")).T,
                value_mat,
            )
        ).astype(jnp.bfloat16),
        "tensor",
        scatter_dimension=0,
        tiled=True,
    ).astype(jnp.float32)
    norm_back_one = jax.vjp(layer_norm, inputs, gain_one, shift_one)[1]
    grad_in_part, grad_gain_one, grad_shift_one = norm_back_one(grad_normed)
    grad_tokens = grad_residual + grad_in_part
    grad_squares = (grad_query_mat, grad_key_mat, grad_value_mat, grad_pos, grad_out_mat.T)
    grad_wides = (grad_up, grad_down.T)
    grad_vecs = jnp.stack(
        (
            grad_gain_one, grad_shift_one, grad_bias_one, grad_bias_two,
            ffn_terms[0], ffn_terms[1], ffn_terms[5],
        )
    )
    grad_vecs, grad_up_row = lax.psum((grad_vecs, ffn_terms[3]), "tensor")
    def share(array):
        return lax.psum_scatter(array, "dp", scatter_dimension=0, tiled=True)

    squares = [share(m) for m in grad_squares]
    wides = [share(m) for m in grad_wides]
    vecs = [share(v) for v in grad_vecs]
    up_part = share(grad_up_row)
    return (
        output.astype(jnp.bfloat16),
        grad_tokens,
        vecs[0],
        vecs[1],
        squares[0],
        squares[1],
        squares[2],
        squares[3],
        vecs[2],
        vecs[3],
        squares[4].T,
        vecs[4],
        vecs[5],
        wides[0],
        up_part,
        wides[1].T,
        vecs[6],
    )


def local_direct(
    tokens,
    block_ids,
    ln1_gain,
    ln1_bias,
    w_query,
    w_key,
    w_value,
    w_pos,
    bias_u,
    bias_w,
    w_out,
    ln2_gain,
    ln2_bias,
    w_up,
    bias_up,
    w_down,
    bias_down,
    cotangent,
):
    total_rows = block_ids.shape[0]
    vectors = (ln1_gain, ln1_bias, bias_u, bias_w, ln2_gain, ln2_bias, bias_down)
    table = angle_table()
    row_table = jnp.asarray(table)
    col_table = jnp.asarray(np.ascontiguousarray(table.T))
    (
        weights, query_u, query_w, key_rows, value_aug, mixed_sums, mixed_cols, rows_all, pos_back,
        near, far, up_rows, grad_full,
    ) = first_call(
        tokens,
        cotangent,
        (w_query, w_key, w_value, w_pos),
        (w_up, w_down.T, w_out.T),
        [vector.reshape(1, -1) for vector in vectors],
        bias_up.reshape(1, -1),
        block_ids.reshape(1, total_rows),
        row_table,
        col_table,
    )
    out, grad_res, grad_att, grad_far, grad_vec, grad_up_part = middle_call(
        mixed_cols, tokens, grad_full, far, near, up_rows
    )
    (
        grad_tokens, grad_query_mat, grad_key_mat, grad_value_mat, grad_pos, grad_up, grad_down,
        grad_out, grad_vecs, grad_up_row,
    ) = last_call(
        weights, query_u, query_w, key_rows, value_aug, mixed_sums, pos_back, col_table, grad_att,
        far, near, rows_all, tokens, grad_res, grad_far, grad_vec, grad_up_part,
    )
    return (
        out,
        grad_tokens,
        grad_vecs[0],
        grad_vecs[1],
        grad_query_mat,
        grad_key_mat,
        grad_value_mat,
        grad_pos,
        grad_vecs[2],
        grad_vecs[3],
        grad_out.T,
        grad_vecs[4],
        grad_vecs[5],
        grad_up,
        grad_up_row.reshape(-1),
        grad_down.T,
        grad_vecs[6],
    )


def solution(mesh):
    in_specs = (
        P(("dp", "tensor"), None),
        P("dp"),
        P("dp"),
        P("dp"),
        P("dp", "tensor"),
        P("dp", "tensor"),
        P("dp", "tensor"),
        P("dp", "tensor"),
        P("dp"),
        P("dp"),
        P("tensor", "dp"),
        P("dp"),
        P("dp"),
        P("dp", "tensor"),
        P("dp"),
        P("tensor", "dp"),
        P("dp"),
        P(("dp", "tensor"), None),
    )
    out_specs = (
        P(("dp", "tensor"), None),
        P(("dp", "tensor"), None),
        P("dp"),
        P("dp"),
        P("dp", "tensor"),
        P("dp", "tensor"),
        P("dp", "tensor"),
        P("dp", "tensor"),
        P("dp"),
        P("dp"),
        P("tensor", "dp"),
        P("dp"),
        P("dp"),
        P("dp", "tensor"),
        P("dp"),
        P("tensor", "dp"),
        P("dp"),
    )
    pieces = D // mesh.shape["dp"]
    whole_tiles = (
        pieces % 16 == 0 and mesh.shape["tensor"] == 2 and mesh.shape["dp"] % (2 * PLANE) == 0
    )
    local = local_direct if whole_tiles else local_plain
    return jax.shard_map(local, mesh=mesh, in_specs=in_specs, out_specs=out_specs, check_vma=False)
```

```python
import functools
import math

import jax
import jax.numpy as jnp
import ml_dtypes
import numpy as np
from jax import lax
from jax.experimental import pallas as pl
from jax.experimental.pallas import tpu as pltpu
from jax.sharding import PartitionSpec as P

D = 512
HEAD = 64
L = 2048


MESH = pl.DeviceIdType.MESH
VECS = 128


def peer_at(offset):
    count = lax.axis_size("dp")
    return lax.rem(lax.axis_index("dp") + offset, count)


PLANE = 4


def place_of(me, count):
    return lax.div(me, PLANE), lax.rem(me, PLANE), count // PLANE


def along(me, count, offset):
    level, spot, levels = place_of(me, count)
    return lax.rem(level + offset, levels) * PLANE + spot


def across(me, count, offset):
    level, spot, _ = place_of(me, count)
    return level * PLANE + lax.rem(spot + offset, PLANE)


def remote(source, target, send_sem, recv_sem, device):
    return pltpu.make_async_remote_copy(
        src_ref=source,
        dst_ref=target,
        send_sem=send_sem,
        recv_sem=recv_sem,
        device_id={"dp": device},
        device_id_type=MESH,
    )


def greet_all(count, with_pair=False):
    barrier = pltpu.get_barrier_semaphore()

    def greet(offset, carry):
        pl.semaphore_signal(
            barrier, inc=1, device_id={"dp": peer_at(offset)}, device_id_type=MESH
        )
        return carry

    lax.fori_loop(1, count, greet, 0)
    if with_pair:
        pl.semaphore_signal(
            barrier, inc=1, device_id={"tensor": 1 - lax.axis_index("tensor")}, device_id_type=MESH
        )
    pl.semaphore_wait(barrier, count if with_pair else count - 1)


def layer_norm(values, gain_vec, shift_vec):
    center = values - jnp.mean(values, axis=-1, keepdims=True)
    spread = jnp.mean(center * center, axis=-1, keepdims=True)
    return center * lax.rsqrt(spread + 1e-05) * gain_vec + shift_vec


def take_rows(array, first_row, row_count):
    return lax.dynamic_slice_in_dim(array, first_row, row_count, 0)


def take_cols(array, first_col, col_count):
    return lax.dynamic_slice_in_dim(array, first_col, col_count, array.ndim - 1)


def contract_rows(left, right):
    return lax.dot_general(
        left, right, (((0,), (0,)), ((), ())), preferred_element_type=jnp.float32
    )


def times_transpose(left, right):
    return lax.dot_general(
        left, right, (((1,), (1,)), ((), ())), preferred_element_type=jnp.float32
    )


def project_cols(weight, row_data):
    return lax.dot_general(
        weight, row_data, (((0,), (1,)), ((), ())), preferred_element_type=jnp.float32
    )


TILE = 256
TILES = L // TILE
AUG = HEAD + 16
LOG2E = 1.4426950408889634


def tiles_seen(tile):
    return min(tile + 2, TILES)


PACK = [TILE * sum(tiles_seen(t) for t in range(tile)) for tile in range(TILES + 1)]


def angle_table():
    freqs = np.exp(np.arange(0, D, 2, dtype=np.float64) * (-math.log(10000.0) / D))
    angles = np.arange(L, dtype=np.float64)[:, None] * freqs[None, :]
    return np.concatenate([np.cos(angles), np.sin(angles)], axis=1).astype(ml_dtypes.bfloat16)


def dot_nn(left, right):
    return jnp.dot(left, right, preferred_element_type=jnp.float32)


def attend_kernel(qu_ref, qw_ref, key_ref, value_ref, pos_ref, ids_ref, row_ref, col_ref, e_ref, o_ref):
    half = D // 2
    for tile in range(TILES):
        rows = slice(tile * TILE, (tile + 1) * TILE)
        width = tiles_seen(tile) * TILE
        both = contract_rows(qw_ref[:, rows], pos_ref[...])
        part_a, part_b = both[:, :half], both[:, half:]
        cos_i = row_ref[rows, :half].astype(jnp.float32)
        sin_i = row_ref[rows, half:].astype(jnp.float32)
        turned = jnp.concatenate(
            [part_a * sin_i + part_b * cos_i, part_b * sin_i - part_a * cos_i], axis=1
        ).astype(jnp.bfloat16)
        scores = dot_nn(turned, col_ref[:, :width]) + contract_rows(
            qu_ref[:, rows], key_ref[:, :width]
        )
        ids_row = ids_ref[:, tile * TILE : width]
        ids_col = jnp.broadcast_to(ids_row[:, :TILE], (8, TILE)).T[:, :1]
        edge = jnp.where(ids_row <= ids_col, scores[:, tile * TILE :], -1e30)
        if tile:
            scores = jnp.concatenate([scores[:, : tile * TILE], edge], axis=1)
        else:
            scores = edge
        peak = jnp.max(scores, axis=1, keepdims=True)
        weights = jnp.exp2(scores - peak).astype(jnp.bfloat16)
        e_ref[:, PACK[tile] : PACK[tile + 1]] = weights
        o_ref[:, rows] = times_transpose(value_ref[:, :width], weights)


def attend_back_kernel(
    e_ref, qu_ref, qw_ref, key_ref, value_ref, pos_ref, aug_ref, scaled_ref, col_ref,
    dqu_ref, dqw_ref, dk_ref, dv_ref, dpos_ref,
):
    half = D // 2
    dk_ref[...] = jnp.zeros_like(dk_ref)
    dv_ref[...] = jnp.zeros_like(dv_ref)
    for tile in range(TILES):
        rows = slice(tile * TILE, (tile + 1) * TILE)
        width = tiles_seen(tile) * TILE
        weights = e_ref[:, PACK[tile] : PACK[tile + 1]]
        grad_probs = contract_rows(aug_ref[:, rows], value_ref[:, :width])
        grad_scores = (weights.astype(jnp.float32) * grad_probs).astype(jnp.bfloat16)
        dv_ref[:, :width] += dot_nn(scaled_ref[:, rows], weights)
        dk_ref[:, :width] += dot_nn(qu_ref[:, rows], grad_scores)
        dqu_ref[:, rows] = times_transpose(key_ref[:, :width], grad_scores)
        turned = times_transpose(col_ref[:, :width], grad_scores)
        part_c, part_s = turned[:half], turned[half:]
        cos_i = col_ref[:half, rows].astype(jnp.float32)
        sin_i = col_ref[half:, rows].astype(jnp.float32)
        both = jnp.concatenate(
            [part_c * sin_i - part_s * cos_i, part_c * cos_i + part_s * sin_i], axis=0
        ).astype(jnp.bfloat16)
        dqw_ref[:, rows] = dot_nn(pos_ref[...], both)
        here = times_transpose(qw_ref[:, rows], both)
        if tile:
            dpos_ref[...] += here
        else:
            dpos_ref[...] = here


def per_head(rows, cols):
    return pl.BlockSpec((None, rows, cols), lambda h: (h, 0, 0))


def shared(rows, cols):
    return pl.BlockSpec((rows, cols), lambda h: (0, 0))


def attend_all(qu, qw, keys, values, pos, ids, row_table, col_table):
    heads = qu.shape[0]
    f32, bf16 = jnp.float32, jnp.bfloat16
    return pl.pallas_call(
        attend_kernel,
        grid=(heads,),
        in_specs=[per_head(HEAD, L)] * 3
        + [per_head(AUG, L), per_head(HEAD, D), shared(1, L), shared(L, D), shared(D, L)],
        out_specs=[per_head(TILE, PACK[-1]), per_head(AUG, L)],
        out_shape=[
            jax.ShapeDtypeStruct((heads, TILE, PACK[-1]), bf16),
            jax.ShapeDtypeStruct((heads, AUG, L), f32),
        ],
        compiler_params=pltpu.CompilerParams(vmem_limit_bytes=56 * 1024 * 1024),
    )(qu, qw, keys, values, pos, ids, row_table, col_table)


def attend_back_all(weights, qu, qw, keys, values, pos, aug, scaled, col_table):
    heads = qu.shape[0]
    f32 = jnp.float32
    return pl.pallas_call(
        attend_back_kernel,
        grid=(heads,),
        in_specs=[per_head(TILE, PACK[-1])]
        + [per_head(HEAD, L)] * 3
        + [per_head(AUG, L), per_head(HEAD, D), per_head(AUG, L), per_head(HEAD, L), shared(D, L)],
        out_specs=[per_head(HEAD, L)] * 4 + [per_head(HEAD, D)],
        out_shape=[jax.ShapeDtypeStruct((heads, HEAD, L), f32)] * 4
        + [jax.ShapeDtypeStruct((heads, HEAD, D), f32)],
        compiler_params=pltpu.CompilerParams(vmem_limit_bytes=56 * 1024 * 1024),
    )(weights, qu, qw, keys, values, pos, aug, scaled, col_table)


def placed(part_vec, length, offset):
    return lax.dynamic_update_slice_in_dim(jnp.zeros((length,), jnp.float32), part_vec, offset, 0)


NEAR = 4 * 256


def first_kernel(
    count, tok_ref, cot_ref, wq_ref, wk_ref, wv_ref, wp_ref, wu_ref, wd_ref, wo_ref, *refs
):
    vec_refs, bup_ref, ids_ref, row_ref, col_ref = refs[:7], refs[7], refs[8], refs[9], refs[10]
    (
        e_ref, qu_ref, qw_ref, key_ref, va_ref, o_ref, mix_ref, norm_ref, pos_ref,
        near_all, far_all, up_all, cot_all,
        near_ref, far_ref, up_ref, vec_ref, tok_all, quf_ref, qwf_ref, turn_ref, rq_ref, vrow_ref, e_buf,
        along_send, along_recv, across_send, across_recv, own_sems, pair_send, pair_recv, e_sems,
    ) = refs[11:]
    half = D // 2
    me, member = lax.axis_index("dp"), lax.axis_index("tensor")
    levels = count // PLANE
    pair = {"tensor": 1 - member}
    own_rows = tok_ref.shape[0]
    own = pl.ds(pl.multiple_of(member * own_rows, own_rows), own_rows)
    parts = (near_ref, far_ref, up_ref)
    wholes = (near_all, far_all, up_all)

    def rows_of(index, device):
        rows = parts[index].shape[0]
        return wholes[index].at[pl.ds(pl.multiple_of(device * rows, rows), rows)]

    def go_along(index, offset):
        return remote(
            parts[index], rows_of(index, me),
            along_send.at[index, offset - 1], along_recv.at[index, offset - 1],
            along(me, count, offset),
        )

    def go_across(index, offset, step):
        owner = along(me, count, levels - step)
        return remote(
            parts[index] if step == 0 else rows_of(index, owner), rows_of(index, owner),
            across_send.at[index, offset - 1, step], across_recv.at[index, offset - 1, step],
            across(me, count, offset),
        )

    def own_copy(index):
        return pltpu.make_async_copy(parts[index], rows_of(index, me), own_sems.at[index])

    def begin_gather(index):
        for offset in range(1, levels):
            go_along(index, offset).start()
        for offset in range(1, PLANE):
            go_across(index, offset, 0).start()
        own_copy(index).start()

    def forward(index):
        for step in range(1, levels):
            go_along(index, step).wait()
            for offset in range(1, PLANE):
                go_across(index, offset, step).start()

    def finish_gather(index):
        for step in range(levels):
            for offset in range(1, PLANE):
                go_across(index, offset, step).wait()
        own_copy(index).wait()

    width = wq_ref.shape[1]
    hidden = wu_ref.shape[1]
    shard = wq_ref.shape[0]
    vec_ref[...] = jnp.zeros_like(vec_ref)
    for place, ref in enumerate(vec_refs):
        vec_ref[place : place + 1, :shard] = ref[...].astype(jnp.float32)
    near_ref[:, NEAR:] = vec_ref[...].T[:shard].astype(jnp.bfloat16)
    for place, ref in enumerate((wq_ref, wk_ref, wv_ref, wp_ref)):
        near_ref[:, place * width : (place + 1) * width] = ref[...]
    far_ref[:, :hidden] = wu_ref[...]
    far_ref[:, hidden : 2 * hidden] = wd_ref[...]
    far_ref[:, 2 * hidden :] = wo_ref[...]
    up_ref[...] = jnp.broadcast_to(bup_ref[...].astype(jnp.float32), up_ref.shape).astype(
        jnp.bfloat16
    )

    def to_pair(source, target, slot):
        return pltpu.make_async_remote_copy(
            src_ref=source,
            dst_ref=target.at[own],
            send_sem=pair_send.at[slot],
            recv_sem=pair_recv.at[slot],
            device_id=pair,
            device_id_type=MESH,
        )

    greet_all(count, True)
    begin_gather(0)
    begin_gather(2)
    exchanges = (to_pair(tok_ref, tok_all, 0), to_pair(cot_ref, cot_all, 1))
    keeps = (
        pltpu.make_async_copy(tok_ref, tok_all.at[own], own_sems.at[3]),
        pltpu.make_async_copy(cot_ref, cot_all.at[own], own_sems.at[4]),
    )
    for copy in exchanges + keeps:
        copy.start()
    forward(0)
    begin_gather(1)
    forward(2)
    finish_gather(0)
    exchanges[0].wait()
    keeps[0].wait()

    vec_block = near_all[:, NEAR:].astype(jnp.float32)
    vec_rows = vec_block.T
    gain, shift = vec_rows[0:1], vec_rows[1:2]
    turn_ref[...] = near_all[:, :768].T
    pos_ref[...] = near_all[:, 768:NEAR].T
    heads = width // HEAD
    own_cols = pl.ds(pl.multiple_of(member * width, width), width)
    vec_cols = near_all[own_cols, NEAR:].astype(jnp.float32)
    bias_u, bias_w = vec_cols[:, 2:3], vec_cols[:, 3:4]
    fold = LOG2E / math.sqrt(HEAD)
    place = lax.broadcasted_iota(jnp.int32, (AUG - HEAD, TILE), 0)
    marks = jnp.where(place < 2, 1.0, 0.0).astype(jnp.bfloat16)
    for tile in range(TILES):
        rows = slice(tile * TILE, (tile + 1) * TILE)
        normed = layer_norm(tok_all[rows, :].astype(jnp.float32), gain, shift)
        normed = normed.astype(jnp.bfloat16)
        norm_ref[rows, :] = normed
        projected = times_transpose(turn_ref[...], normed)
        sum_u = projected[:width] + bias_u
        sum_w = projected[:width] + bias_w
        qu_ref[:, rows] = sum_u.astype(jnp.bfloat16)
        qw_ref[:, rows] = sum_w.astype(jnp.bfloat16)
        quf_ref[:, rows] = (sum_u * fold).astype(jnp.bfloat16)
        qwf_ref[:, rows] = (sum_w * fold).astype(jnp.bfloat16)
        key_ref[:, rows] = projected[width : 2 * width].astype(jnp.bfloat16)
        for head in range(heads):
            values = projected[2 * width + head * HEAD : 2 * width + (head + 1) * HEAD]
            va_ref[head * AUG : head * AUG + HEAD, rows] = values.astype(jnp.bfloat16)
            va_ref[head * AUG + HEAD : (head + 1) * AUG, rows] = marks

    def e_copy(head, slot):
        return pltpu.make_async_copy(e_buf.at[slot], e_ref.at[head], e_sems.at[slot])

    def one_head(head, carry):
        slot = lax.rem(head, 2)
        lines = pl.ds(pl.multiple_of(head * HEAD, HEAD), HEAD)
        more = pl.ds(pl.multiple_of(head * AUG, 16), AUG)
        upper = pl.ds(pl.multiple_of(head * AUG, 16), HEAD)
        lower = pl.ds(pl.multiple_of(head * AUG + HEAD, 16), AUG - HEAD)

        @pl.when(head >= 2)
        def _():
            e_copy(head - 2, slot).wait()

        filler = jnp.zeros((VECS - AUG, va_ref.shape[1]), jnp.bfloat16)
        vrow_ref[...] = jnp.concatenate([va_ref[more, :], filler], axis=0).T
        for tile in range(TILES):
            rows = slice(tile * TILE, (tile + 1) * TILE)
            both = contract_rows(qwf_ref[lines, rows], pos_ref[lines, :])
            part_a, part_b = both[:, :half], both[:, half:]
            cos_i = row_ref[rows, :half].astype(jnp.float32)
            sin_i = row_ref[rows, half:].astype(jnp.float32)
            rq_ref[rows, :half] = (part_a * sin_i + part_b * cos_i).astype(jnp.bfloat16)
            rq_ref[rows, half:] = (part_b * sin_i - part_a * cos_i).astype(jnp.bfloat16)

        def scores_of(tile):
            rows = slice(tile * TILE, (tile + 1) * TILE)
            seen = tiles_seen(tile) * TILE
            scores = dot_nn(rq_ref[rows, :], col_ref[:, :seen]) + contract_rows(
                quf_ref[lines, rows], key_ref[lines, :seen]
            )
            ids_row = ids_ref[:, tile * TILE : seen]
            ids_col = jnp.broadcast_to(ids_row[:, :TILE], (8, TILE)).T[:, :1]
            edge = jnp.where(ids_row <= ids_col, scores[:, tile * TILE :], -1e30)
            if tile:
                return jnp.concatenate([scores[:, : tile * TILE], edge], axis=1)
            return edge

        def use_scores(tile, scores):
            rows = slice(tile * TILE, (tile + 1) * TILE)
            seen = tiles_seen(tile) * TILE
            peak = jnp.max(scores, axis=1, keepdims=True)
            weights = jnp.exp2(scores - peak).astype(jnp.bfloat16)
            e_buf[slot, :, PACK[tile] : PACK[tile + 1]] = weights
            sums = dot_nn(weights, vrow_ref[:seen, :]).T
            inverse = 1.0 / sums[HEAD : HEAD + 1]
            mixed = sums[:HEAD] * inverse
            o_ref[upper, rows] = mixed
            o_ref[lower, rows] = jnp.broadcast_to(inverse, (AUG - HEAD, TILE))
            mix_ref[lines, rows] = mixed.astype(jnp.bfloat16)

        scores = scores_of(0)
        for tile in range(TILES):
            following = scores_of(tile + 1) if tile + 1 < TILES else None
            use_scores(tile, scores)
            scores = following
        e_copy(head, slot).start()

        @pl.when(head == 0)
        def _():
            forward(1)

        return carry

    lax.fori_loop(0, heads, one_head, 0)
    for head in range(max(heads - 2, 0), heads):
        e_copy(head, head % 2).wait()
    exchanges[1].wait()
    keeps[1].wait()
    finish_gather(1)
    finish_gather(2)


VMEM_SPEC = pl.BlockSpec(memory_space=pltpu.VMEM)
ANY_SPEC = pl.BlockSpec(memory_space=pl.ANY)


def first_call(tokens, cotangent, squares, wides, vectors, bup, ids, row_table, col_table):
    count = lax.axis_size("dp")
    levels = count // PLANE
    rows = ids.shape[1]
    shard, width = squares[0].shape
    hidden = wides[0].shape[1]
    heads = width // HEAD
    far_width = 2 * hidden + width
    f32, bf16 = jnp.float32, jnp.bfloat16

    def shape(*dims, kind=bf16):
        return jax.ShapeDtypeStruct(dims, kind)

    return pl.pallas_call(
        functools.partial(first_kernel, count),
        in_specs=[VMEM_SPEC] * 20,
        out_specs=[ANY_SPEC] + [VMEM_SPEC] * 12,
        out_shape=[
            shape(heads, TILE, PACK[-1]),
            shape(width, rows),
            shape(width, rows),
            shape(width, rows),
            shape(heads * AUG, rows),
            shape(heads * AUG, rows, kind=f32),
            shape(width, rows),
            shape(rows, D),
            shape(width, D),
            shape(D, NEAR + VECS),
            shape(D, far_width),
            shape(16 * count, bup.shape[1]),
            shape(rows, D),
        ],
        scratch_shapes=[
            pltpu.VMEM((shard, NEAR + VECS), bf16),
            pltpu.VMEM((shard, far_width), bf16),
            pltpu.VMEM((16, bup.shape[1]), bf16),
            pltpu.VMEM((VECS, VECS), f32),
            pltpu.VMEM((rows, D), bf16),
            pltpu.VMEM((width, rows), bf16),
            pltpu.VMEM((width, rows), bf16),
            pltpu.VMEM((3 * width, D), bf16),
            pltpu.VMEM((rows, D), bf16),
            pltpu.VMEM((rows, VECS), bf16),
            pltpu.VMEM((2, TILE, PACK[-1]), bf16),
            pltpu.SemaphoreType.DMA((3, levels - 1)),
            pltpu.SemaphoreType.DMA((3, levels - 1)),
            pltpu.SemaphoreType.DMA((3, PLANE - 1, levels)),
            pltpu.SemaphoreType.DMA((3, PLANE - 1, levels)),
            pltpu.SemaphoreType.DMA((5,)),
            pltpu.SemaphoreType.DMA((2,)),
            pltpu.SemaphoreType.DMA((2,)),
            pltpu.SemaphoreType.DMA((2,)),
        ],
        compiler_params=pltpu.CompilerParams(
            collective_id=0, has_side_effects=True, vmem_limit_bytes=60 * 1024 * 1024
        ),
    )(tokens, cotangent, *squares, *wides, *vectors, bup, ids, row_table, col_table)


CHUNK = 256
GELU_SCALE = math.sqrt(2.0 / math.pi)


def fold_rows(values):
    return jnp.sum(values.reshape(values.shape[0] // 8, 8, values.shape[1]), axis=0)


def fold_cols(values):
    total = values[:, :128]
    for start in range(128, values.shape[1], 128):
        total = total + values[:, start : start + 128]
    return total


def norm_parts(values):
    center = values - jnp.mean(values, axis=-1, keepdims=True)
    spread = jnp.mean(center * center, axis=-1, keepdims=True)
    rate = lax.rsqrt(spread + 1e-05)
    return center * rate, rate


def norm_grad(grad, gain, normed, rate):
    scaled = grad * gain
    mean = jnp.mean(scaled, axis=-1, keepdims=True)
    along = jnp.mean(scaled * normed, axis=-1, keepdims=True)
    return rate * (scaled - mean - normed * along)


def to_other(source, target, send_sem, recv_sem):
    return pltpu.make_async_remote_copy(
        src_ref=source,
        dst_ref=target,
        send_sem=send_sem,
        recv_sem=recv_sem,
        device_id={"tensor": 1 - lax.axis_index("tensor")},
        device_id_type=MESH,
    )


def dot_tt(left, right):
    return lax.dot_general(
        left, right, (((0,), (1,)), ((), ())), preferred_element_type=jnp.float32
    )


def middle_kernel(
    mix_ref, tok_ref, cot_ref, far_ref, vec_ref, up_ref,
    out_ref, gres_ref, gatt_ref, gfar_ref, vec_out, bup_out,
    send_a, recv_a, res_ref, n2_ref, n2t_ref, cott_ref, act_ref, gh_ref,
    osend, orecv, oacc, gacc, bup_acc, vec_acc, send_sems, recv_sems,
):
    member = lax.axis_index("tensor")
    own_rows = tok_ref.shape[0]
    chunks = own_rows // CHUNK
    own0 = pl.multiple_of(member * own_rows, own_rows)
    oth0 = pl.multiple_of((1 - member) * own_rows, own_rows)
    hidden = act_ref.shape[1]
    up_cols, down_cols = slice(0, hidden), slice(hidden, 2 * hidden)
    out_cols = slice(2 * hidden, far_ref.shape[1])

    def at(base, chunk):
        return pl.ds(pl.multiple_of(base + chunk * CHUNK, CHUNK), CHUNK)

    barrier = pltpu.get_barrier_semaphore()
    pl.semaphore_signal(barrier, inc=1, device_id={"tensor": 1 - member}, device_id_type=MESH)
    pl.semaphore_wait(barrier, 1)

    def pass_on(stage, chunk):
        here = at(0, chunk)
        pairs = (
            (send_a.at[here], recv_a.at[here]),
            (n2_ref.at[at(own0, chunk)], n2_ref.at[at(own0, chunk)]),
            (osend.at[0, here], orecv.at[0, here]),
            (osend.at[1, here], orecv.at[1, here]),
            (gatt_ref.at[at(own0, chunk)], gatt_ref.at[at(own0, chunk)]),
        )
        source, target = pairs[stage]
        return to_other(
            source, target, send_sems.at[stage, chunk], recv_sems.at[stage, chunk]
        )

    vec_rows = vec_ref[:, NEAR:].astype(jnp.float32).T
    gain, shift, down_shift = vec_rows[4:5], vec_rows[5:6], vec_rows[6:7]
    ups = hidden // 128
    up_block = up_ref[pl.ds(pl.multiple_of(member * ups * 16, 16), ups * 16), :].astype(jnp.float32)
    up_shift = jnp.concatenate([up_block[16 * k : 16 * k + 1] for k in range(ups)], axis=1)

    def branch(rows):
        return dot_tt(mix_ref[:, rows], far_ref[:, out_cols])

    for chunk in range(chunks):
        send_a[at(0, chunk), :] = branch(at(oth0, chunk)).astype(jnp.bfloat16)
        pass_on(0, chunk).start()
    for chunk in range(chunks):
        here = at(0, chunk)
        part = branch(at(own0, chunk))
        pass_on(0, chunk).wait()
        residual = tok_ref[here, :].astype(jnp.float32) + part + recv_a[here, :].astype(jnp.float32)
        res_ref[here, :] = residual
        n2_ref[at(own0, chunk), :] = (norm_parts(residual)[0] * gain + shift).astype(jnp.bfloat16)
        pass_on(1, chunk).start()

    bup_acc[...] = jnp.zeros_like(bup_acc)
    vec_acc[...] = jnp.zeros_like(vec_acc)

    def ffn(rows):
        normed = n2_ref[rows, :]
        grads = cot_ref[rows, :]
        value = dot_nn(normed, far_ref[:, up_cols]) + up_shift
        square = value * value
        bend = jnp.tanh(GELU_SCALE * value * (1.0 + 0.044715 * square))
        half = 0.5 * (1.0 + bend)
        active = (value * half).astype(jnp.bfloat16)
        slope = half + 0.5 * value * (1.0 - bend * bend) * (
            GELU_SCALE * (1.0 + 3.0 * 0.044715 * square)
        )
        grad_hidden = (dot_nn(grads, far_ref[:, down_cols]) * slope).astype(jnp.bfloat16)
        act_ref[rows, :] = active
        gh_ref[rows, :] = grad_hidden
        n2t_ref[:, rows] = normed.T
        cott_ref[:, rows] = grads.T
        bup_acc[...] += fold_rows(grad_hidden.astype(jnp.float32))
        return (
            times_transpose(active, far_ref[:, down_cols]),
            times_transpose(grad_hidden, far_ref[:, up_cols]),
        )

    def ffn_own(chunk, carry):
        oacc[at(0, chunk), :], gacc[at(0, chunk), :] = ffn(at(own0, chunk))
        return carry

    def ffn_other(chunk, carry):
        pass_on(1, chunk).wait()
        here = at(0, chunk)
        for stage, part in zip((2, 3), ffn(at(oth0, chunk))):
            osend[stage - 2, here, :] = part.astype(jnp.bfloat16)
            pass_on(stage, chunk).start()
        return carry

    lax.fori_loop(0, 1, ffn_own, 0)
    lax.fori_loop(0, chunks, ffn_other, 0)
    lax.fori_loop(1, chunks, ffn_own, 0)

    def close(chunk, carry):
        here = at(0, chunk)
        pass_on(2, chunk).wait()
        pass_on(3, chunk).wait()
        residual = res_ref[here, :]
        out = residual + oacc[here, :] + orecv[0, here, :].astype(jnp.float32) + down_shift
        out_ref[here, :] = out.astype(jnp.bfloat16)
        grad = gacc[here, :] + orecv[1, here, :].astype(jnp.float32)
        normed, rate = norm_parts(residual)
        top = cot_ref[at(own0, chunk), :].astype(jnp.float32)
        grad_res = top + norm_grad(grad, gain, normed, rate)
        gres_ref[here, :] = grad_res
        gatt_ref[at(own0, chunk), :] = grad_res.astype(jnp.bfloat16)
        pass_on(4, chunk).start()
        vec_acc[0:8, :] += fold_rows(grad * normed)
        vec_acc[8:16, :] += fold_rows(grad)
        vec_acc[16:24, :] += fold_rows(top)
        return carry

    lax.fori_loop(0, chunks, close, 0)
    for part in range(hidden // CHUNK):
        cols = slice(part * CHUNK, (part + 1) * CHUNK)
        gfar_ref[:, cols] = dot_nn(n2t_ref[...], gh_ref[:, cols]).astype(jnp.bfloat16)
        gfar_ref[:, hidden + part * CHUNK : hidden + (part + 1) * CHUNK] = dot_nn(
            cott_ref[...], act_ref[:, cols]
        ).astype(jnp.bfloat16)
    vec_out[...] = jnp.concatenate(
        [jnp.sum(vec_acc[8 * v : 8 * v + 8, :], axis=0, keepdims=True) for v in range(3)]
        + [jnp.zeros((5, vec_acc.shape[1]), jnp.float32)],
        axis=0,
    )
    for k in range(ups):
        bup_out[8 * k : 8 * k + 8, :] = bup_acc[:, 128 * k : 128 * k + 128]
    for chunk in range(chunks):
        pass_on(4, chunk).wait()
    gfar_ref[:, out_cols] = dot_tt(gatt_ref[...], mix_ref[...]).astype(jnp.bfloat16)


def middle_call(mix, tokens, cot_all, far_all, near_all, up_all):
    rows, own_rows = cot_all.shape[0], tokens.shape[0]
    chunks = own_rows // CHUNK
    hidden = (far_all.shape[1] - mix.shape[0]) // 2
    f32, bf16 = jnp.float32, jnp.bfloat16
    return pl.pallas_call(
        middle_kernel,
        in_specs=[VMEM_SPEC] * 6,
        out_specs=[VMEM_SPEC] * 6,
        out_shape=[
            jax.ShapeDtypeStruct((own_rows, D), bf16),
            jax.ShapeDtypeStruct((own_rows, D), f32),
            jax.ShapeDtypeStruct((rows, D), bf16),
            jax.ShapeDtypeStruct(far_all.shape, bf16),
            jax.ShapeDtypeStruct((8, D), f32),
            jax.ShapeDtypeStruct((hidden // 16, 128), f32),
        ],
        scratch_shapes=[
            pltpu.VMEM((own_rows, D), bf16),
            pltpu.VMEM((own_rows, D), bf16),
            pltpu.VMEM((own_rows, D), f32),
            pltpu.VMEM((rows, D), bf16),
            pltpu.VMEM((D, rows), bf16),
            pltpu.VMEM((D, rows), bf16),
            pltpu.VMEM((rows, hidden), bf16),
            pltpu.VMEM((rows, hidden), bf16),
            pltpu.VMEM((2, own_rows, D), bf16),
            pltpu.VMEM((2, own_rows, D), bf16),
            pltpu.VMEM((own_rows, D), f32),
            pltpu.VMEM((own_rows, D), f32),
            pltpu.VMEM((8, hidden), f32),
            pltpu.VMEM((24, D), f32),
            pltpu.SemaphoreType.DMA((5, chunks)),
            pltpu.SemaphoreType.DMA((5, chunks)),
        ],
        compiler_params=pltpu.CompilerParams(
            collective_id=1, has_side_effects=True, vmem_limit_bytes=60 * 1024 * 1024
        ),
    )(mix, tokens, cot_all, far_all, near_all, up_all)


def last_kernel(
    count, e_ref, qu_ref, qw_ref, key_ref, va_ref, o_ref, pos_ref, row_ref, gatt_ref, wout_ref,
    near_ref, norm_ref, tok_ref, gres_ref, gfar_ref, vec_ref, bup_ref,
    gtok_ref, gq_ref, gk_ref, gv_ref, gp_ref, gup_ref, gdown_ref, gout_ref, gvec_ref, gbup_ref,
    e_buf, far_slots, far_along, far_back, near_pack, near_slots, near_along, near_back, vec_mine, vec_other, vec_cols, vec_slots,
    bup_all, bup_slots, aug_ref, scd_ref, dqkv_ref, dk_acc, dv_acc, dpos_ref, both_ref, krow_ref, dqu_ref, bias_acc,
    normt_ref, part_send, part_recv, far_sum, near_sum, vec_sum, bup_sum, vec_acc,
    send_sems, recv_sems, across_send, across_recv, along_send, along_recv,
    pair_send, pair_recv, e_sems,
):
    half = D // 2
    me, member = lax.axis_index("dp"), lax.axis_index("tensor")
    own_rows = tok_ref.shape[0]
    chunks = own_rows // CHUNK
    own0 = pl.multiple_of(member * own_rows, own_rows)
    oth0 = pl.multiple_of((1 - member) * own_rows, own_rows)
    width = qu_ref.shape[0]
    heads = width // HEAD
    score_scale = 1.0 / math.sqrt(HEAD)
    sources = (gfar_ref, near_pack, vec_cols, bup_all)
    slots = (far_slots, near_slots, vec_slots, bup_slots)
    totals = (far_sum, near_sum, vec_sum, bup_sum)

    def at(base, chunk):
        return pl.ds(pl.multiple_of(base + chunk * CHUNK, CHUNK), CHUNK)

    def piece(index, device):
        rows = totals[index].shape[0]
        return sources[index].at[pl.ds(pl.multiple_of(device * rows, rows), rows)]

    def share_to(index, offset):
        peer = peer_at(offset)
        return pltpu.make_async_remote_copy(
            src_ref=piece(index, peer),
            dst_ref=slots[index].at[offset - 1],
            send_sem=send_sems.at[index - 2, offset - 1],
            recv_sem=recv_sems.at[index - 2, offset - 1],
            device_id={"dp": peer},
            device_id_type=MESH,
        )

    def begin_share(index):
        def begin(offset, carry):
            share_to(index, offset).start()
            return carry

        lax.fori_loop(1, count, begin, 0)

    def finish_share(index):
        total = totals[index]
        total[...] = piece(index, me)[...].astype(jnp.float32)

        def finish(offset, carry):
            share_to(index, offset).wait()
            total[...] += slots[index][offset - 1].astype(jnp.float32)
            return carry

        lax.fori_loop(1, count, finish, 0)

    levels = count // PLANE
    along_out, along_in = (far_along, near_along), (far_back, near_back)

    def go_across(index, offset, step):
        peer = across(me, count, offset)
        return remote(
            piece(index, along(peer, count, step)), slots[index].at[offset - 1, step],
            across_send.at[index, offset - 1, step], across_recv.at[index, offset - 1, step], peer,
        )

    def go_along(index, step):
        return remote(
            along_out[index].at[step - 1], along_in[index].at[step - 1],
            along_send.at[index, step - 1], along_recv.at[index, step - 1],
            along(me, count, step),
        )

    order = list(range(1, levels)) + [0]

    def begin_sum(index):
        for step in order:
            for offset in range(1, PLANE):
                go_across(index, offset, step).start()

    def pass_sum(index):
        for step in order:
            total = piece(index, along(me, count, step))[...].astype(jnp.float32)
            for offset in range(1, PLANE):
                go_across(index, offset, step).wait()
                total = total + slots[index][offset - 1, step].astype(jnp.float32)
            if step:
                along_out[index][step - 1] = total.astype(jnp.bfloat16)
                go_along(index, step).start()
            else:
                totals[index][...] = total

    def finish_sum(index):
        for step in range(1, levels):
            go_along(index, step).wait()
            totals[index][...] += along_in[index][step - 1].astype(jnp.float32)

    def e_copy(head, slot):
        return pltpu.make_async_copy(e_ref.at[head], e_buf.at[slot], e_sems.at[slot])

    e_copy(0, 0).start()
    greet_all(count, True)
    begin_sum(0)
    own_bup = pl.ds(pl.multiple_of(member * bup_ref.shape[0], 8), bup_ref.shape[0])
    bup_all[own_bup, :] = bup_ref[...]
    bup_copy = to_other(bup_ref, bup_all.at[own_bup], pair_send.at[chunks], pair_recv.at[chunks])
    bup_copy.start()

    out_mat = wout_ref[:, wout_ref.shape[1] - width :].T
    place = lax.broadcasted_iota(jnp.int32, (AUG - HEAD, CHUNK), 0)
    for tile in range(TILES):
        rows = slice(tile * TILE, (tile + 1) * TILE)
        grads = times_transpose(out_mat, gatt_ref[rows, :])
        grads = grads.astype(jnp.bfloat16).astype(jnp.float32)
        for head in range(heads):
            lines = slice(head * HEAD, (head + 1) * HEAD)
            first = head * AUG
            inverse = o_ref[first + HEAD : first + HEAD + 1, rows]
            mixed = o_ref[first : first + HEAD, rows]
            scaled = grads[lines] * inverse
            low = (scaled * score_scale).astype(jnp.bfloat16)
            inner = -jnp.sum(low.astype(jnp.float32) * mixed, axis=0, keepdims=True)
            high = inner.astype(jnp.bfloat16).astype(jnp.float32)
            tail = jnp.where(place == 0, high, jnp.where(place == 1, inner - high, 0.0))
            scd_ref[lines, rows] = scaled.astype(jnp.bfloat16)
            aug_ref[first : first + HEAD, rows] = low
            aug_ref[first + HEAD : first + AUG, rows] = tail.astype(jnp.bfloat16)

    def one_head(head, carry):
        slot = lax.rem(head, 2)
        first = pl.multiple_of(head * HEAD, HEAD)
        lines = pl.ds(first, HEAD)
        more = pl.ds(pl.multiple_of(head * AUG, 16), AUG)

        @pl.when(head + 1 < heads)
        def _():
            e_copy(head + 1, 1 - slot).start()

        e_copy(head, slot).wait()
        dk_acc[...] = jnp.zeros_like(dk_acc)
        dv_acc[...] = jnp.zeros_like(dv_acc)
        filler = jnp.zeros((VECS - HEAD, key_ref.shape[1]), jnp.bfloat16)
        krow_ref[...] = jnp.concatenate([key_ref[lines, :], filler], axis=0).T

        def grads_of(tile):
            rows = slice(tile * TILE, (tile + 1) * TILE)
            weights = e_buf[slot, :, PACK[tile] : PACK[tile + 1]]
            grad_probs = contract_rows(
                aug_ref[more, rows], va_ref[more, : tiles_seen(tile) * TILE]
            )
            return (weights.astype(jnp.float32) * grad_probs).astype(jnp.bfloat16)

        def use_grads(tile, grad_scores):
            rows = slice(tile * TILE, (tile + 1) * TILE)
            seen = tiles_seen(tile) * TILE
            weights = e_buf[slot, :, PACK[tile] : PACK[tile + 1]]
            dv_acc[:, :seen] += dot_nn(scd_ref[lines, rows], weights)
            dk_acc[:, :seen] += dot_nn(qu_ref[lines, rows], grad_scores)
            dqu_ref[:, rows] = dot_nn(grad_scores, krow_ref[:seen, :]).T[:HEAD]
            turned = dot_nn(grad_scores, row_ref[:seen, :])
            part_c, part_s = turned[:, :half], turned[:, half:]
            cos_i = row_ref[rows, :half].astype(jnp.float32)
            sin_i = row_ref[rows, half:].astype(jnp.float32)
            both_ref[rows, :half] = (part_c * sin_i - part_s * cos_i).astype(jnp.bfloat16)
            both_ref[rows, half:] = (part_c * cos_i + part_s * sin_i).astype(jnp.bfloat16)

        grad_scores = grads_of(0)
        for tile in range(TILES):
            following = grads_of(tile + 1) if tile + 1 < TILES else None
            use_grads(tile, grad_scores)
            grad_scores = following
        grad_u = dqu_ref[...]
        grad_w = times_transpose(pos_ref[lines, :], both_ref[...])
        dqkv_ref[lines, :] = (grad_u + grad_w).astype(jnp.bfloat16)
        bias_acc[lines, :] = fold_cols(grad_u)
        bias_acc[pl.ds(pl.multiple_of(width + first, HEAD), HEAD), :] = fold_cols(grad_w)
        dpos_ref[lines, :] = dot_nn(qw_ref[lines, :], both_ref[...]).astype(jnp.bfloat16)
        key_lines = pl.ds(pl.multiple_of(width + first, HEAD), HEAD)
        value_lines = pl.ds(pl.multiple_of(2 * width + first, HEAD), HEAD)
        dqkv_ref[key_lines, :] = dk_acc[...].astype(jnp.bfloat16)
        dqkv_ref[value_lines, :] = dv_acc[...].astype(jnp.bfloat16)

        @pl.when(head == heads - 2)
        def _():
            pass_sum(0)

        return carry

    lax.fori_loop(0, heads, one_head, 0)

    for tile in range(TILES):
        rows = slice(tile * TILE, (tile + 1) * TILE)
        normt_ref[:, rows] = norm_ref[rows, :].T
    for part in range(3):
        lines = slice(part * width, (part + 1) * width)
        near_pack[:, lines] = times_transpose(normt_ref[...], dqkv_ref[lines, :]).astype(
            jnp.bfloat16
        )
    near_pack[:, 3 * width :] = dpos_ref[...].T
    begin_sum(1)
    bup_copy.wait()
    begin_share(3)

    def pass_on(chunk):
        here = at(0, chunk)
        return to_other(
            part_send.at[here], part_recv.at[here], pair_send.at[chunk], pair_recv.at[chunk]
        )

    def backward(rows):
        return dot_tt(dqkv_ref[:, rows], near_ref[:, : 3 * width])

    for chunk in range(chunks):
        part_send[at(0, chunk), :] = backward(at(oth0, chunk)).astype(jnp.bfloat16)
        pass_on(chunk).start()
    vec_rows = near_ref[:, NEAR:].astype(jnp.float32).T
    gain = vec_rows[0:1]
    vec_acc[...] = jnp.zeros_like(vec_acc)
    for chunk in range(chunks):
        here = at(0, chunk)
        part = backward(at(own0, chunk))
        pass_on(chunk).wait()
        grad = part + part_recv[here, :].astype(jnp.float32)
        normed, rate = norm_parts(tok_ref[here, :].astype(jnp.float32))
        gtok_ref[here, :] = gres_ref[here, :] + norm_grad(grad, gain, normed, rate)
        vec_acc[0:8, :] += fold_rows(grad * normed)
        vec_acc[8:16, :] += fold_rows(grad)
    sums = jnp.sum(bias_acc[...].T, axis=0, keepdims=True)
    own_cols = pl.ds(pl.multiple_of(member * width, width), width)
    vec_mine[...] = jnp.zeros_like(vec_mine)
    vec_mine[0:1, :] = jnp.sum(vec_acc[0:8, :], axis=0, keepdims=True)
    vec_mine[1:2, :] = jnp.sum(vec_acc[8:16, :], axis=0, keepdims=True)
    vec_mine[2:3, own_cols] = sums[:, :width]
    vec_mine[3:4, own_cols] = sums[:, width:]
    vec_mine[4:7, :] = vec_ref[0:3, :]
    vec_copy = to_other(
        vec_mine, vec_other, pair_send.at[chunks + 1], pair_recv.at[chunks + 1]
    )
    vec_copy.start()
    pass_sum(1)
    finish_sum(0)
    gup_ref[...] = far_sum[:, : gup_ref.shape[1]]
    gdown_ref[...] = far_sum[:, gup_ref.shape[1] : 2 * gup_ref.shape[1]]
    gout_ref[...] = far_sum[:, 2 * gup_ref.shape[1] :]
    vec_copy.wait()
    both = vec_mine[...] + vec_other[...]
    vec_cols[...] = jnp.concatenate([both, jnp.zeros((VECS - 8, D), jnp.float32)], axis=0).T
    begin_share(2)
    finish_share(3)
    gbup_ref[...] = jnp.sum(bup_sum[...], axis=0, keepdims=True)
    finish_sum(1)
    for part, ref in enumerate((gq_ref, gk_ref, gv_ref, gp_ref)):
        ref[...] = near_sum[:, part * width : (part + 1) * width]
    finish_share(2)
    gvec_ref[...] = vec_sum[...].T[:8]


def last_call(e, qu, qw, key, va, o, pos, col, gatt, far, near, norm, tok, gres, gfar, vec, bup):
    count = lax.axis_size("dp")
    levels = count // PLANE
    rows, own_rows = norm.shape[0], tok.shape[0]
    chunks = own_rows // CHUNK
    width = qu.shape[0]
    hidden = (far.shape[1] - width) // 2
    shard = D // count
    f32, bf16 = jnp.float32, jnp.bfloat16

    def shape(*dims):
        return jax.ShapeDtypeStruct(dims, f32)

    def room(*dims, kind=f32):
        return pltpu.VMEM(dims, kind)

    return pl.pallas_call(
        functools.partial(last_kernel, count),
        in_specs=[ANY_SPEC] + [VMEM_SPEC] * 16,
        out_specs=[VMEM_SPEC] * 10,
        out_shape=[shape(own_rows, D)]
        + [shape(shard, width)] * 4
        + [shape(shard, hidden)] * 2
        + [shape(shard, width), shape(8, shard), shape(1, 128)],
        scratch_shapes=[
            room(2, TILE, PACK[-1], kind=bf16),
            room(PLANE - 1, levels, shard, far.shape[1], kind=bf16),
            room(levels - 1, shard, far.shape[1], kind=bf16),
            room(levels - 1, shard, far.shape[1], kind=bf16),
            room(D, 4 * width, kind=bf16),
            room(PLANE - 1, levels, shard, 4 * width, kind=bf16),
            room(levels - 1, shard, 4 * width, kind=bf16),
            room(levels - 1, shard, 4 * width, kind=bf16),
            room(8, D),
            room(8, D),
            room(D, VECS),
            room(count - 1, shard, VECS),
            room(8 * count, 128),
            room(count - 1, 8, 128),
            room(va.shape[0], rows, kind=bf16),
            room(width, rows, kind=bf16),
            room(3 * width, rows, kind=bf16),
            room(HEAD, rows),
            room(HEAD, rows),
            room(width, D, kind=bf16),
            room(rows, D, kind=bf16),
            room(rows, VECS, kind=bf16),
            room(HEAD, rows),
            room(2 * width, 128),
            room(D, rows, kind=bf16),
            room(own_rows, D, kind=bf16),
            room(own_rows, D, kind=bf16),
            room(shard, far.shape[1]),
            room(shard, 4 * width),
            room(shard, VECS),
            room(8, 128),
            room(16, D),
            pltpu.SemaphoreType.DMA((2, count - 1)),
            pltpu.SemaphoreType.DMA((2, count - 1)),
            pltpu.SemaphoreType.DMA((2, PLANE - 1, levels)),
            pltpu.SemaphoreType.DMA((2, PLANE - 1, levels)),
            pltpu.SemaphoreType.DMA((2, levels - 1)),
            pltpu.SemaphoreType.DMA((2, levels - 1)),
            pltpu.SemaphoreType.DMA((chunks + 2,)),
            pltpu.SemaphoreType.DMA((chunks + 2,)),
            pltpu.SemaphoreType.DMA((2,)),
        ],
        compiler_params=pltpu.CompilerParams(
            collective_id=2, has_side_effects=True, vmem_limit_bytes=62 * 1024 * 1024
        ),
    )(e, qu, qw, key, va, o, pos, col, gatt, far, near, norm, tok, gres, gfar, vec, bup)


def finish_kernel(number, *refs):
    for source, target in zip(refs[:number], refs[number : 2 * number]):
        target[...] = source[...]
    vec_ref, row_ref = refs[2 * number : 2 * number + 2]
    for place, target in enumerate(refs[2 * number + 2 : -1]):
        target[...] = vec_ref[place : place + 1, :]
    refs[-1][...] = row_ref[...]


def finish_call(mats, vecs, row):
    f32 = jnp.float32
    number = len(mats)
    lines = 7

    def shape(*dims):
        return jax.ShapeDtypeStruct(dims, f32)

    return pl.pallas_call(
        lambda *refs: finish_kernel(
            number, *refs[:number], *refs[number + 2 : 2 * number + 2],
            *refs[number : number + 2], *refs[2 * number + 2 :]
        ),
        in_specs=[VMEM_SPEC] * (number + 2),
        out_specs=[VMEM_SPEC] * (number + lines + 1),
        out_shape=[shape(*m.shape) for m in mats]
        + [shape(1, vecs.shape[1])] * lines
        + [shape(1, row.shape[1])],
    )(*mats, vecs, row)


def local_plain(
    tokens,
    block_ids,
    ln1_gain,
    ln1_bias,
    w_query,
    w_key,
    w_value,
    w_pos,
    bias_u,
    bias_w,
    w_out,
    ln2_gain,
    ln2_bias,
    w_up,
    bias_up,
    w_down,
    bias_down,
    cotangent,
):
    member = lax.axis_index("tensor")
    squares = (w_query, w_key, w_value, w_pos, w_out.T)
    wide = (w_up, w_down.T)
    vectors = (ln1_gain, ln1_bias, bias_u, bias_w, ln2_gain, ln2_bias, bias_down)
    near_mats = [lax.all_gather(m, "dp", axis=0, tiled=True) for m in squares]
    far_mats = [lax.all_gather(m, "dp", axis=0, tiled=True) for m in wide]
    full_vecs = [lax.all_gather(v, "dp", axis=0, tiled=True) for v in vectors]
    up_shift = lax.all_gather(bias_up, "dp", axis=0, tiled=True)
    query_mat, key_mat, value_mat, pos_mat, out_back = near_mats
    out_mat = out_back.T
    up_mat, down_back = far_mats
    down_mat = down_back.T
    gain_one, shift_one, bias_one, bias_two, gain_two, shift_two, down_shift = full_vecs
    gain_one = gain_one.astype(jnp.float32)
    shift_one = shift_one.astype(jnp.float32)
    gain_two = gain_two.astype(jnp.float32)
    shift_two = shift_two.astype(jnp.float32)
    local_width = query_mat.shape[1]
    head_count = local_width // HEAD
    hidden_local = up_mat.shape[1]
    full_hidden = up_shift.shape[0]
    own_u = lax.dynamic_slice_in_dim(
        bias_one.astype(jnp.float32), member * local_width, local_width
    )
    own_w = lax.dynamic_slice_in_dim(
        bias_two.astype(jnp.float32), member * local_width, local_width
    )
    score_scale = 1.0 / math.sqrt(HEAD)
    own_rows = tokens.shape[0]
    inputs = tokens.astype(jnp.float32)
    normed = layer_norm(inputs, gain_one, shift_one)
    rows_all = lax.all_gather(normed.astype(jnp.bfloat16), "tensor", axis=0, tiled=True)
    total_rows = rows_all.shape[0]
    queries_t = project_cols(query_mat, rows_all)
    def heads_of(array):
        return array.astype(jnp.bfloat16).reshape(head_count, HEAD, array.shape[-1])

    ids = block_ids.reshape(1, total_rows)
    sum_u = queries_t + own_u[:, None]
    sum_w = queries_t + own_w[:, None]
    fold = score_scale * LOG2E
    query_u = heads_of(sum_u)
    query_w = heads_of(sum_w)
    key_rows = heads_of(project_cols(key_mat, rows_all))
    ones = jnp.ones((head_count, 2, total_rows), jnp.bfloat16)
    blank = jnp.zeros((head_count, AUG - HEAD - 2, total_rows), jnp.bfloat16)
    value_rows = jnp.concatenate(
        [heads_of(project_cols(value_mat, rows_all)), ones, blank], axis=1
    )
    pos_rows = pos_mat.T.reshape(head_count, HEAD, D)
    table = angle_table()
    row_table = jnp.asarray(table)
    col_table = jnp.asarray(np.ascontiguousarray(table.T))
    weights, mixed_sums = attend_all(
        heads_of(sum_u * fold), heads_of(sum_w * fold), key_rows, value_rows, pos_rows, ids,
        row_table, col_table,
    )
    inv_total = 1.0 / mixed_sums[:, HEAD : HEAD + 1]
    mixed_full = mixed_sums[:, :HEAD] * inv_total
    mixed_cols = mixed_full.reshape(local_width, total_rows).astype(jnp.bfloat16)
    residual = inputs + lax.psum_scatter(
        contract_rows(
            take_cols(mixed_cols, jnp.int32(0), own_rows * lax.axis_size("tensor")), out_mat
        ).astype(jnp.bfloat16),
        "tensor",
        scatter_dimension=0,
        tiled=True,
    ).astype(jnp.float32)
    normed_two = layer_norm(residual, gain_two, shift_two)
    grad_output = cotangent.astype(jnp.float32)
    grad_down_bias = placed(jnp.sum(grad_output, axis=0), D, 0)
    own_up = lax.dynamic_slice_in_dim(
        up_shift.astype(jnp.float32), member * hidden_local, hidden_local
    )
    rows_two = lax.all_gather(normed_two.astype(jnp.bfloat16), "tensor", axis=0, tiled=True)
    hidden = jnp.dot(rows_two, up_mat, preferred_element_type=jnp.float32) + own_up
    active = jax.nn.gelu(hidden).astype(jnp.bfloat16)
    output = (
        residual
        + lax.psum_scatter(
            jnp.dot(
                take_rows(active, jnp.int32(0), own_rows * lax.axis_size("tensor")),
                down_mat,
                preferred_element_type=jnp.float32,
            ).astype(jnp.bfloat16),
            "tensor",
            scatter_dimension=0,
            tiled=True,
        ).astype(jnp.float32)
        + down_shift.astype(jnp.float32)
    )
    grad_full = lax.all_gather(cotangent, "tensor", axis=0, tiled=True)
    grad_active = times_transpose(grad_full, down_mat)
    grad_down = contract_rows(active, grad_full)
    gelu_back = jax.vjp(jax.nn.gelu, hidden)[1]
    grad_hidden = gelu_back(grad_active)[0].astype(jnp.bfloat16)
    grad_up_bias = placed(
        jnp.sum(grad_hidden, axis=0, dtype=jnp.float32), full_hidden, member * hidden_local
    )
    grad_up = contract_rows(rows_two, grad_hidden)
    grad_normed_two = lax.psum_scatter(
        times_transpose(
            take_rows(grad_hidden, jnp.int32(0), own_rows * lax.axis_size("tensor")), up_mat
        ).astype(jnp.bfloat16),
        "tensor",
        scatter_dimension=0,
        tiled=True,
    ).astype(jnp.float32)
    norm_back_two = jax.vjp(layer_norm, residual, gain_two, shift_two)[1]
    grad_resid_part, grad_gain_two, grad_shift_two = norm_back_two(grad_normed_two)
    grad_residual = grad_output + grad_resid_part
    ffn_terms = (grad_gain_two, grad_shift_two, grad_up, grad_up_bias, grad_down, grad_down_bias)
    grad_att = lax.all_gather(grad_residual.astype(jnp.bfloat16), "tensor", axis=0, tiled=True)
    grad_out_mat = jnp.dot(mixed_cols, grad_att, preferred_element_type=jnp.float32)
    grad_mixed = (
        times_transpose(out_mat, grad_att)
        .astype(jnp.bfloat16)
        .reshape(head_count, HEAD, total_rows)
    )
    grad_mixed = grad_mixed.astype(jnp.float32)
    grad_scaled = (grad_mixed * inv_total).astype(jnp.bfloat16)
    grad_low = (grad_mixed * (inv_total * score_scale)).astype(jnp.bfloat16)
    inner = -jnp.sum(grad_low.astype(jnp.float32) * mixed_full, axis=1, keepdims=True)
    inner_high = inner.astype(jnp.bfloat16)
    inner_rest = (inner - inner_high.astype(jnp.float32)).astype(jnp.bfloat16)
    grad_aug = jnp.concatenate([grad_low, inner_high, inner_rest, blank], axis=1)
    dqu, dqw, dk, dv, dpos = attend_back_all(
        weights, query_u, query_w, key_rows, value_rows, pos_rows, grad_aug, grad_scaled, col_table
    )
    grad_keys_all = dk.reshape(local_width, total_rows).astype(jnp.bfloat16)
    grad_values_all = dv.reshape(local_width, total_rows).astype(jnp.bfloat16)
    grad_pos = dpos.reshape(local_width, D).T
    grad_query_u = dqu.reshape(local_width, total_rows)
    grad_query_w = dqw.reshape(local_width, total_rows)
    grad_bias_one = placed(jnp.sum(grad_query_u, axis=1), D, member * local_width)
    grad_bias_two = placed(jnp.sum(grad_query_w, axis=1), D, member * local_width)
    grad_query = (grad_query_u + grad_query_w).astype(jnp.bfloat16)
    grad_query_mat = times_transpose(rows_all.T, grad_query)
    grad_key_mat = times_transpose(rows_all.T, grad_keys_all)
    grad_value_mat = times_transpose(rows_all.T, grad_values_all)
    first_row = jnp.int32(0)
    part_sum = times_transpose(
        take_cols(grad_query, first_row, own_rows * lax.axis_size("tensor")).T, query_mat
    )
    part_sum = part_sum + times_transpose(
        take_cols(grad_keys_all, first_row, own_rows * lax.axis_size("tensor")).T, key_mat
    )
    grad_normed = lax.psum_scatter(
        (
            part_sum
            + times_transpose(
                take_cols(grad_values_all, first_row, own_rows * lax.axis_size("tensor")).T,
                value_mat,
            )
        ).astype(jnp.bfloat16),
        "tensor",
        scatter_dimension=0,
        tiled=True,
    ).astype(jnp.float32)
    norm_back_one = jax.vjp(layer_norm, inputs, gain_one, shift_one)[1]
    grad_in_part, grad_gain_one, grad_shift_one = norm_back_one(grad_normed)
    grad_tokens = grad_residual + grad_in_part
    grad_squares = (grad_query_mat, grad_key_mat, grad_value_mat, grad_pos, grad_out_mat.T)
    grad_wides = (grad_up, grad_down.T)
    grad_vecs = jnp.stack(
        (
            grad_gain_one, grad_shift_one, grad_bias_one, grad_bias_two,
            ffn_terms[0], ffn_terms[1], ffn_terms[5],
        )
    )
    grad_vecs, grad_up_row = lax.psum((grad_vecs, ffn_terms[3]), "tensor")
    def share(array):
        return lax.psum_scatter(array, "dp", scatter_dimension=0, tiled=True)

    squares = [share(m) for m in grad_squares]
    wides = [share(m) for m in grad_wides]
    vecs = [share(v) for v in grad_vecs]
    up_part = share(grad_up_row)
    return (
        output.astype(jnp.bfloat16),
        grad_tokens,
        vecs[0],
        vecs[1],
        squares[0],
        squares[1],
        squares[2],
        squares[3],
        vecs[2],
        vecs[3],
        squares[4].T,
        vecs[4],
        vecs[5],
        wides[0],
        up_part,
        wides[1].T,
        vecs[6],
    )


def local_direct(
    tokens,
    block_ids,
    ln1_gain,
    ln1_bias,
    w_query,
    w_key,
    w_value,
    w_pos,
    bias_u,
    bias_w,
    w_out,
    ln2_gain,
    ln2_bias,
    w_up,
    bias_up,
    w_down,
    bias_down,
    cotangent,
):
    total_rows = block_ids.shape[0]
    vectors = (ln1_gain, ln1_bias, bias_u, bias_w, ln2_gain, ln2_bias, bias_down)
    table = angle_table()
    row_table = jnp.asarray(table)
    col_table = jnp.asarray(np.ascontiguousarray(table.T))
    (
        weights, query_u, query_w, key_rows, value_aug, mixed_sums, mixed_cols, rows_all, pos_back,
        near, far, up_rows, grad_full,
    ) = first_call(
        tokens,
        cotangent,
        (w_query, w_key, w_value, w_pos),
        (w_up, w_down.T, w_out.T),
        [vector.reshape(1, -1) for vector in vectors],
        bias_up.reshape(1, -1),
        block_ids.reshape(1, total_rows),
        row_table,
        col_table,
    )
    out, grad_res, grad_att, grad_far, grad_vec, grad_up_part = middle_call(
        mixed_cols, tokens, grad_full, far, near, up_rows
    )
    (
        grad_tokens, grad_query_mat, grad_key_mat, grad_value_mat, grad_pos, grad_up, grad_down,
        grad_out, grad_vecs, grad_up_row,
    ) = last_call(
        weights, query_u, query_w, key_rows, value_aug, mixed_sums, pos_back, row_table, grad_att,
        far, near, rows_all, tokens, grad_res, grad_far, grad_vec, grad_up_part,
    )
    (
        grad_query_mat, grad_key_mat, grad_value_mat, grad_pos, grad_up, grad_down, grad_out,
        *grad_vecs, grad_up_row,
    ) = finish_call(
        (grad_query_mat, grad_key_mat, grad_value_mat, grad_pos, grad_up, grad_down, grad_out),
        grad_vecs,
        grad_up_row,
    )
    grad_vecs = [vector.reshape(-1) for vector in grad_vecs]
    return (
        out,
        grad_tokens,
        grad_vecs[0],
        grad_vecs[1],
        grad_query_mat,
        grad_key_mat,
        grad_value_mat,
        grad_pos,
        grad_vecs[2],
        grad_vecs[3],
        grad_out.T,
        grad_vecs[4],
        grad_vecs[5],
        grad_up,
        grad_up_row.reshape(-1),
        grad_down.T,
        grad_vecs[6],
    )


def solution(mesh):
    in_specs = (
        P(("dp", "tensor"), None),
        P("dp"),
        P("dp"),
        P("dp"),
        P("dp", "tensor"),
        P("dp", "tensor"),
        P("dp", "tensor"),
        P("dp", "tensor"),
        P("dp"),
        P("dp"),
        P("tensor", "dp"),
        P("dp"),
        P("dp"),
        P("dp", "tensor"),
        P("dp"),
        P("tensor", "dp"),
        P("dp"),
        P(("dp", "tensor"), None),
    )
    out_specs = (
        P(("dp", "tensor"), None),
        P(("dp", "tensor"), None),
        P("dp"),
        P("dp"),
        P("dp", "tensor"),
        P("dp", "tensor"),
        P("dp", "tensor"),
        P("dp", "tensor"),
        P("dp"),
        P("dp"),
        P("tensor", "dp"),
        P("dp"),
        P("dp"),
        P("dp", "tensor"),
        P("dp"),
        P("tensor", "dp"),
        P("dp"),
    )
    pieces = D // mesh.shape["dp"]
    whole_tiles = (
        pieces % 16 == 0 and mesh.shape["tensor"] == 2 and mesh.shape["dp"] % (2 * PLANE) == 0
    )
    local = local_direct if whole_tiles else local_plain
    return jax.shard_map(local, mesh=mesh, in_specs=in_specs, out_specs=out_specs, check_vma=False)
```

```python
import functools
import math

import jax
import jax.numpy as jnp
import ml_dtypes
import numpy as np
from jax import lax
from jax.experimental import pallas as pl
from jax.experimental.pallas import tpu as pltpu
from jax.sharding import PartitionSpec as P

D = 512
HEAD = 64
L = 2048


MESH = pl.DeviceIdType.MESH
VECS = 128


def peer_at(offset):
    count = lax.axis_size("dp")
    return lax.rem(lax.axis_index("dp") + offset, count)


PLANE = 4


def place_of(me, count):
    return lax.div(me, PLANE), lax.rem(me, PLANE), count // PLANE


def along(me, count, offset):
    level, spot, levels = place_of(me, count)
    return lax.rem(level + offset, levels) * PLANE + spot


def across(me, count, offset):
    level, spot, _ = place_of(me, count)
    return level * PLANE + lax.rem(spot + offset, PLANE)


def remote(source, target, send_sem, recv_sem, device):
    return pltpu.make_async_remote_copy(
        src_ref=source,
        dst_ref=target,
        send_sem=send_sem,
        recv_sem=recv_sem,
        device_id={"dp": device},
        device_id_type=MESH,
    )


def greet_all(count, with_pair=False):
    barrier = pltpu.get_barrier_semaphore()

    def greet(offset, carry):
        pl.semaphore_signal(
            barrier, inc=1, device_id={"dp": peer_at(offset)}, device_id_type=MESH
        )
        return carry

    lax.fori_loop(1, count, greet, 0)
    if with_pair:
        pl.semaphore_signal(
            barrier, inc=1, device_id={"tensor": 1 - lax.axis_index("tensor")}, device_id_type=MESH
        )
    pl.semaphore_wait(barrier, count if with_pair else count - 1)


def layer_norm(values, gain_vec, shift_vec):
    center = values - jnp.mean(values, axis=-1, keepdims=True)
    spread = jnp.mean(center * center, axis=-1, keepdims=True)
    return center * lax.rsqrt(spread + 1e-05) * gain_vec + shift_vec


def take_rows(array, first_row, row_count):
    return lax.dynamic_slice_in_dim(array, first_row, row_count, 0)


def take_cols(array, first_col, col_count):
    return lax.dynamic_slice_in_dim(array, first_col, col_count, array.ndim - 1)


def contract_rows(left, right):
    return lax.dot_general(
        left, right, (((0,), (0,)), ((), ())), preferred_element_type=jnp.float32
    )


def times_transpose(left, right):
    return lax.dot_general(
        left, right, (((1,), (1,)), ((), ())), preferred_element_type=jnp.float32
    )


def project_cols(weight, row_data):
    return lax.dot_general(
        weight, row_data, (((0,), (1,)), ((), ())), preferred_element_type=jnp.float32
    )


TILE = 256
TILES = L // TILE
AUG = HEAD + 16
LOG2E = 1.4426950408889634


def tiles_seen(tile):
    return min(tile + 2, TILES)


PACK = [TILE * sum(tiles_seen(t) for t in range(tile)) for tile in range(TILES + 1)]


def angle_table():
    freqs = np.exp(np.arange(0, D, 2, dtype=np.float64) * (-math.log(10000.0) / D))
    angles = np.arange(L, dtype=np.float64)[:, None] * freqs[None, :]
    return np.concatenate([np.cos(angles), np.sin(angles)], axis=1).astype(ml_dtypes.bfloat16)


def dot_nn(left, right):
    return jnp.dot(left, right, preferred_element_type=jnp.float32)


def attend_kernel(qu_ref, qw_ref, key_ref, value_ref, pos_ref, ids_ref, row_ref, col_ref, e_ref, o_ref):
    half = D // 2
    for tile in range(TILES):
        rows = slice(tile * TILE, (tile + 1) * TILE)
        width = tiles_seen(tile) * TILE
        both = contract_rows(qw_ref[:, rows], pos_ref[...])
        part_a, part_b = both[:, :half], both[:, half:]
        cos_i = row_ref[rows, :half].astype(jnp.float32)
        sin_i = row_ref[rows, half:].astype(jnp.float32)
        turned = jnp.concatenate(
            [part_a * sin_i + part_b * cos_i, part_b * sin_i - part_a * cos_i], axis=1
        ).astype(jnp.bfloat16)
        scores = dot_nn(turned, col_ref[:, :width]) + contract_rows(
            qu_ref[:, rows], key_ref[:, :width]
        )
        ids_row = ids_ref[:, tile * TILE : width]
        ids_col = jnp.broadcast_to(ids_row[:, :TILE], (8, TILE)).T[:, :1]
        edge = jnp.where(ids_row <= ids_col, scores[:, tile * TILE :], -1e30)
        if tile:
            scores = jnp.concatenate([scores[:, : tile * TILE], edge], axis=1)
        else:
            scores = edge
        peak = jnp.max(scores, axis=1, keepdims=True)
        weights = jnp.exp2(scores - peak).astype(jnp.bfloat16)
        e_ref[:, PACK[tile] : PACK[tile + 1]] = weights
        o_ref[:, rows] = times_transpose(value_ref[:, :width], weights)


def attend_back_kernel(
    e_ref, qu_ref, qw_ref, key_ref, value_ref, pos_ref, aug_ref, scaled_ref, col_ref,
    dqu_ref, dqw_ref, dk_ref, dv_ref, dpos_ref,
):
    half = D // 2
    dk_ref[...] = jnp.zeros_like(dk_ref)
    dv_ref[...] = jnp.zeros_like(dv_ref)
    for tile in range(TILES):
        rows = slice(tile * TILE, (tile + 1) * TILE)
        width = tiles_seen(tile) * TILE
        weights = e_ref[:, PACK[tile] : PACK[tile + 1]]
        grad_probs = contract_rows(aug_ref[:, rows], value_ref[:, :width])
        grad_scores = (weights.astype(jnp.float32) * grad_probs).astype(jnp.bfloat16)
        dv_ref[:, :width] += dot_nn(scaled_ref[:, rows], weights)
        dk_ref[:, :width] += dot_nn(qu_ref[:, rows], grad_scores)
        dqu_ref[:, rows] = times_transpose(key_ref[:, :width], grad_scores)
        turned = times_transpose(col_ref[:, :width], grad_scores)
        part_c, part_s = turned[:half], turned[half:]
        cos_i = col_ref[:half, rows].astype(jnp.float32)
        sin_i = col_ref[half:, rows].astype(jnp.float32)
        both = jnp.concatenate(
            [part_c * sin_i - part_s * cos_i, part_c * cos_i + part_s * sin_i], axis=0
        ).astype(jnp.bfloat16)
        dqw_ref[:, rows] = dot_nn(pos_ref[...], both)
        here = times_transpose(qw_ref[:, rows], both)
        if tile:
            dpos_ref[...] += here
        else:
            dpos_ref[...] = here


def per_head(rows, cols):
    return pl.BlockSpec((None, rows, cols), lambda h: (h, 0, 0))


def shared(rows, cols):
    return pl.BlockSpec((rows, cols), lambda h: (0, 0))


def attend_all(qu, qw, keys, values, pos, ids, row_table, col_table):
    heads = qu.shape[0]
    f32, bf16 = jnp.float32, jnp.bfloat16
    return pl.pallas_call(
        attend_kernel,
        grid=(heads,),
        in_specs=[per_head(HEAD, L)] * 3
        + [per_head(AUG, L), per_head(HEAD, D), shared(1, L), shared(L, D), shared(D, L)],
        out_specs=[per_head(TILE, PACK[-1]), per_head(AUG, L)],
        out_shape=[
            jax.ShapeDtypeStruct((heads, TILE, PACK[-1]), bf16),
            jax.ShapeDtypeStruct((heads, AUG, L), f32),
        ],
        compiler_params=pltpu.CompilerParams(vmem_limit_bytes=56 * 1024 * 1024),
    )(qu, qw, keys, values, pos, ids, row_table, col_table)


def attend_back_all(weights, qu, qw, keys, values, pos, aug, scaled, col_table):
    heads = qu.shape[0]
    f32 = jnp.float32
    return pl.pallas_call(
        attend_back_kernel,
        grid=(heads,),
        in_specs=[per_head(TILE, PACK[-1])]
        + [per_head(HEAD, L)] * 3
        + [per_head(AUG, L), per_head(HEAD, D), per_head(AUG, L), per_head(HEAD, L), shared(D, L)],
        out_specs=[per_head(HEAD, L)] * 4 + [per_head(HEAD, D)],
        out_shape=[jax.ShapeDtypeStruct((heads, HEAD, L), f32)] * 4
        + [jax.ShapeDtypeStruct((heads, HEAD, D), f32)],
        compiler_params=pltpu.CompilerParams(vmem_limit_bytes=56 * 1024 * 1024),
    )(weights, qu, qw, keys, values, pos, aug, scaled, col_table)


def placed(part_vec, length, offset):
    return lax.dynamic_update_slice_in_dim(jnp.zeros((length,), jnp.float32), part_vec, offset, 0)


NEAR = 4 * 256


def first_kernel(
    count, tok_ref, cot_ref, wq_ref, wk_ref, wv_ref, wp_ref, wu_ref, wd_ref, wo_ref, *refs
):
    vec_refs, bup_ref, ids_ref, row_in, col_in = refs[:7], refs[7], refs[8], refs[9], refs[10]
    (
        e_ref, qu_out, qw_out, key_out, va_out, o_out, mix_out, norm_out, pos_out,
        near_out, far_out, up_all, cot_out,
        qu_ref, qw_ref, key_ref, va_ref, o_ref, mix_ref, norm_ref, pos_ref, first_all, second_all,
        far_all, cot_all, row_ref, col_ref,
        first_ref, second_ref, far_ref, up_ref, vec_ref, tok_all, quf_ref, qwf_ref, turn_ref,
        rq_ref, vrow_ref, e_buf,
        along_send, along_recv, across_send, across_recv, own_sems, pair_send, pair_recv, e_sems,
        load_sems, store_sems, head_sems,
    ) = refs[11:]
    half = D // 2
    me, member = lax.axis_index("dp"), lax.axis_index("tensor")
    levels = count // PLANE
    pair = {"tensor": 1 - member}
    own_rows = tok_ref.shape[0]
    own = pl.ds(pl.multiple_of(member * own_rows, own_rows), own_rows)
    parts = (first_ref, second_ref, far_ref, up_ref)
    wholes = (first_all, second_all, far_all, up_all)

    def rows_of(index, device):
        rows = parts[index].shape[0]
        return wholes[index].at[pl.ds(pl.multiple_of(device * rows, rows), rows)]

    def go_along(index, offset):
        return remote(
            parts[index], rows_of(index, me),
            along_send.at[index, offset - 1], along_recv.at[index, offset - 1],
            along(me, count, offset),
        )

    def go_across(index, offset, step):
        owner = along(me, count, levels - step)
        return remote(
            parts[index] if step == 0 else rows_of(index, owner), rows_of(index, owner),
            across_send.at[index, offset - 1, step], across_recv.at[index, offset - 1, step],
            across(me, count, offset),
        )

    def own_copy(index):
        return pltpu.make_async_copy(parts[index], rows_of(index, me), own_sems.at[index])

    def begin_along(index):
        for offset in range(1, levels):
            go_along(index, offset).start()

    def begin_across(index):
        for offset in range(1, PLANE):
            go_across(index, offset, 0).start()
        own_copy(index).start()

    def forward(index):
        for step in range(1, levels):
            go_along(index, step).wait()
            for offset in range(1, PLANE):
                go_across(index, offset, step).start()

    def finish_gather(index):
        for step in range(levels):
            for offset in range(1, PLANE):
                go_across(index, offset, step).wait()
        own_copy(index).wait()

    width = wq_ref.shape[1]
    hidden = wu_ref.shape[1]
    shard = wq_ref.shape[0]
    vec_ref[...] = jnp.zeros_like(vec_ref)
    for place, ref in enumerate(vec_refs):
        vec_ref[place : place + 1, :shard] = ref[...].astype(jnp.float32)
    pair_width = width // 2
    first_ref[:, 4 * pair_width :] = vec_ref[...].T[:shard].astype(jnp.bfloat16)
    for place, ref in enumerate((wq_ref, wk_ref, wv_ref, wp_ref)):
        cols = slice(place * pair_width, (place + 1) * pair_width)
        first_ref[:, cols] = ref[:, :pair_width]
        second_ref[:, cols] = ref[:, pair_width:]
    far_ref[:, :hidden] = wu_ref[...]
    far_ref[:, hidden : 2 * hidden] = wd_ref[...]
    far_ref[:, 2 * hidden :] = wo_ref[...]
    up_ref[...] = jnp.broadcast_to(bup_ref[...].astype(jnp.float32), up_ref.shape).astype(
        jnp.bfloat16
    )

    def to_pair(source, target, slot):
        return pltpu.make_async_remote_copy(
            src_ref=source,
            dst_ref=target.at[own],
            send_sem=pair_send.at[slot],
            recv_sem=pair_recv.at[slot],
            device_id=pair,
            device_id_type=MESH,
        )

    tables = (
        pltpu.make_async_copy(row_in, row_ref, load_sems.at[0]),
        pltpu.make_async_copy(col_in, col_ref, load_sems.at[1]),
    )
    for load in tables:
        load.start()
    greet_all(count, True)
    begin_along(0)
    begin_across(0)
    begin_along(3)
    begin_across(3)
    exchanges = (to_pair(tok_ref, tok_all, 0), to_pair(cot_ref, cot_all, 1))
    keeps = (
        pltpu.make_async_copy(tok_ref, tok_all.at[own], own_sems.at[4]),
        pltpu.make_async_copy(cot_ref, cot_all.at[own], own_sems.at[5]),
    )
    for copy in exchanges + keeps:
        copy.start()
    forward(0)
    begin_along(1)
    begin_across(1)
    begin_along(2)
    forward(3)
    finish_gather(0)
    exchanges[0].wait()
    keeps[0].wait()

    vec_block = first_all[:, 4 * pair_width :].astype(jnp.float32)
    vec_rows = vec_block.T
    gain, shift = vec_rows[0:1], vec_rows[1:2]
    heads = width // HEAD
    own_cols = pl.ds(pl.multiple_of(member * width, width), width)
    vec_cols = first_all[own_cols, 4 * pair_width :].astype(jnp.float32)
    bias_u, bias_w = vec_cols[:, 2:3], vec_cols[:, 3:4]
    fold = LOG2E / math.sqrt(HEAD)
    place = lax.broadcasted_iota(jnp.int32, (AUG - HEAD, TILE), 0)
    marks = jnp.where(place < 2, 1.0, 0.0).astype(jnp.bfloat16)
    for tile in range(TILES):
        rows = slice(tile * TILE, (tile + 1) * TILE)
        normed = layer_norm(tok_all[rows, :].astype(jnp.float32), gain, shift)
        norm_ref[rows, :] = normed.astype(jnp.bfloat16)

    def project(pair_index):
        source = wholes[pair_index]
        lines = slice(pair_index * pair_width, (pair_index + 1) * pair_width)
        turn_ref[...] = source[:, : 3 * pair_width].T
        pos_ref[lines, :] = source[:, 3 * pair_width : 4 * pair_width].T
        for tile in range(TILES):
            rows = slice(tile * TILE, (tile + 1) * TILE)
            projected = times_transpose(turn_ref[...], norm_ref[rows, :])
            sum_u = projected[:pair_width] + bias_u[lines]
            sum_w = projected[:pair_width] + bias_w[lines]
            qu_ref[lines, rows] = sum_u.astype(jnp.bfloat16)
            qw_ref[lines, rows] = sum_w.astype(jnp.bfloat16)
            quf_ref[lines, rows] = (sum_u * fold).astype(jnp.bfloat16)
            qwf_ref[lines, rows] = (sum_w * fold).astype(jnp.bfloat16)
            key_ref[lines, rows] = projected[pair_width : 2 * pair_width].astype(jnp.bfloat16)
            for place in range(pair_width // HEAD):
                start = 2 * pair_width + place * HEAD
                base = (pair_index * (pair_width // HEAD) + place) * AUG
                values = projected[start : start + HEAD].astype(jnp.bfloat16)
                va_ref[base : base + HEAD, rows] = values
                va_ref[base + HEAD : base + AUG, rows] = marks

    project(0)
    forward(1)
    begin_across(2)
    for load in tables:
        load.wait()
    cols = [pl.ds(part * width, pair_width) for part in range(4)]
    more_cols = [pl.ds(part * width + pair_width, pair_width) for part in range(4)]
    here_cols = [pl.ds(part * pair_width, pair_width) for part in range(4)]
    moves = [(first_all.at[:, here_cols[part]], near_out.at[:, cols[part]]) for part in range(4)]
    moves.append(
        (first_all.at[:, pl.ds(4 * pair_width, VECS)], near_out.at[:, pl.ds(NEAR, VECS)])
    )
    moves.append((norm_ref, norm_out))
    early = len(moves)
    moves += [
        (second_all.at[:, here_cols[part]], near_out.at[:, more_cols[part]]) for part in range(4)
    ]
    moves += [
        (qu_ref, qu_out), (qw_ref, qw_out), (key_ref, key_out), (va_ref, va_out),
        (pos_ref, pos_out), (cot_all, cot_out),
    ]
    stores = [
        pltpu.make_async_copy(source, target, store_sems.at[place])
        for place, (source, target) in enumerate(moves)
    ]
    for store in stores[:early]:
        store.start()

    def head_copies(head):
        lines = pl.ds(pl.multiple_of(head * HEAD, HEAD), HEAD)
        more = pl.ds(pl.multiple_of(head * AUG, 16), AUG)
        return (
            pltpu.make_async_copy(o_ref.at[more], o_out.at[more], head_sems.at[0, head]),
            pltpu.make_async_copy(mix_ref.at[lines], mix_out.at[lines], head_sems.at[1, head]),
        )

    def e_copy(head, slot):
        return pltpu.make_async_copy(e_buf.at[slot], e_ref.at[head], e_sems.at[slot])

    def one_head(head, carry):
        slot = lax.rem(head, 2)
        lines = pl.ds(pl.multiple_of(head * HEAD, HEAD), HEAD)
        more = pl.ds(pl.multiple_of(head * AUG, 16), AUG)
        upper = pl.ds(pl.multiple_of(head * AUG, 16), HEAD)
        lower = pl.ds(pl.multiple_of(head * AUG + HEAD, 16), AUG - HEAD)

        @pl.when(head >= 2)
        def _():
            e_copy(head - 2, slot).wait()

        filler = jnp.zeros((VECS - AUG, va_ref.shape[1]), jnp.bfloat16)
        vrow_ref[...] = jnp.concatenate([va_ref[more, :], filler], axis=0).T
        for tile in range(TILES):
            rows = slice(tile * TILE, (tile + 1) * TILE)
            both = contract_rows(qwf_ref[lines, rows], pos_ref[lines, :])
            part_a, part_b = both[:, :half], both[:, half:]
            cos_i = row_ref[rows, :half].astype(jnp.float32)
            sin_i = row_ref[rows, half:].astype(jnp.float32)
            rq_ref[rows, :half] = (part_a * sin_i + part_b * cos_i).astype(jnp.bfloat16)
            rq_ref[rows, half:] = (part_b * sin_i - part_a * cos_i).astype(jnp.bfloat16)

        def scores_of(tile):
            rows = slice(tile * TILE, (tile + 1) * TILE)
            seen = tiles_seen(tile) * TILE
            scores = dot_nn(rq_ref[rows, :], col_ref[:, :seen]) + contract_rows(
                quf_ref[lines, rows], key_ref[lines, :seen]
            )
            ids_row = ids_ref[:, tile * TILE : seen]
            ids_col = jnp.broadcast_to(ids_row[:, :TILE], (8, TILE)).T[:, :1]
            edge = jnp.where(ids_row <= ids_col, scores[:, tile * TILE :], -1e30)
            if tile:
                return jnp.concatenate([scores[:, : tile * TILE], edge], axis=1)
            return edge

        def use_scores(tile, scores):
            rows = slice(tile * TILE, (tile + 1) * TILE)
            seen = tiles_seen(tile) * TILE
            peak = jnp.max(scores, axis=1, keepdims=True)
            weights = jnp.exp2(scores - peak).astype(jnp.bfloat16)
            e_buf[slot, :, PACK[tile] : PACK[tile + 1]] = weights
            sums = dot_nn(weights, vrow_ref[:seen, :]).T
            inverse = 1.0 / sums[HEAD : HEAD + 1]
            mixed = sums[:HEAD] * inverse
            o_ref[upper, rows] = mixed
            o_ref[lower, rows] = jnp.broadcast_to(inverse, (AUG - HEAD, TILE))
            mix_ref[lines, rows] = mixed.astype(jnp.bfloat16)

        scores = scores_of(0)
        for tile in range(TILES):
            following = scores_of(tile + 1) if tile + 1 < TILES else None
            use_scores(tile, scores)
            scores = following
        e_copy(head, slot).start()
        for copy in head_copies(head):
            copy.start()

        @pl.when(head == 0)
        def _():
            forward(2)

        @pl.when(head == heads // 2 - 1)
        def _():
            finish_gather(1)
            project(1)
            exchanges[1].wait()
            keeps[1].wait()
            for store in stores[early:]:
                store.start()

        return carry

    lax.fori_loop(0, heads, one_head, 0)
    for head in range(max(heads - 2, 0), heads):
        e_copy(head, head % 2).wait()
    finish_gather(3)
    finish_gather(2)
    far_store = pltpu.make_async_copy(far_all, far_out, load_sems.at[2])
    far_store.start()
    for store in stores:
        store.wait()
    for head in range(heads):
        for copy in head_copies(head):
            copy.wait()
    far_store.wait()


VMEM_SPEC = pl.BlockSpec(memory_space=pltpu.VMEM)
ANY_SPEC = pl.BlockSpec(memory_space=pl.ANY)


def first_call(tokens, cotangent, squares, wides, vectors, bup, ids, row_table, col_table):
    count = lax.axis_size("dp")
    levels = count // PLANE
    rows = ids.shape[1]
    shard, width = squares[0].shape
    hidden = wides[0].shape[1]
    heads = width // HEAD
    far_width = 2 * hidden + width
    f32, bf16 = jnp.float32, jnp.bfloat16

    def shape(*dims, kind=bf16):
        return jax.ShapeDtypeStruct(dims, kind)

    return pl.pallas_call(
        functools.partial(first_kernel, count),
        in_specs=[VMEM_SPEC] * 18 + [ANY_SPEC] * 2,
        out_specs=[ANY_SPEC] * 11 + [VMEM_SPEC, ANY_SPEC],
        out_shape=[
            shape(heads, TILE, PACK[-1]),
            shape(width, rows),
            shape(width, rows),
            shape(width, rows),
            shape(heads * AUG, rows),
            shape(heads * AUG, rows, kind=f32),
            shape(width, rows),
            shape(rows, D),
            shape(width, D),
            shape(D, NEAR + VECS),
            shape(D, far_width),
            shape(16 * count, bup.shape[1]),
            shape(rows, D),
        ],
        scratch_shapes=[
            pltpu.VMEM((width, rows), bf16),
            pltpu.VMEM((width, rows), bf16),
            pltpu.VMEM((width, rows), bf16),
            pltpu.VMEM((heads * AUG, rows), bf16),
            pltpu.VMEM((heads * AUG, rows), f32),
            pltpu.VMEM((width, rows), bf16),
            pltpu.VMEM((rows, D), bf16),
            pltpu.VMEM((width, D), bf16),
            pltpu.VMEM((D, NEAR // 2 + VECS), bf16),
            pltpu.VMEM((D, NEAR // 2), bf16),
            pltpu.VMEM((D, far_width), bf16),
            pltpu.VMEM((rows, D), bf16),
            pltpu.VMEM((rows, D), bf16),
            pltpu.VMEM((D, rows), bf16),
            pltpu.VMEM((shard, NEAR // 2 + VECS), bf16),
            pltpu.VMEM((shard, NEAR // 2), bf16),
            pltpu.VMEM((shard, far_width), bf16),
            pltpu.VMEM((16, bup.shape[1]), bf16),
            pltpu.VMEM((VECS, VECS), f32),
            pltpu.VMEM((rows, D), bf16),
            pltpu.VMEM((width, rows), bf16),
            pltpu.VMEM((width, rows), bf16),
            pltpu.VMEM((3 * width // 2, D), bf16),
            pltpu.VMEM((rows, D), bf16),
            pltpu.VMEM((rows, VECS), bf16),
            pltpu.VMEM((2, TILE, PACK[-1]), bf16),
            pltpu.SemaphoreType.DMA((4, levels - 1)),
            pltpu.SemaphoreType.DMA((4, levels - 1)),
            pltpu.SemaphoreType.DMA((4, PLANE - 1, levels)),
            pltpu.SemaphoreType.DMA((4, PLANE - 1, levels)),
            pltpu.SemaphoreType.DMA((6,)),
            pltpu.SemaphoreType.DMA((2,)),
            pltpu.SemaphoreType.DMA((2,)),
            pltpu.SemaphoreType.DMA((2,)),
            pltpu.SemaphoreType.DMA((3,)),
            pltpu.SemaphoreType.DMA((16,)),
            pltpu.SemaphoreType.DMA((2, heads)),
        ],
        compiler_params=pltpu.CompilerParams(
            collective_id=0, has_side_effects=True, vmem_limit_bytes=60 * 1024 * 1024
        ),
    )(tokens, cotangent, *squares, *wides, *vectors, bup, ids, row_table, col_table)


CHUNK = 256
GELU_SCALE = math.sqrt(2.0 / math.pi)


def fold_rows(values):
    return jnp.sum(values.reshape(values.shape[0] // 8, 8, values.shape[1]), axis=0)


def fold_cols(values):
    total = values[:, :128]
    for start in range(128, values.shape[1], 128):
        total = total + values[:, start : start + 128]
    return total


def norm_parts(values):
    center = values - jnp.mean(values, axis=-1, keepdims=True)
    spread = jnp.mean(center * center, axis=-1, keepdims=True)
    rate = lax.rsqrt(spread + 1e-05)
    return center * rate, rate


def norm_grad(grad, gain, normed, rate):
    scaled = grad * gain
    mean = jnp.mean(scaled, axis=-1, keepdims=True)
    along = jnp.mean(scaled * normed, axis=-1, keepdims=True)
    return rate * (scaled - mean - normed * along)


def to_other(source, target, send_sem, recv_sem):
    return pltpu.make_async_remote_copy(
        src_ref=source,
        dst_ref=target,
        send_sem=send_sem,
        recv_sem=recv_sem,
        device_id={"tensor": 1 - lax.axis_index("tensor")},
        device_id_type=MESH,
    )


def dot_tt(left, right):
    return lax.dot_general(
        left, right, (((0,), (1,)), ((), ())), preferred_element_type=jnp.float32
    )


def middle_kernel(
    mix_ref, tok_ref, cot_ref, far_ref, vec_ref, up_ref,
    out_ref, gres_ref, gatt_ref, gfar_ref, vec_out, bup_out,
    send_a, recv_a, res_ref, n2_ref, n2t_ref, cott_ref, act_ref, gh_ref,
    osend, orecv, oacc, gacc, bup_acc, vec_acc, send_sems, recv_sems,
):
    member = lax.axis_index("tensor")
    own_rows = tok_ref.shape[0]
    chunks = own_rows // CHUNK
    own0 = pl.multiple_of(member * own_rows, own_rows)
    oth0 = pl.multiple_of((1 - member) * own_rows, own_rows)
    hidden = act_ref.shape[1]
    up_cols, down_cols = slice(0, hidden), slice(hidden, 2 * hidden)
    out_cols = slice(2 * hidden, far_ref.shape[1])

    def at(base, chunk):
        return pl.ds(pl.multiple_of(base + chunk * CHUNK, CHUNK), CHUNK)

    barrier = pltpu.get_barrier_semaphore()
    pl.semaphore_signal(barrier, inc=1, device_id={"tensor": 1 - member}, device_id_type=MESH)
    pl.semaphore_wait(barrier, 1)

    def pass_on(stage, chunk):
        here = at(0, chunk)
        pairs = (
            (send_a.at[here], recv_a.at[here]),
            (n2_ref.at[at(own0, chunk)], n2_ref.at[at(own0, chunk)]),
            (osend.at[0, here], orecv.at[0, here]),
            (osend.at[1, here], orecv.at[1, here]),
            (gatt_ref.at[at(own0, chunk)], gatt_ref.at[at(own0, chunk)]),
        )
        source, target = pairs[stage]
        return to_other(
            source, target, send_sems.at[stage, chunk], recv_sems.at[stage, chunk]
        )

    vec_rows = vec_ref[:, NEAR:].astype(jnp.float32).T
    gain, shift, down_shift = vec_rows[4:5], vec_rows[5:6], vec_rows[6:7]
    ups = hidden // 128
    up_block = up_ref[pl.ds(pl.multiple_of(member * ups * 16, 16), ups * 16), :].astype(jnp.float32)
    up_shift = jnp.concatenate([up_block[16 * k : 16 * k + 1] for k in range(ups)], axis=1)

    def branch(rows):
        return dot_tt(mix_ref[:, rows], far_ref[:, out_cols])

    for chunk in range(chunks):
        send_a[at(0, chunk), :] = branch(at(oth0, chunk)).astype(jnp.bfloat16)
        pass_on(0, chunk).start()
    for chunk in range(chunks):
        here = at(0, chunk)
        part = branch(at(own0, chunk))
        pass_on(0, chunk).wait()
        residual = tok_ref[here, :].astype(jnp.float32) + part + recv_a[here, :].astype(jnp.float32)
        res_ref[here, :] = residual
        n2_ref[at(own0, chunk), :] = (norm_parts(residual)[0] * gain + shift).astype(jnp.bfloat16)
        pass_on(1, chunk).start()

    bup_acc[...] = jnp.zeros_like(bup_acc)
    vec_acc[...] = jnp.zeros_like(vec_acc)

    def ffn(rows):
        normed = n2_ref[rows, :]
        grads = cot_ref[rows, :]
        value = dot_nn(normed, far_ref[:, up_cols]) + up_shift
        square = value * value
        bend = jnp.tanh(GELU_SCALE * value * (1.0 + 0.044715 * square))
        half = 0.5 * (1.0 + bend)
        active = (value * half).astype(jnp.bfloat16)
        slope = half + 0.5 * value * (1.0 - bend * bend) * (
            GELU_SCALE * (1.0 + 3.0 * 0.044715 * square)
        )
        grad_hidden = (dot_nn(grads, far_ref[:, down_cols]) * slope).astype(jnp.bfloat16)
        act_ref[rows, :] = active
        gh_ref[rows, :] = grad_hidden
        n2t_ref[:, rows] = normed.T
        cott_ref[:, rows] = grads.T
        bup_acc[...] += fold_rows(grad_hidden.astype(jnp.float32))
        return (
            times_transpose(active, far_ref[:, down_cols]),
            times_transpose(grad_hidden, far_ref[:, up_cols]),
        )

    def ffn_own(chunk, carry):
        oacc[at(0, chunk), :], gacc[at(0, chunk), :] = ffn(at(own0, chunk))
        return carry

    def ffn_other(chunk, carry):
        pass_on(1, chunk).wait()
        here = at(0, chunk)
        for stage, part in zip((2, 3), ffn(at(oth0, chunk))):
            osend[stage - 2, here, :] = part.astype(jnp.bfloat16)
            pass_on(stage, chunk).start()
        return carry

    lax.fori_loop(0, 1, ffn_own, 0)
    lax.fori_loop(0, chunks, ffn_other, 0)
    lax.fori_loop(1, chunks, ffn_own, 0)

    def close(chunk, carry):
        here = at(0, chunk)
        pass_on(2, chunk).wait()
        pass_on(3, chunk).wait()
        residual = res_ref[here, :]
        out = residual + oacc[here, :] + orecv[0, here, :].astype(jnp.float32) + down_shift
        out_ref[here, :] = out.astype(jnp.bfloat16)
        grad = gacc[here, :] + orecv[1, here, :].astype(jnp.float32)
        normed, rate = norm_parts(residual)
        top = cot_ref[at(own0, chunk), :].astype(jnp.float32)
        grad_res = top + norm_grad(grad, gain, normed, rate)
        gres_ref[here, :] = grad_res
        gatt_ref[at(own0, chunk), :] = grad_res.astype(jnp.bfloat16)
        pass_on(4, chunk).start()
        vec_acc[0:8, :] += fold_rows(grad * normed)
        vec_acc[8:16, :] += fold_rows(grad)
        vec_acc[16:24, :] += fold_rows(top)
        return carry

    lax.fori_loop(0, chunks, close, 0)
    for part in range(hidden // CHUNK):
        cols = slice(part * CHUNK, (part + 1) * CHUNK)
        gfar_ref[:, cols] = dot_nn(n2t_ref[...], gh_ref[:, cols]).astype(jnp.bfloat16)
        gfar_ref[:, hidden + part * CHUNK : hidden + (part + 1) * CHUNK] = dot_nn(
            cott_ref[...], act_ref[:, cols]
        ).astype(jnp.bfloat16)
    vec_out[...] = jnp.concatenate(
        [jnp.sum(vec_acc[8 * v : 8 * v + 8, :], axis=0, keepdims=True) for v in range(3)]
        + [jnp.zeros((5, vec_acc.shape[1]), jnp.float32)],
        axis=0,
    )
    for k in range(ups):
        bup_out[8 * k : 8 * k + 8, :] = bup_acc[:, 128 * k : 128 * k + 128]
    for chunk in range(chunks):
        pass_on(4, chunk).wait()
    gfar_ref[:, out_cols] = dot_tt(gatt_ref[...], mix_ref[...]).astype(jnp.bfloat16)


def middle_call(mix, tokens, cot_all, far_all, near_all, up_all):
    rows, own_rows = cot_all.shape[0], tokens.shape[0]
    chunks = own_rows // CHUNK
    hidden = (far_all.shape[1] - mix.shape[0]) // 2
    f32, bf16 = jnp.float32, jnp.bfloat16
    return pl.pallas_call(
        middle_kernel,
        in_specs=[VMEM_SPEC] * 6,
        out_specs=[VMEM_SPEC] * 6,
        out_shape=[
            jax.ShapeDtypeStruct((own_rows, D), bf16),
            jax.ShapeDtypeStruct((own_rows, D), f32),
            jax.ShapeDtypeStruct((rows, D), bf16),
            jax.ShapeDtypeStruct(far_all.shape, bf16),
            jax.ShapeDtypeStruct((8, D), f32),
            jax.ShapeDtypeStruct((hidden // 16, 128), f32),
        ],
        scratch_shapes=[
            pltpu.VMEM((own_rows, D), bf16),
            pltpu.VMEM((own_rows, D), bf16),
            pltpu.VMEM((own_rows, D), f32),
            pltpu.VMEM((rows, D), bf16),
            pltpu.VMEM((D, rows), bf16),
            pltpu.VMEM((D, rows), bf16),
            pltpu.VMEM((rows, hidden), bf16),
            pltpu.VMEM((rows, hidden), bf16),
            pltpu.VMEM((2, own_rows, D), bf16),
            pltpu.VMEM((2, own_rows, D), bf16),
            pltpu.VMEM((own_rows, D), f32),
            pltpu.VMEM((own_rows, D), f32),
            pltpu.VMEM((8, hidden), f32),
            pltpu.VMEM((24, D), f32),
            pltpu.SemaphoreType.DMA((5, chunks)),
            pltpu.SemaphoreType.DMA((5, chunks)),
        ],
        compiler_params=pltpu.CompilerParams(
            collective_id=1, has_side_effects=True, vmem_limit_bytes=60 * 1024 * 1024
        ),
    )(mix, tokens, cot_all, far_all, near_all, up_all)


def last_kernel(
    count, e_ref, qu_in, qw_in, key_in, va_in, o_ref, pos_in, row_in, gatt_ref, far_in,
    near_in, norm_in, tok_in, gres_in, gfar_ref, vec_ref, bup_ref,
    gtok_ref, gq_ref, gk_ref, gv_ref, gp_ref, gup_ref, gdown_ref, gout_ref, gvec_ref, gbup_ref,
    qu_ref, qw_ref, key_ref, va_ref, pos_ref, row_ref, wout_ref, near_ref, norm_ref, tok_ref,
    gres_ref, e_buf, far_slots, far_along, far_back, packs, pack_slots, pack_along, pack_back,
    vec_mine, vec_other, vec_cols, vec_slots,
    bup_all, bup_slots, aug_ref, scd_ref, dqkv_ref, dk_acc, dv_acc, dpos_ref, both_ref, krow_ref,
    dqu_ref, bias_acc, normt_ref, part_send, part_recv, far_sum, pack_sums, vec_sum, bup_sum,
    vec_acc, send_sems, recv_sems, across_send, across_recv, along_send, along_recv,
    pair_send, pair_recv, e_sems, load_sems,
):
    half = D // 2
    me, member = lax.axis_index("dp"), lax.axis_index("tensor")
    own_rows = tok_ref.shape[0]
    chunks = own_rows // CHUNK
    own0 = pl.multiple_of(member * own_rows, own_rows)
    oth0 = pl.multiple_of((1 - member) * own_rows, own_rows)
    width = qu_ref.shape[0]
    heads = width // HEAD
    score_scale = 1.0 / math.sqrt(HEAD)
    pair_width = width // 2
    vec_width = gvec_ref.shape[1]
    sources = (gfar_ref, packs.at[0], packs.at[1], vec_cols, bup_all)
    slots = (far_slots, pack_slots.at[0], pack_slots.at[1], vec_slots, bup_slots)
    totals = (far_sum, pack_sums.at[0], pack_sums.at[1], vec_sum, bup_sum)
    moves = (
        (far_in.at[:, pl.ds(far_in.shape[1] - width, width)], wout_ref),
        (norm_in, norm_ref), (qu_in, qu_ref), (qw_in, qw_ref), (key_in, key_ref), (va_in, va_ref),
        (pos_in, pos_ref), (row_in, row_ref), (near_in, near_ref), (tok_in, tok_ref),
        (gres_in, gres_ref),
    )
    loads = [
        pltpu.make_async_copy(source, target, load_sems.at[place])
        for place, (source, target) in enumerate(moves)
    ]

    def at(base, chunk):
        return pl.ds(pl.multiple_of(base + chunk * CHUNK, CHUNK), CHUNK)

    def piece(index, device):
        rows = totals[index].shape[0]
        if index == 3:
            start = pl.multiple_of(lax.div(device * vec_width, VECS) * VECS, VECS)
            return sources[index].at[:, pl.ds(start, VECS)]
        return sources[index].at[pl.ds(pl.multiple_of(device * rows, rows), rows)]

    def share_to(index, offset):
        peer = peer_at(offset)
        return pltpu.make_async_remote_copy(
            src_ref=piece(index, peer),
            dst_ref=slots[index].at[offset - 1],
            send_sem=send_sems.at[index - 3, offset - 1],
            recv_sem=recv_sems.at[index - 3, offset - 1],
            device_id={"dp": peer},
            device_id_type=MESH,
        )

    def begin_share(index):
        def begin(offset, carry):
            share_to(index, offset).start()
            return carry

        lax.fori_loop(1, count, begin, 0)

    def finish_share(index):
        total = totals[index]
        total[...] = piece(index, me)[...].astype(jnp.float32)

        def finish(offset, carry):
            share_to(index, offset).wait()
            total[...] += slots[index][offset - 1].astype(jnp.float32)
            return carry

        lax.fori_loop(1, count, finish, 0)

    levels = count // PLANE
    along_out = (far_along, pack_along.at[0], pack_along.at[1])
    along_in = (far_back, pack_back.at[0], pack_back.at[1])

    def go_across(index, offset, step):
        peer = across(me, count, offset)
        return remote(
            piece(index, along(peer, count, step)), slots[index].at[offset - 1, step],
            across_send.at[index, offset - 1, step], across_recv.at[index, offset - 1, step], peer,
        )

    def go_along(index, step):
        return remote(
            along_out[index].at[step - 1], along_in[index].at[step - 1],
            along_send.at[index, step - 1], along_recv.at[index, step - 1],
            along(me, count, step),
        )

    order = list(range(1, levels)) + [0]

    def begin_sum(index):
        for step in order:
            for offset in range(1, PLANE):
                go_across(index, offset, step).start()

    def pass_sum(index):
        for step in order:
            total = piece(index, along(me, count, step))[...].astype(jnp.float32)
            for offset in range(1, PLANE):
                go_across(index, offset, step).wait()
                total = total + slots[index][offset - 1, step].astype(jnp.float32)
            if step:
                along_out[index][step - 1] = total.astype(jnp.bfloat16)
                go_along(index, step).start()
            else:
                totals[index][...] = total

    def finish_sum(index):
        for step in range(1, levels):
            go_along(index, step).wait()
            totals[index][...] += along_in[index][step - 1].astype(jnp.float32)

    def e_copy(head, slot):
        return pltpu.make_async_copy(e_ref.at[head], e_buf.at[slot], e_sems.at[slot])

    for load in loads[:2]:
        load.start()
    e_copy(0, 0).start()
    for load in loads[2:]:
        load.start()
    greet_all(count, True)
    begin_sum(0)
    own_bup = pl.ds(pl.multiple_of(member * bup_ref.shape[0], 8), bup_ref.shape[0])
    bup_all[own_bup, :] = bup_ref[...]
    bup_copy = to_other(bup_ref, bup_all.at[own_bup], pair_send.at[chunks], pair_recv.at[chunks])
    bup_copy.start()

    loads[0].wait()
    out_mat = wout_ref[...].T
    place = lax.broadcasted_iota(jnp.int32, (AUG - HEAD, CHUNK), 0)
    for tile in range(TILES):
        rows = slice(tile * TILE, (tile + 1) * TILE)
        grads = times_transpose(out_mat, gatt_ref[rows, :])
        grads = grads.astype(jnp.bfloat16).astype(jnp.float32)
        for head in range(heads):
            lines = slice(head * HEAD, (head + 1) * HEAD)
            first = head * AUG
            inverse = o_ref[first + HEAD : first + HEAD + 1, rows]
            mixed = o_ref[first : first + HEAD, rows]
            scaled = grads[lines] * inverse
            low = (scaled * score_scale).astype(jnp.bfloat16)
            inner = -jnp.sum(low.astype(jnp.float32) * mixed, axis=0, keepdims=True)
            high = inner.astype(jnp.bfloat16).astype(jnp.float32)
            tail = jnp.where(place == 0, high, jnp.where(place == 1, inner - high, 0.0))
            scd_ref[lines, rows] = scaled.astype(jnp.bfloat16)
            aug_ref[first : first + HEAD, rows] = low
            aug_ref[first + HEAD : first + AUG, rows] = tail.astype(jnp.bfloat16)
    loads[1].wait()
    for tile in range(TILES):
        rows = slice(tile * TILE, (tile + 1) * TILE)
        normt_ref[:, rows] = norm_ref[rows, :].T
    for load in loads[2:8]:
        load.wait()

    def pack_pair(pair):
        first = pair * pair_width
        grads = jnp.concatenate(
            [
                dqkv_ref[part * width + first : part * width + first + pair_width, :]
                for part in range(3)
            ],
            axis=0,
        )
        packs[pair, :, : 3 * pair_width] = times_transpose(normt_ref[...], grads).astype(
            jnp.bfloat16
        )
        packs[pair, :, 3 * pair_width :] = dpos_ref[first : first + pair_width, :].T

    def one_head(head, carry):
        slot = lax.rem(head, 2)
        first = pl.multiple_of(head * HEAD, HEAD)
        lines = pl.ds(first, HEAD)
        more = pl.ds(pl.multiple_of(head * AUG, 16), AUG)

        @pl.when(head + 1 < heads)
        def _():
            e_copy(head + 1, 1 - slot).start()

        e_copy(head, slot).wait()
        dk_acc[...] = jnp.zeros_like(dk_acc)
        dv_acc[...] = jnp.zeros_like(dv_acc)
        filler = jnp.zeros((VECS - HEAD, key_ref.shape[1]), jnp.bfloat16)
        krow_ref[...] = jnp.concatenate([key_ref[lines, :], filler], axis=0).T

        def grads_of(tile):
            rows = slice(tile * TILE, (tile + 1) * TILE)
            weights = e_buf[slot, :, PACK[tile] : PACK[tile + 1]]
            grad_probs = contract_rows(
                aug_ref[more, rows], va_ref[more, : tiles_seen(tile) * TILE]
            )
            return (weights.astype(jnp.float32) * grad_probs).astype(jnp.bfloat16)

        def use_grads(tile, grad_scores):
            rows = slice(tile * TILE, (tile + 1) * TILE)
            seen = tiles_seen(tile) * TILE
            weights = e_buf[slot, :, PACK[tile] : PACK[tile + 1]]
            dv_acc[:, :seen] += dot_nn(scd_ref[lines, rows], weights)
            dk_acc[:, :seen] += dot_nn(qu_ref[lines, rows], grad_scores)
            dqu_ref[:, rows] = dot_nn(grad_scores, krow_ref[:seen, :]).T[:HEAD]
            turned = dot_nn(grad_scores, row_ref[:seen, :])
            part_c, part_s = turned[:, :half], turned[:, half:]
            cos_i = row_ref[rows, :half].astype(jnp.float32)
            sin_i = row_ref[rows, half:].astype(jnp.float32)
            both_ref[rows, :half] = (part_c * sin_i - part_s * cos_i).astype(jnp.bfloat16)
            both_ref[rows, half:] = (part_c * cos_i + part_s * sin_i).astype(jnp.bfloat16)

        grad_scores = grads_of(0)
        for tile in range(TILES):
            following = grads_of(tile + 1) if tile + 1 < TILES else None
            use_grads(tile, grad_scores)
            grad_scores = following
        grad_u = dqu_ref[...]
        grad_w = times_transpose(pos_ref[lines, :], both_ref[...])
        dqkv_ref[lines, :] = (grad_u + grad_w).astype(jnp.bfloat16)
        bias_acc[lines, :] = fold_cols(grad_u)
        bias_acc[pl.ds(pl.multiple_of(width + first, HEAD), HEAD), :] = fold_cols(grad_w)
        dpos_ref[lines, :] = dot_nn(qw_ref[lines, :], both_ref[...]).astype(jnp.bfloat16)
        key_lines = pl.ds(pl.multiple_of(width + first, HEAD), HEAD)
        value_lines = pl.ds(pl.multiple_of(2 * width + first, HEAD), HEAD)
        dqkv_ref[key_lines, :] = dk_acc[...].astype(jnp.bfloat16)
        dqkv_ref[value_lines, :] = dv_acc[...].astype(jnp.bfloat16)

        @pl.when(head == heads // 2 - 1)
        def _():
            pack_pair(0)
            begin_sum(1)

        @pl.when(head == heads - 2)
        def _():
            pass_sum(0)

        return carry

    lax.fori_loop(0, heads, one_head, 0)

    for load in loads[8:]:
        load.wait()
    bup_copy.wait()
    begin_share(4)

    def pass_on(chunk):
        here = at(0, chunk)
        return to_other(
            part_send.at[here], part_recv.at[here], pair_send.at[chunk], pair_recv.at[chunk]
        )

    def backward(rows):
        return dot_tt(dqkv_ref[:, rows], near_ref[:, : 3 * width])

    for chunk in range(chunks):
        part_send[at(0, chunk), :] = backward(at(oth0, chunk)).astype(jnp.bfloat16)
        pass_on(chunk).start()
    pack_pair(1)
    begin_sum(2)
    pass_sum(1)
    vec_rows = near_ref[:, NEAR:].astype(jnp.float32).T
    gain = vec_rows[0:1]
    vec_acc[...] = jnp.zeros_like(vec_acc)
    for chunk in range(chunks):
        here = at(0, chunk)
        part = backward(at(own0, chunk))
        pass_on(chunk).wait()
        grad = part + part_recv[here, :].astype(jnp.float32)
        normed, rate = norm_parts(tok_ref[here, :].astype(jnp.float32))
        gtok_ref[here, :] = gres_ref[here, :] + norm_grad(grad, gain, normed, rate)
        vec_acc[0:8, :] += fold_rows(grad * normed)
        vec_acc[8:16, :] += fold_rows(grad)
    sums = jnp.sum(bias_acc[...].T, axis=0, keepdims=True)
    own_cols = pl.ds(pl.multiple_of(member * width, width), width)
    vec_mine[...] = jnp.zeros_like(vec_mine)
    vec_mine[0:1, :] = jnp.sum(vec_acc[0:8, :], axis=0, keepdims=True)
    vec_mine[1:2, :] = jnp.sum(vec_acc[8:16, :], axis=0, keepdims=True)
    vec_mine[2:3, own_cols] = sums[:, :width]
    vec_mine[3:4, own_cols] = sums[:, width:]
    vec_mine[4:7, :] = vec_ref[0:3, :]
    vec_copy = to_other(
        vec_mine, vec_other, pair_send.at[chunks + 1], pair_recv.at[chunks + 1]
    )
    vec_copy.start()
    pass_sum(2)
    finish_sum(0)
    gup_ref[...] = far_sum[:, : gup_ref.shape[1]]
    gdown_ref[...] = far_sum[:, gup_ref.shape[1] : 2 * gup_ref.shape[1]]
    gout_ref[...] = far_sum[:, 2 * gup_ref.shape[1] :]
    vec_copy.wait()
    both = vec_mine[...] + vec_other[...]
    vec_cols[...] = both
    begin_share(3)
    finish_share(4)
    gbup_ref[...] = jnp.sum(bup_sum[...], axis=0, keepdims=True)
    for pair in range(2):
        finish_sum(1 + pair)
        for part, ref in enumerate((gq_ref, gk_ref, gv_ref, gp_ref)):
            ref[:, pair * pair_width : (pair + 1) * pair_width] = pack_sums[
                pair, :, part * pair_width : (part + 1) * pair_width
            ]
    finish_share(3)
    spot = lax.rem(me * vec_width, VECS)
    picked = vec_sum[:, :vec_width]
    for start in range(vec_width, VECS, vec_width):
        picked = jnp.where(spot == start, vec_sum[:, start : start + vec_width], picked)
    gvec_ref[...] = picked


def last_call(e, qu, qw, key, va, o, pos, col, gatt, far, near, norm, tok, gres, gfar, vec, bup):
    count = lax.axis_size("dp")
    levels = count // PLANE
    rows, own_rows = norm.shape[0], tok.shape[0]
    chunks = own_rows // CHUNK
    width = qu.shape[0]
    hidden = (far.shape[1] - width) // 2
    shard = D // count
    f32, bf16 = jnp.float32, jnp.bfloat16

    def shape(*dims):
        return jax.ShapeDtypeStruct(dims, f32)

    def room(*dims, kind=f32):
        return pltpu.VMEM(dims, kind)

    return pl.pallas_call(
        functools.partial(last_kernel, count),
        in_specs=[ANY_SPEC] * 5
        + [VMEM_SPEC, ANY_SPEC, ANY_SPEC, VMEM_SPEC]
        + [ANY_SPEC] * 5
        + [VMEM_SPEC] * 3,
        out_specs=[VMEM_SPEC] * 10,
        out_shape=[shape(own_rows, D)]
        + [shape(shard, width)] * 4
        + [shape(shard, hidden)] * 2
        + [shape(shard, width), shape(8, shard), shape(1, 128)],
        scratch_shapes=[
            room(width, rows, kind=bf16),
            room(width, rows, kind=bf16),
            room(width, rows, kind=bf16),
            room(va.shape[0], rows, kind=bf16),
            room(width, D, kind=bf16),
            room(rows, D, kind=bf16),
            room(D, width, kind=bf16),
            room(D, near.shape[1], kind=bf16),
            room(rows, D, kind=bf16),
            room(own_rows, D, kind=bf16),
            room(own_rows, D),
            room(2, TILE, PACK[-1], kind=bf16),
            room(PLANE - 1, levels, shard, far.shape[1], kind=bf16),
            room(levels - 1, shard, far.shape[1], kind=bf16),
            room(levels - 1, shard, far.shape[1], kind=bf16),
            room(2, D, 2 * width, kind=bf16),
            room(2, PLANE - 1, levels, shard, 2 * width, kind=bf16),
            room(2, levels - 1, shard, 2 * width, kind=bf16),
            room(2, levels - 1, shard, 2 * width, kind=bf16),
            room(8, D),
            room(8, D),
            room(8, D),
            room(count - 1, 8, VECS),
            room(8 * count, 128),
            room(count - 1, 8, 128),
            room(va.shape[0], rows, kind=bf16),
            room(width, rows, kind=bf16),
            room(3 * width, rows, kind=bf16),
            room(HEAD, rows),
            room(HEAD, rows),
            room(width, D, kind=bf16),
            room(rows, D, kind=bf16),
            room(rows, VECS, kind=bf16),
            room(HEAD, rows),
            room(2 * width, 128),
            room(D, rows, kind=bf16),
            room(own_rows, D, kind=bf16),
            room(own_rows, D, kind=bf16),
            room(shard, far.shape[1]),
            room(2, shard, 2 * width),
            room(8, VECS),
            room(8, 128),
            room(16, D),
            pltpu.SemaphoreType.DMA((2, count - 1)),
            pltpu.SemaphoreType.DMA((2, count - 1)),
            pltpu.SemaphoreType.DMA((3, PLANE - 1, levels)),
            pltpu.SemaphoreType.DMA((3, PLANE - 1, levels)),
            pltpu.SemaphoreType.DMA((3, levels - 1)),
            pltpu.SemaphoreType.DMA((3, levels - 1)),
            pltpu.SemaphoreType.DMA((chunks + 2,)),
            pltpu.SemaphoreType.DMA((chunks + 2,)),
            pltpu.SemaphoreType.DMA((2,)),
            pltpu.SemaphoreType.DMA((11,)),
        ],
        compiler_params=pltpu.CompilerParams(
            collective_id=2, has_side_effects=True, vmem_limit_bytes=62 * 1024 * 1024
        ),
    )(e, qu, qw, key, va, o, pos, col, gatt, far, near, norm, tok, gres, gfar, vec, bup)


def finish_kernel(number, *refs):
    for source, target in zip(refs[:number], refs[number : 2 * number]):
        target[...] = source[...]
    vec_ref, row_ref = refs[2 * number : 2 * number + 2]
    for place, target in enumerate(refs[2 * number + 2 : -1]):
        target[...] = vec_ref[place : place + 1, :]
    refs[-1][...] = row_ref[...]


def finish_call(mats, vecs, row):
    f32 = jnp.float32
    number = len(mats)
    lines = 7

    def shape(*dims):
        return jax.ShapeDtypeStruct(dims, f32)

    return pl.pallas_call(
        lambda *refs: finish_kernel(
            number, *refs[:number], *refs[number + 2 : 2 * number + 2],
            *refs[number : number + 2], *refs[2 * number + 2 :]
        ),
        in_specs=[VMEM_SPEC] * (number + 2),
        out_specs=[VMEM_SPEC] * (number + lines + 1),
        out_shape=[shape(*m.shape) for m in mats]
        + [shape(1, vecs.shape[1])] * lines
        + [shape(1, row.shape[1])],
    )(*mats, vecs, row)


def local_plain(
    tokens,
    block_ids,
    ln1_gain,
    ln1_bias,
    w_query,
    w_key,
    w_value,
    w_pos,
    bias_u,
    bias_w,
    w_out,
    ln2_gain,
    ln2_bias,
    w_up,
    bias_up,
    w_down,
    bias_down,
    cotangent,
):
    member = lax.axis_index("tensor")
    squares = (w_query, w_key, w_value, w_pos, w_out.T)
    wide = (w_up, w_down.T)
    vectors = (ln1_gain, ln1_bias, bias_u, bias_w, ln2_gain, ln2_bias, bias_down)
    near_mats = [lax.all_gather(m, "dp", axis=0, tiled=True) for m in squares]
    far_mats = [lax.all_gather(m, "dp", axis=0, tiled=True) for m in wide]
    full_vecs = [lax.all_gather(v, "dp", axis=0, tiled=True) for v in vectors]
    up_shift = lax.all_gather(bias_up, "dp", axis=0, tiled=True)
    query_mat, key_mat, value_mat, pos_mat, out_back = near_mats
    out_mat = out_back.T
    up_mat, down_back = far_mats
    down_mat = down_back.T
    gain_one, shift_one, bias_one, bias_two, gain_two, shift_two, down_shift = full_vecs
    gain_one = gain_one.astype(jnp.float32)
    shift_one = shift_one.astype(jnp.float32)
    gain_two = gain_two.astype(jnp.float32)
    shift_two = shift_two.astype(jnp.float32)
    local_width = query_mat.shape[1]
    head_count = local_width // HEAD
    hidden_local = up_mat.shape[1]
    full_hidden = up_shift.shape[0]
    own_u = lax.dynamic_slice_in_dim(
        bias_one.astype(jnp.float32), member * local_width, local_width
    )
    own_w = lax.dynamic_slice_in_dim(
        bias_two.astype(jnp.float32), member * local_width, local_width
    )
    score_scale = 1.0 / math.sqrt(HEAD)
    own_rows = tokens.shape[0]
    inputs = tokens.astype(jnp.float32)
    normed = layer_norm(inputs, gain_one, shift_one)
    rows_all = lax.all_gather(normed.astype(jnp.bfloat16), "tensor", axis=0, tiled=True)
    total_rows = rows_all.shape[0]
    queries_t = project_cols(query_mat, rows_all)
    def heads_of(array):
        return array.astype(jnp.bfloat16).reshape(head_count, HEAD, array.shape[-1])

    ids = block_ids.reshape(1, total_rows)
    sum_u = queries_t + own_u[:, None]
    sum_w = queries_t + own_w[:, None]
    fold = score_scale * LOG2E
    query_u = heads_of(sum_u)
    query_w = heads_of(sum_w)
    key_rows = heads_of(project_cols(key_mat, rows_all))
    ones = jnp.ones((head_count, 2, total_rows), jnp.bfloat16)
    blank = jnp.zeros((head_count, AUG - HEAD - 2, total_rows), jnp.bfloat16)
    value_rows = jnp.concatenate(
        [heads_of(project_cols(value_mat, rows_all)), ones, blank], axis=1
    )
    pos_rows = pos_mat.T.reshape(head_count, HEAD, D)
    table = angle_table()
    row_table = jnp.asarray(table)
    col_table = jnp.asarray(np.ascontiguousarray(table.T))
    weights, mixed_sums = attend_all(
        heads_of(sum_u * fold), heads_of(sum_w * fold), key_rows, value_rows, pos_rows, ids,
        row_table, col_table,
    )
    inv_total = 1.0 / mixed_sums[:, HEAD : HEAD + 1]
    mixed_full = mixed_sums[:, :HEAD] * inv_total
    mixed_cols = mixed_full.reshape(local_width, total_rows).astype(jnp.bfloat16)
    residual = inputs + lax.psum_scatter(
        contract_rows(
            take_cols(mixed_cols, jnp.int32(0), own_rows * lax.axis_size("tensor")), out_mat
        ).astype(jnp.bfloat16),
        "tensor",
        scatter_dimension=0,
        tiled=True,
    ).astype(jnp.float32)
    normed_two = layer_norm(residual, gain_two, shift_two)
    grad_output = cotangent.astype(jnp.float32)
    grad_down_bias = placed(jnp.sum(grad_output, axis=0), D, 0)
    own_up = lax.dynamic_slice_in_dim(
        up_shift.astype(jnp.float32), member * hidden_local, hidden_local
    )
    rows_two = lax.all_gather(normed_two.astype(jnp.bfloat16), "tensor", axis=0, tiled=True)
    hidden = jnp.dot(rows_two, up_mat, preferred_element_type=jnp.float32) + own_up
    active = jax.nn.gelu(hidden).astype(jnp.bfloat16)
    output = (
        residual
        + lax.psum_scatter(
            jnp.dot(
                take_rows(active, jnp.int32(0), own_rows * lax.axis_size("tensor")),
                down_mat,
                preferred_element_type=jnp.float32,
            ).astype(jnp.bfloat16),
            "tensor",
            scatter_dimension=0,
            tiled=True,
        ).astype(jnp.float32)
        + down_shift.astype(jnp.float32)
    )
    grad_full = lax.all_gather(cotangent, "tensor", axis=0, tiled=True)
    grad_active = times_transpose(grad_full, down_mat)
    grad_down = contract_rows(active, grad_full)
    gelu_back = jax.vjp(jax.nn.gelu, hidden)[1]
    grad_hidden = gelu_back(grad_active)[0].astype(jnp.bfloat16)
    grad_up_bias = placed(
        jnp.sum(grad_hidden, axis=0, dtype=jnp.float32), full_hidden, member * hidden_local
    )
    grad_up = contract_rows(rows_two, grad_hidden)
    grad_normed_two = lax.psum_scatter(
        times_transpose(
            take_rows(grad_hidden, jnp.int32(0), own_rows * lax.axis_size("tensor")), up_mat
        ).astype(jnp.bfloat16),
        "tensor",
        scatter_dimension=0,
        tiled=True,
    ).astype(jnp.float32)
    norm_back_two = jax.vjp(layer_norm, residual, gain_two, shift_two)[1]
    grad_resid_part, grad_gain_two, grad_shift_two = norm_back_two(grad_normed_two)
    grad_residual = grad_output + grad_resid_part
    ffn_terms = (grad_gain_two, grad_shift_two, grad_up, grad_up_bias, grad_down, grad_down_bias)
    grad_att = lax.all_gather(grad_residual.astype(jnp.bfloat16), "tensor", axis=0, tiled=True)
    grad_out_mat = jnp.dot(mixed_cols, grad_att, preferred_element_type=jnp.float32)
    grad_mixed = (
        times_transpose(out_mat, grad_att)
        .astype(jnp.bfloat16)
        .reshape(head_count, HEAD, total_rows)
    )
    grad_mixed = grad_mixed.astype(jnp.float32)
    grad_scaled = (grad_mixed * inv_total).astype(jnp.bfloat16)
    grad_low = (grad_mixed * (inv_total * score_scale)).astype(jnp.bfloat16)
    inner = -jnp.sum(grad_low.astype(jnp.float32) * mixed_full, axis=1, keepdims=True)
    inner_high = inner.astype(jnp.bfloat16)
    inner_rest = (inner - inner_high.astype(jnp.float32)).astype(jnp.bfloat16)
    grad_aug = jnp.concatenate([grad_low, inner_high, inner_rest, blank], axis=1)
    dqu, dqw, dk, dv, dpos = attend_back_all(
        weights, query_u, query_w, key_rows, value_rows, pos_rows, grad_aug, grad_scaled, col_table
    )
    grad_keys_all = dk.reshape(local_width, total_rows).astype(jnp.bfloat16)
    grad_values_all = dv.reshape(local_width, total_rows).astype(jnp.bfloat16)
    grad_pos = dpos.reshape(local_width, D).T
    grad_query_u = dqu.reshape(local_width, total_rows)
    grad_query_w = dqw.reshape(local_width, total_rows)
    grad_bias_one = placed(jnp.sum(grad_query_u, axis=1), D, member * local_width)
    grad_bias_two = placed(jnp.sum(grad_query_w, axis=1), D, member * local_width)
    grad_query = (grad_query_u + grad_query_w).astype(jnp.bfloat16)
    grad_query_mat = times_transpose(rows_all.T, grad_query)
    grad_key_mat = times_transpose(rows_all.T, grad_keys_all)
    grad_value_mat = times_transpose(rows_all.T, grad_values_all)
    first_row = jnp.int32(0)
    part_sum = times_transpose(
        take_cols(grad_query, first_row, own_rows * lax.axis_size("tensor")).T, query_mat
    )
    part_sum = part_sum + times_transpose(
        take_cols(grad_keys_all, first_row, own_rows * lax.axis_size("tensor")).T, key_mat
    )
    grad_normed = lax.psum_scatter(
        (
            part_sum
            + times_transpose(
                take_cols(grad_values_all, first_row, own_rows * lax.axis_size("tensor")).T,
                value_mat,
            )
        ).astype(jnp.bfloat16),
        "tensor",
        scatter_dimension=0,
        tiled=True,
    ).astype(jnp.float32)
    norm_back_one = jax.vjp(layer_norm, inputs, gain_one, shift_one)[1]
    grad_in_part, grad_gain_one, grad_shift_one = norm_back_one(grad_normed)
    grad_tokens = grad_residual + grad_in_part
    grad_squares = (grad_query_mat, grad_key_mat, grad_value_mat, grad_pos, grad_out_mat.T)
    grad_wides = (grad_up, grad_down.T)
    grad_vecs = jnp.stack(
        (
            grad_gain_one, grad_shift_one, grad_bias_one, grad_bias_two,
            ffn_terms[0], ffn_terms[1], ffn_terms[5],
        )
    )
    grad_vecs, grad_up_row = lax.psum((grad_vecs, ffn_terms[3]), "tensor")
    def share(array):
        return lax.psum_scatter(array, "dp", scatter_dimension=0, tiled=True)

    squares = [share(m) for m in grad_squares]
    wides = [share(m) for m in grad_wides]
    vecs = [share(v) for v in grad_vecs]
    up_part = share(grad_up_row)
    return (
        output.astype(jnp.bfloat16),
        grad_tokens,
        vecs[0],
        vecs[1],
        squares[0],
        squares[1],
        squares[2],
        squares[3],
        vecs[2],
        vecs[3],
        squares[4].T,
        vecs[4],
        vecs[5],
        wides[0],
        up_part,
        wides[1].T,
        vecs[6],
    )


def local_direct(
    tokens,
    block_ids,
    ln1_gain,
    ln1_bias,
    w_query,
    w_key,
    w_value,
    w_pos,
    bias_u,
    bias_w,
    w_out,
    ln2_gain,
    ln2_bias,
    w_up,
    bias_up,
    w_down,
    bias_down,
    cotangent,
):
    total_rows = block_ids.shape[0]
    vectors = (ln1_gain, ln1_bias, bias_u, bias_w, ln2_gain, ln2_bias, bias_down)
    table = angle_table()
    row_table = jnp.asarray(table)
    col_table = jnp.asarray(np.ascontiguousarray(table.T))
    (
        weights, query_u, query_w, key_rows, value_aug, mixed_sums, mixed_cols, rows_all, pos_back,
        near, far, up_rows, grad_full,
    ) = first_call(
        tokens,
        cotangent,
        (w_query, w_key, w_value, w_pos),
        (w_up, w_down.T, w_out.T),
        [vector.reshape(1, -1) for vector in vectors],
        bias_up.reshape(1, -1),
        block_ids.reshape(1, total_rows),
        row_table,
        col_table,
    )
    out, grad_res, grad_att, grad_far, grad_vec, grad_up_part = middle_call(
        mixed_cols, tokens, grad_full, far, near, up_rows
    )
    (
        grad_tokens, grad_query_mat, grad_key_mat, grad_value_mat, grad_pos, grad_up, grad_down,
        grad_out, grad_vecs, grad_up_row,
    ) = last_call(
        weights, query_u, query_w, key_rows, value_aug, mixed_sums, pos_back, row_table, grad_att,
        far, near, rows_all, tokens, grad_res, grad_far, grad_vec, grad_up_part,
    )
    (
        grad_query_mat, grad_key_mat, grad_value_mat, grad_pos, grad_up, grad_down, grad_out,
        *grad_vecs, grad_up_row,
    ) = finish_call(
        (grad_query_mat, grad_key_mat, grad_value_mat, grad_pos, grad_up, grad_down, grad_out),
        grad_vecs,
        grad_up_row,
    )
    grad_vecs = [vector.reshape(-1) for vector in grad_vecs]
    return (
        out,
        grad_tokens,
        grad_vecs[0],
        grad_vecs[1],
        grad_query_mat,
        grad_key_mat,
        grad_value_mat,
        grad_pos,
        grad_vecs[2],
        grad_vecs[3],
        grad_out.T,
        grad_vecs[4],
        grad_vecs[5],
        grad_up,
        grad_up_row.reshape(-1),
        grad_down.T,
        grad_vecs[6],
    )


def solution(mesh):
    in_specs = (
        P(("dp", "tensor"), None),
        P("dp"),
        P("dp"),
        P("dp"),
        P("dp", "tensor"),
        P("dp", "tensor"),
        P("dp", "tensor"),
        P("dp", "tensor"),
        P("dp"),
        P("dp"),
        P("tensor", "dp"),
        P("dp"),
        P("dp"),
        P("dp", "tensor"),
        P("dp"),
        P("tensor", "dp"),
        P("dp"),
        P(("dp", "tensor"), None),
    )
    out_specs = (
        P(("dp", "tensor"), None),
        P(("dp", "tensor"), None),
        P("dp"),
        P("dp"),
        P("dp", "tensor"),
        P("dp", "tensor"),
        P("dp", "tensor"),
        P("dp", "tensor"),
        P("dp"),
        P("dp"),
        P("tensor", "dp"),
        P("dp"),
        P("dp"),
        P("dp", "tensor"),
        P("dp"),
        P("tensor", "dp"),
        P("dp"),
    )
    pieces = D // mesh.shape["dp"]
    whole_tiles = (
        pieces % 16 == 0 and mesh.shape["tensor"] == 2 and mesh.shape["dp"] % (2 * PLANE) == 0
    )
    local = local_direct if whole_tiles else local_plain
    return jax.shard_map(local, mesh=mesh, in_specs=in_specs, out_specs=out_specs, check_vma=False)
```

```python
import functools
import math

import jax
import jax.numpy as jnp
import ml_dtypes
import numpy as np
from jax import lax
from jax.experimental import pallas as pl
from jax.experimental.pallas import tpu as pltpu
from jax.sharding import PartitionSpec as P

D = 512
HEAD = 64
L = 2048


MESH = pl.DeviceIdType.MESH
VECS = 128


def peer_at(offset):
    count = lax.axis_size("dp")
    return lax.rem(lax.axis_index("dp") + offset, count)


PLANE = 4


def place_of(me, count):
    return lax.div(me, PLANE), lax.rem(me, PLANE), count // PLANE


def along(me, count, offset):
    level, spot, levels = place_of(me, count)
    return lax.rem(level + offset, levels) * PLANE + spot


def across(me, count, offset):
    level, spot, _ = place_of(me, count)
    return level * PLANE + lax.rem(spot + offset, PLANE)


def remote(source, target, send_sem, recv_sem, device):
    return pltpu.make_async_remote_copy(
        src_ref=source,
        dst_ref=target,
        send_sem=send_sem,
        recv_sem=recv_sem,
        device_id={"dp": device},
        device_id_type=MESH,
    )


def greet_all(count, with_pair=False):
    barrier = pltpu.get_barrier_semaphore()

    def greet(offset, carry):
        pl.semaphore_signal(
            barrier, inc=1, device_id={"dp": peer_at(offset)}, device_id_type=MESH
        )
        return carry

    lax.fori_loop(1, count, greet, 0)
    if with_pair:
        pl.semaphore_signal(
            barrier, inc=1, device_id={"tensor": 1 - lax.axis_index("tensor")}, device_id_type=MESH
        )
    pl.semaphore_wait(barrier, count if with_pair else count - 1)


def layer_norm(values, gain_vec, shift_vec):
    center = values - jnp.mean(values, axis=-1, keepdims=True)
    spread = jnp.mean(center * center, axis=-1, keepdims=True)
    return center * lax.rsqrt(spread + 1e-05) * gain_vec + shift_vec


def take_rows(array, first_row, row_count):
    return lax.dynamic_slice_in_dim(array, first_row, row_count, 0)


def take_cols(array, first_col, col_count):
    return lax.dynamic_slice_in_dim(array, first_col, col_count, array.ndim - 1)


def contract_rows(left, right):
    return lax.dot_general(
        left, right, (((0,), (0,)), ((), ())), preferred_element_type=jnp.float32
    )


def times_transpose(left, right):
    return lax.dot_general(
        left, right, (((1,), (1,)), ((), ())), preferred_element_type=jnp.float32
    )


def project_cols(weight, row_data):
    return lax.dot_general(
        weight, row_data, (((0,), (1,)), ((), ())), preferred_element_type=jnp.float32
    )


TILE = 256
TILES = L // TILE
AUG = HEAD + 16
LOG2E = 1.4426950408889634


def tiles_seen(tile):
    return min(tile + 2, TILES)


PACK = [TILE * sum(tiles_seen(t) for t in range(tile)) for tile in range(TILES + 1)]


def angle_table():
    freqs = np.exp(np.arange(0, D, 2, dtype=np.float64) * (-math.log(10000.0) / D))
    angles = np.arange(L, dtype=np.float64)[:, None] * freqs[None, :]
    return np.concatenate([np.cos(angles), np.sin(angles)], axis=1).astype(ml_dtypes.bfloat16)


def dot_nn(left, right):
    return jnp.dot(left, right, preferred_element_type=jnp.float32)


def attend_kernel(qu_ref, qw_ref, key_ref, value_ref, pos_ref, ids_ref, row_ref, col_ref, e_ref, o_ref):
    half = D // 2
    for tile in range(TILES):
        rows = slice(tile * TILE, (tile + 1) * TILE)
        width = tiles_seen(tile) * TILE
        both = contract_rows(qw_ref[:, rows], pos_ref[...])
        part_a, part_b = both[:, :half], both[:, half:]
        cos_i = row_ref[rows, :half].astype(jnp.float32)
        sin_i = row_ref[rows, half:].astype(jnp.float32)
        turned = jnp.concatenate(
            [part_a * sin_i + part_b * cos_i, part_b * sin_i - part_a * cos_i], axis=1
        ).astype(jnp.bfloat16)
        scores = dot_nn(turned, col_ref[:, :width]) + contract_rows(
            qu_ref[:, rows], key_ref[:, :width]
        )
        ids_row = ids_ref[:, tile * TILE : width]
        ids_col = jnp.broadcast_to(ids_row[:, :TILE], (8, TILE)).T[:, :1]
        edge = jnp.where(ids_row <= ids_col, scores[:, tile * TILE :], -1e30)
        if tile:
            scores = jnp.concatenate([scores[:, : tile * TILE], edge], axis=1)
        else:
            scores = edge
        peak = jnp.max(scores, axis=1, keepdims=True)
        weights = jnp.exp2(scores - peak).astype(jnp.bfloat16)
        e_ref[:, PACK[tile] : PACK[tile + 1]] = weights
        o_ref[:, rows] = times_transpose(value_ref[:, :width], weights)


def attend_back_kernel(
    e_ref, qu_ref, qw_ref, key_ref, value_ref, pos_ref, aug_ref, scaled_ref, col_ref,
    dqu_ref, dqw_ref, dk_ref, dv_ref, dpos_ref,
):
    half = D // 2
    dk_ref[...] = jnp.zeros_like(dk_ref)
    dv_ref[...] = jnp.zeros_like(dv_ref)
    for tile in range(TILES):
        rows = slice(tile * TILE, (tile + 1) * TILE)
        width = tiles_seen(tile) * TILE
        weights = e_ref[:, PACK[tile] : PACK[tile + 1]]
        grad_probs = contract_rows(aug_ref[:, rows], value_ref[:, :width])
        grad_scores = (weights.astype(jnp.float32) * grad_probs).astype(jnp.bfloat16)
        dv_ref[:, :width] += dot_nn(scaled_ref[:, rows], weights)
        dk_ref[:, :width] += dot_nn(qu_ref[:, rows], grad_scores)
        dqu_ref[:, rows] = times_transpose(key_ref[:, :width], grad_scores)
        turned = times_transpose(col_ref[:, :width], grad_scores)
        part_c, part_s = turned[:half], turned[half:]
        cos_i = col_ref[:half, rows].astype(jnp.float32)
        sin_i = col_ref[half:, rows].astype(jnp.float32)
        both = jnp.concatenate(
            [part_c * sin_i - part_s * cos_i, part_c * cos_i + part_s * sin_i], axis=0
        ).astype(jnp.bfloat16)
        dqw_ref[:, rows] = dot_nn(pos_ref[...], both)
        here = times_transpose(qw_ref[:, rows], both)
        if tile:
            dpos_ref[...] += here
        else:
            dpos_ref[...] = here


def per_head(rows, cols):
    return pl.BlockSpec((None, rows, cols), lambda h: (h, 0, 0))


def shared(rows, cols):
    return pl.BlockSpec((rows, cols), lambda h: (0, 0))


def attend_all(qu, qw, keys, values, pos, ids, row_table, col_table):
    heads = qu.shape[0]
    f32, bf16 = jnp.float32, jnp.bfloat16
    return pl.pallas_call(
        attend_kernel,
        grid=(heads,),
        in_specs=[per_head(HEAD, L)] * 3
        + [per_head(AUG, L), per_head(HEAD, D), shared(1, L), shared(L, D), shared(D, L)],
        out_specs=[per_head(TILE, PACK[-1]), per_head(AUG, L)],
        out_shape=[
            jax.ShapeDtypeStruct((heads, TILE, PACK[-1]), bf16),
            jax.ShapeDtypeStruct((heads, AUG, L), f32),
        ],
        compiler_params=pltpu.CompilerParams(vmem_limit_bytes=56 * 1024 * 1024),
    )(qu, qw, keys, values, pos, ids, row_table, col_table)


def attend_back_all(weights, qu, qw, keys, values, pos, aug, scaled, col_table):
    heads = qu.shape[0]
    f32 = jnp.float32
    return pl.pallas_call(
        attend_back_kernel,
        grid=(heads,),
        in_specs=[per_head(TILE, PACK[-1])]
        + [per_head(HEAD, L)] * 3
        + [per_head(AUG, L), per_head(HEAD, D), per_head(AUG, L), per_head(HEAD, L), shared(D, L)],
        out_specs=[per_head(HEAD, L)] * 4 + [per_head(HEAD, D)],
        out_shape=[jax.ShapeDtypeStruct((heads, HEAD, L), f32)] * 4
        + [jax.ShapeDtypeStruct((heads, HEAD, D), f32)],
        compiler_params=pltpu.CompilerParams(vmem_limit_bytes=56 * 1024 * 1024),
    )(weights, qu, qw, keys, values, pos, aug, scaled, col_table)


def placed(part_vec, length, offset):
    return lax.dynamic_update_slice_in_dim(jnp.zeros((length,), jnp.float32), part_vec, offset, 0)


NEAR = 4 * 256


def first_kernel(
    count, tok_ref, cot_ref, wq_ref, wk_ref, wv_ref, wp_ref, wu_ref, wd_ref, wo_ref, *refs
):
    vec_refs, bup_ref, ids_ref, row_in, col_in = refs[:7], refs[7], refs[8], refs[9], refs[10]
    (
        e_ref, qu_out, qw_out, key_out, va_out, o_out, mix_out, norm_out, pos_out,
        near_out, far_out, up_all, cot_out,
        qu_ref, qw_ref, key_ref, va_ref, o_ref, mix_ref, norm_ref, pos_ref, first_all, second_all,
        far_all, cot_all, row_ref, col_ref,
        first_ref, second_ref, far_ref, up_ref, vec_ref, tok_all, quf_ref, qwf_ref, turn_ref,
        rq_ref, vrow_ref, e_buf,
        along_send, along_recv, across_send, across_recv, own_sems, pair_send, pair_recv, e_sems,
        load_sems, store_sems, head_sems,
    ) = refs[11:]
    half = D // 2
    me, member = lax.axis_index("dp"), lax.axis_index("tensor")
    levels = count // PLANE
    pair = {"tensor": 1 - member}
    own_rows = tok_ref.shape[0]
    own = pl.ds(pl.multiple_of(member * own_rows, own_rows), own_rows)
    parts = (first_ref, second_ref, far_ref, up_ref)
    wholes = (first_all, second_all, far_all, up_all)

    def rows_of(index, device):
        rows = parts[index].shape[0]
        return wholes[index].at[pl.ds(pl.multiple_of(device * rows, rows), rows)]

    def go_along(index, offset):
        return remote(
            parts[index], rows_of(index, me),
            along_send.at[index, offset - 1], along_recv.at[index, offset - 1],
            along(me, count, offset),
        )

    def go_across(index, offset, step):
        owner = along(me, count, levels - step)
        return remote(
            parts[index] if step == 0 else rows_of(index, owner), rows_of(index, owner),
            across_send.at[index, offset - 1, step], across_recv.at[index, offset - 1, step],
            across(me, count, offset),
        )

    def own_copy(index):
        return pltpu.make_async_copy(parts[index], rows_of(index, me), own_sems.at[index])

    def begin_along(index):
        for offset in range(1, levels):
            go_along(index, offset).start()

    def begin_across(index):
        for offset in range(1, PLANE):
            go_across(index, offset, 0).start()
        own_copy(index).start()

    def forward(index):
        for step in range(1, levels):
            go_along(index, step).wait()
            for offset in range(1, PLANE):
                go_across(index, offset, step).start()

    def finish_gather(index):
        for step in range(levels):
            for offset in range(1, PLANE):
                go_across(index, offset, step).wait()
        own_copy(index).wait()

    width = wq_ref.shape[1]
    hidden = wu_ref.shape[1]
    shard = wq_ref.shape[0]
    vec_ref[...] = jnp.zeros_like(vec_ref)
    for place, ref in enumerate(vec_refs):
        vec_ref[place : place + 1, :shard] = ref[...].astype(jnp.float32)
    pair_width = width // 2
    first_ref[:, 4 * pair_width :] = vec_ref[...].T[:shard].astype(jnp.bfloat16)
    for place, ref in enumerate((wq_ref, wk_ref, wv_ref, wp_ref)):
        cols = slice(place * pair_width, (place + 1) * pair_width)
        first_ref[:, cols] = ref[:, :pair_width]
        second_ref[:, cols] = ref[:, pair_width:]
    far_ref[:, :hidden] = wu_ref[...]
    far_ref[:, hidden : 2 * hidden] = wd_ref[...]
    far_ref[:, 2 * hidden :] = wo_ref[...]
    up_ref[...] = jnp.broadcast_to(bup_ref[...].astype(jnp.float32), up_ref.shape).astype(
        jnp.bfloat16
    )

    def to_pair(source, target, slot):
        return pltpu.make_async_remote_copy(
            src_ref=source,
            dst_ref=target.at[own],
            send_sem=pair_send.at[slot],
            recv_sem=pair_recv.at[slot],
            device_id=pair,
            device_id_type=MESH,
        )

    tables = (
        pltpu.make_async_copy(row_in, row_ref, load_sems.at[0]),
        pltpu.make_async_copy(col_in, col_ref, load_sems.at[1]),
    )
    for load in tables:
        load.start()
    greet_all(count, True)
    begin_along(0)
    begin_across(0)
    begin_along(3)
    begin_across(3)
    exchanges = (to_pair(tok_ref, tok_all, 0), to_pair(cot_ref, cot_all, 1))
    keeps = (
        pltpu.make_async_copy(tok_ref, tok_all.at[own], own_sems.at[4]),
        pltpu.make_async_copy(cot_ref, cot_all.at[own], own_sems.at[5]),
    )
    for copy in exchanges + keeps:
        copy.start()
    forward(0)
    begin_along(1)
    begin_across(1)
    begin_along(2)
    forward(3)
    finish_gather(0)
    exchanges[0].wait()
    keeps[0].wait()

    vec_block = first_all[:, 4 * pair_width :].astype(jnp.float32)
    vec_rows = vec_block.T
    gain, shift = vec_rows[0:1], vec_rows[1:2]
    heads = width // HEAD
    own_cols = pl.ds(pl.multiple_of(member * width, width), width)
    vec_cols = first_all[own_cols, 4 * pair_width :].astype(jnp.float32)
    bias_u, bias_w = vec_cols[:, 2:3], vec_cols[:, 3:4]
    fold = LOG2E / math.sqrt(HEAD)
    place = lax.broadcasted_iota(jnp.int32, (AUG - HEAD, TILE), 0)
    marks = jnp.where(place < 2, 1.0, 0.0).astype(jnp.bfloat16)
    for tile in range(TILES):
        rows = slice(tile * TILE, (tile + 1) * TILE)
        normed = layer_norm(tok_all[rows, :].astype(jnp.float32), gain, shift)
        norm_ref[rows, :] = normed.astype(jnp.bfloat16)

    def project(pair_index):
        source = wholes[pair_index]
        lines = slice(pair_index * pair_width, (pair_index + 1) * pair_width)
        turn_ref[...] = source[:, : 3 * pair_width].T
        pos_ref[lines, :] = source[:, 3 * pair_width : 4 * pair_width].T
        for tile in range(TILES):
            rows = slice(tile * TILE, (tile + 1) * TILE)
            projected = times_transpose(turn_ref[...], norm_ref[rows, :])
            sum_u = projected[:pair_width] + bias_u[lines]
            sum_w = projected[:pair_width] + bias_w[lines]
            qu_ref[lines, rows] = sum_u.astype(jnp.bfloat16)
            qw_ref[lines, rows] = sum_w.astype(jnp.bfloat16)
            quf_ref[lines, rows] = (sum_u * fold).astype(jnp.bfloat16)
            qwf_ref[lines, rows] = (sum_w * fold).astype(jnp.bfloat16)
            key_ref[lines, rows] = projected[pair_width : 2 * pair_width].astype(jnp.bfloat16)
            for place in range(pair_width // HEAD):
                start = 2 * pair_width + place * HEAD
                base = (pair_index * (pair_width // HEAD) + place) * AUG
                values = projected[start : start + HEAD].astype(jnp.bfloat16)
                va_ref[base : base + HEAD, rows] = values
                va_ref[base + HEAD : base + AUG, rows] = marks

    project(0)
    forward(1)
    begin_across(2)
    for load in tables:
        load.wait()
    cols = [pl.ds(part * width, pair_width) for part in range(4)]
    more_cols = [pl.ds(part * width + pair_width, pair_width) for part in range(4)]
    here_cols = [pl.ds(part * pair_width, pair_width) for part in range(4)]
    moves = [(first_all.at[:, here_cols[part]], near_out.at[:, cols[part]]) for part in range(4)]
    moves.append(
        (first_all.at[:, pl.ds(4 * pair_width, VECS)], near_out.at[:, pl.ds(NEAR, VECS)])
    )
    moves.append((norm_ref, norm_out))
    early = len(moves)
    moves += [
        (second_all.at[:, here_cols[part]], near_out.at[:, more_cols[part]]) for part in range(4)
    ]
    moves += [
        (qu_ref, qu_out), (qw_ref, qw_out), (key_ref, key_out), (va_ref, va_out),
        (pos_ref, pos_out), (cot_all, cot_out),
    ]
    stores = [
        pltpu.make_async_copy(source, target, store_sems.at[place])
        for place, (source, target) in enumerate(moves)
    ]
    for store in stores[:early]:
        store.start()

    def head_copies(head):
        lines = pl.ds(pl.multiple_of(head * HEAD, HEAD), HEAD)
        more = pl.ds(pl.multiple_of(head * AUG, 16), AUG)
        return (
            pltpu.make_async_copy(o_ref.at[more], o_out.at[more], head_sems.at[0, head]),
            pltpu.make_async_copy(mix_ref.at[lines], mix_out.at[lines], head_sems.at[1, head]),
        )

    def e_copy(head, slot):
        return pltpu.make_async_copy(e_buf.at[slot], e_ref.at[head], e_sems.at[slot])

    def one_head(head, carry):
        slot = lax.rem(head, 2)
        lines = pl.ds(pl.multiple_of(head * HEAD, HEAD), HEAD)
        more = pl.ds(pl.multiple_of(head * AUG, 16), AUG)
        upper = pl.ds(pl.multiple_of(head * AUG, 16), HEAD)
        lower = pl.ds(pl.multiple_of(head * AUG + HEAD, 16), AUG - HEAD)

        @pl.when(head >= 2)
        def _():
            e_copy(head - 2, slot).wait()

        filler = jnp.zeros((VECS - AUG, va_ref.shape[1]), jnp.bfloat16)
        vrow_ref[...] = jnp.concatenate([va_ref[more, :], filler], axis=0).T
        for tile in range(TILES):
            rows = slice(tile * TILE, (tile + 1) * TILE)
            both = contract_rows(qwf_ref[lines, rows], pos_ref[lines, :])
            part_a, part_b = both[:, :half], both[:, half:]
            cos_i = row_ref[rows, :half].astype(jnp.float32)
            sin_i = row_ref[rows, half:].astype(jnp.float32)
            rq_ref[rows, :half] = (part_a * sin_i + part_b * cos_i).astype(jnp.bfloat16)
            rq_ref[rows, half:] = (part_b * sin_i - part_a * cos_i).astype(jnp.bfloat16)

        def scores_of(tile):
            rows = slice(tile * TILE, (tile + 1) * TILE)
            seen = tiles_seen(tile) * TILE
            scores = dot_nn(rq_ref[rows, :], col_ref[:, :seen]) + contract_rows(
                quf_ref[lines, rows], key_ref[lines, :seen]
            )
            ids_row = ids_ref[:, tile * TILE : seen]
            ids_col = jnp.broadcast_to(ids_row[:, :TILE], (8, TILE)).T[:, :1]
            edge = jnp.where(ids_row <= ids_col, scores[:, tile * TILE :], -1e30)
            if tile:
                return jnp.concatenate([scores[:, : tile * TILE], edge], axis=1)
            return edge

        def use_scores(tile, scores):
            rows = slice(tile * TILE, (tile + 1) * TILE)
            seen = tiles_seen(tile) * TILE
            peak = jnp.max(scores, axis=1, keepdims=True)
            weights = jnp.exp2(scores - peak).astype(jnp.bfloat16)
            e_buf[slot, :, PACK[tile] : PACK[tile + 1]] = weights
            sums = dot_nn(weights, vrow_ref[:seen, :]).T
            inverse = 1.0 / sums[HEAD : HEAD + 1]
            mixed = sums[:HEAD] * inverse
            o_ref[upper, rows] = mixed
            o_ref[lower, rows] = jnp.broadcast_to(inverse, (AUG - HEAD, TILE))
            mix_ref[lines, rows] = mixed.astype(jnp.bfloat16)

        scores = scores_of(0)
        for tile in range(TILES):
            following = scores_of(tile + 1) if tile + 1 < TILES else None
            use_scores(tile, scores)
            scores = following
        e_copy(head, slot).start()
        for copy in head_copies(head):
            copy.start()

        @pl.when(head == 0)
        def _():
            forward(2)

        @pl.when(head == heads // 2 - 1)
        def _():
            finish_gather(1)
            project(1)
            exchanges[1].wait()
            keeps[1].wait()
            for store in stores[early:]:
                store.start()

        return carry

    lax.fori_loop(0, heads, one_head, 0)
    for head in range(max(heads - 2, 0), heads):
        e_copy(head, head % 2).wait()
    finish_gather(3)
    finish_gather(2)
    far_store = pltpu.make_async_copy(far_all, far_out, load_sems.at[2])
    far_store.start()
    for store in stores:
        store.wait()
    for head in range(heads):
        for copy in head_copies(head):
            copy.wait()
    far_store.wait()


VMEM_SPEC = pl.BlockSpec(memory_space=pltpu.VMEM)
ANY_SPEC = pl.BlockSpec(memory_space=pl.ANY)


def first_call(tokens, cotangent, squares, wides, vectors, bup, ids, row_table, col_table):
    count = lax.axis_size("dp")
    levels = count // PLANE
    rows = ids.shape[1]
    shard, width = squares[0].shape
    hidden = wides[0].shape[1]
    heads = width // HEAD
    far_width = 2 * hidden + width
    f32, bf16 = jnp.float32, jnp.bfloat16

    def shape(*dims, kind=bf16):
        return jax.ShapeDtypeStruct(dims, kind)

    return pl.pallas_call(
        functools.partial(first_kernel, count),
        in_specs=[VMEM_SPEC] * 18 + [ANY_SPEC] * 2,
        out_specs=[ANY_SPEC] * 11 + [VMEM_SPEC, ANY_SPEC],
        out_shape=[
            shape(heads, TILE, PACK[-1]),
            shape(width, rows),
            shape(width, rows),
            shape(width, rows),
            shape(heads * AUG, rows),
            shape(heads * AUG, rows, kind=f32),
            shape(width, rows),
            shape(rows, D),
            shape(width, D),
            shape(D, NEAR + VECS),
            shape(D, far_width),
            shape(16 * count, bup.shape[1]),
            shape(rows, D),
        ],
        scratch_shapes=[
            pltpu.VMEM((width, rows), bf16),
            pltpu.VMEM((width, rows), bf16),
            pltpu.VMEM((width, rows), bf16),
            pltpu.VMEM((heads * AUG, rows), bf16),
            pltpu.VMEM((heads * AUG, rows), f32),
            pltpu.VMEM((width, rows), bf16),
            pltpu.VMEM((rows, D), bf16),
            pltpu.VMEM((width, D), bf16),
            pltpu.VMEM((D, NEAR // 2 + VECS), bf16),
            pltpu.VMEM((D, NEAR // 2), bf16),
            pltpu.VMEM((D, far_width), bf16),
            pltpu.VMEM((rows, D), bf16),
            pltpu.VMEM((rows, D), bf16),
            pltpu.VMEM((D, rows), bf16),
            pltpu.VMEM((shard, NEAR // 2 + VECS), bf16),
            pltpu.VMEM((shard, NEAR // 2), bf16),
            pltpu.VMEM((shard, far_width), bf16),
            pltpu.VMEM((16, bup.shape[1]), bf16),
            pltpu.VMEM((VECS, VECS), f32),
            pltpu.VMEM((rows, D), bf16),
            pltpu.VMEM((width, rows), bf16),
            pltpu.VMEM((width, rows), bf16),
            pltpu.VMEM((3 * width // 2, D), bf16),
            pltpu.VMEM((rows, D), bf16),
            pltpu.VMEM((rows, VECS), bf16),
            pltpu.VMEM((2, TILE, PACK[-1]), bf16),
            pltpu.SemaphoreType.DMA((4, levels - 1)),
            pltpu.SemaphoreType.DMA((4, levels - 1)),
            pltpu.SemaphoreType.DMA((4, PLANE - 1, levels)),
            pltpu.SemaphoreType.DMA((4, PLANE - 1, levels)),
            pltpu.SemaphoreType.DMA((6,)),
            pltpu.SemaphoreType.DMA((2,)),
            pltpu.SemaphoreType.DMA((2,)),
            pltpu.SemaphoreType.DMA((2,)),
            pltpu.SemaphoreType.DMA((3,)),
            pltpu.SemaphoreType.DMA((16,)),
            pltpu.SemaphoreType.DMA((2, heads)),
        ],
        compiler_params=pltpu.CompilerParams(
            collective_id=0, has_side_effects=True, vmem_limit_bytes=60 * 1024 * 1024
        ),
    )(tokens, cotangent, *squares, *wides, *vectors, bup, ids, row_table, col_table)


CHUNK = 256
GELU_SCALE = math.sqrt(2.0 / math.pi)


def fold_rows(values):
    return jnp.sum(values.reshape(values.shape[0] // 8, 8, values.shape[1]), axis=0)


def fold_cols(values):
    total = values[:, :128]
    for start in range(128, values.shape[1], 128):
        total = total + values[:, start : start + 128]
    return total


def norm_parts(values):
    center = values - jnp.mean(values, axis=-1, keepdims=True)
    spread = jnp.mean(center * center, axis=-1, keepdims=True)
    rate = lax.rsqrt(spread + 1e-05)
    return center * rate, rate


def norm_grad(grad, gain, normed, rate):
    scaled = grad * gain
    mean = jnp.mean(scaled, axis=-1, keepdims=True)
    along = jnp.mean(scaled * normed, axis=-1, keepdims=True)
    return rate * (scaled - mean - normed * along)


def to_other(source, target, send_sem, recv_sem):
    return pltpu.make_async_remote_copy(
        src_ref=source,
        dst_ref=target,
        send_sem=send_sem,
        recv_sem=recv_sem,
        device_id={"tensor": 1 - lax.axis_index("tensor")},
        device_id_type=MESH,
    )


def dot_tt(left, right):
    return lax.dot_general(
        left, right, (((0,), (1,)), ((), ())), preferred_element_type=jnp.float32
    )


def middle_kernel(
    mix_in, tok_in, cot_in, far_in, near_in, up_ref,
    out_out, gres_out, gatt_out, gfar_out, vec_out, bup_out,
    mix_ref, tok_ref, cot_ref, far_ref, vec_ref, out_ref, gres_ref, gatt_ref, gfar_ref,
    send_a, recv_a, res_ref, n2_ref, n2t_ref, cott_ref, act_ref, gh_ref,
    osend, orecv, oacc, gacc, bup_acc, vec_acc, send_sems, recv_sems, load_sems, store_sems,
):
    member = lax.axis_index("tensor")
    own_rows = tok_ref.shape[0]
    chunks = own_rows // CHUNK
    own0 = pl.multiple_of(member * own_rows, own_rows)
    oth0 = pl.multiple_of((1 - member) * own_rows, own_rows)
    hidden = act_ref.shape[1]
    up_cols, down_cols = slice(0, hidden), slice(hidden, 2 * hidden)
    out_cols = slice(2 * hidden, far_ref.shape[1])
    pieces = (pl.ds(2 * hidden, mix_ref.shape[0]), pl.ds(0, hidden), pl.ds(hidden, hidden))
    moves = (
        (mix_in, mix_ref),
        (far_in.at[:, pieces[0]], far_ref.at[:, pieces[0]]),
        (tok_in, tok_ref),
        (near_in.at[:, pl.ds(NEAR, VECS)], vec_ref),
        (far_in.at[:, pieces[1]], far_ref.at[:, pieces[1]]),
        (cot_in, cot_ref),
        (far_in.at[:, pieces[2]], far_ref.at[:, pieces[2]]),
    )
    loads = [
        pltpu.make_async_copy(source, target, load_sems.at[place])
        for place, (source, target) in enumerate(moves)
    ]
    for load in loads:
        load.start()

    def store(place, source, target):
        return pltpu.make_async_copy(source, target, store_sems.at[place])

    def store_own(chunk):
        here, whole = at(0, chunk), at(own0, chunk)
        return (
            store(chunk, out_ref.at[here], out_out.at[here]),
            store(chunks + chunk, gres_ref.at[here], gres_out.at[here]),
            store(2 * chunks + chunk, gatt_ref.at[whole], gatt_out.at[whole]),
        )

    def store_other(chunk):
        whole = at(oth0, chunk)
        return store(3 * chunks + chunk, gatt_ref.at[whole], gatt_out.at[whole])

    def store_far(place):
        return store(
            4 * chunks + place, gfar_ref.at[:, pieces[place]], gfar_out.at[:, pieces[place]]
        )

    def at(base, chunk):
        return pl.ds(pl.multiple_of(base + chunk * CHUNK, CHUNK), CHUNK)

    barrier = pltpu.get_barrier_semaphore()
    pl.semaphore_signal(barrier, inc=1, device_id={"tensor": 1 - member}, device_id_type=MESH)
    pl.semaphore_wait(barrier, 1)

    def pass_on(stage, chunk):
        here = at(0, chunk)
        pairs = (
            (send_a.at[here], recv_a.at[here]),
            (n2_ref.at[at(own0, chunk)], n2_ref.at[at(own0, chunk)]),
            (osend.at[0, here], orecv.at[0, here]),
            (osend.at[1, here], orecv.at[1, here]),
            (gatt_ref.at[at(own0, chunk)], gatt_ref.at[at(own0, chunk)]),
        )
        source, target = pairs[stage]
        return to_other(
            source, target, send_sems.at[stage, chunk], recv_sems.at[stage, chunk]
        )

    ups = hidden // 128
    up_block = up_ref[pl.ds(pl.multiple_of(member * ups * 16, 16), ups * 16), :].astype(jnp.float32)
    up_shift = jnp.concatenate([up_block[16 * k : 16 * k + 1] for k in range(ups)], axis=1)

    def branch(rows):
        return dot_tt(mix_ref[:, rows], far_ref[:, out_cols])

    for load in loads[:2]:
        load.wait()
    for chunk in range(chunks):
        send_a[at(0, chunk), :] = branch(at(oth0, chunk)).astype(jnp.bfloat16)
        pass_on(0, chunk).start()
    for load in loads[2:4]:
        load.wait()
    vec_rows = vec_ref[...].astype(jnp.float32).T
    gain, shift, down_shift = vec_rows[4:5], vec_rows[5:6], vec_rows[6:7]
    for chunk in range(chunks):
        here = at(0, chunk)
        part = branch(at(own0, chunk))
        pass_on(0, chunk).wait()
        residual = tok_ref[here, :].astype(jnp.float32) + part + recv_a[here, :].astype(jnp.float32)
        res_ref[here, :] = residual
        n2_ref[at(own0, chunk), :] = (norm_parts(residual)[0] * gain + shift).astype(jnp.bfloat16)
        pass_on(1, chunk).start()

    bup_acc[...] = jnp.zeros_like(bup_acc)
    vec_acc[...] = jnp.zeros_like(vec_acc)

    for load in loads[4:]:
        load.wait()

    def products(mine, chunk):
        if not mine:
            pass_on(1, chunk).wait()
        rows = at(own0 if mine else oth0, chunk)
        return (
            dot_nn(n2_ref[rows, :], far_ref[:, up_cols]) + up_shift,
            dot_nn(cot_ref[rows, :], far_ref[:, down_cols]),
        )

    def use_products(mine, chunk, value, grad_active):
        rows, here = at(own0 if mine else oth0, chunk), at(0, chunk)
        square = value * value
        bend = jnp.tanh(value * (GELU_SCALE + GELU_SCALE * 0.044715 * square))
        half = 0.5 + 0.5 * bend
        active = (value * half).astype(jnp.bfloat16)
        steep = value * (2.0 * GELU_SCALE + 6.0 * GELU_SCALE * 0.044715 * square)
        slope = half + half * (1.0 - half) * steep
        grad_hidden = (grad_active * slope).astype(jnp.bfloat16)
        act_ref[rows, :] = active
        gh_ref[rows, :] = grad_hidden
        n2t_ref[:, rows] = n2_ref[rows, :].T
        cott_ref[:, rows] = cot_ref[rows, :].T
        bup_acc[...] += fold_rows(grad_hidden.astype(jnp.float32))
        out_part = times_transpose(active, far_ref[:, down_cols])
        grad_part = times_transpose(grad_hidden, far_ref[:, up_cols])
        if mine:
            oacc[here, :] = out_part
            gacc[here, :] = grad_part
        else:
            osend[0, here, :] = out_part.astype(jnp.bfloat16)
            osend[1, here, :] = grad_part.astype(jnp.bfloat16)
            pass_on(2, chunk).start()
            pass_on(3, chunk).start()

    lead = chunks // 2
    order = [(True, c) for c in range(lead)] + [(False, c) for c in range(chunks)]
    order += [(True, c) for c in range(lead, chunks)]
    current = products(*order[0])
    for place, tile in enumerate(order):
        following = products(*order[place + 1]) if place + 1 < len(order) else None
        use_products(*tile, *current)
        current = following

    def close(chunk, carry):
        here = at(0, chunk)
        pass_on(2, chunk).wait()
        pass_on(3, chunk).wait()
        residual = res_ref[here, :]
        out = residual + oacc[here, :] + orecv[0, here, :].astype(jnp.float32) + down_shift
        out_ref[here, :] = out.astype(jnp.bfloat16)
        grad = gacc[here, :] + orecv[1, here, :].astype(jnp.float32)
        normed, rate = norm_parts(residual)
        top = cot_ref[at(own0, chunk), :].astype(jnp.float32)
        grad_res = top + norm_grad(grad, gain, normed, rate)
        gres_ref[here, :] = grad_res
        gatt_ref[at(own0, chunk), :] = grad_res.astype(jnp.bfloat16)
        pass_on(4, chunk).start()
        for copy in store_own(chunk):
            copy.start()
        vec_acc[0:8, :] += fold_rows(grad * normed)
        vec_acc[8:16, :] += fold_rows(grad)
        vec_acc[16:24, :] += fold_rows(top)
        return carry

    lax.fori_loop(0, chunks, close, 0)
    for part in range(hidden // CHUNK):
        cols = slice(part * CHUNK, (part + 1) * CHUNK)
        gfar_ref[:, cols] = dot_nn(n2t_ref[...], gh_ref[:, cols]).astype(jnp.bfloat16)
    store_far(1).start()
    for part in range(hidden // CHUNK):
        cols = slice(part * CHUNK, (part + 1) * CHUNK)
        gfar_ref[:, hidden + part * CHUNK : hidden + (part + 1) * CHUNK] = dot_nn(
            cott_ref[...], act_ref[:, cols]
        ).astype(jnp.bfloat16)
    store_far(2).start()
    vec_out[...] = jnp.concatenate(
        [jnp.sum(vec_acc[8 * v : 8 * v + 8, :], axis=0, keepdims=True) for v in range(3)]
        + [jnp.zeros((5, vec_acc.shape[1]), jnp.float32)],
        axis=0,
    )
    for k in range(ups):
        bup_out[8 * k : 8 * k + 8, :] = bup_acc[:, 128 * k : 128 * k + 128]
    for chunk in range(chunks):
        pass_on(4, chunk).wait()
        store_other(chunk).start()
    gfar_ref[:, out_cols] = dot_tt(gatt_ref[...], mix_ref[...]).astype(jnp.bfloat16)
    store_far(0).start()
    for chunk in range(chunks):
        for copy in store_own(chunk) + (store_other(chunk),):
            copy.wait()
    for place in range(3):
        store_far(place).wait()


def middle_call(mix, tokens, cot_all, far_all, near_all, up_all):
    rows, own_rows = cot_all.shape[0], tokens.shape[0]
    chunks = own_rows // CHUNK
    hidden = (far_all.shape[1] - mix.shape[0]) // 2
    f32, bf16 = jnp.float32, jnp.bfloat16
    return pl.pallas_call(
        middle_kernel,
        in_specs=[ANY_SPEC] * 5 + [VMEM_SPEC],
        out_specs=[ANY_SPEC] * 4 + [VMEM_SPEC] * 2,
        out_shape=[
            jax.ShapeDtypeStruct((own_rows, D), bf16),
            jax.ShapeDtypeStruct((own_rows, D), f32),
            jax.ShapeDtypeStruct((rows, D), bf16),
            jax.ShapeDtypeStruct(far_all.shape, bf16),
            jax.ShapeDtypeStruct((8, D), f32),
            jax.ShapeDtypeStruct((hidden // 16, 128), f32),
        ],
        scratch_shapes=[
            pltpu.VMEM(mix.shape, bf16),
            pltpu.VMEM(tokens.shape, bf16),
            pltpu.VMEM(cot_all.shape, bf16),
            pltpu.VMEM(far_all.shape, bf16),
            pltpu.VMEM((D, VECS), bf16),
            pltpu.VMEM((own_rows, D), bf16),
            pltpu.VMEM((own_rows, D), f32),
            pltpu.VMEM((rows, D), bf16),
            pltpu.VMEM(far_all.shape, bf16),
            pltpu.VMEM((own_rows, D), bf16),
            pltpu.VMEM((own_rows, D), bf16),
            pltpu.VMEM((own_rows, D), f32),
            pltpu.VMEM((rows, D), bf16),
            pltpu.VMEM((D, rows), bf16),
            pltpu.VMEM((D, rows), bf16),
            pltpu.VMEM((rows, hidden), bf16),
            pltpu.VMEM((rows, hidden), bf16),
            pltpu.VMEM((2, own_rows, D), bf16),
            pltpu.VMEM((2, own_rows, D), bf16),
            pltpu.VMEM((own_rows, D), f32),
            pltpu.VMEM((own_rows, D), f32),
            pltpu.VMEM((8, hidden), f32),
            pltpu.VMEM((24, D), f32),
            pltpu.SemaphoreType.DMA((5, chunks)),
            pltpu.SemaphoreType.DMA((5, chunks)),
            pltpu.SemaphoreType.DMA((7,)),
            pltpu.SemaphoreType.DMA((4 * chunks + 3,)),
        ],
        compiler_params=pltpu.CompilerParams(
            collective_id=1, has_side_effects=True, vmem_limit_bytes=60 * 1024 * 1024
        ),
    )(mix, tokens, cot_all, far_all, near_all, up_all)


def last_kernel(
    count, e_ref, qu_in, qw_in, key_in, va_in, o_in, pos_in, row_in, gatt_in, far_in,
    near_in, norm_in, tok_in, gres_in, gfar_in, vec_ref, bup_ref,
    gtok_out, gq_ref, gk_ref, gv_ref, gp_ref, gup_ref, gdown_ref, gout_ref, gvec_ref, gbup_ref,
    qu_ref, qw_ref, key_ref, va_ref, pos_ref, row_ref, wout_ref, near_ref, norm_ref, tok_ref,
    gres_ref, gfar_ref, gatt_ref, o_ref, gtok_ref, e_buf, far_slots, far_along, far_back, packs, pack_slots, pack_along, pack_back,
    vec_mine, vec_other, vec_cols, vec_slots,
    bup_all, bup_slots, aug_ref, scd_ref, dqkv_ref, dk_acc, dv_acc, dpos_ref, both_ref, krow_ref,
    dqu_ref, bias_acc, normt_ref, part_send, part_recv, far_sum, pack_sums, vec_sum, bup_sum,
    vec_acc, send_sems, recv_sems, across_send, across_recv, along_send, along_recv,
    pair_send, pair_recv, e_sems, load_sems, store_sems,
):
    half = D // 2
    me, member = lax.axis_index("dp"), lax.axis_index("tensor")
    own_rows = tok_ref.shape[0]
    chunks = own_rows // CHUNK
    own0 = pl.multiple_of(member * own_rows, own_rows)
    oth0 = pl.multiple_of((1 - member) * own_rows, own_rows)
    width = qu_ref.shape[0]
    heads = width // HEAD
    score_scale = 1.0 / math.sqrt(HEAD)
    pair_width = width // 2
    vec_width = gvec_ref.shape[1]
    sources = (gfar_ref, packs.at[0], packs.at[1], vec_cols, bup_all)
    slots = (far_slots, pack_slots.at[0], pack_slots.at[1], vec_slots, bup_slots)
    totals = (far_sum, pack_sums.at[0], pack_sums.at[1], vec_sum, bup_sum)
    moves = (
        (gfar_in, gfar_ref), (gatt_in, gatt_ref), (o_in, o_ref),
        (far_in.at[:, pl.ds(far_in.shape[1] - width, width)], wout_ref),
        (norm_in, norm_ref), (qu_in, qu_ref), (qw_in, qw_ref), (key_in, key_ref), (va_in, va_ref),
        (pos_in, pos_ref), (row_in, row_ref), (near_in, near_ref), (tok_in, tok_ref),
        (gres_in, gres_ref),
    )
    loads = [
        pltpu.make_async_copy(source, target, load_sems.at[place])
        for place, (source, target) in enumerate(moves)
    ]

    def at(base, chunk):
        return pl.ds(pl.multiple_of(base + chunk * CHUNK, CHUNK), CHUNK)

    def piece(index, device):
        rows = totals[index].shape[0]
        if index == 3:
            start = pl.multiple_of(lax.div(device * vec_width, VECS) * VECS, VECS)
            return sources[index].at[:, pl.ds(start, VECS)]
        return sources[index].at[pl.ds(pl.multiple_of(device * rows, rows), rows)]

    def share_to(index, offset):
        peer = peer_at(offset)
        return pltpu.make_async_remote_copy(
            src_ref=piece(index, peer),
            dst_ref=slots[index].at[offset - 1],
            send_sem=send_sems.at[index - 3, offset - 1],
            recv_sem=recv_sems.at[index - 3, offset - 1],
            device_id={"dp": peer},
            device_id_type=MESH,
        )

    def begin_share(index):
        def begin(offset, carry):
            share_to(index, offset).start()
            return carry

        lax.fori_loop(1, count, begin, 0)

    def finish_share(index):
        total = totals[index]
        total[...] = piece(index, me)[...].astype(jnp.float32)

        def finish(offset, carry):
            share_to(index, offset).wait()
            total[...] += slots[index][offset - 1].astype(jnp.float32)
            return carry

        lax.fori_loop(1, count, finish, 0)

    levels = count // PLANE
    along_out = (far_along, pack_along.at[0], pack_along.at[1])
    along_in = (far_back, pack_back.at[0], pack_back.at[1])

    def go_across(index, offset, step):
        peer = across(me, count, offset)
        return remote(
            piece(index, along(peer, count, step)), slots[index].at[offset - 1, step],
            across_send.at[index, offset - 1, step], across_recv.at[index, offset - 1, step], peer,
        )

    def go_along(index, step):
        return remote(
            along_out[index].at[step - 1], along_in[index].at[step - 1],
            along_send.at[index, step - 1], along_recv.at[index, step - 1],
            along(me, count, step),
        )

    order = list(range(1, levels)) + [0]

    def begin_sum(index):
        for step in order:
            for offset in range(1, PLANE):
                go_across(index, offset, step).start()

    def pass_sum(index):
        for step in order:
            total = piece(index, along(me, count, step))[...].astype(jnp.float32)
            for offset in range(1, PLANE):
                go_across(index, offset, step).wait()
                total = total + slots[index][offset - 1, step].astype(jnp.float32)
            if step:
                along_out[index][step - 1] = total.astype(jnp.bfloat16)
                go_along(index, step).start()
            else:
                totals[index][...] = total

    def finish_sum(index):
        for step in range(1, levels):
            go_along(index, step).wait()
            totals[index][...] += along_in[index][step - 1].astype(jnp.float32)

    def e_copy(head, slot):
        return pltpu.make_async_copy(e_ref.at[head], e_buf.at[slot], e_sems.at[slot])

    for load in loads[:5]:
        load.start()
    e_copy(0, 0).start()
    for load in loads[5:]:
        load.start()
    greet_all(count, True)
    loads[0].wait()
    begin_sum(0)
    own_bup = pl.ds(pl.multiple_of(member * bup_ref.shape[0], 8), bup_ref.shape[0])
    bup_all[own_bup, :] = bup_ref[...]
    bup_copy = to_other(bup_ref, bup_all.at[own_bup], pair_send.at[chunks], pair_recv.at[chunks])
    bup_copy.start()

    for load in loads[1:4]:
        load.wait()
    out_mat = wout_ref[...].T
    place = lax.broadcasted_iota(jnp.int32, (AUG - HEAD, CHUNK), 0)
    for tile in range(TILES):
        rows = slice(tile * TILE, (tile + 1) * TILE)
        grads = times_transpose(out_mat, gatt_ref[rows, :])
        grads = grads.astype(jnp.bfloat16).astype(jnp.float32)
        for head in range(heads):
            lines = slice(head * HEAD, (head + 1) * HEAD)
            first = head * AUG
            inverse = o_ref[first + HEAD : first + HEAD + 1, rows]
            mixed = o_ref[first : first + HEAD, rows]
            scaled = grads[lines] * inverse
            low = (scaled * score_scale).astype(jnp.bfloat16)
            inner = -jnp.sum(low.astype(jnp.float32) * mixed, axis=0, keepdims=True)
            high = inner.astype(jnp.bfloat16).astype(jnp.float32)
            tail = jnp.where(place == 0, high, jnp.where(place == 1, inner - high, 0.0))
            scd_ref[lines, rows] = scaled.astype(jnp.bfloat16)
            aug_ref[first : first + HEAD, rows] = low
            aug_ref[first + HEAD : first + AUG, rows] = tail.astype(jnp.bfloat16)
    loads[4].wait()
    for tile in range(TILES):
        rows = slice(tile * TILE, (tile + 1) * TILE)
        normt_ref[:, rows] = norm_ref[rows, :].T
    for load in loads[5:11]:
        load.wait()

    def pack_pair(pair):
        first = pair * pair_width
        grads = jnp.concatenate(
            [
                dqkv_ref[part * width + first : part * width + first + pair_width, :]
                for part in range(3)
            ],
            axis=0,
        )
        packs[pair, :, : 3 * pair_width] = times_transpose(normt_ref[...], grads).astype(
            jnp.bfloat16
        )
        packs[pair, :, 3 * pair_width :] = dpos_ref[first : first + pair_width, :].T

    def one_head(head, carry):
        slot = lax.rem(head, 2)
        first = pl.multiple_of(head * HEAD, HEAD)
        lines = pl.ds(first, HEAD)
        more = pl.ds(pl.multiple_of(head * AUG, 16), AUG)

        @pl.when(head + 1 < heads)
        def _():
            e_copy(head + 1, 1 - slot).start()

        e_copy(head, slot).wait()
        dk_acc[...] = jnp.zeros_like(dk_acc)
        dv_acc[...] = jnp.zeros_like(dv_acc)
        filler = jnp.zeros((VECS - HEAD, key_ref.shape[1]), jnp.bfloat16)
        krow_ref[...] = jnp.concatenate([key_ref[lines, :], filler], axis=0).T

        def grads_of(tile):
            rows = slice(tile * TILE, (tile + 1) * TILE)
            weights = e_buf[slot, :, PACK[tile] : PACK[tile + 1]]
            grad_probs = contract_rows(
                aug_ref[more, rows], va_ref[more, : tiles_seen(tile) * TILE]
            )
            return (weights.astype(jnp.float32) * grad_probs).astype(jnp.bfloat16)

        def use_grads(tile, grad_scores):
            rows = slice(tile * TILE, (tile + 1) * TILE)
            seen = tiles_seen(tile) * TILE
            weights = e_buf[slot, :, PACK[tile] : PACK[tile + 1]]
            dv_acc[:, :seen] += dot_nn(scd_ref[lines, rows], weights)
            dk_acc[:, :seen] += dot_nn(qu_ref[lines, rows], grad_scores)
            dqu_ref[:, rows] = dot_nn(grad_scores, krow_ref[:seen, :]).T[:HEAD]
            turned = dot_nn(grad_scores, row_ref[:seen, :])
            part_c, part_s = turned[:, :half], turned[:, half:]
            cos_i = row_ref[rows, :half].astype(jnp.float32)
            sin_i = row_ref[rows, half:].astype(jnp.float32)
            both_ref[rows, :half] = (part_c * sin_i - part_s * cos_i).astype(jnp.bfloat16)
            both_ref[rows, half:] = (part_c * cos_i + part_s * sin_i).astype(jnp.bfloat16)

        grad_scores = grads_of(0)
        for tile in range(TILES):
            following = grads_of(tile + 1) if tile + 1 < TILES else None
            use_grads(tile, grad_scores)
            grad_scores = following
        grad_u = dqu_ref[...]
        grad_w = times_transpose(pos_ref[lines, :], both_ref[...])
        dqkv_ref[lines, :] = (grad_u + grad_w).astype(jnp.bfloat16)
        bias_acc[lines, :] = fold_cols(grad_u)
        bias_acc[pl.ds(pl.multiple_of(width + first, HEAD), HEAD), :] = fold_cols(grad_w)
        dpos_ref[lines, :] = dot_nn(qw_ref[lines, :], both_ref[...]).astype(jnp.bfloat16)
        key_lines = pl.ds(pl.multiple_of(width + first, HEAD), HEAD)
        value_lines = pl.ds(pl.multiple_of(2 * width + first, HEAD), HEAD)
        dqkv_ref[key_lines, :] = dk_acc[...].astype(jnp.bfloat16)
        dqkv_ref[value_lines, :] = dv_acc[...].astype(jnp.bfloat16)

        @pl.when(head == heads // 2 - 1)
        def _():
            pack_pair(0)
            begin_sum(1)

        @pl.when(head == heads - 2)
        def _():
            pass_sum(0)

        return carry

    lax.fori_loop(0, heads, one_head, 0)

    pack_pair(1)
    begin_sum(2)
    for load in loads[11:]:
        load.wait()
    bup_copy.wait()
    begin_share(4)

    def pass_on(chunk):
        here = at(0, chunk)
        return to_other(
            part_send.at[here], part_recv.at[here], pair_send.at[chunk], pair_recv.at[chunk]
        )

    def backward(rows):
        return dot_tt(dqkv_ref[:, rows], near_ref[:, : 3 * width])

    for chunk in range(chunks):
        part_send[at(0, chunk), :] = backward(at(oth0, chunk)).astype(jnp.bfloat16)
        pass_on(chunk).start()
    pass_sum(1)
    vec_rows = near_ref[:, NEAR:].astype(jnp.float32).T
    gain = vec_rows[0:1]
    vec_acc[...] = jnp.zeros_like(vec_acc)
    stores = [
        pltpu.make_async_copy(
            gtok_ref.at[at(0, chunk)], gtok_out.at[at(0, chunk)], store_sems.at[chunk]
        )
        for chunk in range(chunks)
    ]
    for chunk in range(chunks):
        here = at(0, chunk)
        part = backward(at(own0, chunk))
        pass_on(chunk).wait()
        grad = part + part_recv[here, :].astype(jnp.float32)
        normed, rate = norm_parts(tok_ref[here, :].astype(jnp.float32))
        gtok_ref[here, :] = gres_ref[here, :] + norm_grad(grad, gain, normed, rate)
        stores[chunk].start()
        vec_acc[0:8, :] += fold_rows(grad * normed)
        vec_acc[8:16, :] += fold_rows(grad)
    sums = jnp.sum(bias_acc[...].T, axis=0, keepdims=True)
    own_cols = pl.ds(pl.multiple_of(member * width, width), width)
    vec_mine[...] = jnp.zeros_like(vec_mine)
    vec_mine[0:1, :] = jnp.sum(vec_acc[0:8, :], axis=0, keepdims=True)
    vec_mine[1:2, :] = jnp.sum(vec_acc[8:16, :], axis=0, keepdims=True)
    vec_mine[2:3, own_cols] = sums[:, :width]
    vec_mine[3:4, own_cols] = sums[:, width:]
    vec_mine[4:7, :] = vec_ref[0:3, :]
    vec_copy = to_other(
        vec_mine, vec_other, pair_send.at[chunks + 1], pair_recv.at[chunks + 1]
    )
    vec_copy.start()
    finish_sum(0)
    gup_ref[...] = far_sum[:, : gup_ref.shape[1]]
    gdown_ref[...] = far_sum[:, gup_ref.shape[1] : 2 * gup_ref.shape[1]]
    gout_ref[...] = far_sum[:, 2 * gup_ref.shape[1] :]
    vec_copy.wait()
    both = vec_mine[...] + vec_other[...]
    vec_cols[...] = both
    begin_share(3)
    pass_sum(2)
    finish_share(4)
    gbup_ref[...] = jnp.sum(bup_sum[...], axis=0, keepdims=True)
    for pair in range(2):
        finish_sum(1 + pair)
        for part, ref in enumerate((gq_ref, gk_ref, gv_ref, gp_ref)):
            ref[:, pair * pair_width : (pair + 1) * pair_width] = pack_sums[
                pair, :, part * pair_width : (part + 1) * pair_width
            ]
    finish_share(3)
    spot = lax.rem(me * vec_width, VECS)
    picked = vec_sum[:, :vec_width]
    for start in range(vec_width, VECS, vec_width):
        picked = jnp.where(spot == start, vec_sum[:, start : start + vec_width], picked)
    gvec_ref[...] = picked
    for store in stores:
        store.wait()


def last_call(e, qu, qw, key, va, o, pos, col, gatt, far, near, norm, tok, gres, gfar, vec, bup):
    count = lax.axis_size("dp")
    levels = count // PLANE
    rows, own_rows = norm.shape[0], tok.shape[0]
    chunks = own_rows // CHUNK
    width = qu.shape[0]
    hidden = (far.shape[1] - width) // 2
    shard = D // count
    f32, bf16 = jnp.float32, jnp.bfloat16

    def shape(*dims):
        return jax.ShapeDtypeStruct(dims, f32)

    def room(*dims, kind=f32):
        return pltpu.VMEM(dims, kind)

    return pl.pallas_call(
        functools.partial(last_kernel, count),
        in_specs=[ANY_SPEC] * 15 + [VMEM_SPEC] * 2,
        out_specs=[ANY_SPEC] + [VMEM_SPEC] * 9,
        out_shape=[shape(own_rows, D)]
        + [shape(shard, width)] * 4
        + [shape(shard, hidden)] * 2
        + [shape(shard, width), shape(8, shard), shape(1, 128)],
        scratch_shapes=[
            room(width, rows, kind=bf16),
            room(width, rows, kind=bf16),
            room(width, rows, kind=bf16),
            room(va.shape[0], rows, kind=bf16),
            room(width, D, kind=bf16),
            room(rows, D, kind=bf16),
            room(D, width, kind=bf16),
            room(D, near.shape[1], kind=bf16),
            room(rows, D, kind=bf16),
            room(own_rows, D, kind=bf16),
            room(own_rows, D),
            room(D, far.shape[1], kind=bf16),
            room(rows, D, kind=bf16),
            room(o.shape[0], rows),
            room(own_rows, D),
            room(2, TILE, PACK[-1], kind=bf16),
            room(PLANE - 1, levels, shard, far.shape[1], kind=bf16),
            room(levels - 1, shard, far.shape[1], kind=bf16),
            room(levels - 1, shard, far.shape[1], kind=bf16),
            room(2, D, 2 * width, kind=bf16),
            room(2, PLANE - 1, levels, shard, 2 * width, kind=bf16),
            room(2, levels - 1, shard, 2 * width, kind=bf16),
            room(2, levels - 1, shard, 2 * width, kind=bf16),
            room(8, D),
            room(8, D),
            room(8, D),
            room(count - 1, 8, VECS),
            room(8 * count, 128),
            room(count - 1, 8, 128),
            room(va.shape[0], rows, kind=bf16),
            room(width, rows, kind=bf16),
            room(3 * width, rows, kind=bf16),
            room(HEAD, rows),
            room(HEAD, rows),
            room(width, D, kind=bf16),
            room(rows, D, kind=bf16),
            room(rows, VECS, kind=bf16),
            room(HEAD, rows),
            room(2 * width, 128),
            room(D, rows, kind=bf16),
            room(own_rows, D, kind=bf16),
            room(own_rows, D, kind=bf16),
            room(shard, far.shape[1]),
            room(2, shard, 2 * width),
            room(8, VECS),
            room(8, 128),
            room(16, D),
            pltpu.SemaphoreType.DMA((2, count - 1)),
            pltpu.SemaphoreType.DMA((2, count - 1)),
            pltpu.SemaphoreType.DMA((3, PLANE - 1, levels)),
            pltpu.SemaphoreType.DMA((3, PLANE - 1, levels)),
            pltpu.SemaphoreType.DMA((3, levels - 1)),
            pltpu.SemaphoreType.DMA((3, levels - 1)),
            pltpu.SemaphoreType.DMA((chunks + 2,)),
            pltpu.SemaphoreType.DMA((chunks + 2,)),
            pltpu.SemaphoreType.DMA((2,)),
            pltpu.SemaphoreType.DMA((14,)),
            pltpu.SemaphoreType.DMA((chunks,)),
        ],
        compiler_params=pltpu.CompilerParams(
            collective_id=2, has_side_effects=True, vmem_limit_bytes=62 * 1024 * 1024
        ),
    )(e, qu, qw, key, va, o, pos, col, gatt, far, near, norm, tok, gres, gfar, vec, bup)


def finish_call(large, mats, vecs, row):
    f32 = jnp.float32
    lines = 7
    steps = 4

    def body(*refs):
        large_in, refs = refs[: len(large)], refs[len(large) :]
        mats_in, refs = refs[: len(mats)], refs[len(mats) :]
        vec_ref, row_ref, refs = refs[0], refs[1], refs[2:]
        large_out, refs = refs[: len(large)], refs[len(large) :]
        mats_out, refs = refs[: len(mats)], refs[len(mats) :]
        lines_out, row_out, refs = refs[:lines], refs[lines], refs[lines + 1 :]
        rooms, load_sems, store_sems = refs[: len(large)], refs[-2], refs[-1]
        moves = []
        for step in range(steps):
            for place, source in enumerate(large_in):
                size = source.shape[0] // steps
                here = pl.ds(step * size, size)
                moves.append(
                    (
                        pltpu.make_async_copy(
                            source.at[here], rooms[place].at[here], load_sems.at[place, step]
                        ),
                        pltpu.make_async_copy(
                            rooms[place].at[here], large_out[place].at[here],
                            store_sems.at[place, step],
                        ),
                    )
                )
        for load, _ in moves:
            load.start()
        for source, target in zip(mats_in, mats_out):
            target[...] = source[...]
        for place, target in enumerate(lines_out):
            target[...] = vec_ref[place : place + 1, :]
        row_out[...] = row_ref[...]
        for load, store in moves:
            load.wait()
            store.start()
        for _, store in moves:
            store.wait()

    shapes = [jax.ShapeDtypeStruct(m.shape, m.dtype) for m in tuple(large) + tuple(mats)]
    return pl.pallas_call(
        body,
        in_specs=[ANY_SPEC] * len(large) + [VMEM_SPEC] * (len(mats) + 2),
        out_specs=[ANY_SPEC] * len(large) + [VMEM_SPEC] * (len(mats) + lines + 1),
        out_shape=shapes
        + [jax.ShapeDtypeStruct((1, vecs.shape[1]), f32)] * lines
        + [jax.ShapeDtypeStruct((1, row.shape[1]), f32)],
        scratch_shapes=[pltpu.VMEM(m.shape, m.dtype) for m in large]
        + [pltpu.SemaphoreType.DMA((len(large), steps))] * 2,
        compiler_params=pltpu.CompilerParams(vmem_limit_bytes=62 * 1024 * 1024),
    )(*large, *mats, vecs, row)


def local_plain(
    tokens,
    block_ids,
    ln1_gain,
    ln1_bias,
    w_query,
    w_key,
    w_value,
    w_pos,
    bias_u,
    bias_w,
    w_out,
    ln2_gain,
    ln2_bias,
    w_up,
    bias_up,
    w_down,
    bias_down,
    cotangent,
):
    member = lax.axis_index("tensor")
    squares = (w_query, w_key, w_value, w_pos, w_out.T)
    wide = (w_up, w_down.T)
    vectors = (ln1_gain, ln1_bias, bias_u, bias_w, ln2_gain, ln2_bias, bias_down)
    near_mats = [lax.all_gather(m, "dp", axis=0, tiled=True) for m in squares]
    far_mats = [lax.all_gather(m, "dp", axis=0, tiled=True) for m in wide]
    full_vecs = [lax.all_gather(v, "dp", axis=0, tiled=True) for v in vectors]
    up_shift = lax.all_gather(bias_up, "dp", axis=0, tiled=True)
    query_mat, key_mat, value_mat, pos_mat, out_back = near_mats
    out_mat = out_back.T
    up_mat, down_back = far_mats
    down_mat = down_back.T
    gain_one, shift_one, bias_one, bias_two, gain_two, shift_two, down_shift = full_vecs
    gain_one = gain_one.astype(jnp.float32)
    shift_one = shift_one.astype(jnp.float32)
    gain_two = gain_two.astype(jnp.float32)
    shift_two = shift_two.astype(jnp.float32)
    local_width = query_mat.shape[1]
    head_count = local_width // HEAD
    hidden_local = up_mat.shape[1]
    full_hidden = up_shift.shape[0]
    own_u = lax.dynamic_slice_in_dim(
        bias_one.astype(jnp.float32), member * local_width, local_width
    )
    own_w = lax.dynamic_slice_in_dim(
        bias_two.astype(jnp.float32), member * local_width, local_width
    )
    score_scale = 1.0 / math.sqrt(HEAD)
    own_rows = tokens.shape[0]
    inputs = tokens.astype(jnp.float32)
    normed = layer_norm(inputs, gain_one, shift_one)
    rows_all = lax.all_gather(normed.astype(jnp.bfloat16), "tensor", axis=0, tiled=True)
    total_rows = rows_all.shape[0]
    queries_t = project_cols(query_mat, rows_all)
    def heads_of(array):
        return array.astype(jnp.bfloat16).reshape(head_count, HEAD, array.shape[-1])

    ids = block_ids.reshape(1, total_rows)
    sum_u = queries_t + own_u[:, None]
    sum_w = queries_t + own_w[:, None]
    fold = score_scale * LOG2E
    query_u = heads_of(sum_u)
    query_w = heads_of(sum_w)
    key_rows = heads_of(project_cols(key_mat, rows_all))
    ones = jnp.ones((head_count, 2, total_rows), jnp.bfloat16)
    blank = jnp.zeros((head_count, AUG - HEAD - 2, total_rows), jnp.bfloat16)
    value_rows = jnp.concatenate(
        [heads_of(project_cols(value_mat, rows_all)), ones, blank], axis=1
    )
    pos_rows = pos_mat.T.reshape(head_count, HEAD, D)
    table = angle_table()
    row_table = jnp.asarray(table)
    col_table = jnp.asarray(np.ascontiguousarray(table.T))
    weights, mixed_sums = attend_all(
        heads_of(sum_u * fold), heads_of(sum_w * fold), key_rows, value_rows, pos_rows, ids,
        row_table, col_table,
    )
    inv_total = 1.0 / mixed_sums[:, HEAD : HEAD + 1]
    mixed_full = mixed_sums[:, :HEAD] * inv_total
    mixed_cols = mixed_full.reshape(local_width, total_rows).astype(jnp.bfloat16)
    residual = inputs + lax.psum_scatter(
        contract_rows(
            take_cols(mixed_cols, jnp.int32(0), own_rows * lax.axis_size("tensor")), out_mat
        ).astype(jnp.bfloat16),
        "tensor",
        scatter_dimension=0,
        tiled=True,
    ).astype(jnp.float32)
    normed_two = layer_norm(residual, gain_two, shift_two)
    grad_output = cotangent.astype(jnp.float32)
    grad_down_bias = placed(jnp.sum(grad_output, axis=0), D, 0)
    own_up = lax.dynamic_slice_in_dim(
        up_shift.astype(jnp.float32), member * hidden_local, hidden_local
    )
    rows_two = lax.all_gather(normed_two.astype(jnp.bfloat16), "tensor", axis=0, tiled=True)
    hidden = jnp.dot(rows_two, up_mat, preferred_element_type=jnp.float32) + own_up
    active = jax.nn.gelu(hidden).astype(jnp.bfloat16)
    output = (
        residual
        + lax.psum_scatter(
            jnp.dot(
                take_rows(active, jnp.int32(0), own_rows * lax.axis_size("tensor")),
                down_mat,
                preferred_element_type=jnp.float32,
            ).astype(jnp.bfloat16),
            "tensor",
            scatter_dimension=0,
            tiled=True,
        ).astype(jnp.float32)
        + down_shift.astype(jnp.float32)
    )
    grad_full = lax.all_gather(cotangent, "tensor", axis=0, tiled=True)
    grad_active = times_transpose(grad_full, down_mat)
    grad_down = contract_rows(active, grad_full)
    gelu_back = jax.vjp(jax.nn.gelu, hidden)[1]
    grad_hidden = gelu_back(grad_active)[0].astype(jnp.bfloat16)
    grad_up_bias = placed(
        jnp.sum(grad_hidden, axis=0, dtype=jnp.float32), full_hidden, member * hidden_local
    )
    grad_up = contract_rows(rows_two, grad_hidden)
    grad_normed_two = lax.psum_scatter(
        times_transpose(
            take_rows(grad_hidden, jnp.int32(0), own_rows * lax.axis_size("tensor")), up_mat
        ).astype(jnp.bfloat16),
        "tensor",
        scatter_dimension=0,
        tiled=True,
    ).astype(jnp.float32)
    norm_back_two = jax.vjp(layer_norm, residual, gain_two, shift_two)[1]
    grad_resid_part, grad_gain_two, grad_shift_two = norm_back_two(grad_normed_two)
    grad_residual = grad_output + grad_resid_part
    ffn_terms = (grad_gain_two, grad_shift_two, grad_up, grad_up_bias, grad_down, grad_down_bias)
    grad_att = lax.all_gather(grad_residual.astype(jnp.bfloat16), "tensor", axis=0, tiled=True)
    grad_out_mat = jnp.dot(mixed_cols, grad_att, preferred_element_type=jnp.float32)
    grad_mixed = (
        times_transpose(out_mat, grad_att)
        .astype(jnp.bfloat16)
        .reshape(head_count, HEAD, total_rows)
    )
    grad_mixed = grad_mixed.astype(jnp.float32)
    grad_scaled = (grad_mixed * inv_total).astype(jnp.bfloat16)
    grad_low = (grad_mixed * (inv_total * score_scale)).astype(jnp.bfloat16)
    inner = -jnp.sum(grad_low.astype(jnp.float32) * mixed_full, axis=1, keepdims=True)
    inner_high = inner.astype(jnp.bfloat16)
    inner_rest = (inner - inner_high.astype(jnp.float32)).astype(jnp.bfloat16)
    grad_aug = jnp.concatenate([grad_low, inner_high, inner_rest, blank], axis=1)
    dqu, dqw, dk, dv, dpos = attend_back_all(
        weights, query_u, query_w, key_rows, value_rows, pos_rows, grad_aug, grad_scaled, col_table
    )
    grad_keys_all = dk.reshape(local_width, total_rows).astype(jnp.bfloat16)
    grad_values_all = dv.reshape(local_width, total_rows).astype(jnp.bfloat16)
    grad_pos = dpos.reshape(local_width, D).T
    grad_query_u = dqu.reshape(local_width, total_rows)
    grad_query_w = dqw.reshape(local_width, total_rows)
    grad_bias_one = placed(jnp.sum(grad_query_u, axis=1), D, member * local_width)
    grad_bias_two = placed(jnp.sum(grad_query_w, axis=1), D, member * local_width)
    grad_query = (grad_query_u + grad_query_w).astype(jnp.bfloat16)
    grad_query_mat = times_transpose(rows_all.T, grad_query)
    grad_key_mat = times_transpose(rows_all.T, grad_keys_all)
    grad_value_mat = times_transpose(rows_all.T, grad_values_all)
    first_row = jnp.int32(0)
    part_sum = times_transpose(
        take_cols(grad_query, first_row, own_rows * lax.axis_size("tensor")).T, query_mat
    )
    part_sum = part_sum + times_transpose(
        take_cols(grad_keys_all, first_row, own_rows * lax.axis_size("tensor")).T, key_mat
    )
    grad_normed = lax.psum_scatter(
        (
            part_sum
            + times_transpose(
                take_cols(grad_values_all, first_row, own_rows * lax.axis_size("tensor")).T,
                value_mat,
            )
        ).astype(jnp.bfloat16),
        "tensor",
        scatter_dimension=0,
        tiled=True,
    ).astype(jnp.float32)
    norm_back_one = jax.vjp(layer_norm, inputs, gain_one, shift_one)[1]
    grad_in_part, grad_gain_one, grad_shift_one = norm_back_one(grad_normed)
    grad_tokens = grad_residual + grad_in_part
    grad_squares = (grad_query_mat, grad_key_mat, grad_value_mat, grad_pos, grad_out_mat.T)
    grad_wides = (grad_up, grad_down.T)
    grad_vecs = jnp.stack(
        (
            grad_gain_one, grad_shift_one, grad_bias_one, grad_bias_two,
            ffn_terms[0], ffn_terms[1], ffn_terms[5],
        )
    )
    grad_vecs, grad_up_row = lax.psum((grad_vecs, ffn_terms[3]), "tensor")
    def share(array):
        return lax.psum_scatter(array, "dp", scatter_dimension=0, tiled=True)

    squares = [share(m) for m in grad_squares]
    wides = [share(m) for m in grad_wides]
    vecs = [share(v) for v in grad_vecs]
    up_part = share(grad_up_row)
    return (
        output.astype(jnp.bfloat16),
        grad_tokens,
        vecs[0],
        vecs[1],
        squares[0],
        squares[1],
        squares[2],
        squares[3],
        vecs[2],
        vecs[3],
        squares[4].T,
        vecs[4],
        vecs[5],
        wides[0],
        up_part,
        wides[1].T,
        vecs[6],
    )


def local_direct(
    tokens,
    block_ids,
    ln1_gain,
    ln1_bias,
    w_query,
    w_key,
    w_value,
    w_pos,
    bias_u,
    bias_w,
    w_out,
    ln2_gain,
    ln2_bias,
    w_up,
    bias_up,
    w_down,
    bias_down,
    cotangent,
):
    total_rows = block_ids.shape[0]
    vectors = (ln1_gain, ln1_bias, bias_u, bias_w, ln2_gain, ln2_bias, bias_down)
    table = angle_table()
    row_table = jnp.asarray(table)
    col_table = jnp.asarray(np.ascontiguousarray(table.T))
    (
        weights, query_u, query_w, key_rows, value_aug, mixed_sums, mixed_cols, rows_all, pos_back,
        near, far, up_rows, grad_full,
    ) = first_call(
        tokens,
        cotangent,
        (w_query, w_key, w_value, w_pos),
        (w_up, w_down.T, w_out.T),
        [vector.reshape(1, -1) for vector in vectors],
        bias_up.reshape(1, -1),
        block_ids.reshape(1, total_rows),
        row_table,
        col_table,
    )
    out, grad_res, grad_att, grad_far, grad_vec, grad_up_part = middle_call(
        mixed_cols, tokens, grad_full, far, near, up_rows
    )
    (
        grad_tokens, grad_query_mat, grad_key_mat, grad_value_mat, grad_pos, grad_up, grad_down,
        grad_out, grad_vecs, grad_up_row,
    ) = last_call(
        weights, query_u, query_w, key_rows, value_aug, mixed_sums, pos_back, row_table, grad_att,
        far, near, rows_all, tokens, grad_res, grad_far, grad_vec, grad_up_part,
    )
    (
        out, grad_tokens, grad_query_mat, grad_key_mat, grad_value_mat, grad_pos, grad_up,
        grad_down, grad_out, *grad_vecs, grad_up_row,
    ) = finish_call(
        (out, grad_tokens),
        (grad_query_mat, grad_key_mat, grad_value_mat, grad_pos, grad_up, grad_down, grad_out),
        grad_vecs,
        grad_up_row,
    )
    grad_vecs = [vector.reshape(-1) for vector in grad_vecs]
    return (
        out,
        grad_tokens,
        grad_vecs[0],
        grad_vecs[1],
        grad_query_mat,
        grad_key_mat,
        grad_value_mat,
        grad_pos,
        grad_vecs[2],
        grad_vecs[3],
        grad_out.T,
        grad_vecs[4],
        grad_vecs[5],
        grad_up,
        grad_up_row.reshape(-1),
        grad_down.T,
        grad_vecs[6],
    )


def solution(mesh):
    in_specs = (
        P(("dp", "tensor"), None),
        P("dp"),
        P("dp"),
        P("dp"),
        P("dp", "tensor"),
        P("dp", "tensor"),
        P("dp", "tensor"),
        P("dp", "tensor"),
        P("dp"),
        P("dp"),
        P("tensor", "dp"),
        P("dp"),
        P("dp"),
        P("dp", "tensor"),
        P("dp"),
        P("tensor", "dp"),
        P("dp"),
        P(("dp", "tensor"), None),
    )
    out_specs = (
        P(("dp", "tensor"), None),
        P(("dp", "tensor"), None),
        P("dp"),
        P("dp"),
        P("dp", "tensor"),
        P("dp", "tensor"),
        P("dp", "tensor"),
        P("dp", "tensor"),
        P("dp"),
        P("dp"),
        P("tensor", "dp"),
        P("dp"),
        P("dp"),
        P("dp", "tensor"),
        P("dp"),
        P("tensor", "dp"),
        P("dp"),
    )
    pieces = D // mesh.shape["dp"]
    whole_tiles = (
        pieces % 16 == 0 and mesh.shape["tensor"] == 2 and mesh.shape["dp"] % (2 * PLANE) == 0
    )
    local = local_direct if whole_tiles else local_plain
    return jax.shard_map(local, mesh=mesh, in_specs=in_specs, out_specs=out_specs, check_vma=False)
```

```python
import functools
import math

import jax
import jax.numpy as jnp
import ml_dtypes
import numpy as np
from jax import lax
from jax.experimental import pallas as pl
from jax.experimental.pallas import tpu as pltpu
from jax.sharding import PartitionSpec as P

D = 512
HEAD = 64
L = 2048


MESH = pl.DeviceIdType.MESH
VECS = 128


def peer_at(offset):
    count = lax.axis_size("dp")
    return lax.rem(lax.axis_index("dp") + offset, count)


PLANE = 4


def place_of(me, count):
    return lax.div(me, PLANE), lax.rem(me, PLANE), count // PLANE


def along(me, count, offset):
    level, spot, levels = place_of(me, count)
    return lax.rem(level + offset, levels) * PLANE + spot


def across(me, count, offset):
    level, spot, _ = place_of(me, count)
    return level * PLANE + lax.rem(spot + offset, PLANE)


def remote(source, target, send_sem, recv_sem, device):
    return pltpu.make_async_remote_copy(
        src_ref=source,
        dst_ref=target,
        send_sem=send_sem,
        recv_sem=recv_sem,
        device_id={"dp": device},
        device_id_type=MESH,
    )


def greet_all(count, with_pair=False):
    barrier = pltpu.get_barrier_semaphore()

    def greet(offset, carry):
        pl.semaphore_signal(
            barrier, inc=1, device_id={"dp": peer_at(offset)}, device_id_type=MESH
        )
        return carry

    lax.fori_loop(1, count, greet, 0)
    if with_pair:
        pl.semaphore_signal(
            barrier, inc=1, device_id={"tensor": 1 - lax.axis_index("tensor")}, device_id_type=MESH
        )
    pl.semaphore_wait(barrier, count if with_pair else count - 1)


def layer_norm(values, gain_vec, shift_vec):
    center = values - jnp.mean(values, axis=-1, keepdims=True)
    spread = jnp.mean(center * center, axis=-1, keepdims=True)
    return center * lax.rsqrt(spread + 1e-05) * gain_vec + shift_vec


def take_rows(array, first_row, row_count):
    return lax.dynamic_slice_in_dim(array, first_row, row_count, 0)


def take_cols(array, first_col, col_count):
    return lax.dynamic_slice_in_dim(array, first_col, col_count, array.ndim - 1)


def contract_rows(left, right):
    return lax.dot_general(
        left, right, (((0,), (0,)), ((), ())), preferred_element_type=jnp.float32
    )


def times_transpose(left, right):
    return lax.dot_general(
        left, right, (((1,), (1,)), ((), ())), preferred_element_type=jnp.float32
    )


def project_cols(weight, row_data):
    return lax.dot_general(
        weight, row_data, (((0,), (1,)), ((), ())), preferred_element_type=jnp.float32
    )


TILE = 256
TILES = L // TILE
AUG = HEAD + 16
LOG2E = 1.4426950408889634


def tiles_seen(tile):
    return min(tile + 2, TILES)


PACK = [TILE * sum(tiles_seen(t) for t in range(tile)) for tile in range(TILES + 1)]


def angle_table():
    freqs = np.exp(np.arange(0, D, 2, dtype=np.float64) * (-math.log(10000.0) / D))
    angles = np.arange(L, dtype=np.float64)[:, None] * freqs[None, :]
    return np.concatenate([np.cos(angles), np.sin(angles)], axis=1).astype(ml_dtypes.bfloat16)


def dot_nn(left, right):
    return jnp.dot(left, right, preferred_element_type=jnp.float32)


def attend_kernel(qu_ref, qw_ref, key_ref, value_ref, pos_ref, ids_ref, row_ref, col_ref, e_ref, o_ref):
    half = D // 2
    for tile in range(TILES):
        rows = slice(tile * TILE, (tile + 1) * TILE)
        width = tiles_seen(tile) * TILE
        both = contract_rows(qw_ref[:, rows], pos_ref[...])
        part_a, part_b = both[:, :half], both[:, half:]
        cos_i = row_ref[rows, :half].astype(jnp.float32)
        sin_i = row_ref[rows, half:].astype(jnp.float32)
        turned = jnp.concatenate(
            [part_a * sin_i + part_b * cos_i, part_b * sin_i - part_a * cos_i], axis=1
        ).astype(jnp.bfloat16)
        scores = dot_nn(turned, col_ref[:, :width]) + contract_rows(
            qu_ref[:, rows], key_ref[:, :width]
        )
        ids_row = ids_ref[:, tile * TILE : width]
        ids_col = jnp.broadcast_to(ids_row[:, :TILE], (8, TILE)).T[:, :1]
        edge = jnp.where(ids_row <= ids_col, scores[:, tile * TILE :], -1e30)
        if tile:
            scores = jnp.concatenate([scores[:, : tile * TILE], edge], axis=1)
        else:
            scores = edge
        peak = jnp.max(scores, axis=1, keepdims=True)
        weights = jnp.exp2(scores - peak).astype(jnp.bfloat16)
        e_ref[:, PACK[tile] : PACK[tile + 1]] = weights
        o_ref[:, rows] = times_transpose(value_ref[:, :width], weights)


def attend_back_kernel(
    e_ref, qu_ref, qw_ref, key_ref, value_ref, pos_ref, aug_ref, scaled_ref, col_ref,
    dqu_ref, dqw_ref, dk_ref, dv_ref, dpos_ref,
):
    half = D // 2
    dk_ref[...] = jnp.zeros_like(dk_ref)
    dv_ref[...] = jnp.zeros_like(dv_ref)
    for tile in range(TILES):
        rows = slice(tile * TILE, (tile + 1) * TILE)
        width = tiles_seen(tile) * TILE
        weights = e_ref[:, PACK[tile] : PACK[tile + 1]]
        grad_probs = contract_rows(aug_ref[:, rows], value_ref[:, :width])
        grad_scores = (weights.astype(jnp.float32) * grad_probs).astype(jnp.bfloat16)
        dv_ref[:, :width] += dot_nn(scaled_ref[:, rows], weights)
        dk_ref[:, :width] += dot_nn(qu_ref[:, rows], grad_scores)
        dqu_ref[:, rows] = times_transpose(key_ref[:, :width], grad_scores)
        turned = times_transpose(col_ref[:, :width], grad_scores)
        part_c, part_s = turned[:half], turned[half:]
        cos_i = col_ref[:half, rows].astype(jnp.float32)
        sin_i = col_ref[half:, rows].astype(jnp.float32)
        both = jnp.concatenate(
            [part_c * sin_i - part_s * cos_i, part_c * cos_i + part_s * sin_i], axis=0
        ).astype(jnp.bfloat16)
        dqw_ref[:, rows] = dot_nn(pos_ref[...], both)
        here = times_transpose(qw_ref[:, rows], both)
        if tile:
            dpos_ref[...] += here
        else:
            dpos_ref[...] = here


def per_head(rows, cols):
    return pl.BlockSpec((None, rows, cols), lambda h: (h, 0, 0))


def shared(rows, cols):
    return pl.BlockSpec((rows, cols), lambda h: (0, 0))


def attend_all(qu, qw, keys, values, pos, ids, row_table, col_table):
    heads = qu.shape[0]
    f32, bf16 = jnp.float32, jnp.bfloat16
    return pl.pallas_call(
        attend_kernel,
        grid=(heads,),
        in_specs=[per_head(HEAD, L)] * 3
        + [per_head(AUG, L), per_head(HEAD, D), shared(1, L), shared(L, D), shared(D, L)],
        out_specs=[per_head(TILE, PACK[-1]), per_head(AUG, L)],
        out_shape=[
            jax.ShapeDtypeStruct((heads, TILE, PACK[-1]), bf16),
            jax.ShapeDtypeStruct((heads, AUG, L), f32),
        ],
        compiler_params=pltpu.CompilerParams(vmem_limit_bytes=56 * 1024 * 1024),
    )(qu, qw, keys, values, pos, ids, row_table, col_table)


def attend_back_all(weights, qu, qw, keys, values, pos, aug, scaled, col_table):
    heads = qu.shape[0]
    f32 = jnp.float32
    return pl.pallas_call(
        attend_back_kernel,
        grid=(heads,),
        in_specs=[per_head(TILE, PACK[-1])]
        + [per_head(HEAD, L)] * 3
        + [per_head(AUG, L), per_head(HEAD, D), per_head(AUG, L), per_head(HEAD, L), shared(D, L)],
        out_specs=[per_head(HEAD, L)] * 4 + [per_head(HEAD, D)],
        out_shape=[jax.ShapeDtypeStruct((heads, HEAD, L), f32)] * 4
        + [jax.ShapeDtypeStruct((heads, HEAD, D), f32)],
        compiler_params=pltpu.CompilerParams(vmem_limit_bytes=56 * 1024 * 1024),
    )(weights, qu, qw, keys, values, pos, aug, scaled, col_table)


def placed(part_vec, length, offset):
    return lax.dynamic_update_slice_in_dim(jnp.zeros((length,), jnp.float32), part_vec, offset, 0)


NEAR = 4 * 256


def first_kernel(
    count, tok_ref, cot_ref, wq_ref, wk_ref, wv_ref, wp_ref, wu_ref, wd_ref, wo_ref, *refs
):
    vec_refs, bup_ref, ids_ref, row_in, col_in = refs[:7], refs[7], refs[8], refs[9], refs[10]
    (
        e_ref, qu_out, qw_out, key_out, va_out, o_out, mix_out, norm_out, pos_out,
        near_out, far_out, up_all, cot_out,
        qu_ref, qw_ref, key_ref, va_ref, o_ref, mix_ref, norm_ref, pos_ref, first_all, second_all,
        far_all, cot_all, row_ref, col_ref,
        first_ref, second_ref, far_ref, up_ref, vec_ref, tok_all, quf_ref, qwf_ref, turn_ref,
        rq_ref, vrow_ref, hat_ref, e_buf,
        along_send, along_recv, across_send, across_recv, own_sems, pair_send, pair_recv, e_sems,
        load_sems, store_sems, head_sems,
    ) = refs[11:]
    half = D // 2
    me, member = lax.axis_index("dp"), lax.axis_index("tensor")
    levels = count // PLANE
    pair = {"tensor": 1 - member}
    own_rows = tok_ref.shape[0]
    own = pl.ds(pl.multiple_of(member * own_rows, own_rows), own_rows)
    parts = (first_ref, second_ref, far_ref, up_ref)
    wholes = (first_all, second_all, far_all, up_all)

    def rows_of(index, device):
        rows = parts[index].shape[0]
        return wholes[index].at[pl.ds(pl.multiple_of(device * rows, rows), rows)]

    def go_along(index, offset):
        return remote(
            parts[index], rows_of(index, me),
            along_send.at[index, offset - 1], along_recv.at[index, offset - 1],
            along(me, count, offset),
        )

    def go_across(index, offset, step):
        owner = along(me, count, levels - step)
        return remote(
            parts[index] if step == 0 else rows_of(index, owner), rows_of(index, owner),
            across_send.at[index, offset - 1, step], across_recv.at[index, offset - 1, step],
            across(me, count, offset),
        )

    def own_copy(index):
        return pltpu.make_async_copy(parts[index], rows_of(index, me), own_sems.at[index])

    def begin_along(index):
        for offset in range(1, levels):
            go_along(index, offset).start()

    def begin_across(index):
        for offset in range(1, PLANE):
            go_across(index, offset, 0).start()
        own_copy(index).start()

    def forward(index):
        for step in range(1, levels):
            go_along(index, step).wait()
            for offset in range(1, PLANE):
                go_across(index, offset, step).start()

    def finish_gather(index):
        for step in range(levels):
            for offset in range(1, PLANE):
                go_across(index, offset, step).wait()
        own_copy(index).wait()

    width = wq_ref.shape[1]
    hidden = wu_ref.shape[1]
    shard = wq_ref.shape[0]
    vec_ref[...] = jnp.zeros_like(vec_ref)
    for place, ref in enumerate(vec_refs):
        vec_ref[place : place + 1, :shard] = ref[...].astype(jnp.float32)
    pair_width = width // 2
    first_ref[:, 4 * pair_width :] = vec_ref[...].T[:shard].astype(jnp.bfloat16)
    for place, ref in enumerate((wq_ref, wk_ref, wv_ref, wp_ref)):
        cols = slice(place * pair_width, (place + 1) * pair_width)
        first_ref[:, cols] = ref[:, :pair_width]
        second_ref[:, cols] = ref[:, pair_width:]
    far_ref[:, :hidden] = wu_ref[...]
    far_ref[:, hidden : 2 * hidden] = wd_ref[...]
    far_ref[:, 2 * hidden :] = wo_ref[...]
    up_ref[...] = jnp.broadcast_to(bup_ref[...].astype(jnp.float32), up_ref.shape).astype(
        jnp.bfloat16
    )

    def to_pair(source, target, slot):
        return pltpu.make_async_remote_copy(
            src_ref=source,
            dst_ref=target.at[own],
            send_sem=pair_send.at[slot],
            recv_sem=pair_recv.at[slot],
            device_id=pair,
            device_id_type=MESH,
        )

    tables = (
        pltpu.make_async_copy(row_in, row_ref, load_sems.at[0]),
        pltpu.make_async_copy(col_in, col_ref, load_sems.at[1]),
    )
    for load in tables:
        load.start()
    greet_all(count, True)
    begin_along(0)
    begin_across(0)
    begin_along(3)
    begin_across(3)
    exchanges = (to_pair(tok_ref, tok_all, 0), to_pair(cot_ref, cot_all, 1))
    keeps = (
        pltpu.make_async_copy(tok_ref, tok_all.at[own], own_sems.at[4]),
        pltpu.make_async_copy(cot_ref, cot_all.at[own], own_sems.at[5]),
    )
    for copy in exchanges + keeps:
        copy.start()
    forward(0)
    begin_along(1)
    begin_across(1)
    begin_along(2)
    forward(3)
    exchanges[0].wait()
    keeps[0].wait()
    for tile in range(TILES):
        rows = slice(tile * TILE, (tile + 1) * TILE)
        hat_ref[rows, :] = norm_parts(tok_all[rows, :].astype(jnp.float32))[0]
    finish_gather(0)

    vec_block = first_all[:, 4 * pair_width :].astype(jnp.float32)
    vec_rows = vec_block.T
    gain, shift = vec_rows[0:1], vec_rows[1:2]
    heads = width // HEAD
    own_cols = pl.ds(pl.multiple_of(member * width, width), width)
    vec_cols = first_all[own_cols, 4 * pair_width :].astype(jnp.float32)
    bias_u, bias_w = vec_cols[:, 2:3], vec_cols[:, 3:4]
    fold = LOG2E / math.sqrt(HEAD)
    place = lax.broadcasted_iota(jnp.int32, (AUG - HEAD, TILE), 0)
    marks = jnp.where(place < 2, 1.0, 0.0).astype(jnp.bfloat16)
    for tile in range(TILES):
        rows = slice(tile * TILE, (tile + 1) * TILE)
        norm_ref[rows, :] = (hat_ref[rows, :] * gain + shift).astype(jnp.bfloat16)

    def project(pair_index):
        source = wholes[pair_index]
        lines = slice(pair_index * pair_width, (pair_index + 1) * pair_width)
        turn_ref[...] = source[:, : 3 * pair_width].T
        pos_ref[lines, :] = source[:, 3 * pair_width : 4 * pair_width].T
        for tile in range(TILES):
            rows = slice(tile * TILE, (tile + 1) * TILE)
            projected = times_transpose(turn_ref[...], norm_ref[rows, :])
            sum_u = projected[:pair_width] + bias_u[lines]
            sum_w = projected[:pair_width] + bias_w[lines]
            qu_ref[lines, rows] = sum_u.astype(jnp.bfloat16)
            qw_ref[lines, rows] = sum_w.astype(jnp.bfloat16)
            quf_ref[lines, rows] = (sum_u * fold).astype(jnp.bfloat16)
            qwf_ref[lines, rows] = (sum_w * fold).astype(jnp.bfloat16)
            key_ref[lines, rows] = projected[pair_width : 2 * pair_width].astype(jnp.bfloat16)
            for place in range(pair_width // HEAD):
                start = 2 * pair_width + place * HEAD
                base = (pair_index * (pair_width // HEAD) + place) * AUG
                values = projected[start : start + HEAD].astype(jnp.bfloat16)
                va_ref[base : base + HEAD, rows] = values
                va_ref[base + HEAD : base + AUG, rows] = marks

    project(0)
    forward(1)
    begin_across(2)
    for load in tables:
        load.wait()
    cols = [pl.ds(part * width, pair_width) for part in range(4)]
    more_cols = [pl.ds(part * width + pair_width, pair_width) for part in range(4)]
    here_cols = [pl.ds(part * pair_width, pair_width) for part in range(4)]
    moves = [(first_all.at[:, here_cols[part]], near_out.at[:, cols[part]]) for part in range(4)]
    moves.append(
        (first_all.at[:, pl.ds(4 * pair_width, VECS)], near_out.at[:, pl.ds(NEAR, VECS)])
    )
    moves.append((norm_ref, norm_out))
    early = len(moves)
    moves += [
        (second_all.at[:, here_cols[part]], near_out.at[:, more_cols[part]]) for part in range(4)
    ]
    moves += [
        (qu_ref, qu_out), (qw_ref, qw_out), (key_ref, key_out), (va_ref, va_out),
        (pos_ref, pos_out), (cot_all, cot_out),
    ]
    stores = [
        pltpu.make_async_copy(source, target, store_sems.at[place])
        for place, (source, target) in enumerate(moves)
    ]
    for store in stores[:early]:
        store.start()

    def head_copies(head):
        lines = pl.ds(pl.multiple_of(head * HEAD, HEAD), HEAD)
        more = pl.ds(pl.multiple_of(head * AUG, 16), AUG)
        return (
            pltpu.make_async_copy(o_ref.at[more], o_out.at[more], head_sems.at[0, head]),
            pltpu.make_async_copy(mix_ref.at[lines], mix_out.at[lines], head_sems.at[1, head]),
        )

    cut = PACK[TILES - 2]
    spans = (pl.ds(0, cut), pl.ds(cut, PACK[-1] - cut))

    def e_copy(head, slot, part):
        return pltpu.make_async_copy(
            e_buf.at[slot, :, spans[part]], e_ref.at[head, :, spans[part]], e_sems.at[slot, part]
        )

    def one_head(head, carry):
        slot = lax.rem(head, 2)
        lines = pl.ds(pl.multiple_of(head * HEAD, HEAD), HEAD)
        more = pl.ds(pl.multiple_of(head * AUG, 16), AUG)
        upper = pl.ds(pl.multiple_of(head * AUG, 16), HEAD)
        lower = pl.ds(pl.multiple_of(head * AUG + HEAD, 16), AUG - HEAD)

        @pl.when(head >= 2)
        def _():
            for part in range(2):
                e_copy(head - 2, slot, part).wait()

        filler = jnp.zeros((VECS - AUG, va_ref.shape[1]), jnp.bfloat16)
        vrow_ref[...] = jnp.concatenate([va_ref[more, :], filler], axis=0).T
        for tile in range(TILES):
            rows = slice(tile * TILE, (tile + 1) * TILE)
            both = contract_rows(qwf_ref[lines, rows], pos_ref[lines, :])
            part_a, part_b = both[:, :half], both[:, half:]
            cos_i = row_ref[rows, :half].astype(jnp.float32)
            sin_i = row_ref[rows, half:].astype(jnp.float32)
            rq_ref[rows, :half] = (part_a * sin_i + part_b * cos_i).astype(jnp.bfloat16)
            rq_ref[rows, half:] = (part_b * sin_i - part_a * cos_i).astype(jnp.bfloat16)

        def scores_of(tile):
            rows = slice(tile * TILE, (tile + 1) * TILE)
            seen = tiles_seen(tile) * TILE
            scores = dot_nn(rq_ref[rows, :], col_ref[:, :seen]) + contract_rows(
                quf_ref[lines, rows], key_ref[lines, :seen]
            )
            ids_row = ids_ref[:, tile * TILE : seen]
            ids_col = jnp.broadcast_to(ids_row[:, :TILE], (8, TILE)).T[:, :1]
            edge = jnp.where(ids_row <= ids_col, scores[:, tile * TILE :], -1e30)
            if tile:
                return jnp.concatenate([scores[:, : tile * TILE], edge], axis=1)
            return edge

        def use_scores(tile, scores):
            rows = slice(tile * TILE, (tile + 1) * TILE)
            seen = tiles_seen(tile) * TILE
            peak = jnp.max(scores, axis=1, keepdims=True)
            weights = jnp.exp2(scores - peak).astype(jnp.bfloat16)
            e_buf[slot, :, PACK[tile] : PACK[tile + 1]] = weights
            sums = dot_nn(weights, vrow_ref[:seen, :]).T
            inverse = 1.0 / sums[HEAD : HEAD + 1]
            mixed = sums[:HEAD] * inverse
            o_ref[upper, rows] = mixed
            o_ref[lower, rows] = jnp.broadcast_to(inverse, (AUG - HEAD, TILE))
            mix_ref[lines, rows] = mixed.astype(jnp.bfloat16)

        scores = scores_of(0)
        for tile in range(TILES):
            following = scores_of(tile + 1) if tile + 1 < TILES else None
            use_scores(tile, scores)
            scores = following
            if tile == TILES - 3:
                e_copy(head, slot, 0).start()
        e_copy(head, slot, 1).start()
        for copy in head_copies(head):
            copy.start()

        @pl.when(head == 0)
        def _():
            forward(2)

        @pl.when(head == heads // 2 - 1)
        def _():
            finish_gather(1)
            project(1)
            exchanges[1].wait()
            keeps[1].wait()
            for store in stores[early:]:
                store.start()

        return carry

    lax.fori_loop(0, heads, one_head, 0)
    for head in range(max(heads - 2, 0), heads):
        for part in range(2):
            e_copy(head, head % 2, part).wait()
    finish_gather(3)
    finish_gather(2)
    far_store = pltpu.make_async_copy(far_all, far_out, load_sems.at[2])
    far_store.start()
    for store in stores:
        store.wait()
    for head in range(heads):
        for copy in head_copies(head):
            copy.wait()
    far_store.wait()


VMEM_SPEC = pl.BlockSpec(memory_space=pltpu.VMEM)
ANY_SPEC = pl.BlockSpec(memory_space=pl.ANY)


def first_call(tokens, cotangent, squares, wides, vectors, bup, ids, row_table, col_table):
    count = lax.axis_size("dp")
    levels = count // PLANE
    rows = ids.shape[1]
    shard, width = squares[0].shape
    hidden = wides[0].shape[1]
    heads = width // HEAD
    far_width = 2 * hidden + width
    f32, bf16 = jnp.float32, jnp.bfloat16

    def shape(*dims, kind=bf16):
        return jax.ShapeDtypeStruct(dims, kind)

    return pl.pallas_call(
        functools.partial(first_kernel, count),
        in_specs=[VMEM_SPEC] * 18 + [ANY_SPEC] * 2,
        out_specs=[ANY_SPEC] * 11 + [VMEM_SPEC, ANY_SPEC],
        out_shape=[
            shape(heads, TILE, PACK[-1]),
            shape(width, rows),
            shape(width, rows),
            shape(width, rows),
            shape(heads * AUG, rows),
            shape(heads * AUG, rows, kind=f32),
            shape(width, rows),
            shape(rows, D),
            shape(width, D),
            shape(D, NEAR + VECS),
            shape(D, far_width),
            shape(16 * count, bup.shape[1]),
            shape(rows, D),
        ],
        scratch_shapes=[
            pltpu.VMEM((width, rows), bf16),
            pltpu.VMEM((width, rows), bf16),
            pltpu.VMEM((width, rows), bf16),
            pltpu.VMEM((heads * AUG, rows), bf16),
            pltpu.VMEM((heads * AUG, rows), f32),
            pltpu.VMEM((width, rows), bf16),
            pltpu.VMEM((rows, D), bf16),
            pltpu.VMEM((width, D), bf16),
            pltpu.VMEM((D, NEAR // 2 + VECS), bf16),
            pltpu.VMEM((D, NEAR // 2), bf16),
            pltpu.VMEM((D, far_width), bf16),
            pltpu.VMEM((rows, D), bf16),
            pltpu.VMEM((rows, D), bf16),
            pltpu.VMEM((D, rows), bf16),
            pltpu.VMEM((shard, NEAR // 2 + VECS), bf16),
            pltpu.VMEM((shard, NEAR // 2), bf16),
            pltpu.VMEM((shard, far_width), bf16),
            pltpu.VMEM((16, bup.shape[1]), bf16),
            pltpu.VMEM((VECS, VECS), f32),
            pltpu.VMEM((rows, D), bf16),
            pltpu.VMEM((width, rows), bf16),
            pltpu.VMEM((width, rows), bf16),
            pltpu.VMEM((3 * width // 2, D), bf16),
            pltpu.VMEM((rows, D), bf16),
            pltpu.VMEM((rows, VECS), bf16),
            pltpu.VMEM((rows, D), f32),
            pltpu.VMEM((2, TILE, PACK[-1]), bf16),
            pltpu.SemaphoreType.DMA((4, levels - 1)),
            pltpu.SemaphoreType.DMA((4, levels - 1)),
            pltpu.SemaphoreType.DMA((4, PLANE - 1, levels)),
            pltpu.SemaphoreType.DMA((4, PLANE - 1, levels)),
            pltpu.SemaphoreType.DMA((6,)),
            pltpu.SemaphoreType.DMA((2,)),
            pltpu.SemaphoreType.DMA((2,)),
            pltpu.SemaphoreType.DMA((2, 2)),
            pltpu.SemaphoreType.DMA((3,)),
            pltpu.SemaphoreType.DMA((16,)),
            pltpu.SemaphoreType.DMA((2, heads)),
        ],
        compiler_params=pltpu.CompilerParams(
            collective_id=0, has_side_effects=True, vmem_limit_bytes=60 * 1024 * 1024
        ),
    )(tokens, cotangent, *squares, *wides, *vectors, bup, ids, row_table, col_table)


CHUNK = 256
GELU_SCALE = math.sqrt(2.0 / math.pi)


def fold_rows(values):
    return jnp.sum(values.reshape(values.shape[0] // 8, 8, values.shape[1]), axis=0)


def fold_cols(values):
    total = values[:, :128]
    for start in range(128, values.shape[1], 128):
        total = total + values[:, start : start + 128]
    return total


def norm_parts(values):
    center = values - jnp.mean(values, axis=-1, keepdims=True)
    spread = jnp.mean(center * center, axis=-1, keepdims=True)
    rate = lax.rsqrt(spread + 1e-05)
    return center * rate, rate


def norm_grad(grad, gain, normed, rate):
    scaled = grad * gain
    mean = jnp.mean(scaled, axis=-1, keepdims=True)
    along = jnp.mean(scaled * normed, axis=-1, keepdims=True)
    return rate * (scaled - mean - normed * along)


def to_other(source, target, send_sem, recv_sem):
    return pltpu.make_async_remote_copy(
        src_ref=source,
        dst_ref=target,
        send_sem=send_sem,
        recv_sem=recv_sem,
        device_id={"tensor": 1 - lax.axis_index("tensor")},
        device_id_type=MESH,
    )


def dot_tt(left, right):
    return lax.dot_general(
        left, right, (((0,), (1,)), ((), ())), preferred_element_type=jnp.float32
    )


def middle_kernel(
    mix_in, tok_in, cot_in, far_in, near_in, up_ref,
    out_out, gres_out, gatt_out, gfar_out, vec_out, bup_out,
    mix_ref, tok_ref, cot_ref, far_ref, vec_ref, out_ref, gres_ref, gatt_ref, gfar_ref,
    send_a, recv_a, res_ref, n2_ref, n2t_ref, cott_ref, act_ref, gh_ref,
    osend, orecv, oacc, gacc, bup_acc, vec_acc, send_sems, recv_sems, load_sems, store_sems,
):
    member = lax.axis_index("tensor")
    own_rows = tok_ref.shape[0]
    chunks = own_rows // CHUNK
    own0 = pl.multiple_of(member * own_rows, own_rows)
    oth0 = pl.multiple_of((1 - member) * own_rows, own_rows)
    hidden = act_ref.shape[1]
    up_cols, down_cols = slice(0, hidden), slice(hidden, 2 * hidden)
    out_cols = slice(2 * hidden, far_ref.shape[1])
    pieces = (pl.ds(2 * hidden, mix_ref.shape[0]), pl.ds(0, hidden), pl.ds(hidden, hidden))
    moves = (
        (mix_in, mix_ref),
        (far_in.at[:, pieces[0]], far_ref.at[:, pieces[0]]),
        (tok_in, tok_ref),
        (near_in.at[:, pl.ds(NEAR, VECS)], vec_ref),
        (far_in.at[:, pieces[1]], far_ref.at[:, pieces[1]]),
        (cot_in, cot_ref),
        (far_in.at[:, pieces[2]], far_ref.at[:, pieces[2]]),
    )
    loads = [
        pltpu.make_async_copy(source, target, load_sems.at[place])
        for place, (source, target) in enumerate(moves)
    ]
    for load in loads:
        load.start()

    def store(place, source, target):
        return pltpu.make_async_copy(source, target, store_sems.at[place])

    def store_own(chunk):
        here, whole = at(0, chunk), at(own0, chunk)
        return (
            store(chunk, out_ref.at[here], out_out.at[here]),
            store(chunks + chunk, gres_ref.at[here], gres_out.at[here]),
            store(2 * chunks + chunk, gatt_ref.at[whole], gatt_out.at[whole]),
        )

    def store_other(chunk):
        whole = at(oth0, chunk)
        return store(3 * chunks + chunk, gatt_ref.at[whole], gatt_out.at[whole])

    def store_far(place):
        return store(
            4 * chunks + place, gfar_ref.at[:, pieces[place]], gfar_out.at[:, pieces[place]]
        )

    def at(base, chunk):
        return pl.ds(pl.multiple_of(base + chunk * CHUNK, CHUNK), CHUNK)

    barrier = pltpu.get_barrier_semaphore()
    pl.semaphore_signal(barrier, inc=1, device_id={"tensor": 1 - member}, device_id_type=MESH)
    pl.semaphore_wait(barrier, 1)

    def pass_on(stage, chunk):
        here = at(0, chunk)
        pairs = (
            (send_a.at[here], recv_a.at[here]),
            (n2_ref.at[at(own0, chunk)], n2_ref.at[at(own0, chunk)]),
            (osend.at[0, here], orecv.at[0, here]),
            (osend.at[1, here], orecv.at[1, here]),
            (gatt_ref.at[at(own0, chunk)], gatt_ref.at[at(own0, chunk)]),
        )
        source, target = pairs[stage]
        return to_other(
            source, target, send_sems.at[stage, chunk], recv_sems.at[stage, chunk]
        )

    ups = hidden // 128
    up_block = up_ref[pl.ds(pl.multiple_of(member * ups * 16, 16), ups * 16), :].astype(jnp.float32)
    up_shift = jnp.concatenate([up_block[16 * k : 16 * k + 1] for k in range(ups)], axis=1)

    def branch(rows):
        return dot_tt(mix_ref[:, rows], far_ref[:, out_cols])

    for load in loads[:2]:
        load.wait()
    for chunk in range(chunks):
        send_a[at(0, chunk), :] = branch(at(oth0, chunk)).astype(jnp.bfloat16)
        pass_on(0, chunk).start()
    for load in loads[2:4]:
        load.wait()
    vec_rows = vec_ref[...].astype(jnp.float32).T
    gain, shift, down_shift = vec_rows[4:5], vec_rows[5:6], vec_rows[6:7]
    for chunk in range(chunks):
        here = at(0, chunk)
        part = branch(at(own0, chunk))
        pass_on(0, chunk).wait()
        residual = tok_ref[here, :].astype(jnp.float32) + part + recv_a[here, :].astype(jnp.float32)
        res_ref[here, :] = residual
        n2_ref[at(own0, chunk), :] = (norm_parts(residual)[0] * gain + shift).astype(jnp.bfloat16)
        pass_on(1, chunk).start()

    bup_acc[...] = jnp.zeros_like(bup_acc)
    vec_acc[...] = jnp.zeros_like(vec_acc)

    for load in loads[4:]:
        load.wait()

    def products(mine, chunk):
        if not mine:
            pass_on(1, chunk).wait()
        rows = at(own0 if mine else oth0, chunk)
        return (
            dot_nn(n2_ref[rows, :], far_ref[:, up_cols]) + up_shift,
            dot_nn(cot_ref[rows, :], far_ref[:, down_cols]),
        )

    def use_products(mine, chunk, value, grad_active):
        rows, here = at(own0 if mine else oth0, chunk), at(0, chunk)
        square = value * value
        bend = jnp.tanh(value * (GELU_SCALE + GELU_SCALE * 0.044715 * square))
        half = 0.5 + 0.5 * bend
        active = (value * half).astype(jnp.bfloat16)
        steep = value * (2.0 * GELU_SCALE + 6.0 * GELU_SCALE * 0.044715 * square)
        slope = half + half * (1.0 - half) * steep
        grad_hidden = (grad_active * slope).astype(jnp.bfloat16)
        act_ref[rows, :] = active
        gh_ref[rows, :] = grad_hidden
        n2t_ref[:, rows] = n2_ref[rows, :].T
        cott_ref[:, rows] = cot_ref[rows, :].T
        bup_acc[...] += fold_rows(grad_hidden.astype(jnp.float32))
        out_part = times_transpose(active, far_ref[:, down_cols])
        grad_part = times_transpose(grad_hidden, far_ref[:, up_cols])
        if mine:
            oacc[here, :] = out_part
            gacc[here, :] = grad_part
        else:
            osend[0, here, :] = out_part.astype(jnp.bfloat16)
            osend[1, here, :] = grad_part.astype(jnp.bfloat16)
            pass_on(2, chunk).start()
            pass_on(3, chunk).start()

    lead = chunks // 2
    order = [(True, c) for c in range(lead)] + [(False, c) for c in range(chunks)]
    order += [(True, c) for c in range(lead, chunks)]
    current = products(*order[0])
    for place, tile in enumerate(order):
        following = products(*order[place + 1]) if place + 1 < len(order) else None
        use_products(*tile, *current)
        current = following

    def close(chunk, carry):
        here = at(0, chunk)
        pass_on(2, chunk).wait()
        pass_on(3, chunk).wait()
        residual = res_ref[here, :]
        out = residual + oacc[here, :] + orecv[0, here, :].astype(jnp.float32) + down_shift
        out_ref[here, :] = out.astype(jnp.bfloat16)
        grad = gacc[here, :] + orecv[1, here, :].astype(jnp.float32)
        normed, rate = norm_parts(residual)
        top = cot_ref[at(own0, chunk), :].astype(jnp.float32)
        grad_res = top + norm_grad(grad, gain, normed, rate)
        gres_ref[here, :] = grad_res
        gatt_ref[at(own0, chunk), :] = grad_res.astype(jnp.bfloat16)
        pass_on(4, chunk).start()
        for copy in store_own(chunk):
            copy.start()
        vec_acc[0:8, :] += fold_rows(grad * normed)
        vec_acc[8:16, :] += fold_rows(grad)
        vec_acc[16:24, :] += fold_rows(top)
        return carry

    lax.fori_loop(0, chunks, close, 0)
    for part in range(hidden // CHUNK):
        cols = slice(part * CHUNK, (part + 1) * CHUNK)
        gfar_ref[:, cols] = dot_nn(n2t_ref[...], gh_ref[:, cols]).astype(jnp.bfloat16)
    store_far(1).start()
    for part in range(hidden // CHUNK):
        cols = slice(part * CHUNK, (part + 1) * CHUNK)
        gfar_ref[:, hidden + part * CHUNK : hidden + (part + 1) * CHUNK] = dot_nn(
            cott_ref[...], act_ref[:, cols]
        ).astype(jnp.bfloat16)
    store_far(2).start()
    vec_out[...] = jnp.concatenate(
        [jnp.sum(vec_acc[8 * v : 8 * v + 8, :], axis=0, keepdims=True) for v in range(3)]
        + [jnp.zeros((5, vec_acc.shape[1]), jnp.float32)],
        axis=0,
    )
    for k in range(ups):
        bup_out[8 * k : 8 * k + 8, :] = bup_acc[:, 128 * k : 128 * k + 128]
    for chunk in range(chunks):
        pass_on(4, chunk).wait()
        store_other(chunk).start()
    gfar_ref[:, out_cols] = dot_tt(gatt_ref[...], mix_ref[...]).astype(jnp.bfloat16)
    store_far(0).start()
    for chunk in range(chunks):
        for copy in store_own(chunk) + (store_other(chunk),):
            copy.wait()
    for place in range(3):
        store_far(place).wait()


def middle_call(mix, tokens, cot_all, far_all, near_all, up_all):
    rows, own_rows = cot_all.shape[0], tokens.shape[0]
    chunks = own_rows // CHUNK
    hidden = (far_all.shape[1] - mix.shape[0]) // 2
    f32, bf16 = jnp.float32, jnp.bfloat16
    return pl.pallas_call(
        middle_kernel,
        in_specs=[ANY_SPEC] * 5 + [VMEM_SPEC],
        out_specs=[ANY_SPEC] * 4 + [VMEM_SPEC] * 2,
        out_shape=[
            jax.ShapeDtypeStruct((own_rows, D), bf16),
            jax.ShapeDtypeStruct((own_rows, D), f32),
            jax.ShapeDtypeStruct((rows, D), bf16),
            jax.ShapeDtypeStruct(far_all.shape, bf16),
            jax.ShapeDtypeStruct((8, D), f32),
            jax.ShapeDtypeStruct((hidden // 16, 128), f32),
        ],
        scratch_shapes=[
            pltpu.VMEM(mix.shape, bf16),
            pltpu.VMEM(tokens.shape, bf16),
            pltpu.VMEM(cot_all.shape, bf16),
            pltpu.VMEM(far_all.shape, bf16),
            pltpu.VMEM((D, VECS), bf16),
            pltpu.VMEM((own_rows, D), bf16),
            pltpu.VMEM((own_rows, D), f32),
            pltpu.VMEM((rows, D), bf16),
            pltpu.VMEM(far_all.shape, bf16),
            pltpu.VMEM((own_rows, D), bf16),
            pltpu.VMEM((own_rows, D), bf16),
            pltpu.VMEM((own_rows, D), f32),
            pltpu.VMEM((rows, D), bf16),
            pltpu.VMEM((D, rows), bf16),
            pltpu.VMEM((D, rows), bf16),
            pltpu.VMEM((rows, hidden), bf16),
            pltpu.VMEM((rows, hidden), bf16),
            pltpu.VMEM((2, own_rows, D), bf16),
            pltpu.VMEM((2, own_rows, D), bf16),
            pltpu.VMEM((own_rows, D), f32),
            pltpu.VMEM((own_rows, D), f32),
            pltpu.VMEM((8, hidden), f32),
            pltpu.VMEM((24, D), f32),
            pltpu.SemaphoreType.DMA((5, chunks)),
            pltpu.SemaphoreType.DMA((5, chunks)),
            pltpu.SemaphoreType.DMA((7,)),
            pltpu.SemaphoreType.DMA((4 * chunks + 3,)),
        ],
        compiler_params=pltpu.CompilerParams(
            collective_id=1, has_side_effects=True, vmem_limit_bytes=60 * 1024 * 1024
        ),
    )(mix, tokens, cot_all, far_all, near_all, up_all)


def last_kernel(
    count, e_ref, qu_in, qw_in, key_in, va_in, o_in, pos_in, row_in, gatt_in, far_in,
    near_in, norm_in, tok_in, gres_in, gfar_in, vec_ref, bup_ref,
    gtok_out, gq_ref, gk_ref, gv_ref, gp_ref, gup_ref, gdown_ref, gout_ref, gvec_ref, gbup_ref,
    qu_ref, qw_ref, key_ref, va_ref, pos_ref, row_ref, wout_ref, near_ref, norm_ref, tok_ref,
    gres_ref, gfar_ref, gatt_ref, o_ref, gtok_ref, e_buf, far_slots, far_along, far_back, packs, pack_slots, pack_along, pack_back,
    vec_mine, vec_other, vec_cols, vec_slots,
    bup_all, bup_slots, aug_ref, scd_ref, dqkv_ref, dk_acc, dv_acc, dpos_ref, both_ref, krow_ref,
    dqu_ref, bias_acc, normt_ref, part_send, part_recv, far_sum, pack_sums, vec_sum, bup_sum,
    vec_acc, send_sems, recv_sems, across_send, across_recv, along_send, along_recv,
    pair_send, pair_recv, e_sems, load_sems, store_sems,
):
    half = D // 2
    me, member = lax.axis_index("dp"), lax.axis_index("tensor")
    own_rows = tok_ref.shape[0]
    chunks = own_rows // CHUNK
    own0 = pl.multiple_of(member * own_rows, own_rows)
    oth0 = pl.multiple_of((1 - member) * own_rows, own_rows)
    width = qu_ref.shape[0]
    heads = width // HEAD
    score_scale = 1.0 / math.sqrt(HEAD)
    pair_width = width // 2
    vec_width = gvec_ref.shape[1]
    sources = (gfar_ref, packs.at[0], packs.at[1], vec_cols, bup_all)
    slots = (far_slots, pack_slots.at[0], pack_slots.at[1], vec_slots, bup_slots)
    totals = (far_sum, pack_sums.at[0], pack_sums.at[1], vec_sum, bup_sum)
    moves = (
        (gfar_in, gfar_ref), (gatt_in, gatt_ref), (o_in, o_ref),
        (far_in.at[:, pl.ds(far_in.shape[1] - width, width)], wout_ref),
        (norm_in, norm_ref), (qu_in, qu_ref), (qw_in, qw_ref), (key_in, key_ref), (va_in, va_ref),
        (pos_in, pos_ref), (row_in, row_ref), (near_in, near_ref), (tok_in, tok_ref),
        (gres_in, gres_ref),
    )
    loads = [
        pltpu.make_async_copy(source, target, load_sems.at[place])
        for place, (source, target) in enumerate(moves)
    ]

    def at(base, chunk):
        return pl.ds(pl.multiple_of(base + chunk * CHUNK, CHUNK), CHUNK)

    def piece(index, device):
        rows = totals[index].shape[0]
        if index == 3:
            start = pl.multiple_of(lax.div(device * vec_width, VECS) * VECS, VECS)
            return sources[index].at[:, pl.ds(start, VECS)]
        return sources[index].at[pl.ds(pl.multiple_of(device * rows, rows), rows)]

    def share_to(index, offset):
        peer = peer_at(offset)
        return pltpu.make_async_remote_copy(
            src_ref=piece(index, peer),
            dst_ref=slots[index].at[offset - 1],
            send_sem=send_sems.at[index - 3, offset - 1],
            recv_sem=recv_sems.at[index - 3, offset - 1],
            device_id={"dp": peer},
            device_id_type=MESH,
        )

    def begin_share(index):
        def begin(offset, carry):
            share_to(index, offset).start()
            return carry

        lax.fori_loop(1, count, begin, 0)

    def finish_share(index):
        total = totals[index]
        total[...] = piece(index, me)[...].astype(jnp.float32)

        def finish(offset, carry):
            share_to(index, offset).wait()
            total[...] += slots[index][offset - 1].astype(jnp.float32)
            return carry

        lax.fori_loop(1, count, finish, 0)

    levels = count // PLANE
    along_out = (far_along, pack_along.at[0], pack_along.at[1])
    along_in = (far_back, pack_back.at[0], pack_back.at[1])

    def go_across(index, offset, step):
        peer = across(me, count, offset)
        return remote(
            piece(index, along(peer, count, step)), slots[index].at[offset - 1, step],
            across_send.at[index, offset - 1, step], across_recv.at[index, offset - 1, step], peer,
        )

    def go_along(index, step):
        return remote(
            along_out[index].at[step - 1], along_in[index].at[step - 1],
            along_send.at[index, step - 1], along_recv.at[index, step - 1],
            along(me, count, step),
        )

    order = list(range(1, levels)) + [0]

    def begin_sum(index):
        for step in order:
            for offset in range(1, PLANE):
                go_across(index, offset, step).start()

    def pass_sum(index):
        for step in order:
            total = piece(index, along(me, count, step))[...].astype(jnp.float32)
            for offset in range(1, PLANE):
                go_across(index, offset, step).wait()
                total = total + slots[index][offset - 1, step].astype(jnp.float32)
            if step:
                along_out[index][step - 1] = total.astype(jnp.bfloat16)
                go_along(index, step).start()
            else:
                totals[index][...] = total

    def finish_sum(index):
        for step in range(1, levels):
            go_along(index, step).wait()
            totals[index][...] += along_in[index][step - 1].astype(jnp.float32)

    def e_copy(head, slot):
        return pltpu.make_async_copy(e_ref.at[head], e_buf.at[slot], e_sems.at[slot])

    for load in loads[:5]:
        load.start()
    e_copy(0, 0).start()
    for load in loads[5:]:
        load.start()
    greet_all(count, True)
    loads[0].wait()
    begin_sum(0)
    own_bup = pl.ds(pl.multiple_of(member * bup_ref.shape[0], 8), bup_ref.shape[0])
    bup_all[own_bup, :] = bup_ref[...]
    bup_copy = to_other(bup_ref, bup_all.at[own_bup], pair_send.at[chunks], pair_recv.at[chunks])
    bup_copy.start()

    for load in loads[1:4]:
        load.wait()
    out_mat = wout_ref[...].T
    place = lax.broadcasted_iota(jnp.int32, (AUG - HEAD, CHUNK), 0)
    for tile in range(TILES):
        rows = slice(tile * TILE, (tile + 1) * TILE)
        grads = times_transpose(out_mat, gatt_ref[rows, :])
        grads = grads.astype(jnp.bfloat16).astype(jnp.float32)
        for head in range(heads):
            lines = slice(head * HEAD, (head + 1) * HEAD)
            first = head * AUG
            inverse = o_ref[first + HEAD : first + HEAD + 1, rows]
            mixed = o_ref[first : first + HEAD, rows]
            scaled = grads[lines] * inverse
            low = (scaled * score_scale).astype(jnp.bfloat16)
            inner = -jnp.sum(low.astype(jnp.float32) * mixed, axis=0, keepdims=True)
            high = inner.astype(jnp.bfloat16).astype(jnp.float32)
            tail = jnp.where(place == 0, high, jnp.where(place == 1, inner - high, 0.0))
            scd_ref[lines, rows] = scaled.astype(jnp.bfloat16)
            aug_ref[first : first + HEAD, rows] = low
            aug_ref[first + HEAD : first + AUG, rows] = tail.astype(jnp.bfloat16)
    loads[4].wait()
    for tile in range(TILES):
        rows = slice(tile * TILE, (tile + 1) * TILE)
        normt_ref[:, rows] = norm_ref[rows, :].T
    for load in loads[5:11]:
        load.wait()

    def pack_pair(pair):
        first = pair * pair_width
        grads = jnp.concatenate(
            [
                dqkv_ref[part * width + first : part * width + first + pair_width, :]
                for part in range(3)
            ],
            axis=0,
        )
        packs[pair, :, : 3 * pair_width] = times_transpose(normt_ref[...], grads).astype(
            jnp.bfloat16
        )
        packs[pair, :, 3 * pair_width :] = dpos_ref[first : first + pair_width, :].T

    def one_head(head, carry):
        slot = lax.rem(head, 2)
        first = pl.multiple_of(head * HEAD, HEAD)
        lines = pl.ds(first, HEAD)
        more = pl.ds(pl.multiple_of(head * AUG, 16), AUG)

        @pl.when(head + 1 < heads)
        def _():
            e_copy(head + 1, 1 - slot).start()

        e_copy(head, slot).wait()
        dk_acc[...] = jnp.zeros_like(dk_acc)
        dv_acc[...] = jnp.zeros_like(dv_acc)
        filler = jnp.zeros((VECS - HEAD, key_ref.shape[1]), jnp.bfloat16)
        krow_ref[...] = jnp.concatenate([key_ref[lines, :], filler], axis=0).T

        def grads_of(tile):
            rows = slice(tile * TILE, (tile + 1) * TILE)
            weights = e_buf[slot, :, PACK[tile] : PACK[tile + 1]]
            grad_probs = contract_rows(
                aug_ref[more, rows], va_ref[more, : tiles_seen(tile) * TILE]
            )
            return (weights.astype(jnp.float32) * grad_probs).astype(jnp.bfloat16)

        def use_grads(tile, grad_scores):
            rows = slice(tile * TILE, (tile + 1) * TILE)
            seen = tiles_seen(tile) * TILE
            weights = e_buf[slot, :, PACK[tile] : PACK[tile + 1]]
            dv_acc[:, :seen] += dot_nn(scd_ref[lines, rows], weights)
            dk_acc[:, :seen] += dot_nn(qu_ref[lines, rows], grad_scores)
            dqu_ref[:, rows] = dot_nn(grad_scores, krow_ref[:seen, :]).T[:HEAD]
            turned = dot_nn(grad_scores, row_ref[:seen, :])
            part_c, part_s = turned[:, :half], turned[:, half:]
            cos_i = row_ref[rows, :half].astype(jnp.float32)
            sin_i = row_ref[rows, half:].astype(jnp.float32)
            both_ref[rows, :half] = (part_c * sin_i - part_s * cos_i).astype(jnp.bfloat16)
            both_ref[rows, half:] = (part_c * cos_i + part_s * sin_i).astype(jnp.bfloat16)

        grad_scores = grads_of(0)
        for tile in range(TILES):
            following = grads_of(tile + 1) if tile + 1 < TILES else None
            use_grads(tile, grad_scores)
            grad_scores = following
        grad_u = dqu_ref[...]
        grad_w = times_transpose(pos_ref[lines, :], both_ref[...])
        dqkv_ref[lines, :] = (grad_u + grad_w).astype(jnp.bfloat16)
        bias_acc[lines, :] = fold_cols(grad_u)
        bias_acc[pl.ds(pl.multiple_of(width + first, HEAD), HEAD), :] = fold_cols(grad_w)
        dpos_ref[lines, :] = dot_nn(qw_ref[lines, :], both_ref[...]).astype(jnp.bfloat16)
        key_lines = pl.ds(pl.multiple_of(width + first, HEAD), HEAD)
        value_lines = pl.ds(pl.multiple_of(2 * width + first, HEAD), HEAD)
        dqkv_ref[key_lines, :] = dk_acc[...].astype(jnp.bfloat16)
        dqkv_ref[value_lines, :] = dv_acc[...].astype(jnp.bfloat16)

        @pl.when(head == heads // 2 - 1)
        def _():
            pack_pair(0)
            begin_sum(1)

        @pl.when(head == heads - 2)
        def _():
            pass_sum(0)

        return carry

    lax.fori_loop(0, heads, one_head, 0)

    pack_pair(1)
    begin_sum(2)
    for load in loads[11:]:
        load.wait()
    bup_copy.wait()
    begin_share(4)

    def pass_on(chunk):
        here = at(0, chunk)
        return to_other(
            part_send.at[here], part_recv.at[here], pair_send.at[chunk], pair_recv.at[chunk]
        )

    def backward(rows):
        return dot_tt(dqkv_ref[:, rows], near_ref[:, : 3 * width])

    for chunk in range(chunks):
        part_send[at(0, chunk), :] = backward(at(oth0, chunk)).astype(jnp.bfloat16)
        pass_on(chunk).start()
    pass_sum(1)
    vec_rows = near_ref[:, NEAR:].astype(jnp.float32).T
    gain = vec_rows[0:1]
    vec_acc[...] = jnp.zeros_like(vec_acc)
    stores = [
        pltpu.make_async_copy(
            gtok_ref.at[at(0, chunk)], gtok_out.at[at(0, chunk)], store_sems.at[chunk]
        )
        for chunk in range(chunks)
    ]
    for chunk in range(chunks):
        here = at(0, chunk)
        part = backward(at(own0, chunk))
        pass_on(chunk).wait()
        grad = part + part_recv[here, :].astype(jnp.float32)
        normed, rate = norm_parts(tok_ref[here, :].astype(jnp.float32))
        gtok_ref[here, :] = gres_ref[here, :] + norm_grad(grad, gain, normed, rate)
        stores[chunk].start()
        vec_acc[0:8, :] += fold_rows(grad * normed)
        vec_acc[8:16, :] += fold_rows(grad)
    sums = jnp.sum(bias_acc[...].T, axis=0, keepdims=True)
    own_cols = pl.ds(pl.multiple_of(member * width, width), width)
    vec_mine[...] = jnp.zeros_like(vec_mine)
    vec_mine[0:1, :] = jnp.sum(vec_acc[0:8, :], axis=0, keepdims=True)
    vec_mine[1:2, :] = jnp.sum(vec_acc[8:16, :], axis=0, keepdims=True)
    vec_mine[2:3, own_cols] = sums[:, :width]
    vec_mine[3:4, own_cols] = sums[:, width:]
    vec_mine[4:7, :] = vec_ref[0:3, :]
    vec_copy = to_other(
        vec_mine, vec_other, pair_send.at[chunks + 1], pair_recv.at[chunks + 1]
    )
    vec_copy.start()
    finish_sum(0)
    gup_ref[...] = far_sum[:, : gup_ref.shape[1]]
    gdown_ref[...] = far_sum[:, gup_ref.shape[1] : 2 * gup_ref.shape[1]]
    gout_ref[...] = far_sum[:, 2 * gup_ref.shape[1] :]
    vec_copy.wait()
    both = vec_mine[...] + vec_other[...]
    vec_cols[...] = both
    begin_share(3)
    pass_sum(2)
    finish_share(4)
    gbup_ref[...] = jnp.sum(bup_sum[...], axis=0, keepdims=True)
    for pair in range(2):
        finish_sum(1 + pair)
        for part, ref in enumerate((gq_ref, gk_ref, gv_ref, gp_ref)):
            ref[:, pair * pair_width : (pair + 1) * pair_width] = pack_sums[
                pair, :, part * pair_width : (part + 1) * pair_width
            ]
    finish_share(3)
    spot = lax.rem(me * vec_width, VECS)
    picked = vec_sum[:, :vec_width]
    for start in range(vec_width, VECS, vec_width):
        picked = jnp.where(spot == start, vec_sum[:, start : start + vec_width], picked)
    gvec_ref[...] = picked
    for store in stores:
        store.wait()


def last_call(e, qu, qw, key, va, o, pos, col, gatt, far, near, norm, tok, gres, gfar, vec, bup):
    count = lax.axis_size("dp")
    levels = count // PLANE
    rows, own_rows = norm.shape[0], tok.shape[0]
    chunks = own_rows // CHUNK
    width = qu.shape[0]
    hidden = (far.shape[1] - width) // 2
    shard = D // count
    f32, bf16 = jnp.float32, jnp.bfloat16

    def shape(*dims):
        return jax.ShapeDtypeStruct(dims, f32)

    def room(*dims, kind=f32):
        return pltpu.VMEM(dims, kind)

    return pl.pallas_call(
        functools.partial(last_kernel, count),
        in_specs=[ANY_SPEC] * 15 + [VMEM_SPEC] * 2,
        out_specs=[ANY_SPEC] + [VMEM_SPEC] * 9,
        out_shape=[shape(own_rows, D)]
        + [shape(shard, width)] * 4
        + [shape(shard, hidden)] * 2
        + [shape(shard, width), shape(8, shard), shape(1, 128)],
        scratch_shapes=[
            room(width, rows, kind=bf16),
            room(width, rows, kind=bf16),
            room(width, rows, kind=bf16),
            room(va.shape[0], rows, kind=bf16),
            room(width, D, kind=bf16),
            room(rows, D, kind=bf16),
            room(D, width, kind=bf16),
            room(D, near.shape[1], kind=bf16),
            room(rows, D, kind=bf16),
            room(own_rows, D, kind=bf16),
            room(own_rows, D),
            room(D, far.shape[1], kind=bf16),
            room(rows, D, kind=bf16),
            room(o.shape[0], rows),
            room(own_rows, D),
            room(2, TILE, PACK[-1], kind=bf16),
            room(PLANE - 1, levels, shard, far.shape[1], kind=bf16),
            room(levels - 1, shard, far.shape[1], kind=bf16),
            room(levels - 1, shard, far.shape[1], kind=bf16),
            room(2, D, 2 * width, kind=bf16),
            room(2, PLANE - 1, levels, shard, 2 * width, kind=bf16),
            room(2, levels - 1, shard, 2 * width, kind=bf16),
            room(2, levels - 1, shard, 2 * width, kind=bf16),
            room(8, D),
            room(8, D),
            room(8, D),
            room(count - 1, 8, VECS),
            room(8 * count, 128),
            room(count - 1, 8, 128),
            room(va.shape[0], rows, kind=bf16),
            room(width, rows, kind=bf16),
            room(3 * width, rows, kind=bf16),
            room(HEAD, rows),
            room(HEAD, rows),
            room(width, D, kind=bf16),
            room(rows, D, kind=bf16),
            room(rows, VECS, kind=bf16),
            room(HEAD, rows),
            room(2 * width, 128),
            room(D, rows, kind=bf16),
            room(own_rows, D, kind=bf16),
            room(own_rows, D, kind=bf16),
            room(shard, far.shape[1]),
            room(2, shard, 2 * width),
            room(8, VECS),
            room(8, 128),
            room(16, D),
            pltpu.SemaphoreType.DMA((2, count - 1)),
            pltpu.SemaphoreType.DMA((2, count - 1)),
            pltpu.SemaphoreType.DMA((3, PLANE - 1, levels)),
            pltpu.SemaphoreType.DMA((3, PLANE - 1, levels)),
            pltpu.SemaphoreType.DMA((3, levels - 1)),
            pltpu.SemaphoreType.DMA((3, levels - 1)),
            pltpu.SemaphoreType.DMA((chunks + 2,)),
            pltpu.SemaphoreType.DMA((chunks + 2,)),
            pltpu.SemaphoreType.DMA((2,)),
            pltpu.SemaphoreType.DMA((14,)),
            pltpu.SemaphoreType.DMA((chunks,)),
        ],
        compiler_params=pltpu.CompilerParams(
            collective_id=2, has_side_effects=True, vmem_limit_bytes=62 * 1024 * 1024
        ),
    )(e, qu, qw, key, va, o, pos, col, gatt, far, near, norm, tok, gres, gfar, vec, bup)


def finish_kernel(number, *refs):
    for source, target in zip(refs[:number], refs[number : 2 * number]):
        target[...] = source[...]
    vec_ref, row_ref = refs[2 * number : 2 * number + 2]
    for place, target in enumerate(refs[2 * number + 2 : -1]):
        target[...] = vec_ref[place : place + 1, :]
    refs[-1][...] = row_ref[...]


def finish_call(mats, vecs, row):
    f32 = jnp.float32
    number = len(mats)
    lines = 7

    def shape(*dims):
        return jax.ShapeDtypeStruct(dims, f32)

    return pl.pallas_call(
        lambda *refs: finish_kernel(
            number, *refs[:number], *refs[number + 2 : 2 * number + 2],
            *refs[number : number + 2], *refs[2 * number + 2 :]
        ),
        in_specs=[VMEM_SPEC] * (number + 2),
        out_specs=[VMEM_SPEC] * (number + lines + 1),
        out_shape=[shape(*m.shape) for m in mats]
        + [shape(1, vecs.shape[1])] * lines
        + [shape(1, row.shape[1])],
    )(*mats, vecs, row)


def local_plain(
    tokens,
    block_ids,
    ln1_gain,
    ln1_bias,
    w_query,
    w_key,
    w_value,
    w_pos,
    bias_u,
    bias_w,
    w_out,
    ln2_gain,
    ln2_bias,
    w_up,
    bias_up,
    w_down,
    bias_down,
    cotangent,
):
    member = lax.axis_index("tensor")
    squares = (w_query, w_key, w_value, w_pos, w_out.T)
    wide = (w_up, w_down.T)
    vectors = (ln1_gain, ln1_bias, bias_u, bias_w, ln2_gain, ln2_bias, bias_down)
    near_mats = [lax.all_gather(m, "dp", axis=0, tiled=True) for m in squares]
    far_mats = [lax.all_gather(m, "dp", axis=0, tiled=True) for m in wide]
    full_vecs = [lax.all_gather(v, "dp", axis=0, tiled=True) for v in vectors]
    up_shift = lax.all_gather(bias_up, "dp", axis=0, tiled=True)
    query_mat, key_mat, value_mat, pos_mat, out_back = near_mats
    out_mat = out_back.T
    up_mat, down_back = far_mats
    down_mat = down_back.T
    gain_one, shift_one, bias_one, bias_two, gain_two, shift_two, down_shift = full_vecs
    gain_one = gain_one.astype(jnp.float32)
    shift_one = shift_one.astype(jnp.float32)
    gain_two = gain_two.astype(jnp.float32)
    shift_two = shift_two.astype(jnp.float32)
    local_width = query_mat.shape[1]
    head_count = local_width // HEAD
    hidden_local = up_mat.shape[1]
    full_hidden = up_shift.shape[0]
    own_u = lax.dynamic_slice_in_dim(
        bias_one.astype(jnp.float32), member * local_width, local_width
    )
    own_w = lax.dynamic_slice_in_dim(
        bias_two.astype(jnp.float32), member * local_width, local_width
    )
    score_scale = 1.0 / math.sqrt(HEAD)
    own_rows = tokens.shape[0]
    inputs = tokens.astype(jnp.float32)
    normed = layer_norm(inputs, gain_one, shift_one)
    rows_all = lax.all_gather(normed.astype(jnp.bfloat16), "tensor", axis=0, tiled=True)
    total_rows = rows_all.shape[0]
    queries_t = project_cols(query_mat, rows_all)
    def heads_of(array):
        return array.astype(jnp.bfloat16).reshape(head_count, HEAD, array.shape[-1])

    ids = block_ids.reshape(1, total_rows)
    sum_u = queries_t + own_u[:, None]
    sum_w = queries_t + own_w[:, None]
    fold = score_scale * LOG2E
    query_u = heads_of(sum_u)
    query_w = heads_of(sum_w)
    key_rows = heads_of(project_cols(key_mat, rows_all))
    ones = jnp.ones((head_count, 2, total_rows), jnp.bfloat16)
    blank = jnp.zeros((head_count, AUG - HEAD - 2, total_rows), jnp.bfloat16)
    value_rows = jnp.concatenate(
        [heads_of(project_cols(value_mat, rows_all)), ones, blank], axis=1
    )
    pos_rows = pos_mat.T.reshape(head_count, HEAD, D)
    table = angle_table()
    row_table = jnp.asarray(table)
    col_table = jnp.asarray(np.ascontiguousarray(table.T))
    weights, mixed_sums = attend_all(
        heads_of(sum_u * fold), heads_of(sum_w * fold), key_rows, value_rows, pos_rows, ids,
        row_table, col_table,
    )
    inv_total = 1.0 / mixed_sums[:, HEAD : HEAD + 1]
    mixed_full = mixed_sums[:, :HEAD] * inv_total
    mixed_cols = mixed_full.reshape(local_width, total_rows).astype(jnp.bfloat16)
    residual = inputs + lax.psum_scatter(
        contract_rows(
            take_cols(mixed_cols, jnp.int32(0), own_rows * lax.axis_size("tensor")), out_mat
        ).astype(jnp.bfloat16),
        "tensor",
        scatter_dimension=0,
        tiled=True,
    ).astype(jnp.float32)
    normed_two = layer_norm(residual, gain_two, shift_two)
    grad_output = cotangent.astype(jnp.float32)
    grad_down_bias = placed(jnp.sum(grad_output, axis=0), D, 0)
    own_up = lax.dynamic_slice_in_dim(
        up_shift.astype(jnp.float32), member * hidden_local, hidden_local
    )
    rows_two = lax.all_gather(normed_two.astype(jnp.bfloat16), "tensor", axis=0, tiled=True)
    hidden = jnp.dot(rows_two, up_mat, preferred_element_type=jnp.float32) + own_up
    active = jax.nn.gelu(hidden).astype(jnp.bfloat16)
    output = (
        residual
        + lax.psum_scatter(
            jnp.dot(
                take_rows(active, jnp.int32(0), own_rows * lax.axis_size("tensor")),
                down_mat,
                preferred_element_type=jnp.float32,
            ).astype(jnp.bfloat16),
            "tensor",
            scatter_dimension=0,
            tiled=True,
        ).astype(jnp.float32)
        + down_shift.astype(jnp.float32)
    )
    grad_full = lax.all_gather(cotangent, "tensor", axis=0, tiled=True)
    grad_active = times_transpose(grad_full, down_mat)
    grad_down = contract_rows(active, grad_full)
    gelu_back = jax.vjp(jax.nn.gelu, hidden)[1]
    grad_hidden = gelu_back(grad_active)[0].astype(jnp.bfloat16)
    grad_up_bias = placed(
        jnp.sum(grad_hidden, axis=0, dtype=jnp.float32), full_hidden, member * hidden_local
    )
    grad_up = contract_rows(rows_two, grad_hidden)
    grad_normed_two = lax.psum_scatter(
        times_transpose(
            take_rows(grad_hidden, jnp.int32(0), own_rows * lax.axis_size("tensor")), up_mat
        ).astype(jnp.bfloat16),
        "tensor",
        scatter_dimension=0,
        tiled=True,
    ).astype(jnp.float32)
    norm_back_two = jax.vjp(layer_norm, residual, gain_two, shift_two)[1]
    grad_resid_part, grad_gain_two, grad_shift_two = norm_back_two(grad_normed_two)
    grad_residual = grad_output + grad_resid_part
    ffn_terms = (grad_gain_two, grad_shift_two, grad_up, grad_up_bias, grad_down, grad_down_bias)
    grad_att = lax.all_gather(grad_residual.astype(jnp.bfloat16), "tensor", axis=0, tiled=True)
    grad_out_mat = jnp.dot(mixed_cols, grad_att, preferred_element_type=jnp.float32)
    grad_mixed = (
        times_transpose(out_mat, grad_att)
        .astype(jnp.bfloat16)
        .reshape(head_count, HEAD, total_rows)
    )
    grad_mixed = grad_mixed.astype(jnp.float32)
    grad_scaled = (grad_mixed * inv_total).astype(jnp.bfloat16)
    grad_low = (grad_mixed * (inv_total * score_scale)).astype(jnp.bfloat16)
    inner = -jnp.sum(grad_low.astype(jnp.float32) * mixed_full, axis=1, keepdims=True)
    inner_high = inner.astype(jnp.bfloat16)
    inner_rest = (inner - inner_high.astype(jnp.float32)).astype(jnp.bfloat16)
    grad_aug = jnp.concatenate([grad_low, inner_high, inner_rest, blank], axis=1)
    dqu, dqw, dk, dv, dpos = attend_back_all(
        weights, query_u, query_w, key_rows, value_rows, pos_rows, grad_aug, grad_scaled, col_table
    )
    grad_keys_all = dk.reshape(local_width, total_rows).astype(jnp.bfloat16)
    grad_values_all = dv.reshape(local_width, total_rows).astype(jnp.bfloat16)
    grad_pos = dpos.reshape(local_width, D).T
    grad_query_u = dqu.reshape(local_width, total_rows)
    grad_query_w = dqw.reshape(local_width, total_rows)
    grad_bias_one = placed(jnp.sum(grad_query_u, axis=1), D, member * local_width)
    grad_bias_two = placed(jnp.sum(grad_query_w, axis=1), D, member * local_width)
    grad_query = (grad_query_u + grad_query_w).astype(jnp.bfloat16)
    grad_query_mat = times_transpose(rows_all.T, grad_query)
    grad_key_mat = times_transpose(rows_all.T, grad_keys_all)
    grad_value_mat = times_transpose(rows_all.T, grad_values_all)
    first_row = jnp.int32(0)
    part_sum = times_transpose(
        take_cols(grad_query, first_row, own_rows * lax.axis_size("tensor")).T, query_mat
    )
    part_sum = part_sum + times_transpose(
        take_cols(grad_keys_all, first_row, own_rows * lax.axis_size("tensor")).T, key_mat
    )
    grad_normed = lax.psum_scatter(
        (
            part_sum
            + times_transpose(
                take_cols(grad_values_all, first_row, own_rows * lax.axis_size("tensor")).T,
                value_mat,
            )
        ).astype(jnp.bfloat16),
        "tensor",
        scatter_dimension=0,
        tiled=True,
    ).astype(jnp.float32)
    norm_back_one = jax.vjp(layer_norm, inputs, gain_one, shift_one)[1]
    grad_in_part, grad_gain_one, grad_shift_one = norm_back_one(grad_normed)
    grad_tokens = grad_residual + grad_in_part
    grad_squares = (grad_query_mat, grad_key_mat, grad_value_mat, grad_pos, grad_out_mat.T)
    grad_wides = (grad_up, grad_down.T)
    grad_vecs = jnp.stack(
        (
            grad_gain_one, grad_shift_one, grad_bias_one, grad_bias_two,
            ffn_terms[0], ffn_terms[1], ffn_terms[5],
        )
    )
    grad_vecs, grad_up_row = lax.psum((grad_vecs, ffn_terms[3]), "tensor")
    def share(array):
        return lax.psum_scatter(array, "dp", scatter_dimension=0, tiled=True)

    squares = [share(m) for m in grad_squares]
    wides = [share(m) for m in grad_wides]
    vecs = [share(v) for v in grad_vecs]
    up_part = share(grad_up_row)
    return (
        output.astype(jnp.bfloat16),
        grad_tokens,
        vecs[0],
        vecs[1],
        squares[0],
        squares[1],
        squares[2],
        squares[3],
        vecs[2],
        vecs[3],
        squares[4].T,
        vecs[4],
        vecs[5],
        wides[0],
        up_part,
        wides[1].T,
        vecs[6],
    )


def local_direct(
    tokens,
    block_ids,
    ln1_gain,
    ln1_bias,
    w_query,
    w_key,
    w_value,
    w_pos,
    bias_u,
    bias_w,
    w_out,
    ln2_gain,
    ln2_bias,
    w_up,
    bias_up,
    w_down,
    bias_down,
    cotangent,
):
    total_rows = block_ids.shape[0]
    vectors = (ln1_gain, ln1_bias, bias_u, bias_w, ln2_gain, ln2_bias, bias_down)
    table = angle_table()
    row_table = jnp.asarray(table)
    col_table = jnp.asarray(np.ascontiguousarray(table.T))
    (
        weights, query_u, query_w, key_rows, value_aug, mixed_sums, mixed_cols, rows_all, pos_back,
        near, far, up_rows, grad_full,
    ) = first_call(
        tokens,
        cotangent,
        (w_query, w_key, w_value, w_pos),
        (w_up, w_down.T, w_out.T),
        [vector.reshape(1, -1) for vector in vectors],
        bias_up.reshape(1, -1),
        block_ids.reshape(1, total_rows),
        row_table,
        col_table,
    )
    out, grad_res, grad_att, grad_far, grad_vec, grad_up_part = middle_call(
        mixed_cols, tokens, grad_full, far, near, up_rows
    )
    (
        grad_tokens, grad_query_mat, grad_key_mat, grad_value_mat, grad_pos, grad_up, grad_down,
        grad_out, grad_vecs, grad_up_row,
    ) = last_call(
        weights, query_u, query_w, key_rows, value_aug, mixed_sums, pos_back, row_table, grad_att,
        far, near, rows_all, tokens, grad_res, grad_far, grad_vec, grad_up_part,
    )
    (
        grad_query_mat, grad_key_mat, grad_value_mat, grad_pos, grad_up, grad_down, grad_out,
        *grad_vecs, grad_up_row,
    ) = finish_call(
        (grad_query_mat, grad_key_mat, grad_value_mat, grad_pos, grad_up, grad_down, grad_out),
        grad_vecs,
        grad_up_row,
    )
    grad_vecs = [vector.reshape(-1) for vector in grad_vecs]
    return (
        out,
        grad_tokens,
        grad_vecs[0],
        grad_vecs[1],
        grad_query_mat,
        grad_key_mat,
        grad_value_mat,
        grad_pos,
        grad_vecs[2],
        grad_vecs[3],
        grad_out.T,
        grad_vecs[4],
        grad_vecs[5],
        grad_up,
        grad_up_row.reshape(-1),
        grad_down.T,
        grad_vecs[6],
    )


def solution(mesh):
    in_specs = (
        P(("dp", "tensor"), None),
        P("dp"),
        P("dp"),
        P("dp"),
        P("dp", "tensor"),
        P("dp", "tensor"),
        P("dp", "tensor"),
        P("dp", "tensor"),
        P("dp"),
        P("dp"),
        P("tensor", "dp"),
        P("dp"),
        P("dp"),
        P("dp", "tensor"),
        P("dp"),
        P("tensor", "dp"),
        P("dp"),
        P(("dp", "tensor"), None),
    )
    out_specs = (
        P(("dp", "tensor"), None),
        P(("dp", "tensor"), None),
        P("dp"),
        P("dp"),
        P("dp", "tensor"),
        P("dp", "tensor"),
        P("dp", "tensor"),
        P("dp", "tensor"),
        P("dp"),
        P("dp"),
        P("tensor", "dp"),
        P("dp"),
        P("dp"),
        P("dp", "tensor"),
        P("dp"),
        P("tensor", "dp"),
        P("dp"),
    )
    pieces = D // mesh.shape["dp"]
    whole_tiles = (
        pieces % 16 == 0 and mesh.shape["tensor"] == 2 and mesh.shape["dp"] % (2 * PLANE) == 0
    )
    local = local_direct if whole_tiles else local_plain
    return jax.shard_map(local, mesh=mesh, in_specs=in_specs, out_specs=out_specs, check_vma=False)
```

```python
import functools
import math

import jax
import jax.numpy as jnp
import ml_dtypes
import numpy as np
from jax import lax
from jax.experimental import pallas as pl
from jax.experimental.pallas import tpu as pltpu
from jax.sharding import PartitionSpec as P

D = 512
HEAD = 64
L = 2048


MESH = pl.DeviceIdType.MESH
VECS = 128


def peer_at(offset):
    count = lax.axis_size("dp")
    return lax.rem(lax.axis_index("dp") + offset, count)


PLANE = 4


def place_of(me, count):
    return lax.div(me, PLANE), lax.rem(me, PLANE), count // PLANE


def along(me, count, offset):
    level, spot, levels = place_of(me, count)
    return lax.rem(level + offset, levels) * PLANE + spot


def across(me, count, offset):
    level, spot, _ = place_of(me, count)
    return level * PLANE + lax.rem(spot + offset, PLANE)


def remote(source, target, send_sem, recv_sem, device):
    return pltpu.make_async_remote_copy(
        src_ref=source,
        dst_ref=target,
        send_sem=send_sem,
        recv_sem=recv_sem,
        device_id={"dp": device},
        device_id_type=MESH,
    )


def greet_all(count, with_pair=False):
    barrier = pltpu.get_barrier_semaphore()

    def greet(offset, carry):
        pl.semaphore_signal(
            barrier, inc=1, device_id={"dp": peer_at(offset)}, device_id_type=MESH
        )
        return carry

    lax.fori_loop(1, count, greet, 0)
    if with_pair:
        pl.semaphore_signal(
            barrier, inc=1, device_id={"tensor": 1 - lax.axis_index("tensor")}, device_id_type=MESH
        )
    pl.semaphore_wait(barrier, count if with_pair else count - 1)


def layer_norm(values, gain_vec, shift_vec):
    center = values - jnp.mean(values, axis=-1, keepdims=True)
    spread = jnp.mean(center * center, axis=-1, keepdims=True)
    return center * lax.rsqrt(spread + 1e-05) * gain_vec + shift_vec


def take_rows(array, first_row, row_count):
    return lax.dynamic_slice_in_dim(array, first_row, row_count, 0)


def take_cols(array, first_col, col_count):
    return lax.dynamic_slice_in_dim(array, first_col, col_count, array.ndim - 1)


def contract_rows(left, right):
    return lax.dot_general(
        left, right, (((0,), (0,)), ((), ())), preferred_element_type=jnp.float32
    )


def times_transpose(left, right):
    return lax.dot_general(
        left, right, (((1,), (1,)), ((), ())), preferred_element_type=jnp.float32
    )


def project_cols(weight, row_data):
    return lax.dot_general(
        weight, row_data, (((0,), (1,)), ((), ())), preferred_element_type=jnp.float32
    )


TILE = 256
TILES = L // TILE
AUG = HEAD + 16
LOG2E = 1.4426950408889634


def tiles_seen(tile):
    return min(tile + 2, TILES)


PACK = [TILE * sum(tiles_seen(t) for t in range(tile)) for tile in range(TILES + 1)]


def angle_table():
    freqs = np.exp(np.arange(0, D, 2, dtype=np.float64) * (-math.log(10000.0) / D))
    angles = np.arange(L, dtype=np.float64)[:, None] * freqs[None, :]
    return np.concatenate([np.cos(angles), np.sin(angles)], axis=1).astype(ml_dtypes.bfloat16)


def dot_nn(left, right):
    return jnp.dot(left, right, preferred_element_type=jnp.float32)


def attend_kernel(qu_ref, qw_ref, key_ref, value_ref, pos_ref, ids_ref, row_ref, col_ref, e_ref, o_ref):
    half = D // 2
    for tile in range(TILES):
        rows = slice(tile * TILE, (tile + 1) * TILE)
        width = tiles_seen(tile) * TILE
        both = contract_rows(qw_ref[:, rows], pos_ref[...])
        part_a, part_b = both[:, :half], both[:, half:]
        cos_i = row_ref[rows, :half].astype(jnp.float32)
        sin_i = row_ref[rows, half:].astype(jnp.float32)
        turned = jnp.concatenate(
            [part_a * sin_i + part_b * cos_i, part_b * sin_i - part_a * cos_i], axis=1
        ).astype(jnp.bfloat16)
        scores = dot_nn(turned, col_ref[:, :width]) + contract_rows(
            qu_ref[:, rows], key_ref[:, :width]
        )
        ids_row = ids_ref[:, tile * TILE : width]
        ids_col = jnp.broadcast_to(ids_row[:, :TILE], (8, TILE)).T[:, :1]
        edge = jnp.where(ids_row <= ids_col, scores[:, tile * TILE :], -1e30)
        if tile:
            scores = jnp.concatenate([scores[:, : tile * TILE], edge], axis=1)
        else:
            scores = edge
        peak = jnp.max(scores, axis=1, keepdims=True)
        weights = jnp.exp2(scores - peak).astype(jnp.bfloat16)
        e_ref[:, PACK[tile] : PACK[tile + 1]] = weights
        o_ref[:, rows] = times_transpose(value_ref[:, :width], weights)


def attend_back_kernel(
    e_ref, qu_ref, qw_ref, key_ref, value_ref, pos_ref, aug_ref, scaled_ref, col_ref,
    dqu_ref, dqw_ref, dk_ref, dv_ref, dpos_ref,
):
    half = D // 2
    dk_ref[...] = jnp.zeros_like(dk_ref)
    dv_ref[...] = jnp.zeros_like(dv_ref)
    for tile in range(TILES):
        rows = slice(tile * TILE, (tile + 1) * TILE)
        width = tiles_seen(tile) * TILE
        weights = e_ref[:, PACK[tile] : PACK[tile + 1]]
        grad_probs = contract_rows(aug_ref[:, rows], value_ref[:, :width])
        grad_scores = (weights.astype(jnp.float32) * grad_probs).astype(jnp.bfloat16)
        dv_ref[:, :width] += dot_nn(scaled_ref[:, rows], weights)
        dk_ref[:, :width] += dot_nn(qu_ref[:, rows], grad_scores)
        dqu_ref[:, rows] = times_transpose(key_ref[:, :width], grad_scores)
        turned = times_transpose(col_ref[:, :width], grad_scores)
        part_c, part_s = turned[:half], turned[half:]
        cos_i = col_ref[:half, rows].astype(jnp.float32)
        sin_i = col_ref[half:, rows].astype(jnp.float32)
        both = jnp.concatenate(
            [part_c * sin_i - part_s * cos_i, part_c * cos_i + part_s * sin_i], axis=0
        ).astype(jnp.bfloat16)
        dqw_ref[:, rows] = dot_nn(pos_ref[...], both)
        here = times_transpose(qw_ref[:, rows], both)
        if tile:
            dpos_ref[...] += here
        else:
            dpos_ref[...] = here


def per_head(rows, cols):
    return pl.BlockSpec((None, rows, cols), lambda h: (h, 0, 0))


def shared(rows, cols):
    return pl.BlockSpec((rows, cols), lambda h: (0, 0))


def attend_all(qu, qw, keys, values, pos, ids, row_table, col_table):
    heads = qu.shape[0]
    f32, bf16 = jnp.float32, jnp.bfloat16
    return pl.pallas_call(
        attend_kernel,
        grid=(heads,),
        in_specs=[per_head(HEAD, L)] * 3
        + [per_head(AUG, L), per_head(HEAD, D), shared(1, L), shared(L, D), shared(D, L)],
        out_specs=[per_head(TILE, PACK[-1]), per_head(AUG, L)],
        out_shape=[
            jax.ShapeDtypeStruct((heads, TILE, PACK[-1]), bf16),
            jax.ShapeDtypeStruct((heads, AUG, L), f32),
        ],
        compiler_params=pltpu.CompilerParams(vmem_limit_bytes=56 * 1024 * 1024),
    )(qu, qw, keys, values, pos, ids, row_table, col_table)


def attend_back_all(weights, qu, qw, keys, values, pos, aug, scaled, col_table):
    heads = qu.shape[0]
    f32 = jnp.float32
    return pl.pallas_call(
        attend_back_kernel,
        grid=(heads,),
        in_specs=[per_head(TILE, PACK[-1])]
        + [per_head(HEAD, L)] * 3
        + [per_head(AUG, L), per_head(HEAD, D), per_head(AUG, L), per_head(HEAD, L), shared(D, L)],
        out_specs=[per_head(HEAD, L)] * 4 + [per_head(HEAD, D)],
        out_shape=[jax.ShapeDtypeStruct((heads, HEAD, L), f32)] * 4
        + [jax.ShapeDtypeStruct((heads, HEAD, D), f32)],
        compiler_params=pltpu.CompilerParams(vmem_limit_bytes=56 * 1024 * 1024),
    )(weights, qu, qw, keys, values, pos, aug, scaled, col_table)


def placed(part_vec, length, offset):
    return lax.dynamic_update_slice_in_dim(jnp.zeros((length,), jnp.float32), part_vec, offset, 0)


NEAR = 4 * 256


def first_kernel(
    count, tok_ref, cot_ref, wq_ref, wk_ref, wv_ref, wp_ref, wu_ref, wd_ref, wo_ref, *refs
):
    vec_refs, bup_ref, ids_ref, row_in, col_in = refs[:7], refs[7], refs[8], refs[9], refs[10]
    (
        e_ref, qu_out, qw_out, key_out, va_out, o_out, mix_out, norm_out, pos_out,
        near_out, far_out, up_all, cot_out,
        qu_ref, qw_ref, key_ref, va_ref, o_ref, mix_ref, norm_ref, pos_ref, first_all, second_all,
        far_all, cot_all, row_ref, col_ref,
        first_ref, second_ref, far_ref, up_ref, vec_ref, tok_all, quf_ref, qwf_ref, turn_ref,
        rq_ref, vrow_ref, hat_ref, e_buf,
        along_send, along_recv, across_send, across_recv, own_sems, pair_send, pair_recv, e_sems,
        load_sems, store_sems, head_sems,
    ) = refs[11:]
    half = D // 2
    me, member = lax.axis_index("dp"), lax.axis_index("tensor")
    levels = count // PLANE
    pair = {"tensor": 1 - member}
    own_rows = tok_ref.shape[0]
    own = pl.ds(pl.multiple_of(member * own_rows, own_rows), own_rows)
    parts = (first_ref, second_ref, far_ref, up_ref)
    wholes = (first_all, second_all, far_all, up_all)

    def rows_of(index, device):
        rows = parts[index].shape[0]
        return wholes[index].at[pl.ds(pl.multiple_of(device * rows, rows), rows)]

    def go_along(index, offset):
        return remote(
            parts[index], rows_of(index, me),
            along_send.at[index, offset - 1], along_recv.at[index, offset - 1],
            along(me, count, offset),
        )

    def go_across(index, offset, step):
        owner = along(me, count, levels - step)
        return remote(
            parts[index] if step == 0 else rows_of(index, owner), rows_of(index, owner),
            across_send.at[index, offset - 1, step], across_recv.at[index, offset - 1, step],
            across(me, count, offset),
        )

    def own_copy(index):
        return pltpu.make_async_copy(parts[index], rows_of(index, me), own_sems.at[index])

    def begin_along(index):
        for offset in range(1, levels):
            go_along(index, offset).start()

    def begin_across(index):
        for offset in range(1, PLANE):
            go_across(index, offset, 0).start()
        own_copy(index).start()

    def forward(index):
        for step in range(1, levels):
            go_along(index, step).wait()
            for offset in range(1, PLANE):
                go_across(index, offset, step).start()

    def finish_gather(index):
        for step in range(levels):
            for offset in range(1, PLANE):
                go_across(index, offset, step).wait()
        own_copy(index).wait()

    width = wq_ref.shape[1]
    hidden = wu_ref.shape[1]
    shard = wq_ref.shape[0]
    vec_ref[...] = jnp.zeros_like(vec_ref)
    for place, ref in enumerate(vec_refs):
        vec_ref[place : place + 1, :shard] = ref[...].astype(jnp.float32)
    pair_width = width // 2
    first_ref[:, 4 * pair_width :] = vec_ref[...].T[:shard].astype(jnp.bfloat16)
    for place, ref in enumerate((wq_ref, wk_ref, wv_ref, wp_ref)):
        cols = slice(place * pair_width, (place + 1) * pair_width)
        first_ref[:, cols] = ref[:, :pair_width]
        second_ref[:, cols] = ref[:, pair_width:]
    far_ref[:, :hidden] = wu_ref[...]
    far_ref[:, hidden : 2 * hidden] = wd_ref[...]
    far_ref[:, 2 * hidden :] = wo_ref[...]
    up_ref[...] = jnp.broadcast_to(bup_ref[...].astype(jnp.float32), up_ref.shape).astype(
        jnp.bfloat16
    )

    def to_pair(source, target, slot):
        return pltpu.make_async_remote_copy(
            src_ref=source,
            dst_ref=target.at[own],
            send_sem=pair_send.at[slot],
            recv_sem=pair_recv.at[slot],
            device_id=pair,
            device_id_type=MESH,
        )

    tables = (
        pltpu.make_async_copy(row_in, row_ref, load_sems.at[0]),
        pltpu.make_async_copy(col_in, col_ref, load_sems.at[1]),
    )
    for load in tables:
        load.start()
    greet_all(count, True)
    begin_along(0)
    begin_across(0)
    begin_along(3)
    begin_across(3)
    exchanges = (to_pair(tok_ref, tok_all, 0), to_pair(cot_ref, cot_all, 1))
    keeps = (
        pltpu.make_async_copy(tok_ref, tok_all.at[own], own_sems.at[4]),
        pltpu.make_async_copy(cot_ref, cot_all.at[own], own_sems.at[5]),
    )
    for copy in exchanges + keeps:
        copy.start()
    forward(0)
    begin_along(1)
    begin_across(1)
    begin_along(2)
    forward(3)
    exchanges[0].wait()
    keeps[0].wait()
    for tile in range(TILES):
        rows = slice(tile * TILE, (tile + 1) * TILE)
        hat_ref[rows, :] = norm_parts(tok_all[rows, :].astype(jnp.float32))[0]
    finish_gather(0)

    vec_block = first_all[:, 4 * pair_width :].astype(jnp.float32)
    vec_rows = vec_block.T
    gain, shift = vec_rows[0:1], vec_rows[1:2]
    heads = width // HEAD
    own_cols = pl.ds(pl.multiple_of(member * width, width), width)
    vec_cols = first_all[own_cols, 4 * pair_width :].astype(jnp.float32)
    bias_u, bias_w = vec_cols[:, 2:3], vec_cols[:, 3:4]
    fold = LOG2E / math.sqrt(HEAD)
    place = lax.broadcasted_iota(jnp.int32, (AUG - HEAD, TILE), 0)
    marks = jnp.where(place < 2, 1.0, 0.0).astype(jnp.bfloat16)
    for tile in range(TILES):
        rows = slice(tile * TILE, (tile + 1) * TILE)
        norm_ref[rows, :] = (hat_ref[rows, :] * gain + shift).astype(jnp.bfloat16)

    def project(pair_index):
        source = wholes[pair_index]
        lines = slice(pair_index * pair_width, (pair_index + 1) * pair_width)
        turn_ref[...] = source[:, : 3 * pair_width].T
        pos_ref[lines, :] = source[:, 3 * pair_width : 4 * pair_width].T
        for tile in range(TILES):
            rows = slice(tile * TILE, (tile + 1) * TILE)
            projected = times_transpose(turn_ref[...], norm_ref[rows, :])
            sum_u = projected[:pair_width] + bias_u[lines]
            sum_w = projected[:pair_width] + bias_w[lines]
            qu_ref[lines, rows] = sum_u.astype(jnp.bfloat16)
            qw_ref[lines, rows] = sum_w.astype(jnp.bfloat16)
            quf_ref[lines, rows] = (sum_u * fold).astype(jnp.bfloat16)
            qwf_ref[lines, rows] = (sum_w * fold).astype(jnp.bfloat16)
            key_ref[lines, rows] = projected[pair_width : 2 * pair_width].astype(jnp.bfloat16)
            for place in range(pair_width // HEAD):
                start = 2 * pair_width + place * HEAD
                base = (pair_index * (pair_width // HEAD) + place) * AUG
                values = projected[start : start + HEAD].astype(jnp.bfloat16)
                va_ref[base : base + HEAD, rows] = values
                va_ref[base + HEAD : base + AUG, rows] = marks

    project(0)
    forward(1)
    begin_across(2)
    for load in tables:
        load.wait()
    cols = [pl.ds(part * width, pair_width) for part in range(4)]
    more_cols = [pl.ds(part * width + pair_width, pair_width) for part in range(4)]
    here_cols = [pl.ds(part * pair_width, pair_width) for part in range(4)]
    moves = [(first_all.at[:, here_cols[part]], near_out.at[:, cols[part]]) for part in range(4)]
    moves.append(
        (first_all.at[:, pl.ds(4 * pair_width, VECS)], near_out.at[:, pl.ds(NEAR, VECS)])
    )
    moves.append((norm_ref, norm_out))
    early = len(moves)
    moves += [
        (second_all.at[:, here_cols[part]], near_out.at[:, more_cols[part]]) for part in range(4)
    ]
    moves += [
        (qu_ref, qu_out), (qw_ref, qw_out), (key_ref, key_out), (va_ref, va_out),
        (pos_ref, pos_out), (cot_all, cot_out),
    ]
    stores = [
        pltpu.make_async_copy(source, target, store_sems.at[place])
        for place, (source, target) in enumerate(moves)
    ]
    for store in stores[:early]:
        store.start()

    def head_copies(head):
        lines = pl.ds(pl.multiple_of(head * HEAD, HEAD), HEAD)
        more = pl.ds(pl.multiple_of(head * AUG, 16), AUG)
        return (
            pltpu.make_async_copy(o_ref.at[more], o_out.at[more], head_sems.at[0, head]),
            pltpu.make_async_copy(mix_ref.at[lines], mix_out.at[lines], head_sems.at[1, head]),
        )

    cut = PACK[TILES - 2]
    spans = (pl.ds(0, cut), pl.ds(cut, PACK[-1] - cut))

    def e_copy(head, slot, part):
        return pltpu.make_async_copy(
            e_buf.at[slot, :, spans[part]], e_ref.at[head, :, spans[part]], e_sems.at[slot, part]
        )

    def one_head(head, carry):
        slot = lax.rem(head, 2)
        lines = pl.ds(pl.multiple_of(head * HEAD, HEAD), HEAD)
        more = pl.ds(pl.multiple_of(head * AUG, 16), AUG)
        upper = pl.ds(pl.multiple_of(head * AUG, 16), HEAD)
        lower = pl.ds(pl.multiple_of(head * AUG + HEAD, 16), AUG - HEAD)

        @pl.when(head >= 2)
        def _():
            for part in range(2):
                e_copy(head - 2, slot, part).wait()

        filler = jnp.zeros((VECS - AUG, va_ref.shape[1]), jnp.bfloat16)
        vrow_ref[...] = jnp.concatenate([va_ref[more, :], filler], axis=0).T
        for tile in range(TILES):
            rows = slice(tile * TILE, (tile + 1) * TILE)
            both = contract_rows(qwf_ref[lines, rows], pos_ref[lines, :])
            part_a, part_b = both[:, :half], both[:, half:]
            cos_i = row_ref[rows, :half].astype(jnp.float32)
            sin_i = row_ref[rows, half:].astype(jnp.float32)
            rq_ref[rows, :half] = (part_a * sin_i + part_b * cos_i).astype(jnp.bfloat16)
            rq_ref[rows, half:] = (part_b * sin_i - part_a * cos_i).astype(jnp.bfloat16)

        def scores_of(tile):
            rows = slice(tile * TILE, (tile + 1) * TILE)
            seen = tiles_seen(tile) * TILE
            scores = dot_nn(rq_ref[rows, :], col_ref[:, :seen]) + contract_rows(
                quf_ref[lines, rows], key_ref[lines, :seen]
            )
            ids_row = ids_ref[:, tile * TILE : seen]
            ids_col = jnp.broadcast_to(ids_row[:, :TILE], (8, TILE)).T[:, :1]
            edge = jnp.where(ids_row <= ids_col, scores[:, tile * TILE :], -1e30)
            if tile:
                return jnp.concatenate([scores[:, : tile * TILE], edge], axis=1)
            return edge

        def use_scores(tile, scores):
            rows = slice(tile * TILE, (tile + 1) * TILE)
            seen = tiles_seen(tile) * TILE
            peak = jnp.max(scores, axis=1, keepdims=True)
            weights = jnp.exp2(scores - peak).astype(jnp.bfloat16)
            e_buf[slot, :, PACK[tile] : PACK[tile + 1]] = weights
            sums = dot_nn(weights, vrow_ref[:seen, :]).T
            inverse = 1.0 / sums[HEAD : HEAD + 1]
            mixed = sums[:HEAD] * inverse
            o_ref[upper, rows] = mixed
            o_ref[lower, rows] = jnp.broadcast_to(inverse, (AUG - HEAD, TILE))
            mix_ref[lines, rows] = mixed.astype(jnp.bfloat16)

        scores = scores_of(0)
        for tile in range(TILES):
            following = scores_of(tile + 1) if tile + 1 < TILES else None
            use_scores(tile, scores)
            scores = following
            if tile == TILES - 3:
                e_copy(head, slot, 0).start()
        e_copy(head, slot, 1).start()
        for copy in head_copies(head):
            copy.start()

        @pl.when(head == 0)
        def _():
            forward(2)

        @pl.when(head == heads // 2 - 1)
        def _():
            finish_gather(1)
            project(1)
            exchanges[1].wait()
            keeps[1].wait()
            for store in stores[early:]:
                store.start()

        return carry

    lax.fori_loop(0, heads, one_head, 0)
    for head in range(max(heads - 2, 0), heads):
        for part in range(2):
            e_copy(head, head % 2, part).wait()
    finish_gather(3)
    finish_gather(2)
    far_store = pltpu.make_async_copy(far_all, far_out, load_sems.at[2])
    far_store.start()
    for store in stores:
        store.wait()
    for head in range(heads):
        for copy in head_copies(head):
            copy.wait()
    far_store.wait()


VMEM_SPEC = pl.BlockSpec(memory_space=pltpu.VMEM)
ANY_SPEC = pl.BlockSpec(memory_space=pl.ANY)


def first_call(tokens, cotangent, squares, wides, vectors, bup, ids, row_table, col_table):
    count = lax.axis_size("dp")
    levels = count // PLANE
    rows = ids.shape[1]
    shard, width = squares[0].shape
    hidden = wides[0].shape[1]
    heads = width // HEAD
    far_width = 2 * hidden + width
    f32, bf16 = jnp.float32, jnp.bfloat16

    def shape(*dims, kind=bf16):
        return jax.ShapeDtypeStruct(dims, kind)

    return pl.pallas_call(
        functools.partial(first_kernel, count),
        in_specs=[VMEM_SPEC] * 18 + [ANY_SPEC] * 2,
        out_specs=[ANY_SPEC] * 11 + [VMEM_SPEC, ANY_SPEC],
        out_shape=[
            shape(heads, TILE, PACK[-1]),
            shape(width, rows),
            shape(width, rows),
            shape(width, rows),
            shape(heads * AUG, rows),
            shape(heads * AUG, rows, kind=f32),
            shape(width, rows),
            shape(rows, D),
            shape(width, D),
            shape(D, NEAR + VECS),
            shape(D, far_width),
            shape(16 * count, bup.shape[1]),
            shape(rows, D),
        ],
        scratch_shapes=[
            pltpu.VMEM((width, rows), bf16),
            pltpu.VMEM((width, rows), bf16),
            pltpu.VMEM((width, rows), bf16),
            pltpu.VMEM((heads * AUG, rows), bf16),
            pltpu.VMEM((heads * AUG, rows), f32),
            pltpu.VMEM((width, rows), bf16),
            pltpu.VMEM((rows, D), bf16),
            pltpu.VMEM((width, D), bf16),
            pltpu.VMEM((D, NEAR // 2 + VECS), bf16),
            pltpu.VMEM((D, NEAR // 2), bf16),
            pltpu.VMEM((D, far_width), bf16),
            pltpu.VMEM((rows, D), bf16),
            pltpu.VMEM((rows, D), bf16),
            pltpu.VMEM((D, rows), bf16),
            pltpu.VMEM((shard, NEAR // 2 + VECS), bf16),
            pltpu.VMEM((shard, NEAR // 2), bf16),
            pltpu.VMEM((shard, far_width), bf16),
            pltpu.VMEM((16, bup.shape[1]), bf16),
            pltpu.VMEM((VECS, VECS), f32),
            pltpu.VMEM((rows, D), bf16),
            pltpu.VMEM((width, rows), bf16),
            pltpu.VMEM((width, rows), bf16),
            pltpu.VMEM((3 * width // 2, D), bf16),
            pltpu.VMEM((rows, D), bf16),
            pltpu.VMEM((rows, VECS), bf16),
            pltpu.VMEM((rows, D), f32),
            pltpu.VMEM((2, TILE, PACK[-1]), bf16),
            pltpu.SemaphoreType.DMA((4, levels - 1)),
            pltpu.SemaphoreType.DMA((4, levels - 1)),
            pltpu.SemaphoreType.DMA((4, PLANE - 1, levels)),
            pltpu.SemaphoreType.DMA((4, PLANE - 1, levels)),
            pltpu.SemaphoreType.DMA((6,)),
            pltpu.SemaphoreType.DMA((2,)),
            pltpu.SemaphoreType.DMA((2,)),
            pltpu.SemaphoreType.DMA((2, 2)),
            pltpu.SemaphoreType.DMA((3,)),
            pltpu.SemaphoreType.DMA((16,)),
            pltpu.SemaphoreType.DMA((2, heads)),
        ],
        compiler_params=pltpu.CompilerParams(
            collective_id=0, has_side_effects=True, vmem_limit_bytes=60 * 1024 * 1024
        ),
    )(tokens, cotangent, *squares, *wides, *vectors, bup, ids, row_table, col_table)


CHUNK = 256
GELU_SCALE = math.sqrt(2.0 / math.pi)


def fold_rows(values):
    return jnp.sum(values.reshape(values.shape[0] // 8, 8, values.shape[1]), axis=0)


def fold_cols(values):
    total = values[:, :128]
    for start in range(128, values.shape[1], 128):
        total = total + values[:, start : start + 128]
    return total


def norm_parts(values):
    center = values - jnp.mean(values, axis=-1, keepdims=True)
    spread = jnp.mean(center * center, axis=-1, keepdims=True)
    rate = lax.rsqrt(spread + 1e-05)
    return center * rate, rate


def norm_grad(grad, gain, normed, rate):
    scaled = grad * gain
    mean = jnp.mean(scaled, axis=-1, keepdims=True)
    along = jnp.mean(scaled * normed, axis=-1, keepdims=True)
    return rate * (scaled - mean - normed * along)


def to_other(source, target, send_sem, recv_sem):
    return pltpu.make_async_remote_copy(
        src_ref=source,
        dst_ref=target,
        send_sem=send_sem,
        recv_sem=recv_sem,
        device_id={"tensor": 1 - lax.axis_index("tensor")},
        device_id_type=MESH,
    )


def dot_tt(left, right):
    return lax.dot_general(
        left, right, (((0,), (1,)), ((), ())), preferred_element_type=jnp.float32
    )


def middle_kernel(
    mix_in, tok_in, cot_in, far_in, near_in, up_ref,
    out_out, gres_out, gatt_out, gfar_out, vec_out, bup_out,
    mix_ref, tok_ref, cot_ref, far_ref, vec_ref, out_ref, gres_ref, gatt_ref, gfar_ref,
    send_a, recv_a, res_ref, n2_ref, n2t_ref, cott_ref, act_ref, gh_ref,
    osend, orecv, oacc, gacc, bup_acc, vec_acc, send_sems, recv_sems, load_sems, store_sems,
):
    member = lax.axis_index("tensor")
    own_rows = tok_ref.shape[0]
    chunks = own_rows // CHUNK
    own0 = pl.multiple_of(member * own_rows, own_rows)
    oth0 = pl.multiple_of((1 - member) * own_rows, own_rows)
    hidden = act_ref.shape[1]
    up_cols, down_cols = slice(0, hidden), slice(hidden, 2 * hidden)
    out_cols = slice(2 * hidden, far_ref.shape[1])
    pieces = (pl.ds(2 * hidden, mix_ref.shape[0]), pl.ds(0, hidden), pl.ds(hidden, hidden))
    moves = (
        (mix_in, mix_ref),
        (far_in.at[:, pieces[0]], far_ref.at[:, pieces[0]]),
        (tok_in, tok_ref),
        (near_in.at[:, pl.ds(NEAR, VECS)], vec_ref),
        (far_in.at[:, pieces[1]], far_ref.at[:, pieces[1]]),
        (cot_in, cot_ref),
        (far_in.at[:, pieces[2]], far_ref.at[:, pieces[2]]),
    )
    loads = [
        pltpu.make_async_copy(source, target, load_sems.at[place])
        for place, (source, target) in enumerate(moves)
    ]
    for load in loads:
        load.start()

    def store(place, source, target):
        return pltpu.make_async_copy(source, target, store_sems.at[place])

    def store_own(chunk):
        here, whole = at(0, chunk), at(own0, chunk)
        return (
            store(chunk, out_ref.at[here], out_out.at[here]),
            store(chunks + chunk, gres_ref.at[here], gres_out.at[here]),
            store(2 * chunks + chunk, gatt_ref.at[whole], gatt_out.at[whole]),
        )

    def store_other(chunk):
        whole = at(oth0, chunk)
        return store(3 * chunks + chunk, gatt_ref.at[whole], gatt_out.at[whole])

    def store_far(place):
        return store(
            4 * chunks + place, gfar_ref.at[:, pieces[place]], gfar_out.at[:, pieces[place]]
        )

    def at(base, chunk):
        return pl.ds(pl.multiple_of(base + chunk * CHUNK, CHUNK), CHUNK)

    barrier = pltpu.get_barrier_semaphore()
    pl.semaphore_signal(barrier, inc=1, device_id={"tensor": 1 - member}, device_id_type=MESH)
    pl.semaphore_wait(barrier, 1)

    def pass_on(stage, chunk):
        here = at(0, chunk)
        pairs = (
            (send_a.at[here], recv_a.at[here]),
            (n2_ref.at[at(own0, chunk)], n2_ref.at[at(own0, chunk)]),
            (osend.at[0, here], orecv.at[0, here]),
            (osend.at[1, here], orecv.at[1, here]),
            (gatt_ref.at[at(own0, chunk)], gatt_ref.at[at(own0, chunk)]),
        )
        source, target = pairs[stage]
        return to_other(
            source, target, send_sems.at[stage, chunk], recv_sems.at[stage, chunk]
        )

    ups = hidden // 128
    up_block = up_ref[pl.ds(pl.multiple_of(member * ups * 16, 16), ups * 16), :].astype(jnp.float32)
    up_shift = jnp.concatenate([up_block[16 * k : 16 * k + 1] for k in range(ups)], axis=1)

    def branch(rows):
        return dot_tt(mix_ref[:, rows], far_ref[:, out_cols])

    for load in loads[:2]:
        load.wait()
    for chunk in range(chunks):
        send_a[at(0, chunk), :] = branch(at(oth0, chunk)).astype(jnp.bfloat16)
        pass_on(0, chunk).start()
    for load in loads[2:4]:
        load.wait()
    vec_rows = vec_ref[...].astype(jnp.float32).T
    gain, shift, down_shift = vec_rows[4:5], vec_rows[5:6], vec_rows[6:7]
    for chunk in range(chunks):
        here = at(0, chunk)
        part = branch(at(own0, chunk))
        pass_on(0, chunk).wait()
        residual = tok_ref[here, :].astype(jnp.float32) + part + recv_a[here, :].astype(jnp.float32)
        res_ref[here, :] = residual
        n2_ref[at(own0, chunk), :] = (norm_parts(residual)[0] * gain + shift).astype(jnp.bfloat16)
        pass_on(1, chunk).start()

    bup_acc[...] = jnp.zeros_like(bup_acc)
    vec_acc[...] = jnp.zeros_like(vec_acc)

    for load in loads[4:]:
        load.wait()

    def products(mine, chunk):
        if not mine:
            pass_on(1, chunk).wait()
        rows = at(own0 if mine else oth0, chunk)
        return (
            dot_nn(n2_ref[rows, :], far_ref[:, up_cols]) + up_shift,
            dot_nn(cot_ref[rows, :], far_ref[:, down_cols]),
        )

    def use_products(mine, chunk, value, grad_active):
        rows, here = at(own0 if mine else oth0, chunk), at(0, chunk)
        square = value * value
        bend = jnp.tanh(value * (GELU_SCALE + GELU_SCALE * 0.044715 * square))
        half = 0.5 + 0.5 * bend
        active = (value * half).astype(jnp.bfloat16)
        steep = value * (2.0 * GELU_SCALE + 6.0 * GELU_SCALE * 0.044715 * square)
        slope = half + half * (1.0 - half) * steep
        grad_hidden = (grad_active * slope).astype(jnp.bfloat16)
        act_ref[rows, :] = active
        gh_ref[rows, :] = grad_hidden
        n2t_ref[:, rows] = n2_ref[rows, :].T
        cott_ref[:, rows] = cot_ref[rows, :].T
        bup_acc[...] += fold_rows(grad_hidden.astype(jnp.float32))
        out_part = times_transpose(active, far_ref[:, down_cols])
        grad_part = times_transpose(grad_hidden, far_ref[:, up_cols])
        if mine:
            oacc[here, :] = out_part
            gacc[here, :] = grad_part
        else:
            osend[0, here, :] = out_part.astype(jnp.bfloat16)
            osend[1, here, :] = grad_part.astype(jnp.bfloat16)
            pass_on(2, chunk).start()
            pass_on(3, chunk).start()

    lead = chunks // 2
    order = [(True, c) for c in range(lead)] + [(False, c) for c in range(chunks)]
    order += [(True, c) for c in range(lead, chunks)]
    current = products(*order[0])
    for place, tile in enumerate(order):
        following = products(*order[place + 1]) if place + 1 < len(order) else None
        use_products(*tile, *current)
        current = following

    def close(chunk, carry):
        here = at(0, chunk)
        pass_on(2, chunk).wait()
        pass_on(3, chunk).wait()
        residual = res_ref[here, :]
        out = residual + oacc[here, :] + orecv[0, here, :].astype(jnp.float32) + down_shift
        out_ref[here, :] = out.astype(jnp.bfloat16)
        grad = gacc[here, :] + orecv[1, here, :].astype(jnp.float32)
        normed, rate = norm_parts(residual)
        top = cot_ref[at(own0, chunk), :].astype(jnp.float32)
        grad_res = top + norm_grad(grad, gain, normed, rate)
        gres_ref[here, :] = grad_res
        gatt_ref[at(own0, chunk), :] = grad_res.astype(jnp.bfloat16)
        pass_on(4, chunk).start()
        for copy in store_own(chunk):
            copy.start()
        vec_acc[0:8, :] += fold_rows(grad * normed)
        vec_acc[8:16, :] += fold_rows(grad)
        vec_acc[16:24, :] += fold_rows(top)
        return carry

    lax.fori_loop(0, chunks, close, 0)
    for part in range(hidden // CHUNK):
        cols = slice(part * CHUNK, (part + 1) * CHUNK)
        gfar_ref[:, cols] = dot_nn(n2t_ref[...], gh_ref[:, cols]).astype(jnp.bfloat16)
    store_far(1).start()
    for part in range(hidden // CHUNK):
        cols = slice(part * CHUNK, (part + 1) * CHUNK)
        gfar_ref[:, hidden + part * CHUNK : hidden + (part + 1) * CHUNK] = dot_nn(
            cott_ref[...], act_ref[:, cols]
        ).astype(jnp.bfloat16)
    store_far(2).start()
    vec_out[...] = jnp.concatenate(
        [jnp.sum(vec_acc[8 * v : 8 * v + 8, :], axis=0, keepdims=True) for v in range(3)]
        + [jnp.zeros((5, vec_acc.shape[1]), jnp.float32)],
        axis=0,
    )
    for k in range(ups):
        bup_out[8 * k : 8 * k + 8, :] = bup_acc[:, 128 * k : 128 * k + 128]
    for chunk in range(chunks):
        pass_on(4, chunk).wait()
        store_other(chunk).start()
    gfar_ref[:, out_cols] = dot_tt(gatt_ref[...], mix_ref[...]).astype(jnp.bfloat16)
    store_far(0).start()
    for chunk in range(chunks):
        for copy in store_own(chunk) + (store_other(chunk),):
            copy.wait()
    for place in range(3):
        store_far(place).wait()


def middle_call(mix, tokens, cot_all, far_all, near_all, up_all):
    rows, own_rows = cot_all.shape[0], tokens.shape[0]
    chunks = own_rows // CHUNK
    hidden = (far_all.shape[1] - mix.shape[0]) // 2
    f32, bf16 = jnp.float32, jnp.bfloat16
    return pl.pallas_call(
        middle_kernel,
        in_specs=[ANY_SPEC] * 5 + [VMEM_SPEC],
        out_specs=[ANY_SPEC] * 4 + [VMEM_SPEC] * 2,
        out_shape=[
            jax.ShapeDtypeStruct((own_rows, D), bf16),
            jax.ShapeDtypeStruct((own_rows, D), f32),
            jax.ShapeDtypeStruct((rows, D), bf16),
            jax.ShapeDtypeStruct(far_all.shape, bf16),
            jax.ShapeDtypeStruct((8, D), f32),
            jax.ShapeDtypeStruct((hidden // 16, 128), f32),
        ],
        scratch_shapes=[
            pltpu.VMEM(mix.shape, bf16),
            pltpu.VMEM(tokens.shape, bf16),
            pltpu.VMEM(cot_all.shape, bf16),
            pltpu.VMEM(far_all.shape, bf16),
            pltpu.VMEM((D, VECS), bf16),
            pltpu.VMEM((own_rows, D), bf16),
            pltpu.VMEM((own_rows, D), f32),
            pltpu.VMEM((rows, D), bf16),
            pltpu.VMEM(far_all.shape, bf16),
            pltpu.VMEM((own_rows, D), bf16),
            pltpu.VMEM((own_rows, D), bf16),
            pltpu.VMEM((own_rows, D), f32),
            pltpu.VMEM((rows, D), bf16),
            pltpu.VMEM((D, rows), bf16),
            pltpu.VMEM((D, rows), bf16),
            pltpu.VMEM((rows, hidden), bf16),
            pltpu.VMEM((rows, hidden), bf16),
            pltpu.VMEM((2, own_rows, D), bf16),
            pltpu.VMEM((2, own_rows, D), bf16),
            pltpu.VMEM((own_rows, D), f32),
            pltpu.VMEM((own_rows, D), f32),
            pltpu.VMEM((8, hidden), f32),
            pltpu.VMEM((24, D), f32),
            pltpu.SemaphoreType.DMA((5, chunks)),
            pltpu.SemaphoreType.DMA((5, chunks)),
            pltpu.SemaphoreType.DMA((7,)),
            pltpu.SemaphoreType.DMA((4 * chunks + 3,)),
        ],
        compiler_params=pltpu.CompilerParams(
            collective_id=1, has_side_effects=True, vmem_limit_bytes=60 * 1024 * 1024
        ),
    )(mix, tokens, cot_all, far_all, near_all, up_all)


def last_kernel(
    count, e_ref, qu_in, qw_in, key_in, va_in, o_in, pos_in, row_in, gatt_in, far_in,
    near_in, norm_in, tok_in, gres_in, gfar_in, vec_ref, bup_ref,
    gtok_out, gq_ref, gk_ref, gv_ref, gp_ref, gup_ref, gdown_ref, gout_ref, gvec_ref, gbup_ref,
    qu_ref, qw_ref, key_ref, va_ref, pos_ref, row_ref, wout_ref, near_ref, norm_ref, tok_ref,
    gres_ref, gfar_ref, gatt_ref, o_ref, gtok_ref, e_buf, far_slots, far_along, far_back, packs, pack_slots, pack_along, pack_back,
    vec_mine, vec_other, vec_cols, vec_slots,
    bup_all, bup_slots, aug_ref, scd_ref, dqkv_ref, dk_acc, dv_acc, dpos_ref, both_ref, krow_ref,
    dqu_ref, bias_acc, normt_ref, part_send, part_recv, far_sum, pack_sums, vec_sum, bup_sum,
    vec_acc, send_sems, recv_sems, across_send, across_recv, along_send, along_recv,
    pair_send, pair_recv, e_sems, load_sems, store_sems,
):
    half = D // 2
    me, member = lax.axis_index("dp"), lax.axis_index("tensor")
    own_rows = tok_ref.shape[0]
    chunks = own_rows // CHUNK
    own0 = pl.multiple_of(member * own_rows, own_rows)
    oth0 = pl.multiple_of((1 - member) * own_rows, own_rows)
    width = qu_ref.shape[0]
    heads = width // HEAD
    score_scale = 1.0 / math.sqrt(HEAD)
    pair_width = width // 2
    vec_width = gvec_ref.shape[1]
    sources = (gfar_ref, packs.at[0], packs.at[1], vec_cols, bup_all)
    slots = (far_slots, pack_slots.at[0], pack_slots.at[1], vec_slots, bup_slots)
    totals = (far_sum, pack_sums.at[0], pack_sums.at[1], vec_sum, bup_sum)
    moves = (
        (gfar_in, gfar_ref), (gatt_in, gatt_ref), (o_in, o_ref),
        (far_in.at[:, pl.ds(far_in.shape[1] - width, width)], wout_ref),
        (norm_in, norm_ref), (qu_in, qu_ref), (qw_in, qw_ref), (key_in, key_ref), (va_in, va_ref),
        (pos_in, pos_ref), (row_in, row_ref), (near_in, near_ref), (tok_in, tok_ref),
        (gres_in, gres_ref),
    )
    loads = [
        pltpu.make_async_copy(source, target, load_sems.at[place])
        for place, (source, target) in enumerate(moves)
    ]

    def at(base, chunk):
        return pl.ds(pl.multiple_of(base + chunk * CHUNK, CHUNK), CHUNK)

    def piece(index, device):
        rows = totals[index].shape[0]
        if index == 3:
            start = pl.multiple_of(lax.div(device * vec_width, VECS) * VECS, VECS)
            return sources[index].at[:, pl.ds(start, VECS)]
        return sources[index].at[pl.ds(pl.multiple_of(device * rows, rows), rows)]

    def share_to(index, offset):
        peer = peer_at(offset)
        return pltpu.make_async_remote_copy(
            src_ref=piece(index, peer),
            dst_ref=slots[index].at[offset - 1],
            send_sem=send_sems.at[index - 3, offset - 1],
            recv_sem=recv_sems.at[index - 3, offset - 1],
            device_id={"dp": peer},
            device_id_type=MESH,
        )

    def begin_share(index):
        def begin(offset, carry):
            share_to(index, offset).start()
            return carry

        lax.fori_loop(1, count, begin, 0)

    def finish_share(index):
        total = totals[index]
        total[...] = piece(index, me)[...].astype(jnp.float32)

        def finish(offset, carry):
            share_to(index, offset).wait()
            total[...] += slots[index][offset - 1].astype(jnp.float32)
            return carry

        lax.fori_loop(1, count, finish, 0)

    levels = count // PLANE
    along_out = (far_along, pack_along.at[0], pack_along.at[1])
    along_in = (far_back, pack_back.at[0], pack_back.at[1])

    def go_across(index, offset, step):
        peer = across(me, count, offset)
        return remote(
            piece(index, along(peer, count, step)), slots[index].at[offset - 1, step],
            across_send.at[index, offset - 1, step], across_recv.at[index, offset - 1, step], peer,
        )

    def go_along(index, step):
        return remote(
            along_out[index].at[step - 1], along_in[index].at[step - 1],
            along_send.at[index, step - 1], along_recv.at[index, step - 1],
            along(me, count, step),
        )

    order = list(range(1, levels)) + [0]

    def begin_sum(index):
        for step in order:
            for offset in range(1, PLANE):
                go_across(index, offset, step).start()

    def pass_sum(index):
        for step in order:
            total = piece(index, along(me, count, step))[...].astype(jnp.float32)
            for offset in range(1, PLANE):
                go_across(index, offset, step).wait()
                total = total + slots[index][offset - 1, step].astype(jnp.float32)
            if step:
                along_out[index][step - 1] = total.astype(jnp.bfloat16)
                go_along(index, step).start()
            else:
                totals[index][...] = total

    def finish_sum(index):
        for step in range(1, levels):
            go_along(index, step).wait()
            totals[index][...] += along_in[index][step - 1].astype(jnp.float32)

    def e_copy(head, slot):
        return pltpu.make_async_copy(e_ref.at[head], e_buf.at[slot], e_sems.at[slot])

    for load in loads[:5]:
        load.start()
    e_copy(0, 0).start()
    for load in loads[5:]:
        load.start()
    greet_all(count, True)
    loads[0].wait()
    begin_sum(0)
    own_bup = pl.ds(pl.multiple_of(member * bup_ref.shape[0], 8), bup_ref.shape[0])
    bup_all[own_bup, :] = bup_ref[...]
    bup_copy = to_other(bup_ref, bup_all.at[own_bup], pair_send.at[chunks], pair_recv.at[chunks])
    bup_copy.start()

    for load in loads[1:4]:
        load.wait()
    out_mat = wout_ref[...].T
    place = lax.broadcasted_iota(jnp.int32, (AUG - HEAD, CHUNK), 0)
    for tile in range(TILES):
        rows = slice(tile * TILE, (tile + 1) * TILE)
        grads = times_transpose(out_mat, gatt_ref[rows, :])
        grads = grads.astype(jnp.bfloat16).astype(jnp.float32)
        for head in range(heads):
            lines = slice(head * HEAD, (head + 1) * HEAD)
            first = head * AUG
            inverse = o_ref[first + HEAD : first + HEAD + 1, rows]
            mixed = o_ref[first : first + HEAD, rows]
            scaled = grads[lines] * inverse
            low = (scaled * score_scale).astype(jnp.bfloat16)
            inner = -jnp.sum(low.astype(jnp.float32) * mixed, axis=0, keepdims=True)
            high = inner.astype(jnp.bfloat16).astype(jnp.float32)
            tail = jnp.where(place == 0, high, jnp.where(place == 1, inner - high, 0.0))
            scd_ref[lines, rows] = scaled.astype(jnp.bfloat16)
            aug_ref[first : first + HEAD, rows] = low
            aug_ref[first + HEAD : first + AUG, rows] = tail.astype(jnp.bfloat16)
    loads[4].wait()
    for tile in range(TILES):
        rows = slice(tile * TILE, (tile + 1) * TILE)
        normt_ref[:, rows] = norm_ref[rows, :].T
    for load in loads[5:11]:
        load.wait()

    def pack_pair(pair):
        first = pair * pair_width
        grads = jnp.concatenate(
            [
                dqkv_ref[part * width + first : part * width + first + pair_width, :]
                for part in range(3)
            ],
            axis=0,
        )
        packs[pair, :, : 3 * pair_width] = times_transpose(normt_ref[...], grads).astype(
            jnp.bfloat16
        )
        packs[pair, :, 3 * pair_width :] = dpos_ref[first : first + pair_width, :].T

    def one_head(head, carry):
        slot = lax.rem(head, 2)
        first = pl.multiple_of(head * HEAD, HEAD)
        lines = pl.ds(first, HEAD)
        more = pl.ds(pl.multiple_of(head * AUG, 16), AUG)

        @pl.when(head + 1 < heads)
        def _():
            e_copy(head + 1, 1 - slot).start()

        e_copy(head, slot).wait()
        dk_acc[...] = jnp.zeros_like(dk_acc)
        dv_acc[...] = jnp.zeros_like(dv_acc)
        filler = jnp.zeros((VECS - HEAD, key_ref.shape[1]), jnp.bfloat16)
        krow_ref[...] = jnp.concatenate([key_ref[lines, :], filler], axis=0).T

        def grads_of(tile):
            rows = slice(tile * TILE, (tile + 1) * TILE)
            weights = e_buf[slot, :, PACK[tile] : PACK[tile + 1]]
            grad_probs = contract_rows(
                aug_ref[more, rows], va_ref[more, : tiles_seen(tile) * TILE]
            )
            return (weights.astype(jnp.float32) * grad_probs).astype(jnp.bfloat16)

        def use_grads(tile, grad_scores):
            rows = slice(tile * TILE, (tile + 1) * TILE)
            seen = tiles_seen(tile) * TILE
            weights = e_buf[slot, :, PACK[tile] : PACK[tile + 1]]
            dv_acc[:, :seen] += dot_nn(scd_ref[lines, rows], weights)
            dk_acc[:, :seen] += dot_nn(qu_ref[lines, rows], grad_scores)
            dqu_ref[:, rows] = dot_nn(grad_scores, krow_ref[:seen, :]).T[:HEAD]
            turned = dot_nn(grad_scores, row_ref[:seen, :])
            part_c, part_s = turned[:, :half], turned[:, half:]
            cos_i = row_ref[rows, :half].astype(jnp.float32)
            sin_i = row_ref[rows, half:].astype(jnp.float32)
            both_ref[rows, :half] = (part_c * sin_i - part_s * cos_i).astype(jnp.bfloat16)
            both_ref[rows, half:] = (part_c * cos_i + part_s * sin_i).astype(jnp.bfloat16)

        grad_scores = grads_of(0)
        for tile in range(TILES):
            following = grads_of(tile + 1) if tile + 1 < TILES else None
            use_grads(tile, grad_scores)
            grad_scores = following
        grad_u = dqu_ref[...]
        grad_w = times_transpose(pos_ref[lines, :], both_ref[...])
        dqkv_ref[lines, :] = (grad_u + grad_w).astype(jnp.bfloat16)
        bias_acc[lines, :] = fold_cols(grad_u)
        bias_acc[pl.ds(pl.multiple_of(width + first, HEAD), HEAD), :] = fold_cols(grad_w)
        dpos_ref[lines, :] = dot_nn(qw_ref[lines, :], both_ref[...]).astype(jnp.bfloat16)
        key_lines = pl.ds(pl.multiple_of(width + first, HEAD), HEAD)
        value_lines = pl.ds(pl.multiple_of(2 * width + first, HEAD), HEAD)
        dqkv_ref[key_lines, :] = dk_acc[...].astype(jnp.bfloat16)
        dqkv_ref[value_lines, :] = dv_acc[...].astype(jnp.bfloat16)

        @pl.when(head == heads // 2 - 1)
        def _():
            pack_pair(0)
            begin_sum(1)

        @pl.when(head == heads - 2)
        def _():
            pass_sum(0)

        return carry

    lax.fori_loop(0, heads, one_head, 0)

    pack_pair(1)
    begin_sum(2)
    for load in loads[11:]:
        load.wait()
    bup_copy.wait()
    begin_share(4)

    def pass_on(chunk):
        here = at(0, chunk)
        return to_other(
            part_send.at[here], part_recv.at[here], pair_send.at[chunk], pair_recv.at[chunk]
        )

    def backward(rows):
        return dot_tt(dqkv_ref[:, rows], near_ref[:, : 3 * width])

    for chunk in range(chunks):
        part_send[at(0, chunk), :] = backward(at(oth0, chunk)).astype(jnp.bfloat16)
        pass_on(chunk).start()
    vec_rows = near_ref[:, NEAR:].astype(jnp.float32).T
    gain = vec_rows[0:1]
    vec_acc[...] = jnp.zeros_like(vec_acc)
    stores = [
        pltpu.make_async_copy(
            gtok_ref.at[at(0, chunk)], gtok_out.at[at(0, chunk)], store_sems.at[chunk]
        )
        for chunk in range(chunks)
    ]
    for chunk in range(chunks):
        here = at(0, chunk)
        part = backward(at(own0, chunk))
        pass_on(chunk).wait()
        grad = part + part_recv[here, :].astype(jnp.float32)
        normed, rate = norm_parts(tok_ref[here, :].astype(jnp.float32))
        gtok_ref[here, :] = gres_ref[here, :] + norm_grad(grad, gain, normed, rate)
        stores[chunk].start()
        vec_acc[0:8, :] += fold_rows(grad * normed)
        vec_acc[8:16, :] += fold_rows(grad)
    sums = jnp.sum(bias_acc[...].T, axis=0, keepdims=True)
    own_cols = pl.ds(pl.multiple_of(member * width, width), width)
    vec_mine[...] = jnp.zeros_like(vec_mine)
    vec_mine[0:1, :] = jnp.sum(vec_acc[0:8, :], axis=0, keepdims=True)
    vec_mine[1:2, :] = jnp.sum(vec_acc[8:16, :], axis=0, keepdims=True)
    vec_mine[2:3, own_cols] = sums[:, :width]
    vec_mine[3:4, own_cols] = sums[:, width:]
    vec_mine[4:7, :] = vec_ref[0:3, :]
    vec_copy = to_other(
        vec_mine, vec_other, pair_send.at[chunks + 1], pair_recv.at[chunks + 1]
    )
    vec_copy.start()
    pass_sum(1)
    finish_sum(0)
    gup_ref[...] = far_sum[:, : gup_ref.shape[1]]
    gdown_ref[...] = far_sum[:, gup_ref.shape[1] : 2 * gup_ref.shape[1]]
    gout_ref[...] = far_sum[:, 2 * gup_ref.shape[1] :]
    vec_copy.wait()
    both = vec_mine[...] + vec_other[...]
    vec_cols[...] = both
    begin_share(3)
    pass_sum(2)
    finish_share(4)
    gbup_ref[...] = jnp.sum(bup_sum[...], axis=0, keepdims=True)
    for pair in range(2):
        finish_sum(1 + pair)
        for part, ref in enumerate((gq_ref, gk_ref, gv_ref, gp_ref)):
            ref[:, pair * pair_width : (pair + 1) * pair_width] = pack_sums[
                pair, :, part * pair_width : (part + 1) * pair_width
            ]
    finish_share(3)
    spot = lax.rem(me * vec_width, VECS)
    picked = vec_sum[:, :vec_width]
    for start in range(vec_width, VECS, vec_width):
        picked = jnp.where(spot == start, vec_sum[:, start : start + vec_width], picked)
    gvec_ref[...] = picked
    for store in stores:
        store.wait()


def last_call(e, qu, qw, key, va, o, pos, col, gatt, far, near, norm, tok, gres, gfar, vec, bup):
    count = lax.axis_size("dp")
    levels = count // PLANE
    rows, own_rows = norm.shape[0], tok.shape[0]
    chunks = own_rows // CHUNK
    width = qu.shape[0]
    hidden = (far.shape[1] - width) // 2
    shard = D // count
    f32, bf16 = jnp.float32, jnp.bfloat16

    def shape(*dims):
        return jax.ShapeDtypeStruct(dims, f32)

    def room(*dims, kind=f32):
        return pltpu.VMEM(dims, kind)

    return pl.pallas_call(
        functools.partial(last_kernel, count),
        in_specs=[ANY_SPEC] * 15 + [VMEM_SPEC] * 2,
        out_specs=[ANY_SPEC] + [VMEM_SPEC] * 9,
        out_shape=[shape(own_rows, D)]
        + [shape(shard, width)] * 4
        + [shape(shard, hidden)] * 2
        + [shape(shard, width), shape(8, shard), shape(1, 128)],
        scratch_shapes=[
            room(width, rows, kind=bf16),
            room(width, rows, kind=bf16),
            room(width, rows, kind=bf16),
            room(va.shape[0], rows, kind=bf16),
            room(width, D, kind=bf16),
            room(rows, D, kind=bf16),
            room(D, width, kind=bf16),
            room(D, near.shape[1], kind=bf16),
            room(rows, D, kind=bf16),
            room(own_rows, D, kind=bf16),
            room(own_rows, D),
            room(D, far.shape[1], kind=bf16),
            room(rows, D, kind=bf16),
            room(o.shape[0], rows),
            room(own_rows, D),
            room(2, TILE, PACK[-1], kind=bf16),
            room(PLANE - 1, levels, shard, far.shape[1], kind=bf16),
            room(levels - 1, shard, far.shape[1], kind=bf16),
            room(levels - 1, shard, far.shape[1], kind=bf16),
            room(2, D, 2 * width, kind=bf16),
            room(2, PLANE - 1, levels, shard, 2 * width, kind=bf16),
            room(2, levels - 1, shard, 2 * width, kind=bf16),
            room(2, levels - 1, shard, 2 * width, kind=bf16),
            room(8, D),
            room(8, D),
            room(8, D),
            room(count - 1, 8, VECS),
            room(8 * count, 128),
            room(count - 1, 8, 128),
            room(va.shape[0], rows, kind=bf16),
            room(width, rows, kind=bf16),
            room(3 * width, rows, kind=bf16),
            room(HEAD, rows),
            room(HEAD, rows),
            room(width, D, kind=bf16),
            room(rows, D, kind=bf16),
            room(rows, VECS, kind=bf16),
            room(HEAD, rows),
            room(2 * width, 128),
            room(D, rows, kind=bf16),
            room(own_rows, D, kind=bf16),
            room(own_rows, D, kind=bf16),
            room(shard, far.shape[1]),
            room(2, shard, 2 * width),
            room(8, VECS),
            room(8, 128),
            room(16, D),
            pltpu.SemaphoreType.DMA((2, count - 1)),
            pltpu.SemaphoreType.DMA((2, count - 1)),
            pltpu.SemaphoreType.DMA((3, PLANE - 1, levels)),
            pltpu.SemaphoreType.DMA((3, PLANE - 1, levels)),
            pltpu.SemaphoreType.DMA((3, levels - 1)),
            pltpu.SemaphoreType.DMA((3, levels - 1)),
            pltpu.SemaphoreType.DMA((chunks + 2,)),
            pltpu.SemaphoreType.DMA((chunks + 2,)),
            pltpu.SemaphoreType.DMA((2,)),
            pltpu.SemaphoreType.DMA((14,)),
            pltpu.SemaphoreType.DMA((chunks,)),
        ],
        compiler_params=pltpu.CompilerParams(
            collective_id=2, has_side_effects=True, vmem_limit_bytes=62 * 1024 * 1024
        ),
    )(e, qu, qw, key, va, o, pos, col, gatt, far, near, norm, tok, gres, gfar, vec, bup)


def finish_kernel(number, *refs):
    for source, target in zip(refs[:number], refs[number : 2 * number]):
        target[...] = source[...]
    vec_ref, row_ref = refs[2 * number : 2 * number + 2]
    for place, target in enumerate(refs[2 * number + 2 : -1]):
        target[...] = vec_ref[place : place + 1, :]
    refs[-1][...] = row_ref[...]


def finish_call(mats, vecs, row):
    f32 = jnp.float32
    number = len(mats)
    lines = 7

    def shape(*dims):
        return jax.ShapeDtypeStruct(dims, f32)

    return pl.pallas_call(
        lambda *refs: finish_kernel(
            number, *refs[:number], *refs[number + 2 : 2 * number + 2],
            *refs[number : number + 2], *refs[2 * number + 2 :]
        ),
        in_specs=[VMEM_SPEC] * (number + 2),
        out_specs=[VMEM_SPEC] * (number + lines + 1),
        out_shape=[shape(*m.shape) for m in mats]
        + [shape(1, vecs.shape[1])] * lines
        + [shape(1, row.shape[1])],
    )(*mats, vecs, row)


def local_plain(
    tokens,
    block_ids,
    ln1_gain,
    ln1_bias,
    w_query,
    w_key,
    w_value,
    w_pos,
    bias_u,
    bias_w,
    w_out,
    ln2_gain,
    ln2_bias,
    w_up,
    bias_up,
    w_down,
    bias_down,
    cotangent,
):
    member = lax.axis_index("tensor")
    squares = (w_query, w_key, w_value, w_pos, w_out.T)
    wide = (w_up, w_down.T)
    vectors = (ln1_gain, ln1_bias, bias_u, bias_w, ln2_gain, ln2_bias, bias_down)
    near_mats = [lax.all_gather(m, "dp", axis=0, tiled=True) for m in squares]
    far_mats = [lax.all_gather(m, "dp", axis=0, tiled=True) for m in wide]
    full_vecs = [lax.all_gather(v, "dp", axis=0, tiled=True) for v in vectors]
    up_shift = lax.all_gather(bias_up, "dp", axis=0, tiled=True)
    query_mat, key_mat, value_mat, pos_mat, out_back = near_mats
    out_mat = out_back.T
    up_mat, down_back = far_mats
    down_mat = down_back.T
    gain_one, shift_one, bias_one, bias_two, gain_two, shift_two, down_shift = full_vecs
    gain_one = gain_one.astype(jnp.float32)
    shift_one = shift_one.astype(jnp.float32)
    gain_two = gain_two.astype(jnp.float32)
    shift_two = shift_two.astype(jnp.float32)
    local_width = query_mat.shape[1]
    head_count = local_width // HEAD
    hidden_local = up_mat.shape[1]
    full_hidden = up_shift.shape[0]
    own_u = lax.dynamic_slice_in_dim(
        bias_one.astype(jnp.float32), member * local_width, local_width
    )
    own_w = lax.dynamic_slice_in_dim(
        bias_two.astype(jnp.float32), member * local_width, local_width
    )
    score_scale = 1.0 / math.sqrt(HEAD)
    own_rows = tokens.shape[0]
    inputs = tokens.astype(jnp.float32)
    normed = layer_norm(inputs, gain_one, shift_one)
    rows_all = lax.all_gather(normed.astype(jnp.bfloat16), "tensor", axis=0, tiled=True)
    total_rows = rows_all.shape[0]
    queries_t = project_cols(query_mat, rows_all)
    def heads_of(array):
        return array.astype(jnp.bfloat16).reshape(head_count, HEAD, array.shape[-1])

    ids = block_ids.reshape(1, total_rows)
    sum_u = queries_t + own_u[:, None]
    sum_w = queries_t + own_w[:, None]
    fold = score_scale * LOG2E
    query_u = heads_of(sum_u)
    query_w = heads_of(sum_w)
    key_rows = heads_of(project_cols(key_mat, rows_all))
    ones = jnp.ones((head_count, 2, total_rows), jnp.bfloat16)
    blank = jnp.zeros((head_count, AUG - HEAD - 2, total_rows), jnp.bfloat16)
    value_rows = jnp.concatenate(
        [heads_of(project_cols(value_mat, rows_all)), ones, blank], axis=1
    )
    pos_rows = pos_mat.T.reshape(head_count, HEAD, D)
    table = angle_table()
    row_table = jnp.asarray(table)
    col_table = jnp.asarray(np.ascontiguousarray(table.T))
    weights, mixed_sums = attend_all(
        heads_of(sum_u * fold), heads_of(sum_w * fold), key_rows, value_rows, pos_rows, ids,
        row_table, col_table,
    )
    inv_total = 1.0 / mixed_sums[:, HEAD : HEAD + 1]
    mixed_full = mixed_sums[:, :HEAD] * inv_total
    mixed_cols = mixed_full.reshape(local_width, total_rows).astype(jnp.bfloat16)
    residual = inputs + lax.psum_scatter(
        contract_rows(
            take_cols(mixed_cols, jnp.int32(0), own_rows * lax.axis_size("tensor")), out_mat
        ).astype(jnp.bfloat16),
        "tensor",
        scatter_dimension=0,
        tiled=True,
    ).astype(jnp.float32)
    normed_two = layer_norm(residual, gain_two, shift_two)
    grad_output = cotangent.astype(jnp.float32)
    grad_down_bias = placed(jnp.sum(grad_output, axis=0), D, 0)
    own_up = lax.dynamic_slice_in_dim(
        up_shift.astype(jnp.float32), member * hidden_local, hidden_local
    )
    rows_two = lax.all_gather(normed_two.astype(jnp.bfloat16), "tensor", axis=0, tiled=True)
    hidden = jnp.dot(rows_two, up_mat, preferred_element_type=jnp.float32) + own_up
    active = jax.nn.gelu(hidden).astype(jnp.bfloat16)
    output = (
        residual
        + lax.psum_scatter(
            jnp.dot(
                take_rows(active, jnp.int32(0), own_rows * lax.axis_size("tensor")),
                down_mat,
                preferred_element_type=jnp.float32,
            ).astype(jnp.bfloat16),
            "tensor",
            scatter_dimension=0,
            tiled=True,
        ).astype(jnp.float32)
        + down_shift.astype(jnp.float32)
    )
    grad_full = lax.all_gather(cotangent, "tensor", axis=0, tiled=True)
    grad_active = times_transpose(grad_full, down_mat)
    grad_down = contract_rows(active, grad_full)
    gelu_back = jax.vjp(jax.nn.gelu, hidden)[1]
    grad_hidden = gelu_back(grad_active)[0].astype(jnp.bfloat16)
    grad_up_bias = placed(
        jnp.sum(grad_hidden, axis=0, dtype=jnp.float32), full_hidden, member * hidden_local
    )
    grad_up = contract_rows(rows_two, grad_hidden)
    grad_normed_two = lax.psum_scatter(
        times_transpose(
            take_rows(grad_hidden, jnp.int32(0), own_rows * lax.axis_size("tensor")), up_mat
        ).astype(jnp.bfloat16),
        "tensor",
        scatter_dimension=0,
        tiled=True,
    ).astype(jnp.float32)
    norm_back_two = jax.vjp(layer_norm, residual, gain_two, shift_two)[1]
    grad_resid_part, grad_gain_two, grad_shift_two = norm_back_two(grad_normed_two)
    grad_residual = grad_output + grad_resid_part
    ffn_terms = (grad_gain_two, grad_shift_two, grad_up, grad_up_bias, grad_down, grad_down_bias)
    grad_att = lax.all_gather(grad_residual.astype(jnp.bfloat16), "tensor", axis=0, tiled=True)
    grad_out_mat = jnp.dot(mixed_cols, grad_att, preferred_element_type=jnp.float32)
    grad_mixed = (
        times_transpose(out_mat, grad_att)
        .astype(jnp.bfloat16)
        .reshape(head_count, HEAD, total_rows)
    )
    grad_mixed = grad_mixed.astype(jnp.float32)
    grad_scaled = (grad_mixed * inv_total).astype(jnp.bfloat16)
    grad_low = (grad_mixed * (inv_total * score_scale)).astype(jnp.bfloat16)
    inner = -jnp.sum(grad_low.astype(jnp.float32) * mixed_full, axis=1, keepdims=True)
    inner_high = inner.astype(jnp.bfloat16)
    inner_rest = (inner - inner_high.astype(jnp.float32)).astype(jnp.bfloat16)
    grad_aug = jnp.concatenate([grad_low, inner_high, inner_rest, blank], axis=1)
    dqu, dqw, dk, dv, dpos = attend_back_all(
        weights, query_u, query_w, key_rows, value_rows, pos_rows, grad_aug, grad_scaled, col_table
    )
    grad_keys_all = dk.reshape(local_width, total_rows).astype(jnp.bfloat16)
    grad_values_all = dv.reshape(local_width, total_rows).astype(jnp.bfloat16)
    grad_pos = dpos.reshape(local_width, D).T
    grad_query_u = dqu.reshape(local_width, total_rows)
    grad_query_w = dqw.reshape(local_width, total_rows)
    grad_bias_one = placed(jnp.sum(grad_query_u, axis=1), D, member * local_width)
    grad_bias_two = placed(jnp.sum(grad_query_w, axis=1), D, member * local_width)
    grad_query = (grad_query_u + grad_query_w).astype(jnp.bfloat16)
    grad_query_mat = times_transpose(rows_all.T, grad_query)
    grad_key_mat = times_transpose(rows_all.T, grad_keys_all)
    grad_value_mat = times_transpose(rows_all.T, grad_values_all)
    first_row = jnp.int32(0)
    part_sum = times_transpose(
        take_cols(grad_query, first_row, own_rows * lax.axis_size("tensor")).T, query_mat
    )
    part_sum = part_sum + times_transpose(
        take_cols(grad_keys_all, first_row, own_rows * lax.axis_size("tensor")).T, key_mat
    )
    grad_normed = lax.psum_scatter(
        (
            part_sum
            + times_transpose(
                take_cols(grad_values_all, first_row, own_rows * lax.axis_size("tensor")).T,
                value_mat,
            )
        ).astype(jnp.bfloat16),
        "tensor",
        scatter_dimension=0,
        tiled=True,
    ).astype(jnp.float32)
    norm_back_one = jax.vjp(layer_norm, inputs, gain_one, shift_one)[1]
    grad_in_part, grad_gain_one, grad_shift_one = norm_back_one(grad_normed)
    grad_tokens = grad_residual + grad_in_part
    grad_squares = (grad_query_mat, grad_key_mat, grad_value_mat, grad_pos, grad_out_mat.T)
    grad_wides = (grad_up, grad_down.T)
    grad_vecs = jnp.stack(
        (
            grad_gain_one, grad_shift_one, grad_bias_one, grad_bias_two,
            ffn_terms[0], ffn_terms[1], ffn_terms[5],
        )
    )
    grad_vecs, grad_up_row = lax.psum((grad_vecs, ffn_terms[3]), "tensor")
    def share(array):
        return lax.psum_scatter(array, "dp", scatter_dimension=0, tiled=True)

    squares = [share(m) for m in grad_squares]
    wides = [share(m) for m in grad_wides]
    vecs = [share(v) for v in grad_vecs]
    up_part = share(grad_up_row)
    return (
        output.astype(jnp.bfloat16),
        grad_tokens,
        vecs[0],
        vecs[1],
        squares[0],
        squares[1],
        squares[2],
        squares[3],
        vecs[2],
        vecs[3],
        squares[4].T,
        vecs[4],
        vecs[5],
        wides[0],
        up_part,
        wides[1].T,
        vecs[6],
    )


def local_direct(
    tokens,
    block_ids,
    ln1_gain,
    ln1_bias,
    w_query,
    w_key,
    w_value,
    w_pos,
    bias_u,
    bias_w,
    w_out,
    ln2_gain,
    ln2_bias,
    w_up,
    bias_up,
    w_down,
    bias_down,
    cotangent,
):
    total_rows = block_ids.shape[0]
    vectors = (ln1_gain, ln1_bias, bias_u, bias_w, ln2_gain, ln2_bias, bias_down)
    table = angle_table()
    row_table = jnp.asarray(table)
    col_table = jnp.asarray(np.ascontiguousarray(table.T))
    (
        weights, query_u, query_w, key_rows, value_aug, mixed_sums, mixed_cols, rows_all, pos_back,
        near, far, up_rows, grad_full,
    ) = first_call(
        tokens,
        cotangent,
        (w_query, w_key, w_value, w_pos),
        (w_up, w_down.T, w_out.T),
        [vector.reshape(1, -1) for vector in vectors],
        bias_up.reshape(1, -1),
        block_ids.reshape(1, total_rows),
        row_table,
        col_table,
    )
    out, grad_res, grad_att, grad_far, grad_vec, grad_up_part = middle_call(
        mixed_cols, tokens, grad_full, far, near, up_rows
    )
    (
        grad_tokens, grad_query_mat, grad_key_mat, grad_value_mat, grad_pos, grad_up, grad_down,
        grad_out, grad_vecs, grad_up_row,
    ) = last_call(
        weights, query_u, query_w, key_rows, value_aug, mixed_sums, pos_back, row_table, grad_att,
        far, near, rows_all, tokens, grad_res, grad_far, grad_vec, grad_up_part,
    )
    (
        grad_query_mat, grad_key_mat, grad_value_mat, grad_pos, grad_up, grad_down, grad_out,
        *grad_vecs, grad_up_row,
    ) = finish_call(
        (grad_query_mat, grad_key_mat, grad_value_mat, grad_pos, grad_up, grad_down, grad_out),
        grad_vecs,
        grad_up_row,
    )
    grad_vecs = [vector.reshape(-1) for vector in grad_vecs]
    return (
        out,
        grad_tokens,
        grad_vecs[0],
        grad_vecs[1],
        grad_query_mat,
        grad_key_mat,
        grad_value_mat,
        grad_pos,
        grad_vecs[2],
        grad_vecs[3],
        grad_out.T,
        grad_vecs[4],
        grad_vecs[5],
        grad_up,
        grad_up_row.reshape(-1),
        grad_down.T,
        grad_vecs[6],
    )


def solution(mesh):
    in_specs = (
        P(("dp", "tensor"), None),
        P("dp"),
        P("dp"),
        P("dp"),
        P("dp", "tensor"),
        P("dp", "tensor"),
        P("dp", "tensor"),
        P("dp", "tensor"),
        P("dp"),
        P("dp"),
        P("tensor", "dp"),
        P("dp"),
        P("dp"),
        P("dp", "tensor"),
        P("dp"),
        P("tensor", "dp"),
        P("dp"),
        P(("dp", "tensor"), None),
    )
    out_specs = (
        P(("dp", "tensor"), None),
        P(("dp", "tensor"), None),
        P("dp"),
        P("dp"),
        P("dp", "tensor"),
        P("dp", "tensor"),
        P("dp", "tensor"),
        P("dp", "tensor"),
        P("dp"),
        P("dp"),
        P("tensor", "dp"),
        P("dp"),
        P("dp"),
        P("dp", "tensor"),
        P("dp"),
        P("tensor", "dp"),
        P("dp"),
    )
    pieces = D // mesh.shape["dp"]
    whole_tiles = (
        pieces % 16 == 0 and mesh.shape["tensor"] == 2 and mesh.shape["dp"] % (2 * PLANE) == 0
    )
    local = local_direct if whole_tiles else local_plain
    return jax.shard_map(local, mesh=mesh, in_specs=in_specs, out_specs=out_specs, check_vma=False)
```
